32 devices in a mesh: groups: 2 (over y), blk: 16 (over z, x, core).
Axes of the slice: x: 2, y: 2, z: 4, core: 2. Of those that a mesh axis runs over, the one named last changes fastest.
Arguments:
- activations: bfloat16 [6144, 8192], P(('groups', 'blk')), parts along dimension 0, may hold values from -6 to 6
- cotangent: bfloat16 [6144, 1024], P(('groups', 'blk')), parts along dimension 0, may hold values from -1.5 to 1.5
- token_layout_row: int32 [6144], P(('groups', 'blk')), parts along dimension 0, may hold values from 0 to 6143, as said below
- tenant_first_row: int32 [64], P('groups'), parts along dimension 0, may hold values from 0 to 6016, as said below
- frozen_value_weight: bfloat16 [8192, 1024], P('blk'), may hold values from -0.1875 to 0.1875
- adapter_down_maps: bfloat16 [96, 16, 8192], P(('groups', 'blk')), parts along dimension 0, may hold values from -0.0625 to 0.0625
- adapter_up_maps: bfloat16 [96, 16, 1024], P(('groups', 'blk')), parts along dimension 0, may hold values from -0.59765625 to 0.59765625
Outputs:
- layout_input_gradient: bfloat16 [12288, 8192], P(('groups', 'blk')), parts along dimension 0
- down_map_gradient: float32 [96, 16, 8192], P(('groups', 'blk')), parts along dimension 0
- up_map_gradient: float32 [96, 16, 1024], P(('groups', 'blk')), parts along dimension 0
The draws below stay inside these ranges and needn't reach their ends.
There are 2 independent parts, one for each index of `groups`. The reference program is written for one: setup_inputs(seed, part) draws one part's arguments, and reference() takes and returns one part's arrays. A program takes and returns all parts, laid end to end along the dimension named above; an argument that names none is the same for every part. Nothing has to cross between parts.
Inputs may be any that keep to these rules, and one draw needn't show every extreme that they name: `token_layout_row`: distinct rows. Each token lies in a block of its tenant, and a tenant's tokens fill its rows in order from its first row, so only its last block has empty rows. Of the tokens of one device at most 24 lie in the 384 rows of any one device, and some device receives exactly 24 from every device. `tenant_first_row`: distinct multiples of 128, rising with the tenant id around the closed order of blocks. Every tenant has one block or more. The blocks of one tenant lie on at most 5 consecutive devices counted cyclically, and some tenant's lie on exactly that many.
All inputs are finite; a program needn't handle non-finite values.
Results may differ from the reference program's by a relative error of at most 0.0029.
Values may be sent and summed in bfloat16 or wider, within the bound.
No kernel may reach another device: no remote copies, remote signals or barrier semaphores. Data moves between devices by JAX's collectives and lax.ppermute only.
A program may use at most 128 MiB of HBM per device.

```python
import jax
import jax.numpy as jnp
from jax import lax

MODEL_WIDTH = 8192
VALUE_OUTPUTS = 1024
ADAPTER_RANK = 16
BLOCK = 128
HOPS = 4
LAST_FILL = 31
BPD = 3
TENANTS = 32
LAYOUT_BLOCKS = 48
LAYOUT_ROWS = 6144
TOK_DEV = 192
TOKENS = 3072
N_BLK = 16


def layout(key):
    key_order, key_turn, key_fill, key_pair, key_place = jax.random.split(key, 5)
    order = jax.random.permutation(key_order, TENANTS)
    spare = LAYOUT_BLOCKS - TENANTS - HOPS * BPD
    others = TENANTS - 1
    ranks = jnp.arange(others, dtype=jnp.int32)
    extra = spare // others + (ranks < spare % others).astype(jnp.int32)
    counts = jnp.ones((TENANTS,), jnp.int32).at[order[1:]].add(extra).at[order[0]].add(HOPS * BPD)
    ends = jnp.cumsum(counts).astype(jnp.int32)
    firsts = ends - counts
    heavy_first = firsts[order[0]]
    turned = (BPD - 1 - heavy_first) % BPD + BPD * jax.random.randint(key_turn, (), 0, N_BLK)
    starts = (firsts + turned) % LAYOUT_BLOCKS
    pairing = jax.random.permutation(key_pair, TENANTS)
    spread = jax.random.randint(key_fill, (TENANTS // 2,), 0, LAST_FILL + 1).astype(jnp.int32)
    tail = jnp.zeros((TENANTS,), jnp.int32).at[pairing[0::2]].set(LAST_FILL + spread)
    tail = tail.at[pairing[1::2]].set(LAST_FILL - spread)
    filled = (counts - 1) * BLOCK + 1 + tail
    all_rows = jnp.arange(LAYOUT_ROWS, dtype=jnp.int32)
    relative = (all_rows // BLOCK - turned) % LAYOUT_BLOCKS
    owning_tenant = jnp.searchsorted(ends, relative, side='right').astype(jnp.int32)
    inside = (relative - firsts[owning_tenant]) * BLOCK + all_rows % BLOCK
    used = inside < filled[owning_tenant]
    picked = jnp.nonzero(used, size=TOKENS)[0].astype(jnp.int32)
    serial = jnp.arange(TOKENS, dtype=jnp.int32)
    source = serial % N_BLK
    place = serial // N_BLK
    scores = jax.random.randint(key_place, (N_BLK, TOK_DEV), 0, 1 << 20).astype(jnp.int32) * TOK_DEV
    scores = scores + jnp.arange(TOK_DEV, dtype=jnp.int32)[None, :]
    shuffle = jnp.argsort(scores, axis=1).astype(jnp.int32)
    target = source * TOK_DEV + shuffle[source, place]
    rows_out = jnp.zeros((TOKENS,), jnp.int32).at[target].set(picked)
    return (rows_out, (starts * BLOCK).astype(jnp.int32))


def draw_token_layout_row(key, part):
    rows_out, offsets = layout(key)
    return rows_out


def draw_tenant_first_row(key, part):
    rows_out, offsets = layout(key)
    return offsets


def block_scale(rng, shape, shards, low, high):
    loudness = 1.0
    for dim, parts in shards:
        draws = jax.random.uniform(jax.random.fold_in(jax.random.fold_in(rng, 6), dim), (parts,), jnp.float32, low / len(shards), high / len(shards))
        loudness = loudness * jnp.repeat(jnp.exp(draws), shape[dim] // parts).reshape((-1,) + (1,) * (len(shape) - 1 - dim))
    return loudness


def scatter_about(stream_key, shape, deviation, bound, cuts=(), held_as=jnp.bfloat16):
    entries = jax.random.normal(stream_key, shape, jnp.float32) * deviation
    if len(cuts) > 0:
        entries = block_scale(stream_key, shape, cuts, -0.22, 0.18) * entries
    return jnp.clip(entries, min=-bound, max=bound).astype(held_as)


def setup_inputs(seed: int = 0, part: int = 0) -> dict:
    streams_of = jax.random.split(jax.random.key(seed), 8)
    part_keys = jax.random.split(jax.random.fold_in(streams_of[7], part), 8)
    return {
        "activations": scatter_about(part_keys[0], (TOKENS, MODEL_WIDTH), 1.0, 6.0, ((0, 16),)),
        "cotangent": scatter_about(part_keys[1], (TOKENS, VALUE_OUTPUTS), 0.25, 1.5, ((0, 16),)),
        "token_layout_row": draw_token_layout_row(jax.random.fold_in(jax.random.fold_in(streams_of[7], part), 71), part),
        "tenant_first_row": draw_tenant_first_row(jax.random.fold_in(jax.random.fold_in(streams_of[7], part), 71), part),
        "frozen_value_weight": scatter_about(streams_of[4], (MODEL_WIDTH, VALUE_OUTPUTS), VALUE_OUTPUTS ** -0.5, 0.1875, ((0, 16),)),
        "adapter_down_maps": scatter_about(part_keys[5], (LAYOUT_BLOCKS, ADAPTER_RANK, MODEL_WIDTH), MODEL_WIDTH ** -0.5, 0.0625, ((0, 16),)),
        "adapter_up_maps": scatter_about(part_keys[6], (LAYOUT_BLOCKS, ADAPTER_RANK, VALUE_OUTPUTS), 0.1, 0.59765625, ((0, 16),)),
    }


adapter_scale = 2.0


def reference(activations, cotangent, token_layout_row, tenant_first_row, frozen_value_weight, adapter_down_maps, adapter_up_maps):
    act_rows = jnp.zeros((LAYOUT_ROWS, MODEL_WIDTH), jnp.bfloat16).at[token_layout_row].set(activations)
    cot_rows = jnp.zeros((LAYOUT_ROWS, VALUE_OUTPUTS), jnp.bfloat16).at[token_layout_row].set(cotangent)
    start_ids = (tenant_first_row // BLOCK).astype(jnp.int32)
    block_numbers = jnp.arange(LAYOUT_BLOCKS, dtype=jnp.int32)
    latest = jnp.max(jnp.where(start_ids[None, :] <= block_numbers[:, None], start_ids[None, :], -1), axis=1)
    segment_begin = jnp.where(latest >= 0, latest, jnp.max(start_ids)).astype(jnp.int32)

    def single_block(block_id):
        act_block = lax.dynamic_slice_in_dim(act_rows, block_id * BLOCK, BLOCK, 0)
        cot_block = lax.dynamic_slice_in_dim(cot_rows, block_id * BLOCK, BLOCK, 0)
        owning_tenant = segment_begin[block_id]
        adapter_down_matrix = adapter_down_maps[owning_tenant]
        adapter_up_matrix = adapter_up_maps[owning_tenant]
        hidden = jnp.dot(act_block, adapter_down_matrix.T, preferred_element_type=jnp.float32).astype(jnp.bfloat16)
        incoming_gradient = jnp.dot(cot_block, adapter_up_matrix.T, preferred_element_type=jnp.float32).astype(jnp.bfloat16)
        partial_down = jnp.dot(incoming_gradient.T, act_block, preferred_element_type=jnp.float32)
        partial_up = jnp.dot(hidden.T, cot_block, preferred_element_type=jnp.float32)
        adapter_block = (adapter_scale * jnp.dot(incoming_gradient, adapter_down_matrix, preferred_element_type=jnp.float32)).astype(jnp.bfloat16)
        return partial_down, partial_up, adapter_block

    partial_down_list, partial_up_list, adapter_block_list = lax.map(single_block, block_numbers)
    down_map_gradient = adapter_scale * jax.ops.segment_sum(partial_down_list, segment_begin, num_segments=LAYOUT_BLOCKS)
    up_map_gradient = adapter_scale * jax.ops.segment_sum(partial_up_list, segment_begin, num_segments=LAYOUT_BLOCKS)
    adapter_rows = adapter_block_list.reshape(LAYOUT_ROWS, MODEL_WIDTH)
    token_gradient = jnp.dot(cotangent, frozen_value_weight.T, preferred_element_type=jnp.float32)
    token_gradient = token_gradient + adapter_rows[token_layout_row].astype(jnp.float32)
    layout_input_gradient = jnp.zeros((LAYOUT_ROWS, MODEL_WIDTH), jnp.bfloat16).at[token_layout_row].set(token_gradient.astype(jnp.bfloat16))
    return layout_input_gradient, down_map_gradient, up_map_gradient
```

```python
import jax
import jax.numpy as jnp
from jax import lax
from jax.sharding import PartitionSpec as P

BLOCK = 128
HOPS = 4
LANES = 128

adapter_scale = 2.0


def moved(value, steps):
    count = lax.axis_size("blk")
    return lax.ppermute(value, "blk", [(i, (i + steps) % count) for i in range(count)])


def dot(a, b, dims, precision=None):
    return lax.dot_general(
        a, b, (dims, ((), ())), preferred_element_type=jnp.float32, precision=precision
    )


def starts_of(blocks, start_ids):
    latest = jnp.max(
        jnp.where(start_ids[None, :] <= blocks[:, None], start_ids[None, :], -1), axis=1
    )
    return jnp.where(latest >= 0, latest, jnp.max(start_ids))


def folded(wide, rank):
    total = wide[:, :LANES]
    for k in range(LANES, wide.shape[1], LANES):
        total = total + wide[:, k : k + LANES]
    fold = jnp.arange(LANES)[:, None] % rank == jnp.arange(rank)[None, :]
    return dot(total, fold.astype(jnp.float32), ((1,), (0,)), lax.Precision.HIGHEST)


def spread(narrow, slot, width):
    rank = narrow.shape[1]
    columns = jnp.arange(width, dtype=jnp.int32)
    tiles = (columns[None, :] % rank == jnp.arange(rank)[:, None]).astype(jnp.bfloat16)
    wide = dot(narrow, tiles, ((1,), (0,)))
    return jnp.where(columns[None, :] // rank == slot[:, None], wide, 0.0).astype(jnp.bfloat16)


def chosen(wide, slot, rank):
    columns = jnp.arange(wide.shape[1], dtype=jnp.int32)
    return folded(jnp.where(columns[None, :] // rank == slot[:, None], wide, 0.0), rank)


def feature_share(act, maps, grad_in, slot):
    rank = grad_in.shape[1]
    rows, width = act.shape[0], maps.shape[0]
    limit = max(8, (24 << 20) // (6 * width))
    pieces = 1
    while rows // pieces > limit or rows % pieces:
        pieces += 1

    def part(act, grad_in, slot):
        hidden = chosen(dot(act, maps, ((1,), (1,))), slot, rank)
        return hidden, dot(spread(grad_in, slot, width), act, ((0,), (0,)))

    if pieces == 1:
        return part(act, grad_in, slot)

    def step(total, xs):
        hidden, down = part(*xs)
        return total + down, hidden

    total, hidden = lax.scan(
        step,
        jnp.zeros((width, act.shape[1]), jnp.float32),
        (
            act.reshape(pieces, rows // pieces, -1),
            grad_in.reshape(pieces, rows // pieces, -1),
            slot.reshape(pieces, rows // pieces),
        ),
    )
    return hidden.reshape(rows, rank), total


def local(
    activations,
    cotangent,
    token_layout_row,
    tenant_first_row,
    frozen_value_weight,
    adapter_down_maps,
    adapter_up_maps,
):
    devices = lax.axis_size("blk")
    device = lax.axis_index("blk")
    tokens = activations.shape[0]
    resident, rank, width = adapter_down_maps.shape
    out_width = cotangent.shape[1]
    resident_rows = resident * BLOCK
    slots = resident * devices
    slot_cap = resident_rows // devices
    start_ids = tenant_first_row // BLOCK

    weight = lax.all_gather(frozen_value_weight, "blk", axis=0, tiled=True)
    rows_all = lax.all_gather(token_layout_row, "blk", axis=0, tiled=True)
    up_all = lax.all_gather(adapter_up_maps, "blk", axis=0, tiled=True)
    up_all = up_all.reshape(slots * rank, out_width)
    act_f = lax.all_to_all(activations, "blk", split_axis=1, concat_axis=0, tiled=True)
    down_flat = adapter_down_maps.reshape(resident * rank, width)
    maps_f = lax.all_to_all(down_flat, "blk", split_axis=1, concat_axis=0, tiled=True)

    target = token_layout_row // resident_rows
    order = jnp.arange(tokens, dtype=jnp.int32)
    before = (target[:, None] == target[None, :]) & (order[None, :] < order[:, None])
    slot = target * slot_cap + jnp.sum(before.astype(jnp.int32), axis=1)
    places = jnp.arange(resident_rows, dtype=jnp.int32)
    send = (places[:, None] == slot[None, :]).astype(jnp.bfloat16)
    send_cot = dot(send, cotangent, ((1,), (0,))).astype(jnp.bfloat16)
    recv_cot = lax.all_to_all(send_cot, "blk", split_axis=0, concat_axis=0, tiled=True)

    first_row = device * resident_rows
    row_of = (rows_all[None, :] - first_row == places[:, None]).astype(jnp.bfloat16)
    mine = (rows_all // resident_rows == device).reshape(devices, tokens)
    earlier = (order[:, None] < order[None, :]).astype(jnp.bfloat16)
    place = dot(mine.astype(jnp.bfloat16), earlier, ((1,), (0,))).astype(jnp.int32)
    place = place + slot_cap * jnp.arange(devices, dtype=jnp.int32)[:, None]
    place = jnp.where(mine, place, -1).reshape(-1)
    place_of = (place[:, None] == places[None, :]).astype(jnp.bfloat16)
    arrange = dot(row_of, place_of, ((1,), (0,))).astype(jnp.bfloat16)
    cot_rows = dot(arrange, recv_cot, ((1,), (0,))).astype(jnp.bfloat16)

    own_slot = starts_of(token_layout_row // BLOCK, start_ids)
    all_up = dot(cotangent, up_all, ((1,), (1,)))
    grad_in = chosen(all_up, own_slot, rank).astype(jnp.bfloat16)
    grad_all = lax.all_gather(grad_in, "blk", axis=0, tiled=True)

    slot_all = starts_of(rows_all // BLOCK, start_ids)
    hidden, down_f = feature_share(act_f, maps_f, grad_all, slot_all)
    down_home = lax.all_to_all(
        (adapter_scale * down_f).astype(jnp.bfloat16), "blk", split_axis=0, concat_axis=1, tiled=True
    )
    down_map_gradient = down_home.astype(jnp.float32).reshape(resident, rank, width)
    hidden = lax.psum(hidden, "blk").astype(jnp.bfloat16)

    first_block = device * resident
    block_numbers = first_block + jnp.arange(resident, dtype=jnp.int32)
    begin = starts_of(block_numbers, start_ids)
    is_local = (begin >= first_block) & (begin <= block_numbers)
    home_slot = jnp.clip(begin - first_block, 0, resident - 1)
    last_map = lax.dynamic_index_in_dim(
        adapter_down_maps, home_slot[resident - 1], 0, keepdims=False
    )
    carried = jnp.zeros_like(last_map)
    for step in range(1, HOPS + 1):
        home = (device - step) % devices
        carried = jnp.where(begin[0] // resident == home, moved(last_map, step), carried)

    grad_rows = dot(row_of, grad_all, ((1,), (0,))).astype(jnp.bfloat16)
    hidden_rows = dot(row_of, hidden, ((1,), (0,))).astype(jnp.bfloat16)
    adapter_rows = []
    up_parts = []
    for b in range(resident):
        rows = slice(b * BLOCK, (b + 1) * BLOCK)
        down = carried
        for k in range(b + 1):
            down = jnp.where(is_local[b] & (home_slot[b] == k), adapter_down_maps[k], down)
        adapter_rows.append(
            (adapter_scale * dot(grad_rows[rows], down, ((1,), (0,)))).astype(jnp.bfloat16)
        )
        up_parts.append(dot(hidden_rows[rows], cot_rows[rows], ((0,), (0,))))
    adapter_rows = jnp.concatenate(adapter_rows, axis=0)

    tail = sum(jnp.where(is_local[b], 0.0, up_parts[b]) for b in range(resident))
    far = jnp.zeros_like(tail)
    for step in range(1, HOPS + 1):
        other = (device + step) % devices * resident
        theirs = starts_of(other[None], start_ids)[0]
        far = far + jnp.where(theirs // resident == device, moved(tail, -step), 0.0)
    up_grads = []
    for k in range(resident):
        total = jnp.where(begin[resident - 1] == first_block + k, far, 0.0)
        for b in range(resident):
            total = total + jnp.where(is_local[b] & (home_slot[b] == k), up_parts[b], 0.0)
        up_grads.append(adapter_scale * total)
    up_map_gradient = jnp.stack(up_grads)

    frozen_rows = dot(cot_rows, weight, ((1,), (1,)))
    layout_input_gradient = (frozen_rows + adapter_rows.astype(jnp.float32)).astype(jnp.bfloat16)
    return (layout_input_gradient, down_map_gradient, up_map_gradient)


def solution(mesh):
    return jax.shard_map(
        local,
        mesh=mesh,
        in_specs=(
            P(("groups", "blk"), None),
            P(("groups", "blk"), None),
            P(("groups", "blk")),
            P("groups"),
            P("blk", None),
            P(("groups", "blk"), None, None),
            P(("groups", "blk"), None, None),
        ),
        out_specs=(
            P(("groups", "blk"), None),
            P(("groups", "blk"), None, None),
            P(("groups", "blk"), None, None),
        ),
        check_vma=False,
    )
```

```python
import jax
import jax.numpy as jnp
from jax import lax
from jax.experimental import pallas as pl
from jax.experimental.pallas import tpu as pltpu
from jax.sharding import PartitionSpec as P

BLOCK = 128
HOPS = 4
LANES = 128

adapter_scale = 2.0


def moved(value, steps):
    count = lax.axis_size("blk")
    return lax.ppermute(value, "blk", [(i, (i + steps) % count) for i in range(count)])


def to_all(value):
    count = lax.axis_size("blk")
    copies = jnp.broadcast_to(value[None], (count,) + value.shape)
    return lax.all_to_all(copies, "blk", split_axis=0, concat_axis=0)


def gathered_half(weight):
    count, groups = lax.axis_size("blk"), lax.axis_size("groups")
    part = weight.shape[0] // groups
    piece = lax.dynamic_slice_in_dim(weight, lax.axis_index("groups") * part, part, 0)
    same_core = [
        [g * count + chip * 2 + core for chip in range(count // 2) for g in range(groups)]
        for core in range(2)
    ]
    return lax.all_gather(
        piece, ("groups", "blk"), axis_index_groups=same_core, axis=0, tiled=True
    )


def half_kernel(side, cot, grad, weight, down, *rest):
    out = rest[-1]
    rank = grad.shape[1]
    frozen = dot(cot[...], weight[...], ((1,), (1,)))
    for b in range(cot.shape[0] // BLOCK):
        rows = slice(b * BLOCK, (b + 1) * BLOCK)
        lora = adapter_scale * dot(
            grad[rows, :], down[b * rank : (b + 1) * rank, :], ((1,), (0,))
        )
        out[rows, :] = (frozen[rows] + lora.astype(jnp.bfloat16).astype(jnp.float32)).astype(
            jnp.bfloat16
        )


def write_half(side, cot, grad, weight, down, stripe, out=None):
    rows, depth = cot.shape
    width = down.shape[1]
    specs = [
        pl.BlockSpec((rows, depth), lambda j, side: (0, 0)),
        pl.BlockSpec(grad.shape, lambda j, side: (0, 0)),
        pl.BlockSpec((stripe, depth), lambda j, side: (j, 0)),
        pl.BlockSpec((down.shape[0], stripe), lambda j, side: (0, 2 * j + side[0])),
    ]
    args = [side, cot, grad, weight, down]
    alias = {}
    if out is not None:
        specs.append(pl.BlockSpec(memory_space=pl.ANY))
        args.append(out)
        alias = {5: 0}
    return pl.pallas_call(
        half_kernel,
        grid_spec=pltpu.PrefetchScalarGridSpec(
            num_scalar_prefetch=1,
            grid=(weight.shape[0] // stripe,),
            in_specs=specs,
            out_specs=pl.BlockSpec((rows, stripe), lambda j, side: (0, 2 * j + side[0])),
        ),
        out_shape=jax.ShapeDtypeStruct((rows, width), jnp.bfloat16),
        input_output_aliases=alias,
        cost_estimate=pl.CostEstimate(
            flops=rows * depth * width,
            bytes_accessed=weight.size * 2 + rows * width,
            transcendentals=0,
        ),
        compiler_params=pltpu.CompilerParams(vmem_limit_bytes=24 << 20),
    )(*args)


def dot(a, b, dims, precision=None):
    return lax.dot_general(
        a, b, (dims, ((), ())), preferred_element_type=jnp.float32, precision=precision
    )


def starts_of(blocks, start_ids):
    latest = jnp.max(
        jnp.where(start_ids[None, :] <= blocks[:, None], start_ids[None, :], -1), axis=1
    )
    return jnp.where(latest >= 0, latest, jnp.max(start_ids))


def folded(wide, rank):
    total = wide[:, :LANES]
    for k in range(LANES, wide.shape[1], LANES):
        total = total + wide[:, k : k + LANES]
    fold = jnp.arange(LANES)[:, None] % rank == jnp.arange(rank)[None, :]
    return dot(total, fold.astype(jnp.float32), ((1,), (0,)), lax.Precision.HIGHEST)


def spread(narrow, slot, width):
    rank = narrow.shape[1]
    columns = jnp.arange(width, dtype=jnp.int32)
    tiles = (columns[None, :] % rank == jnp.arange(rank)[:, None]).astype(jnp.bfloat16)
    wide = dot(narrow, tiles, ((1,), (0,)))
    return jnp.where(columns[None, :] // rank == slot[:, None], wide, 0.0).astype(jnp.bfloat16)


def chosen(wide, slot, rank):
    columns = jnp.arange(wide.shape[1], dtype=jnp.int32)
    return folded(jnp.where(columns[None, :] // rank == slot[:, None], wide, 0.0), rank)


def feature_share(act, maps, grad_in, slot):
    rank = grad_in.shape[1]
    rows, width = act.shape[0], maps.shape[0]
    limit = max(8, (24 << 20) // (6 * width))
    pieces = 1
    while rows // pieces > limit or rows % pieces:
        pieces += 1

    def part(act, grad_in, slot):
        hidden = chosen(dot(act, maps, ((1,), (1,))), slot, rank)
        return hidden, dot(spread(grad_in, slot, width), act, ((0,), (0,)))

    if pieces == 1:
        return part(act, grad_in, slot)

    def step(total, xs):
        hidden, down = part(*xs)
        return total + down, hidden

    total, hidden = lax.scan(
        step,
        jnp.zeros((width, act.shape[1]), jnp.float32),
        (
            act.reshape(pieces, rows // pieces, -1),
            grad_in.reshape(pieces, rows // pieces, -1),
            slot.reshape(pieces, rows // pieces),
        ),
    )
    return hidden.reshape(rows, rank), total


def local(
    activations,
    cotangent,
    token_layout_row,
    tenant_first_row,
    frozen_value_weight,
    adapter_down_maps,
    adapter_up_maps,
):
    devices = lax.axis_size("blk")
    device = lax.axis_index("blk")
    tokens = activations.shape[0]
    resident, rank, width = adapter_down_maps.shape
    out_width = cotangent.shape[1]
    resident_rows = resident * BLOCK
    slots = resident * devices
    slot_cap = resident_rows // devices
    start_ids = tenant_first_row // BLOCK

    core = device % 2
    own_half = gathered_half(frozen_value_weight)
    swap = [(i, i ^ 1) for i in range(devices)]
    other_half = lax.ppermute(own_half, "blk", swap)
    rows_all = to_all(token_layout_row).reshape(-1)
    up_all = lax.all_gather(adapter_up_maps, "blk", axis=0, tiled=True)
    up_all = up_all.reshape(slots * rank, out_width)
    act_f = lax.all_to_all(activations, "blk", split_axis=1, concat_axis=0, tiled=True)
    down_flat = adapter_down_maps.reshape(resident * rank, width)
    maps_f = lax.all_to_all(down_flat, "blk", split_axis=1, concat_axis=0, tiled=True)

    target = token_layout_row // resident_rows
    order = jnp.arange(tokens, dtype=jnp.int32)
    before = (target[:, None] == target[None, :]) & (order[None, :] < order[:, None])
    slot = target * slot_cap + jnp.sum(before.astype(jnp.int32), axis=1)
    places = jnp.arange(resident_rows, dtype=jnp.int32)
    send = (places[:, None] == slot[None, :]).astype(jnp.bfloat16)
    send_cot = dot(send, cotangent, ((1,), (0,))).astype(jnp.bfloat16)
    recv_cot = lax.all_to_all(send_cot, "blk", split_axis=0, concat_axis=0, tiled=True)

    first_row = device * resident_rows
    row_of = (rows_all[None, :] - first_row == places[:, None]).astype(jnp.bfloat16)
    mine = (rows_all // resident_rows == device).reshape(devices, tokens)
    earlier = (order[:, None] < order[None, :]).astype(jnp.bfloat16)
    place = dot(mine.astype(jnp.bfloat16), earlier, ((1,), (0,))).astype(jnp.int32)
    place = place + slot_cap * jnp.arange(devices, dtype=jnp.int32)[:, None]
    place = jnp.where(mine, place, -1).reshape(-1)
    place_of = (place[:, None] == places[None, :]).astype(jnp.bfloat16)
    arrange = dot(row_of, place_of, ((1,), (0,))).astype(jnp.bfloat16)
    cot_rows = dot(arrange, recv_cot, ((1,), (0,))).astype(jnp.bfloat16)

    own_slot = starts_of(token_layout_row // BLOCK, start_ids)
    all_up = dot(cotangent, up_all, ((1,), (1,)))
    grad_in = chosen(all_up, own_slot, rank).astype(jnp.bfloat16)
    grad_all = to_all(grad_in.T).transpose(0, 2, 1).reshape(-1, rank)

    slot_all = starts_of(rows_all // BLOCK, start_ids)
    hidden, down_f = feature_share(act_f, maps_f, grad_all, slot_all)
    down_home = lax.all_to_all(
        (adapter_scale * down_f).astype(jnp.bfloat16), "blk", split_axis=0, concat_axis=1, tiled=True
    )
    down_map_gradient = down_home.astype(jnp.float32).reshape(resident, rank, width)
    hidden = hidden.reshape(devices, tokens, rank).transpose(0, 2, 1)
    hidden = lax.all_to_all(hidden, "blk", split_axis=0, concat_axis=0)
    hidden = to_all(jnp.sum(hidden, axis=0).astype(jnp.bfloat16))
    hidden = hidden.transpose(0, 2, 1).reshape(-1, rank)

    first_block = device * resident
    block_numbers = first_block + jnp.arange(resident, dtype=jnp.int32)
    begin = starts_of(block_numbers, start_ids)
    is_local = (begin >= first_block) & (begin <= block_numbers)
    home_slot = jnp.clip(begin - first_block, 0, resident - 1)
    last_map = lax.dynamic_index_in_dim(
        adapter_down_maps, home_slot[resident - 1], 0, keepdims=False
    )
    carried = jnp.zeros_like(last_map)
    for step in range(1, HOPS + 1):
        home = (device - step) % devices
        carried = jnp.where(begin[0] // resident == home, moved(last_map, step), carried)

    grad_rows = dot(row_of, grad_all, ((1,), (0,))).astype(jnp.bfloat16)
    hidden_rows = dot(row_of, hidden, ((1,), (0,))).astype(jnp.bfloat16)
    down_blocks = []
    up_parts = []
    for b in range(resident):
        rows = slice(b * BLOCK, (b + 1) * BLOCK)
        down = carried
        for k in range(b + 1):
            down = jnp.where(is_local[b] & (home_slot[b] == k), adapter_down_maps[k], down)
        down_blocks.append(down)
        up_parts.append(dot(hidden_rows[rows], cot_rows[rows], ((0,), (0,))))
    down_blocks = jnp.concatenate(down_blocks, axis=0)

    tail = sum(jnp.where(is_local[b], 0.0, up_parts[b]) for b in range(resident))
    far = jnp.zeros_like(tail)
    for step in range(1, HOPS + 1):
        other = (device + step) % devices * resident
        theirs = starts_of(other[None], start_ids)[0]
        far = far + jnp.where(theirs // resident == device, moved(tail, -step), 0.0)
    up_grads = []
    for k in range(resident):
        total = jnp.where(begin[resident - 1] == first_block + k, far, 0.0)
        for b in range(resident):
            total = total + jnp.where(is_local[b] & (home_slot[b] == k), up_parts[b], 0.0)
        up_grads.append(adapter_scale * total)
    up_map_gradient = jnp.stack(up_grads)

    stripe = frozen_value_weight.shape[0]
    if stripe % LANES == 0:
        own = core.astype(jnp.int32).reshape(1)
        out = write_half(own, cot_rows, grad_rows, own_half, down_blocks, stripe)
        out = write_half(1 - own, cot_rows, grad_rows, other_half, down_blocks, stripe, out)
    else:
        first = jnp.where(core == 0, own_half, other_half)
        second = jnp.where(core == 0, other_half, own_half)
        pairs = [half.reshape(-1, 1, stripe, out_width) for half in (first, second)]
        weight = jnp.concatenate(pairs, axis=1).reshape(width, out_width)
        out = dot(cot_rows, weight, ((1,), (1,)))
        lora = [
            dot(
                grad_rows[b * BLOCK : (b + 1) * BLOCK],
                down_blocks[b * rank : (b + 1) * rank],
                ((1,), (0,)),
            )
            for b in range(resident)
        ]
        lora = (adapter_scale * jnp.concatenate(lora, axis=0)).astype(jnp.bfloat16)
        out = (out + lora.astype(jnp.float32)).astype(jnp.bfloat16)
    return (out, down_map_gradient, up_map_gradient)


def solution(mesh):
    return jax.shard_map(
        local,
        mesh=mesh,
        in_specs=(
            P(("groups", "blk"), None),
            P(("groups", "blk"), None),
            P(("groups", "blk")),
            P("groups"),
            P("blk", None),
            P(("groups", "blk"), None, None),
            P(("groups", "blk"), None, None),
        ),
        out_specs=(
            P(("groups", "blk"), None),
            P(("groups", "blk"), None, None),
            P(("groups", "blk"), None, None),
        ),
        check_vma=False,
    )
```

```python
import jax
import jax.numpy as jnp
from jax import lax
from jax.experimental import pallas as pl
from jax.experimental.pallas import tpu as pltpu
from jax.sharding import PartitionSpec as P

BLOCK = 128
HOPS = 4
LANES = 128
DIGIT = 64

adapter_scale = 2.0


def permuted(value, pairs):
    return lax.ppermute(value, "blk", pairs)


def moved(value, steps):
    count = lax.axis_size("blk")
    return permuted(value, [(i, (i + steps) % count) for i in range(count)])


def to_all(value):
    count = lax.axis_size("blk")
    copies = jnp.broadcast_to(value[None], (count,) + value.shape)
    return lax.all_to_all(copies, "blk", split_axis=0, concat_axis=0)


def dot(a, b, dims):
    return lax.dot_general(a, b, (dims, ((), ())), preferred_element_type=jnp.float32)


def starts_of(blocks, start_ids):
    latest = jnp.max(
        jnp.where(start_ids[None, :] <= blocks[:, None], start_ids[None, :], -1), axis=1
    )
    return jnp.where(latest >= 0, latest, jnp.max(start_ids))


def as_digits(rows):
    return jnp.stack(
        [rows % DIGIT, rows // DIGIT % DIGIT, rows // (DIGIT * DIGIT)]
    ).astype(jnp.bfloat16)


def from_digits(digits):
    low, middle, high = digits.astype(jnp.int32)
    return (high * DIGIT + middle) * DIGIT + low


def ring_shards(weight):
    count, device = lax.axis_size("blk"), lax.axis_index("blk")
    chips = count // 2
    order = list(range(0, chips, 2)) + list(range(chips - 1, 0, -2))
    place = [order.index(chip) for chip in range(chips)]
    chip, core = device // 2, device % 2

    def along(step):
        return [
            (2 * c + k, 2 * order[(place[c] + step) % chips] + k)
            for c in range(chips)
            for k in range(2)
        ]

    def origin(step):
        return jnp.array(order, jnp.int32)[
            (jnp.array(place, jnp.int32)[chip] + step + chips) % chips
        ]

    def both(piece, source, per, part):
        other = permuted(piece, [(i, i ^ 1) for i in range(count)])
        return [
            (piece, (2 * source + core) * per + part),
            (other, (2 * source + 1 - core) * per + part),
        ]

    groups = [both(weight, chip, 1, 0)]
    up = down = weight
    for step in range(1, chips // 2):
        up, down = permuted(up, along(1)), permuted(down, along(-1))
        groups.append(both(up, origin(-step), 1, 0) + both(down, origin(step), 1, 0))
    half = weight.shape[0] // 2
    up, down = permuted(up[:half], along(1)), permuted(down[half:], along(-1))
    far = origin(chips // 2)
    groups.append(both(up, far, 2, 0) + both(down, far, 2, 1))
    return groups


def stripes_kernel(where, cot, grad, down, *rest):
    out = rest[-1]
    rank = grad.shape[1]

    def product(weight):
        frozen = dot(cot[...], weight[...], ((1,), (1,)))
        for b in range(cot.shape[0] // BLOCK):
            rows = slice(b * BLOCK, (b + 1) * BLOCK)
            lora = adapter_scale * dot(
                grad[rows, :], down[b * rank : (b + 1) * rank, :], ((1,), (0,))
            )
            lora = lora.astype(jnp.bfloat16).astype(jnp.float32)
            out[rows, :] = (frozen[rows] + lora).astype(jnp.bfloat16)

    for number in range(where.shape[0]):
        pl.when(pl.program_id(0) == number)(lambda weight=rest[number]: product(weight))


def write_stripes(group, cot, grad, down, out=None):
    rows, depth = cot.shape
    width = down.shape[1]
    count = len(group)
    stripe = group[0][0].shape[0]
    where = jnp.stack([place for _, place in group]).astype(jnp.int32)
    specs = [
        pl.BlockSpec((rows, depth), lambda j, where: (0, 0)),
        pl.BlockSpec(grad.shape, lambda j, where: (0, 0)),
        pl.BlockSpec((down.shape[0], stripe), lambda j, where: (0, where[j])),
    ] + [pl.BlockSpec((stripe, depth), lambda j, where: (0, 0)) for _ in group]
    args = [where, cot, grad, down] + [piece for piece, _ in group]
    alias = {}
    if out is not None:
        specs.append(pl.BlockSpec(memory_space=pl.ANY))
        args.append(out)
        alias = {len(args) - 1: 0}
    return pl.pallas_call(
        stripes_kernel,
        grid_spec=pltpu.PrefetchScalarGridSpec(
            num_scalar_prefetch=1,
            grid=(count,),
            in_specs=specs,
            out_specs=pl.BlockSpec((rows, stripe), lambda j, where: (0, where[j])),
        ),
        out_shape=jax.ShapeDtypeStruct((rows, width), jnp.bfloat16),
        input_output_aliases=alias,
        cost_estimate=pl.CostEstimate(
            flops=2 * rows * depth * stripe * count,
            bytes_accessed=2 * (depth + rows) * stripe * count,
            transcendentals=0,
        ),
        compiler_params=pltpu.CompilerParams(vmem_limit_bytes=32 << 20),
    )(*args)


def small_stripes(groups, cot, grad, down, rank):
    depth = cot.shape[1]
    weight = jnp.zeros((down.shape[1], depth), jnp.bfloat16)
    for piece, place in sum(groups, []):
        weight = lax.dynamic_update_slice(weight, piece, (place * piece.shape[0], 0))
    lora = [
        dot(
            grad[b * BLOCK : (b + 1) * BLOCK], down[b * rank : (b + 1) * rank], ((1,), (0,))
        )
        for b in range(cot.shape[0] // BLOCK)
    ]
    lora = (adapter_scale * jnp.concatenate(lora, axis=0)).astype(jnp.bfloat16)
    out = dot(cot, weight, ((1,), (1,)))
    return (out + lora.astype(jnp.float32)).astype(jnp.bfloat16)


def slot_chunks(width):
    size = min(width, 768)
    while width % size:
        size -= LANES
    return [slice(k, k + size) for k in range(0, width, size)]


def own_rows(slot, first, size, rank):
    index = first // rank + lax.broadcasted_iota(jnp.int32, (size // rank, rank, 1), 0)
    return index == slot[...][None]


def hidden_kernel(act, maps, slot, out):
    rank = out.shape[0]
    tokens = out.shape[1] // act.shape[0]
    rows = jnp.concatenate([act[k, :tokens, :] for k in range(act.shape[0])], axis=0)
    total = jnp.zeros(out.shape, jnp.float32)
    for part in slot_chunks(maps.shape[0]):
        size = part.stop - part.start
        each = dot(maps[part, :], rows, ((1,), (1,))).reshape(size // rank, rank, -1)
        total += jnp.sum(
            jnp.where(own_rows(slot, part.start, size, rank), each, 0.0), axis=0
        )
    out[...] = total


def down_kernel(act, grad, slot, out, total):
    rank = grad.shape[0]
    tokens = grad.shape[1] // act.shape[0]
    rows = jnp.concatenate([act[k, :tokens, :] for k in range(act.shape[0])], axis=0)
    step = pl.program_id(0)

    @pl.when(step == 0)
    def _():
        total[...] = jnp.zeros_like(total)

    wide = grad[...].astype(jnp.float32)[None]
    for part in slot_chunks(total.shape[0]):
        size = part.stop - part.start
        placed = jnp.where(own_rows(slot, part.start, size, rank), wide, 0.0)
        placed = placed.reshape(size, -1).astype(jnp.bfloat16)
        total[part, :] += dot(placed, rows, ((1,), (0,)))

    @pl.when(step == pl.num_programs(0) - 1)
    def _():
        out[...] = (adapter_scale * total[...]).astype(out.dtype)


def feature_calls(devices, tokens, packed, features, width, rank):
    pair = 2
    while pair * tokens % LANES:
        pair *= 2
    grid = (devices // pair,)
    act = pl.BlockSpec((pair, packed, features), lambda j: (j, 0, 0))
    slot = pl.BlockSpec((1, pair * tokens), lambda j: (0, j))
    small = pl.BlockSpec((rank, pair * tokens), lambda j: (0, j))
    whole = pl.BlockSpec((width, features), lambda j: (0, 0))
    every = devices * tokens
    cost = pl.CostEstimate(
        flops=2 * every * width * features,
        bytes_accessed=2 * every * features,
        transcendentals=0,
    )
    params = pltpu.CompilerParams(vmem_limit_bytes=48 << 20)
    hidden = pl.pallas_call(
        hidden_kernel,
        grid=grid,
        in_specs=[act, whole, slot],
        out_specs=small,
        out_shape=jax.ShapeDtypeStruct((rank, every), jnp.float32),
        cost_estimate=cost,
        compiler_params=params,
    )
    down = pl.pallas_call(
        down_kernel,
        grid=grid,
        in_specs=[act, small, slot],
        out_specs=whole,
        out_shape=jax.ShapeDtypeStruct((width, features), jnp.bfloat16),
        scratch_shapes=[pltpu.VMEM((width, features), jnp.float32)],
        cost_estimate=cost,
        compiler_params=params,
    )
    return hidden, down


def local(
    activations,
    cotangent,
    token_layout_row,
    tenant_first_row,
    frozen_value_weight,
    adapter_down_maps,
    adapter_up_maps,
):
    devices = lax.axis_size("blk")
    device = lax.axis_index("blk")
    tokens = activations.shape[0]
    resident, rank, width = adapter_down_maps.shape
    out_width = cotangent.shape[1]
    features = width // devices
    resident_rows = resident * BLOCK
    slots = resident * devices
    slot_cap = resident_rows // devices
    start_ids = tenant_first_row // BLOCK

    groups = ring_shards(frozen_value_weight)

    padded = -(-tokens // LANES) * LANES
    digits = as_digits(jnp.pad(token_layout_row, (0, padded - tokens)))
    digits = digits.reshape(-1, LANES)
    count = digits.shape[0]
    digits = jnp.pad(digits, ((0, resident * rank - count), (0, 0)))
    shared = jnp.concatenate([adapter_up_maps.reshape(-1, out_width), digits], axis=1)
    shared = lax.all_gather(shared, "blk", axis=0, tiled=False)
    up_all = shared[:, :, :out_width].reshape(slots * rank, out_width)
    rows_all = shared[:, :count, out_width:].reshape(devices, 3, padded)[:, :, :tokens]
    rows_all = from_digits(rows_all.transpose(1, 0, 2)).reshape(-1)

    target = token_layout_row // resident_rows
    order = jnp.arange(tokens, dtype=jnp.int32)
    before = (target[:, None] == target[None, :]) & (order[None, :] < order[:, None])
    place = target * slot_cap + jnp.sum(before.astype(jnp.int32), axis=1)
    places = jnp.arange(resident_rows, dtype=jnp.int32)
    send = (places[:, None] == place[None, :]).astype(jnp.bfloat16)
    send_cot = dot(send, cotangent, ((1,), (0,))).astype(jnp.bfloat16)
    send_cot = send_cot.reshape(devices, slot_cap, out_width)
    folds = out_width // features
    packed = [
        activations.reshape(tokens, devices, features).transpose(1, 0, 2),
        adapter_down_maps.reshape(-1, devices, features).transpose(1, 0, 2),
    ] + [send_cot[:, :, k * features : (k + 1) * features] for k in range(folds)]
    packed = jnp.concatenate(packed, axis=1)
    received = lax.all_to_all(packed, "blk", split_axis=0, concat_axis=0)
    maps_f = received[:, tokens : tokens + resident * rank].reshape(slots * rank, features)
    recv_cot = received[:, tokens + resident * rank :]
    recv_cot = [
        recv_cot[:, k * slot_cap : (k + 1) * slot_cap].reshape(resident_rows, features)
        for k in range(folds)
    ]

    first_row = device * resident_rows
    row_of = (rows_all[None, :] - first_row == places[:, None]).astype(jnp.bfloat16)
    mine = (rows_all // resident_rows == device).reshape(devices, tokens)
    earlier = (order[:, None] < order[None, :]).astype(jnp.bfloat16)
    at = dot(mine.astype(jnp.bfloat16), earlier, ((1,), (0,))).astype(jnp.int32)
    at = at + slot_cap * jnp.arange(devices, dtype=jnp.int32)[:, None]
    at = jnp.where(mine, at, -1).reshape(-1)
    arrange = dot(
        row_of, (at[:, None] == places[None, :]).astype(jnp.bfloat16), ((1,), (0,))
    ).astype(jnp.bfloat16)
    cot_rows = jnp.concatenate(
        [dot(arrange, part, ((1,), (0,))).astype(jnp.bfloat16) for part in recv_cot], axis=1
    )

    own_slot = starts_of(token_layout_row // BLOCK, start_ids)
    every_up = dot(up_all, cotangent, ((1,), (1,))).reshape(slots, rank, tokens)
    own = jnp.arange(slots, dtype=jnp.int32)[:, None, None] == own_slot[None, None, :]
    grad_in = jnp.sum(jnp.where(own, every_up, 0.0), axis=0).astype(jnp.bfloat16)
    grad_all = to_all(grad_in).transpose(1, 0, 2).reshape(rank, -1)

    slot_all = starts_of(rows_all // BLOCK, start_ids)[None]
    hidden_call, down_call = feature_calls(
        devices, tokens, packed.shape[1], features, slots * rank, rank
    )
    hidden = hidden_call(received, maps_f, slot_all)
    hidden = hidden.reshape(rank, devices, tokens).transpose(1, 0, 2)
    hidden = lax.all_to_all(hidden, "blk", split_axis=0, concat_axis=0)
    hidden = to_all(jnp.sum(hidden, axis=0).astype(jnp.bfloat16))
    hidden = hidden.transpose(1, 0, 2).reshape(rank, -1)
    down_f = down_call(received, grad_all, slot_all)
    down_home = lax.all_to_all(down_f, "blk", split_axis=0, concat_axis=1, tiled=True)
    down_map_gradient = down_home.astype(jnp.float32).reshape(resident, rank, width)

    first_block = device * resident
    block_numbers = first_block + jnp.arange(resident, dtype=jnp.int32)
    begin = starts_of(block_numbers, start_ids)
    is_local = (begin >= first_block) & (begin <= block_numbers)
    home_slot = jnp.clip(begin - first_block, 0, resident - 1)
    last_map = lax.dynamic_index_in_dim(
        adapter_down_maps, home_slot[resident - 1], 0, keepdims=False
    )
    carried = jnp.zeros_like(last_map)
    for step in range(1, HOPS + 1):
        home = (device - step) % devices
        carried = jnp.where(begin[0] // resident == home, moved(last_map, step), carried)

    grad_rows = dot(row_of, grad_all, ((1,), (1,))).astype(jnp.bfloat16)
    hidden_rows = dot(row_of, hidden, ((1,), (1,))).astype(jnp.bfloat16)
    down_blocks = []
    up_parts = []
    for b in range(resident):
        rows = slice(b * BLOCK, (b + 1) * BLOCK)
        down = carried
        for k in range(b + 1):
            down = jnp.where(is_local[b] & (home_slot[b] == k), adapter_down_maps[k], down)
        down_blocks.append(down)
        up_parts.append(dot(hidden_rows[rows], cot_rows[rows], ((0,), (0,))))
    down_blocks = jnp.concatenate(down_blocks, axis=0)

    tail = sum(jnp.where(is_local[b], 0.0, up_parts[b]) for b in range(resident))
    far = jnp.zeros_like(tail)
    for step in range(1, HOPS + 1):
        other = (device + step) % devices * resident
        theirs = starts_of(other[None], start_ids)[0]
        far = far + jnp.where(theirs // resident == device, moved(tail, -step), 0.0)
    up_grads = []
    for k in range(resident):
        total = jnp.where(begin[resident - 1] == first_block + k, far, 0.0)
        for b in range(resident):
            total = total + jnp.where(is_local[b] & (home_slot[b] == k), up_parts[b], 0.0)
        up_grads.append(adapter_scale * total)
    up_map_gradient = jnp.stack(up_grads)

    if frozen_value_weight.shape[0] % (2 * LANES) == 0:
        out = None
        for group in groups:
            out = write_stripes(group, cot_rows, grad_rows, down_blocks, out)
    else:
        out = small_stripes(groups, cot_rows, grad_rows, down_blocks, rank)
    return (out, down_map_gradient, up_map_gradient)


def solution(mesh):
    return jax.shard_map(
        local,
        mesh=mesh,
        in_specs=(
            P(("groups", "blk"), None),
            P(("groups", "blk"), None),
            P(("groups", "blk")),
            P("groups"),
            P("blk", None),
            P(("groups", "blk"), None, None),
            P(("groups", "blk"), None, None),
        ),
        out_specs=(
            P(("groups", "blk"), None),
            P(("groups", "blk"), None, None),
            P(("groups", "blk"), None, None),
        ),
        check_vma=False,
    )
```

```python
import jax
import jax.numpy as jnp
from jax import lax
from jax.experimental import pallas as pl
from jax.experimental.pallas import tpu as pltpu
from jax.sharding import PartitionSpec as P

BLOCK = 128
HOPS = 4
LANES = 128
DIGIT = 64

adapter_scale = 2.0


def permuted(value, pairs):
    return lax.ppermute(value, "blk", pairs)


def moved(value, steps):
    count = lax.axis_size("blk")
    return permuted(value, [(i, (i + steps) % count) for i in range(count)])


def to_all(value):
    count = lax.axis_size("blk")
    copies = jnp.broadcast_to(value[None], (count,) + value.shape)
    return lax.all_to_all(copies, "blk", split_axis=0, concat_axis=0)


def dot(a, b, dims):
    return lax.dot_general(a, b, (dims, ((), ())), preferred_element_type=jnp.float32)


def starts_of(blocks, start_ids):
    latest = jnp.max(
        jnp.where(start_ids[None, :] <= blocks[:, None], start_ids[None, :], -1), axis=1
    )
    return jnp.where(latest >= 0, latest, jnp.max(start_ids))


def as_digits(rows):
    return jnp.stack(
        [rows % DIGIT, rows // DIGIT % DIGIT, rows // (DIGIT * DIGIT)]
    ).astype(jnp.bfloat16)


def from_digits(digits):
    low, middle, high = digits.astype(jnp.int32)
    return (high * DIGIT + middle) * DIGIT + low


def ring_shards(weight):
    count, device = lax.axis_size("blk"), lax.axis_index("blk")
    chips = count // 2
    order = list(range(0, chips, 2)) + list(range(chips - 1, 0, -2))
    place = [order.index(chip) for chip in range(chips)]
    chip, core = device // 2, device % 2

    def along(step):
        return [
            (2 * c + k, 2 * order[(place[c] + step) % chips] + k)
            for c in range(chips)
            for k in range(2)
        ]

    def origin(step):
        return jnp.array(order, jnp.int32)[
            (jnp.array(place, jnp.int32)[chip] + step + chips) % chips
        ]

    def both(piece, source, per, part):
        other = permuted(piece, [(i, i ^ 1) for i in range(count)])
        return [
            (piece, (2 * source + core) * per + part),
            (other, (2 * source + 1 - core) * per + part),
        ]

    groups = [both(weight, chip, 1, 0)]
    up = down = weight
    for step in range(1, chips // 2):
        up, down = permuted(up, along(1)), permuted(down, along(-1))
        groups.append(both(up, origin(-step), 1, 0) + both(down, origin(step), 1, 0))
    half = weight.shape[0] // 2
    up, down = permuted(up[:half], along(1)), permuted(down[half:], along(-1))
    far = origin(chips // 2)
    groups.append(both(up, far, 2, 0) + both(down, far, 2, 1))
    return groups


def stripes_kernel(where, cot, grad, down, *rest):
    out = rest[-1]
    rank = grad.shape[1]

    def product(weight):
        frozen = dot(cot[...], weight[...], ((1,), (1,)))
        for b in range(cot.shape[0] // BLOCK):
            rows = slice(b * BLOCK, (b + 1) * BLOCK)
            lora = adapter_scale * dot(
                grad[rows, :], down[b * rank : (b + 1) * rank, :], ((1,), (0,))
            )
            lora = lora.astype(jnp.bfloat16).astype(jnp.float32)
            out[rows, :] = (frozen[rows] + lora).astype(jnp.bfloat16)

    for number in range(where.shape[0]):
        pl.when(pl.program_id(0) == number)(lambda weight=rest[number]: product(weight))


def write_stripes(group, cot, grad, down, out=None):
    rows, depth = cot.shape
    width = down.shape[1]
    count = len(group)
    stripe = group[0][0].shape[0]
    where = jnp.stack([place for _, place in group]).astype(jnp.int32)
    specs = [
        pl.BlockSpec((rows, depth), lambda j, where: (0, 0)),
        pl.BlockSpec(grad.shape, lambda j, where: (0, 0)),
        pl.BlockSpec((down.shape[0], stripe), lambda j, where: (0, where[j])),
    ] + [pl.BlockSpec((stripe, depth), lambda j, where: (0, 0)) for _ in group]
    args = [where, cot, grad, down] + [piece for piece, _ in group]
    alias = {}
    if out is not None:
        specs.append(pl.BlockSpec(memory_space=pl.ANY))
        args.append(out)
        alias = {len(args) - 1: 0}
    return pl.pallas_call(
        stripes_kernel,
        grid_spec=pltpu.PrefetchScalarGridSpec(
            num_scalar_prefetch=1,
            grid=(count,),
            in_specs=specs,
            out_specs=pl.BlockSpec((rows, stripe), lambda j, where: (0, where[j])),
        ),
        out_shape=jax.ShapeDtypeStruct((rows, width), jnp.bfloat16),
        input_output_aliases=alias,
        cost_estimate=pl.CostEstimate(
            flops=2 * rows * depth * stripe * count,
            bytes_accessed=2 * (depth + rows) * stripe * count,
            transcendentals=0,
        ),
        compiler_params=pltpu.CompilerParams(vmem_limit_bytes=32 << 20),
    )(*args)


def small_stripes(groups, cot, grad, down, rank):
    depth = cot.shape[1]
    weight = jnp.zeros((down.shape[1], depth), jnp.bfloat16)
    for piece, place in sum(groups, []):
        weight = lax.dynamic_update_slice(weight, piece, (place * piece.shape[0], 0))
    lora = [
        dot(
            grad[b * BLOCK : (b + 1) * BLOCK], down[b * rank : (b + 1) * rank], ((1,), (0,))
        )
        for b in range(cot.shape[0] // BLOCK)
    ]
    lora = (adapter_scale * jnp.concatenate(lora, axis=0)).astype(jnp.bfloat16)
    out = dot(cot, weight, ((1,), (1,)))
    return (out + lora.astype(jnp.float32)).astype(jnp.bfloat16)


def pack_kernel(rows, act, maps, cot, out):
    tokens, features = act.shape
    cap = (out.shape[1] - tokens - maps.shape[0]) * features // cot.shape[1]
    target = pl.program_id(0)
    resident_rows = cap * pl.num_programs(0)
    mine = rows[...] // resident_rows == target
    first = lax.broadcasted_iota(jnp.int32, (tokens, tokens), 0)
    later = lax.broadcasted_iota(jnp.int32, (tokens, tokens), 1)
    earlier = jnp.where(first < later, 1.0, 0.0).astype(jnp.bfloat16)
    chosen = jnp.broadcast_to(jnp.where(mine, 1.0, 0.0), (8, tokens)).astype(jnp.bfloat16)
    place = dot(chosen, earlier, ((1,), (0,)))[:1].astype(jnp.int32)
    place = jnp.where(mine, place, -1)
    send = lax.broadcasted_iota(jnp.int32, (cap, tokens), 0) == place
    send = jnp.where(send, 1.0, 0.0).astype(jnp.bfloat16)
    sent = [
        dot(send, cot[:, k : k + features], ((1,), (0,)))
        for k in range(0, cot.shape[1], features)
    ]
    out[0, :tokens, :] = act[...]
    out[0, tokens : tokens + maps.shape[0], :] = maps[...]
    out[0, tokens + maps.shape[0] :, :] = jnp.concatenate(sent, axis=0).astype(out.dtype)


def pack(rows, act, maps, cot, devices, cap):
    tokens, width = act.shape
    features = width // devices
    total = tokens + maps.shape[0] + cap * cot.shape[1] // features
    return pl.pallas_call(
        pack_kernel,
        grid=(devices,),
        in_specs=[
            pl.BlockSpec((1, tokens), lambda j: (0, 0)),
            pl.BlockSpec((tokens, features), lambda j: (0, j)),
            pl.BlockSpec((maps.shape[0], features), lambda j: (0, j)),
            pl.BlockSpec(cot.shape, lambda j: (0, 0)),
        ],
        out_specs=pl.BlockSpec((1, total, features), lambda j: (j, 0, 0)),
        out_shape=jax.ShapeDtypeStruct((devices, total, features), act.dtype),
        cost_estimate=pl.CostEstimate(
            flops=2 * devices * cap * tokens * cot.shape[1],
            bytes_accessed=4 * devices * total * features,
            transcendentals=0,
        ),
        compiler_params=pltpu.CompilerParams(vmem_limit_bytes=24 << 20),
    )(rows[None], act, maps, cot)


def slot_chunks(width):
    size = min(width, 768)
    while width % size:
        size -= LANES
    return [slice(k, k + size) for k in range(0, width, size)]


def own_rows(slot, first, size, rank):
    index = first // rank + lax.broadcasted_iota(jnp.int32, (size // rank, rank, 1), 0)
    return index == slot[...][None]


def hidden_kernel(act, maps, slot, out):
    rank = out.shape[0]
    tokens = out.shape[1] // act.shape[0]
    rows = jnp.concatenate([act[k, :tokens, :] for k in range(act.shape[0])], axis=0)
    total = jnp.zeros(out.shape, jnp.float32)
    for part in slot_chunks(maps.shape[0]):
        size = part.stop - part.start
        each = dot(maps[part, :], rows, ((1,), (1,))).reshape(size // rank, rank, -1)
        total += jnp.sum(
            jnp.where(own_rows(slot, part.start, size, rank), each, 0.0), axis=0
        )
    out[...] = total


def down_kernel(act, grad, slot, out, total):
    rank = grad.shape[0]
    tokens = grad.shape[1] // act.shape[0]
    rows = jnp.concatenate([act[k, :tokens, :] for k in range(act.shape[0])], axis=0)
    step = pl.program_id(0)

    @pl.when(step == 0)
    def _():
        total[...] = jnp.zeros_like(total)

    wide = grad[...].astype(jnp.float32)[None]
    for part in slot_chunks(total.shape[0]):
        size = part.stop - part.start
        placed = jnp.where(own_rows(slot, part.start, size, rank), wide, 0.0)
        placed = placed.reshape(size, -1).astype(jnp.bfloat16)
        total[part, :] += dot(placed, rows, ((1,), (0,)))

    @pl.when(step == pl.num_programs(0) - 1)
    def _():
        out[...] = (adapter_scale * total[...]).astype(out.dtype)


def feature_calls(devices, tokens, packed, features, width, rank):
    pair = 2
    while pair * tokens % LANES:
        pair *= 2
    grid = (devices // pair,)
    act = pl.BlockSpec((pair, packed, features), lambda j: (j, 0, 0))
    slot = pl.BlockSpec((1, pair * tokens), lambda j: (0, j))
    small = pl.BlockSpec((rank, pair * tokens), lambda j: (0, j))
    whole = pl.BlockSpec((width, features), lambda j: (0, 0))
    every = devices * tokens
    cost = pl.CostEstimate(
        flops=2 * every * width * features,
        bytes_accessed=2 * every * features,
        transcendentals=0,
    )
    params = pltpu.CompilerParams(vmem_limit_bytes=48 << 20)
    hidden = pl.pallas_call(
        hidden_kernel,
        grid=grid,
        in_specs=[act, whole, slot],
        out_specs=small,
        out_shape=jax.ShapeDtypeStruct((rank, every), jnp.float32),
        cost_estimate=cost,
        compiler_params=params,
    )
    down = pl.pallas_call(
        down_kernel,
        grid=grid,
        in_specs=[act, small, slot],
        out_specs=whole,
        out_shape=jax.ShapeDtypeStruct((width, features), jnp.bfloat16),
        scratch_shapes=[pltpu.VMEM((width, features), jnp.float32)],
        cost_estimate=cost,
        compiler_params=params,
    )
    return hidden, down


def local(
    activations,
    cotangent,
    token_layout_row,
    tenant_first_row,
    frozen_value_weight,
    adapter_down_maps,
    adapter_up_maps,
):
    devices = lax.axis_size("blk")
    device = lax.axis_index("blk")
    tokens = activations.shape[0]
    resident, rank, width = adapter_down_maps.shape
    out_width = cotangent.shape[1]
    features = width // devices
    resident_rows = resident * BLOCK
    slots = resident * devices
    slot_cap = resident_rows // devices
    start_ids = tenant_first_row // BLOCK

    groups = ring_shards(frozen_value_weight)

    padded = -(-tokens // LANES) * LANES
    digits = as_digits(jnp.pad(token_layout_row, (0, padded - tokens)))
    digits = digits.reshape(-1, LANES)
    count = digits.shape[0]
    digits = jnp.pad(digits, ((0, resident * rank - count), (0, 0)))
    shared = jnp.concatenate([adapter_up_maps.reshape(-1, out_width), digits], axis=1)
    shared = lax.all_gather(shared, "blk", axis=0, tiled=False)
    up_all = shared[:, :, :out_width].reshape(slots * rank, out_width)
    rows_all = shared[:, :count, out_width:].reshape(devices, 3, padded)[:, :, :tokens]
    rows_all = from_digits(rows_all.transpose(1, 0, 2)).reshape(-1)

    own_slot = starts_of(token_layout_row // BLOCK, start_ids)
    every_up = dot(up_all, cotangent, ((1,), (1,))).reshape(slots, rank, tokens)
    own = jnp.arange(slots, dtype=jnp.int32)[:, None, None] == own_slot[None, None, :]
    grad_in = jnp.sum(jnp.where(own, every_up, 0.0), axis=0).astype(jnp.bfloat16)

    order = jnp.arange(tokens, dtype=jnp.int32)
    places = jnp.arange(resident_rows, dtype=jnp.int32)
    folds = out_width // features
    flat_maps = adapter_down_maps.reshape(-1, width)
    if features % LANES == 0 and slot_cap % 8 == 0:
        packed = pack(token_layout_row, activations, flat_maps, cotangent, devices, slot_cap)
    else:
        target = token_layout_row // resident_rows
        before = (target[:, None] == target[None, :]) & (order[None, :] < order[:, None])
        place = target * slot_cap + jnp.sum(before.astype(jnp.int32), axis=1)
        send = (places[:, None] == place[None, :]).astype(jnp.bfloat16)
        send_cot = dot(send, cotangent, ((1,), (0,))).astype(jnp.bfloat16)
        send_cot = send_cot.reshape(devices, slot_cap, out_width)
        packed = [
            activations.reshape(tokens, devices, features).transpose(1, 0, 2),
            flat_maps.reshape(-1, devices, features).transpose(1, 0, 2),
        ] + [send_cot[:, :, k * features : (k + 1) * features] for k in range(folds)]
        packed = jnp.concatenate(packed, axis=1)
    received = lax.all_to_all(packed, "blk", split_axis=0, concat_axis=0)
    grad_in, received = lax.optimization_barrier((grad_in, received))
    maps_f = received[:, tokens : tokens + resident * rank].reshape(slots * rank, features)
    recv_cot = received[:, tokens + resident * rank :]
    recv_cot = [
        recv_cot[:, k * slot_cap : (k + 1) * slot_cap].reshape(resident_rows, features)
        for k in range(folds)
    ]

    first_row = device * resident_rows
    row_of = (rows_all[None, :] - first_row == places[:, None]).astype(jnp.bfloat16)
    mine = (rows_all // resident_rows == device).reshape(devices, tokens)
    earlier = (order[:, None] < order[None, :]).astype(jnp.bfloat16)
    at = dot(mine.astype(jnp.bfloat16), earlier, ((1,), (0,))).astype(jnp.int32)
    at = at + slot_cap * jnp.arange(devices, dtype=jnp.int32)[:, None]
    at = jnp.where(mine, at, -1).reshape(-1)
    arrange = dot(
        row_of, (at[:, None] == places[None, :]).astype(jnp.bfloat16), ((1,), (0,))
    ).astype(jnp.bfloat16)
    cot_rows = jnp.concatenate(
        [dot(arrange, part, ((1,), (0,))).astype(jnp.bfloat16) for part in recv_cot], axis=1
    )

    grad_all = to_all(grad_in).transpose(1, 0, 2).reshape(rank, -1)
    slot_all = starts_of(rows_all // BLOCK, start_ids)[None]
    hidden_call, down_call = feature_calls(
        devices, tokens, packed.shape[1], features, slots * rank, rank
    )
    hidden = hidden_call(received, maps_f, slot_all)
    hidden = hidden.reshape(rank, devices, tokens).transpose(1, 0, 2)
    hidden = lax.all_to_all(hidden, "blk", split_axis=0, concat_axis=0)
    hidden = to_all(jnp.sum(hidden, axis=0).astype(jnp.bfloat16))
    hidden = hidden.transpose(1, 0, 2).reshape(rank, -1)
    down_f = down_call(received, grad_all, slot_all)
    down_home = lax.all_to_all(down_f, "blk", split_axis=0, concat_axis=1, tiled=True)
    down_map_gradient = down_home.astype(jnp.float32).reshape(resident, rank, width)

    first_block = device * resident
    block_numbers = first_block + jnp.arange(resident, dtype=jnp.int32)
    begin = starts_of(block_numbers, start_ids)
    is_local = (begin >= first_block) & (begin <= block_numbers)
    home_slot = jnp.clip(begin - first_block, 0, resident - 1)
    last_map = lax.dynamic_index_in_dim(
        adapter_down_maps, home_slot[resident - 1], 0, keepdims=False
    )
    carried = jnp.zeros_like(last_map)
    for step in range(1, HOPS + 1):
        home = (device - step) % devices
        carried = jnp.where(begin[0] // resident == home, moved(last_map, step), carried)

    grad_rows = dot(row_of, grad_all, ((1,), (1,))).astype(jnp.bfloat16)
    hidden_rows = dot(row_of, hidden, ((1,), (1,))).astype(jnp.bfloat16)
    down_blocks = []
    up_parts = []
    for b in range(resident):
        rows = slice(b * BLOCK, (b + 1) * BLOCK)
        down = carried
        for k in range(b + 1):
            down = jnp.where(is_local[b] & (home_slot[b] == k), adapter_down_maps[k], down)
        down_blocks.append(down)
        up_parts.append(dot(hidden_rows[rows], cot_rows[rows], ((0,), (0,))))
    down_blocks = jnp.concatenate(down_blocks, axis=0)

    tail = sum(jnp.where(is_local[b], 0.0, up_parts[b]) for b in range(resident))
    far = jnp.zeros_like(tail)
    for step in range(1, HOPS + 1):
        other = (device + step) % devices * resident
        theirs = starts_of(other[None], start_ids)[0]
        far = far + jnp.where(theirs // resident == device, moved(tail, -step), 0.0)
    up_grads = []
    for k in range(resident):
        total = jnp.where(begin[resident - 1] == first_block + k, far, 0.0)
        for b in range(resident):
            total = total + jnp.where(is_local[b] & (home_slot[b] == k), up_parts[b], 0.0)
        up_grads.append(adapter_scale * total)
    up_map_gradient = jnp.stack(up_grads)

    if frozen_value_weight.shape[0] % (2 * LANES) == 0:
        out = None
        for group in groups:
            out = write_stripes(group, cot_rows, grad_rows, down_blocks, out)
    else:
        out = small_stripes(groups, cot_rows, grad_rows, down_blocks, rank)
    return (out, down_map_gradient, up_map_gradient)


def solution(mesh):
    return jax.shard_map(
        local,
        mesh=mesh,
        in_specs=(
            P(("groups", "blk"), None),
            P(("groups", "blk"), None),
            P(("groups", "blk")),
            P("groups"),
            P("blk", None),
            P(("groups", "blk"), None, None),
            P(("groups", "blk"), None, None),
        ),
        out_specs=(
            P(("groups", "blk"), None),
            P(("groups", "blk"), None, None),
            P(("groups", "blk"), None, None),
        ),
        check_vma=False,
    )
```

```python
import jax
import jax.numpy as jnp
from jax import lax
from jax.experimental import pallas as pl
from jax.experimental.pallas import tpu as pltpu
from jax.sharding import PartitionSpec as P

BLOCK = 128
HOPS = 4
LANES = 128
DIGIT = 64

adapter_scale = 2.0


def permuted(value, pairs):
    return lax.ppermute(value, "blk", pairs)


def moved(value, steps):
    count = lax.axis_size("blk")
    return permuted(value, [(i, (i + steps) % count) for i in range(count)])


def to_all(value):
    count = lax.axis_size("blk")
    copies = jnp.broadcast_to(value[None], (count,) + value.shape)
    return lax.all_to_all(copies, "blk", split_axis=0, concat_axis=0)


def after(value, *others):
    anywhere = pl.BlockSpec(memory_space=pl.ANY)
    return pl.pallas_call(
        lambda *refs: None,
        in_specs=[anywhere] * (1 + len(others)),
        out_specs=anywhere,
        out_shape=jax.ShapeDtypeStruct(value.shape, value.dtype),
        input_output_aliases={0: 0},
        cost_estimate=pl.CostEstimate(flops=0, bytes_accessed=0, transcendentals=0),
    )(value, *others)


def dot(a, b, dims):
    return lax.dot_general(a, b, (dims, ((), ())), preferred_element_type=jnp.float32)


def starts_of(blocks, start_ids):
    latest = jnp.max(
        jnp.where(start_ids[None, :] <= blocks[:, None], start_ids[None, :], -1), axis=1
    )
    return jnp.where(latest >= 0, latest, jnp.max(start_ids))


def as_digits(rows):
    return jnp.stack(
        [rows % DIGIT, rows // DIGIT % DIGIT, rows // (DIGIT * DIGIT)]
    ).astype(jnp.bfloat16)


def from_digits(digits):
    low, middle, high = digits.astype(jnp.int32)
    return (high * DIGIT + middle) * DIGIT + low


def ring_shards(weight, ties):
    count, device = lax.axis_size("blk"), lax.axis_index("blk")
    chips = count // 2
    order = list(range(0, chips, 2)) + list(range(chips - 1, 0, -2))
    place = [order.index(chip) for chip in range(chips)]
    chip, core = device // 2, device % 2

    def along(step):
        return [
            (2 * c + k, 2 * order[(place[c] + step) % chips] + k)
            for c in range(chips)
            for k in range(2)
        ]

    def origin(step):
        return jnp.array(order, jnp.int32)[
            (jnp.array(place, jnp.int32)[chip] + step + chips) % chips
        ]

    def both(piece, source, per, part):
        other = permuted(piece, [(i, i ^ 1) for i in range(count)])
        return [
            (piece, (2 * source + core) * per + part),
            (other, (2 * source + 1 - core) * per + part),
        ]

    groups = [both(weight, chip, 1, 0)]
    up = down = weight
    for step in range(1, chips // 2):
        up, down = permuted(up, along(1)), permuted(down, along(-1))
        groups.append(both(up, origin(-step), 1, 0) + both(down, origin(step), 1, 0))
        if step in ties:
            up, down = after(up, ties[step]), after(down, ties[step])
    half = weight.shape[0] // 2
    up, down = permuted(up[:half], along(1)), permuted(down[half:], along(-1))
    far = origin(chips // 2)
    groups.append(both(up, far, 2, 0) + both(down, far, 2, 1))
    return groups


def stripes_kernel(where, cot, grad, down, *rest):
    out = rest[-1]
    rank = grad.shape[1]

    def product(weight):
        frozen = dot(cot[...], weight[...], ((1,), (1,)))
        for b in range(cot.shape[0] // BLOCK):
            rows = slice(b * BLOCK, (b + 1) * BLOCK)
            lora = adapter_scale * dot(
                grad[rows, :], down[b * rank : (b + 1) * rank, :], ((1,), (0,))
            )
            lora = lora.astype(jnp.bfloat16).astype(jnp.float32)
            out[rows, :] = (frozen[rows] + lora).astype(jnp.bfloat16)

    for number in range(where.shape[0]):
        pl.when(pl.program_id(0) == number)(lambda weight=rest[number]: product(weight))


def write_stripes(group, cot, grad, down, out=None):
    rows, depth = cot.shape
    width = down.shape[1]
    count = len(group)
    stripe = group[0][0].shape[0]
    where = jnp.stack([place for _, place in group]).astype(jnp.int32)
    specs = [
        pl.BlockSpec((rows, depth), lambda j, where: (0, 0)),
        pl.BlockSpec(grad.shape, lambda j, where: (0, 0)),
        pl.BlockSpec((down.shape[0], stripe), lambda j, where: (0, where[j])),
    ] + [pl.BlockSpec((stripe, depth), lambda j, where: (0, 0)) for _ in group]
    args = [where, cot, grad, down] + [piece for piece, _ in group]
    alias = {}
    if out is not None:
        specs.append(pl.BlockSpec(memory_space=pl.ANY))
        args.append(out)
        alias = {len(args) - 1: 0}
    return pl.pallas_call(
        stripes_kernel,
        grid_spec=pltpu.PrefetchScalarGridSpec(
            num_scalar_prefetch=1,
            grid=(count,),
            in_specs=specs,
            out_specs=pl.BlockSpec((rows, stripe), lambda j, where: (0, where[j])),
        ),
        out_shape=jax.ShapeDtypeStruct((rows, width), jnp.bfloat16),
        input_output_aliases=alias,
        cost_estimate=pl.CostEstimate(
            flops=2 * rows * depth * stripe * count,
            bytes_accessed=2 * (depth + rows) * stripe * count,
            transcendentals=0,
        ),
        compiler_params=pltpu.CompilerParams(vmem_limit_bytes=32 << 20),
    )(*args)


def small_stripes(groups, cot, grad, down, rank):
    depth = cot.shape[1]
    weight = jnp.zeros((down.shape[1], depth), jnp.bfloat16)
    for piece, place in sum(groups, []):
        weight = lax.dynamic_update_slice(weight, piece, (place * piece.shape[0], 0))
    lora = [
        dot(
            grad[b * BLOCK : (b + 1) * BLOCK], down[b * rank : (b + 1) * rank], ((1,), (0,))
        )
        for b in range(cot.shape[0] // BLOCK)
    ]
    lora = (adapter_scale * jnp.concatenate(lora, axis=0)).astype(jnp.bfloat16)
    out = dot(cot, weight, ((1,), (1,)))
    return (out + lora.astype(jnp.float32)).astype(jnp.bfloat16)


def pack_kernel(rows, act, maps, cot, out, rows_out):
    tokens, features = act.shape
    cap = (out.shape[1] - tokens - maps.shape[0]) * features // cot.shape[1]
    target = pl.program_id(0)
    resident_rows = cap * pl.num_programs(0)
    mine = rows[...] // resident_rows == target
    first = lax.broadcasted_iota(jnp.int32, (tokens, tokens), 0)
    later = lax.broadcasted_iota(jnp.int32, (tokens, tokens), 1)
    earlier = jnp.where(first < later, 1.0, 0.0).astype(jnp.bfloat16)
    chosen = jnp.broadcast_to(jnp.where(mine, 1.0, 0.0), (8, tokens)).astype(jnp.bfloat16)
    place = dot(chosen, earlier, ((1,), (0,)))[:1].astype(jnp.int32)
    place = jnp.where(mine, place, -1)
    send = lax.broadcasted_iota(jnp.int32, (cap, tokens), 0) == place
    send = jnp.where(send, 1.0, 0.0).astype(jnp.bfloat16)
    sent = [
        dot(send, cot[:, k : k + features], ((1,), (0,)))
        for k in range(0, cot.shape[1], features)
    ]
    rows_out[...] = rows[...]
    out[0, :tokens, :] = act[...]
    out[0, tokens : tokens + maps.shape[0], :] = maps[...]
    out[0, tokens + maps.shape[0] :, :] = jnp.concatenate(sent, axis=0).astype(out.dtype)


def pack(rows, act, maps, cot, devices, cap):
    tokens, width = act.shape
    features = width // devices
    total = tokens + maps.shape[0] + cap * cot.shape[1] // features
    return pl.pallas_call(
        pack_kernel,
        grid=(devices,),
        in_specs=[
            pl.BlockSpec((1, tokens), lambda j: (0, 0)),
            pl.BlockSpec((tokens, features), lambda j: (0, j)),
            pl.BlockSpec((maps.shape[0], features), lambda j: (0, j)),
            pl.BlockSpec(cot.shape, lambda j: (0, 0)),
        ],
        out_specs=[
            pl.BlockSpec((1, total, features), lambda j: (j, 0, 0)),
            pl.BlockSpec((1, tokens), lambda j: (0, 0)),
        ],
        out_shape=[
            jax.ShapeDtypeStruct((devices, total, features), act.dtype),
            jax.ShapeDtypeStruct((1, tokens), rows.dtype),
        ],
        cost_estimate=pl.CostEstimate(
            flops=2 * devices * cap * tokens * cot.shape[1],
            bytes_accessed=4 * devices * total * features,
            transcendentals=0,
        ),
        compiler_params=pltpu.CompilerParams(vmem_limit_bytes=24 << 20),
    )(rows[None], act, maps, cot)


def slot_chunks(width):
    size = min(width, 768)
    while width % size:
        size //= 2
    return [slice(k, k + size) for k in range(0, width, size)]


def own_rows(slot, first, size, rank):
    index = first // rank + lax.broadcasted_iota(jnp.int32, (size // rank, rank, 1), 0)
    return index == slot[...][None]


def hidden_kernel(act, maps, slot, out):
    rank = out.shape[0]
    tokens = out.shape[1] // act.shape[0]
    rows = jnp.concatenate([act[k, :tokens, :] for k in range(act.shape[0])], axis=0)
    total = jnp.zeros(out.shape, jnp.float32)
    share = maps.shape[1]
    for part in slot_chunks(maps.shape[0] * share):
        size = part.stop - part.start
        some = maps[part.start // share : part.stop // share].reshape(size, -1)
        each = dot(some, rows, ((1,), (1,))).reshape(size // rank, rank, -1)
        total += jnp.sum(
            jnp.where(own_rows(slot, part.start, size, rank), each, 0.0), axis=0
        )
    out[...] = total


def down_kernel(act, grad, slot, out, total):
    rank = grad.shape[0]
    tokens = grad.shape[1] // act.shape[0]
    rows = jnp.concatenate([act[k, :tokens, :] for k in range(act.shape[0])], axis=0)
    step = pl.program_id(0)

    @pl.when(step == 0)
    def _():
        total[...] = jnp.zeros_like(total)

    wide = grad[...].astype(jnp.float32)[None]
    for part in slot_chunks(total.shape[0]):
        size = part.stop - part.start
        placed = jnp.where(own_rows(slot, part.start, size, rank), wide, 0.0)
        placed = placed.reshape(size, -1).astype(jnp.bfloat16)
        total[part, :] += dot(placed, rows, ((1,), (0,)))

    @pl.when(step == pl.num_programs(0) - 1)
    def _():
        out[...] = (adapter_scale * total[...]).astype(out.dtype)


def feature_calls(devices, tokens, packed, features, width, rank):
    share = width // devices
    pair = 2
    while pair * tokens % LANES:
        pair *= 2
    grid = (devices // pair,)
    act = pl.BlockSpec((pair, packed, features), lambda j: (j, 0, 0))
    slot = pl.BlockSpec((1, pair * tokens), lambda j: (0, j))
    small = pl.BlockSpec((rank, pair * tokens), lambda j: (0, j))
    whole = pl.BlockSpec((width, features), lambda j: (0, 0))
    every = devices * tokens
    cost = pl.CostEstimate(
        flops=2 * every * width * features,
        bytes_accessed=2 * every * features,
        transcendentals=0,
    )
    params = pltpu.CompilerParams(vmem_limit_bytes=48 << 20)
    hidden = pl.pallas_call(
        hidden_kernel,
        grid=grid,
        in_specs=[
            act,
            pl.BlockSpec((devices, share, features), lambda j: (0, tokens // share, 0)),
            slot,
        ],
        out_specs=small,
        out_shape=jax.ShapeDtypeStruct((rank, every), jnp.float32),
        cost_estimate=cost,
        compiler_params=params,
    )
    down = pl.pallas_call(
        down_kernel,
        grid=grid,
        in_specs=[act, small, slot],
        out_specs=whole,
        out_shape=jax.ShapeDtypeStruct((width, features), jnp.bfloat16),
        scratch_shapes=[pltpu.VMEM((width, features), jnp.float32)],
        cost_estimate=cost,
        compiler_params=params,
    )
    return hidden, down


def local(
    activations,
    cotangent,
    token_layout_row,
    tenant_first_row,
    frozen_value_weight,
    adapter_down_maps,
    adapter_up_maps,
):
    devices = lax.axis_size("blk")
    device = lax.axis_index("blk")
    tokens = activations.shape[0]
    resident, rank, width = adapter_down_maps.shape
    out_width = cotangent.shape[1]
    features = width // devices
    resident_rows = resident * BLOCK
    slots = resident * devices
    slot_cap = resident_rows // devices
    start_ids = tenant_first_row // BLOCK

    order = jnp.arange(tokens, dtype=jnp.int32)
    places = jnp.arange(resident_rows, dtype=jnp.int32)
    folds = out_width // features
    flat_maps = adapter_down_maps.reshape(-1, width)
    if features % LANES == 0 and slot_cap % 8 == 0:
        packed, rows_sent = pack(
            token_layout_row, activations, flat_maps, cotangent, devices, slot_cap
        )
        rows_sent = rows_sent[0]
    else:
        target = token_layout_row // resident_rows
        before = (target[:, None] == target[None, :]) & (order[None, :] < order[:, None])
        place = target * slot_cap + jnp.sum(before.astype(jnp.int32), axis=1)
        send = (places[:, None] == place[None, :]).astype(jnp.bfloat16)
        send_cot = dot(send, cotangent, ((1,), (0,))).astype(jnp.bfloat16)
        send_cot = send_cot.reshape(devices, slot_cap, out_width)
        packed = [
            activations.reshape(tokens, devices, features).transpose(1, 0, 2),
            flat_maps.reshape(-1, devices, features).transpose(1, 0, 2),
        ] + [send_cot[:, :, k * features : (k + 1) * features] for k in range(folds)]
        packed = jnp.concatenate(packed, axis=1)
        rows_sent = token_layout_row

    padded = -(-tokens // LANES) * LANES
    digits = as_digits(jnp.pad(rows_sent, (0, padded - tokens)))
    digits = digits.reshape(-1, LANES)
    count = digits.shape[0]
    digits = jnp.pad(digits, ((0, resident * rank - count), (0, 0)))
    shared = jnp.concatenate([adapter_up_maps.reshape(-1, out_width), digits], axis=1)
    shared = lax.all_gather(shared, "blk", axis=0, tiled=False)
    up_all = shared[:, :, :out_width].reshape(slots * rank, out_width)
    rows_all = shared[:, :count, out_width:].reshape(devices, 3, padded)[:, :, :tokens]
    rows_all = from_digits(rows_all.transpose(1, 0, 2)).reshape(-1)

    own_slot = starts_of(token_layout_row // BLOCK, start_ids)
    every_up = dot(up_all, cotangent, ((1,), (1,))).reshape(slots, rank, tokens)
    own = jnp.arange(slots, dtype=jnp.int32)[:, None, None] == own_slot[None, None, :]
    grad_in = jnp.sum(jnp.where(own, every_up, 0.0), axis=0).astype(jnp.bfloat16)

    first_row = device * resident_rows
    row_of = (rows_all[None, :] - first_row == places[:, None]).astype(jnp.bfloat16)
    mine = (rows_all // resident_rows == device).reshape(devices, tokens)
    earlier = (order[:, None] < order[None, :]).astype(jnp.bfloat16)
    at = dot(mine.astype(jnp.bfloat16), earlier, ((1,), (0,))).astype(jnp.int32)
    at = at + slot_cap * jnp.arange(devices, dtype=jnp.int32)[:, None]
    at = jnp.where(mine, at, -1).reshape(-1)
    arrange = dot(
        row_of, (at[:, None] == places[None, :]).astype(jnp.bfloat16), ((1,), (0,))
    ).astype(jnp.bfloat16)

    first_block = device * resident
    block_numbers = first_block + jnp.arange(resident, dtype=jnp.int32)
    begin = starts_of(block_numbers, start_ids)
    is_local = (begin >= first_block) & (begin <= block_numbers)
    home_slot = jnp.clip(begin - first_block, 0, resident - 1)
    last_map = lax.dynamic_index_in_dim(
        adapter_down_maps, home_slot[resident - 1], 0, keepdims=False
    )
    last_map = after(last_map, shared)
    carried = jnp.zeros_like(last_map)
    for step in range(1, HOPS + 1):
        home = (device - step) % devices
        carried = jnp.where(begin[0] // resident == home, moved(last_map, step), carried)

    down_blocks = []
    for b in range(resident):
        down = carried
        for k in range(b + 1):
            down = jnp.where(is_local[b] & (home_slot[b] == k), adapter_down_maps[k], down)
        down_blocks.append(down)
    down_blocks = jnp.concatenate(down_blocks, axis=0)
    slot_all = starts_of(rows_all // BLOCK, start_ids)[None]

    received = lax.all_to_all(packed, "blk", split_axis=0, concat_axis=0)
    recv_cot = received[:, tokens + resident * rank :]
    recv_cot = [
        recv_cot[:, k * slot_cap : (k + 1) * slot_cap].reshape(resident_rows, features)
        for k in range(folds)
    ]

    cot_rows = jnp.concatenate(
        [dot(arrange, part, ((1,), (0,))).astype(jnp.bfloat16) for part in recv_cot], axis=1
    )

    grad_in = after(grad_in, received)
    grad_all = to_all(grad_in).transpose(1, 0, 2).reshape(rank, -1)
    hidden_call, down_call = feature_calls(
        devices, tokens, packed.shape[1], features, slots * rank, rank
    )
    slot_all = after(slot_all, arrange, down_blocks)
    hidden = hidden_call(received, received, slot_all)
    slot_all = after(slot_all, hidden)
    hidden = hidden.reshape(rank, devices, tokens).transpose(1, 0, 2)
    hidden = lax.all_to_all(hidden, "blk", split_axis=0, concat_axis=0)
    hidden = to_all(jnp.sum(hidden, axis=0).astype(jnp.bfloat16))
    hidden = hidden.transpose(1, 0, 2).reshape(rank, -1)
    down_f = down_call(received, grad_all, slot_all)
    down_home = lax.all_to_all(down_f, "blk", split_axis=0, concat_axis=1, tiled=True)
    down_map_gradient = down_home.astype(jnp.float32).reshape(resident, rank, width)

    grad_rows = dot(row_of, grad_all, ((1,), (1,))).astype(jnp.bfloat16)
    grad_rows = after(grad_rows, down_f)
    hidden_rows = dot(row_of, hidden, ((1,), (1,))).astype(jnp.bfloat16)
    up_parts = []
    for b in range(resident):
        rows = slice(b * BLOCK, (b + 1) * BLOCK)
        up_parts.append(dot(hidden_rows[rows], cot_rows[rows], ((0,), (0,))))

    tail = sum(jnp.where(is_local[b], 0.0, up_parts[b]) for b in range(resident))
    far = jnp.zeros_like(tail)
    for step in range(1, HOPS + 1):
        other = (device + step) % devices * resident
        theirs = starts_of(other[None], start_ids)[0]
        far = far + jnp.where(theirs // resident == device, moved(tail, -step), 0.0)
    up_grads = []
    for k in range(resident):
        total = jnp.where(begin[resident - 1] == first_block + k, far, 0.0)
        for b in range(resident):
            total = total + jnp.where(is_local[b] & (home_slot[b] == k), up_parts[b], 0.0)
        up_grads.append(adapter_scale * total)
    up_map_gradient = jnp.stack(up_grads)

    chips = devices // 2
    groups = ring_shards(
        frozen_value_weight, {chips // 2 - 2: down_f, chips // 2 - 1: hidden}
    )
    if frozen_value_weight.shape[0] % (2 * LANES) == 0:
        out = None
        for group in groups:
            out = write_stripes(group, cot_rows, grad_rows, down_blocks, out)
    else:
        out = small_stripes(groups, cot_rows, grad_rows, down_blocks, rank)
    return (out, down_map_gradient, up_map_gradient)


def solution(mesh):
    return jax.shard_map(
        local,
        mesh=mesh,
        in_specs=(
            P(("groups", "blk"), None),
            P(("groups", "blk"), None),
            P(("groups", "blk")),
            P("groups"),
            P("blk", None),
            P(("groups", "blk"), None, None),
            P(("groups", "blk"), None, None),
        ),
        out_specs=(
            P(("groups", "blk"), None),
            P(("groups", "blk"), None, None),
            P(("groups", "blk"), None, None),
        ),
        check_vma=False,
    )
```

```python
import functools

import jax
import jax.numpy as jnp
from jax import lax
from jax.experimental import pallas as pl
from jax.experimental.pallas import tpu as pltpu
from jax.sharding import PartitionSpec as P

BLOCK = 128
HOPS = 4
LANES = 128
DIGIT = 64
VMEM = 56 << 20

adapter_scale = 2.0


def permuted(value, pairs):
    return lax.ppermute(value, "blk", pairs)


def moved(value, steps):
    count = lax.axis_size("blk")
    return permuted(value, [(i, (i + steps) % count) for i in range(count)])


def to_all(value):
    count = lax.axis_size("blk")
    copies = jnp.broadcast_to(value[None], (count,) + value.shape)
    return lax.all_to_all(copies, "blk", split_axis=0, concat_axis=0)


def after(value, *others):
    anywhere = pl.BlockSpec(memory_space=pl.ANY)
    return pl.pallas_call(
        lambda *refs: None,
        in_specs=[anywhere] * (1 + len(others)),
        out_specs=anywhere,
        out_shape=jax.ShapeDtypeStruct(value.shape, value.dtype),
        input_output_aliases={0: 0},
        cost_estimate=pl.CostEstimate(flops=0, bytes_accessed=0, transcendentals=0),
    )(value, *others)


def dot(a, b, dims):
    return lax.dot_general(a, b, (dims, ((), ())), preferred_element_type=jnp.float32)


def starts_of(blocks, start_ids):
    latest = jnp.max(
        jnp.where(start_ids[None, :] <= blocks[:, None], start_ids[None, :], -1), axis=1
    )
    return jnp.where(latest >= 0, latest, jnp.max(start_ids))


def as_digits(rows):
    return rows % DIGIT, rows // DIGIT % DIGIT, rows // (DIGIT * DIGIT)


def from_digits(digits):
    low, middle, high = [digits[:, k].astype(jnp.int32) for k in range(3)]
    return (high * DIGIT + middle) * DIGIT + low


def ring_shards(weight, ties):
    count, device = lax.axis_size("blk"), lax.axis_index("blk")
    chips = count // 2
    order = list(range(0, chips, 2)) + list(range(chips - 1, 0, -2))
    place = [order.index(chip) for chip in range(chips)]
    chip, core = device // 2, device % 2

    def along(step):
        return [
            (2 * c + k, 2 * order[(place[c] + step) % chips] + k)
            for c in range(chips)
            for k in range(2)
        ]

    def origin(step):
        return jnp.array(order, jnp.int32)[
            (jnp.array(place, jnp.int32)[chip] + step + chips) % chips
        ]

    def both(piece, source, per, part):
        other = permuted(piece, [(i, i ^ 1) for i in range(count)])
        return [
            (piece, (2 * source + core) * per + part),
            (other, (2 * source + 1 - core) * per + part),
        ]

    groups = [both(weight, chip, 1, 0)]
    up = down = weight
    for step in range(1, chips // 2):
        up, down = permuted(up, along(1)), permuted(down, along(-1))
        groups.append(both(up, origin(-step), 1, 0) + both(down, origin(step), 1, 0))
        if step in ties:
            up, down = after(up, ties[step]), after(down, ties[step])
    half = weight.shape[0] // 2
    up, down = permuted(up[:half], along(1)), permuted(down[half:], along(-1))
    far = origin(chips // 2)
    groups.append(both(up, far, 2, 0) + both(down, far, 2, 1))
    return groups


def stripes_kernel(where, cot, grad, down, *rest):
    out = rest[-1]
    rank = grad.shape[1]

    def product(weight):
        frozen = dot(cot[...], weight[...], ((1,), (1,)))
        for b in range(cot.shape[0] // BLOCK):
            rows = slice(b * BLOCK, (b + 1) * BLOCK)
            lora = adapter_scale * dot(
                grad[rows, :], down[b * rank : (b + 1) * rank, :], ((1,), (0,))
            )
            lora = lora.astype(jnp.bfloat16).astype(jnp.float32)
            out[rows, :] = (frozen[rows] + lora).astype(jnp.bfloat16)

    for number in range(where.shape[0]):
        pl.when(pl.program_id(0) == number)(lambda weight=rest[number]: product(weight))


def write_stripes(group, cot, grad, down, out=None):
    rows, depth = cot.shape
    width = down.shape[1]
    count = len(group)
    stripe = group[0][0].shape[0]
    where = jnp.stack([place for _, place in group]).astype(jnp.int32)
    specs = [
        pl.BlockSpec((rows, depth), lambda j, where: (0, 0)),
        pl.BlockSpec(grad.shape, lambda j, where: (0, 0)),
        pl.BlockSpec((down.shape[0], stripe), lambda j, where: (0, where[j])),
    ] + [pl.BlockSpec((stripe, depth), lambda j, where: (0, 0)) for _ in group]
    args = [where, cot, grad, down] + [piece for piece, _ in group]
    alias = {}
    if out is not None:
        specs.append(pl.BlockSpec(memory_space=pl.ANY))
        args.append(out)
        alias = {len(args) - 1: 0}
    return pl.pallas_call(
        stripes_kernel,
        grid_spec=pltpu.PrefetchScalarGridSpec(
            num_scalar_prefetch=1,
            grid=(count,),
            in_specs=specs,
            out_specs=pl.BlockSpec((rows, stripe), lambda j, where: (0, where[j])),
        ),
        out_shape=jax.ShapeDtypeStruct((rows, width), jnp.bfloat16),
        input_output_aliases=alias,
        cost_estimate=pl.CostEstimate(
            flops=2 * rows * depth * stripe * count,
            bytes_accessed=2 * (depth + rows) * stripe * count,
            transcendentals=0,
        ),
        compiler_params=pltpu.CompilerParams(vmem_limit_bytes=VMEM),
    )(*args)


def small_stripes(groups, cot, grad, down, rank):
    depth = cot.shape[1]
    weight = jnp.zeros((down.shape[1], depth), jnp.bfloat16)
    for piece, place in sum(groups, []):
        weight = lax.dynamic_update_slice(weight, piece, (place * piece.shape[0], 0))
    lora = [
        dot(
            grad[b * BLOCK : (b + 1) * BLOCK], down[b * rank : (b + 1) * rank], ((1,), (0,))
        )
        for b in range(cot.shape[0] // BLOCK)
    ]
    lora = (adapter_scale * jnp.concatenate(lora, axis=0)).astype(jnp.bfloat16)
    out = dot(cot, weight, ((1,), (1,)))
    return (out + lora.astype(jnp.float32)).astype(jnp.bfloat16)


def pack_kernel(rows, wide_rows, act, maps, cot, out):
    tokens, features = act.shape
    shared = maps.shape[0]
    cap = shared * features // cot.shape[1]
    target = pl.program_id(0)
    mine = rows[...] // (cap * pl.num_programs(0)) == target
    first = lax.broadcasted_iota(jnp.int32, (tokens, tokens), 0)
    later = lax.broadcasted_iota(jnp.int32, (tokens, tokens), 1)
    earlier = jnp.where(first < later, 1.0, 0.0).astype(jnp.bfloat16)
    chosen = jnp.broadcast_to(jnp.where(mine, 1.0, 0.0), (8, tokens)).astype(jnp.bfloat16)
    place = dot(chosen, earlier, ((1,), (0,)))[:1].astype(jnp.int32)
    place = jnp.where(mine, place, -1)
    send = lax.broadcasted_iota(jnp.int32, (cap, tokens), 0) == place
    send = jnp.where(send, 1.0, 0.0).astype(jnp.bfloat16)
    sent = [
        dot(send, cot[:, k : k + features], ((1,), (0,)))
        for k in range(0, cot.shape[1], features)
    ]
    which = lax.broadcasted_iota(jnp.int32, (16, features), 0)
    low, middle, high = as_digits(wide_rows[...])
    digits = jnp.where(which == 0, low, jnp.where(which == 1, middle, high))
    out[0, :tokens, :] = act[...]
    out[0, tokens : tokens + shared, :] = maps[...]
    out[0, tokens + shared : tokens + 2 * shared, :] = jnp.concatenate(sent, axis=0).astype(
        out.dtype
    )
    out[0, tokens + 2 * shared :, :] = digits.astype(jnp.float32).astype(out.dtype)


def pack(rows, act, maps, cot, devices, cap):
    tokens, width = act.shape
    features = width // devices
    shared = maps.shape[0]
    total = tokens + 2 * shared + 16
    if features % LANES == 0 and cap % 8 == 0 and features >= tokens:
        return pl.pallas_call(
            pack_kernel,
            grid=(devices,),
            in_specs=[
                pl.BlockSpec((1, tokens), lambda j: (0, 0)),
                pl.BlockSpec((1, features), lambda j: (0, 0)),
                pl.BlockSpec((tokens, features), lambda j: (0, j)),
                pl.BlockSpec((shared, features), lambda j: (0, j)),
                pl.BlockSpec(cot.shape, lambda j: (0, 0)),
            ],
            out_specs=pl.BlockSpec((1, total, features), lambda j: (j, 0, 0)),
            out_shape=jax.ShapeDtypeStruct((devices, total, features), act.dtype),
            cost_estimate=pl.CostEstimate(
                flops=2 * devices * cap * tokens * cot.shape[1],
                bytes_accessed=4 * devices * total * features,
                transcendentals=0,
            ),
            compiler_params=pltpu.CompilerParams(vmem_limit_bytes=VMEM),
        )(rows[None], jnp.pad(rows, (0, features - tokens))[None], act, maps, cot)
    target = rows // (cap * devices)
    order = jnp.arange(tokens, dtype=jnp.int32)
    before = (target[:, None] == target[None, :]) & (order[None, :] < order[:, None])
    place = target * cap + jnp.sum(before.astype(jnp.int32), axis=1)
    send = jnp.arange(cap * devices, dtype=jnp.int32)[:, None] == place[None, :]
    sent = dot(send.astype(jnp.bfloat16), cot, ((1,), (0,))).astype(jnp.bfloat16)
    sent = sent.reshape(devices, cap, cot.shape[1])
    digits = jnp.stack(as_digits(rows)).astype(jnp.bfloat16)
    digits = jnp.pad(digits, ((0, 0), (0, -tokens % features))).reshape(-1, features)
    digits = jnp.pad(digits, ((0, 16 - digits.shape[0]), (0, 0)))
    parts = [
        act.reshape(tokens, devices, features).transpose(1, 0, 2),
        maps.reshape(shared, devices, features).transpose(1, 0, 2),
    ]
    parts += [sent[:, :, k : k + features] for k in range(0, cot.shape[1], features)]
    parts += [jnp.broadcast_to(digits[None], (devices,) + digits.shape)]
    return jnp.concatenate(parts, axis=1)


def slot_chunks(width):
    size = min(width, 768)
    while width % size:
        size //= 2
    return [slice(k, k + size) for k in range(0, width, size)]


def slot_of(rows, starts):
    blocks = rows // BLOCK
    latest = jnp.max(jnp.where(starts <= blocks, starts, -1), axis=0, keepdims=True)
    return jnp.where(latest >= 0, latest, jnp.max(starts))


def own_rows(slot, first, size, rank):
    index = first // rank + lax.broadcasted_iota(jnp.int32, (size // rank, rank, 1), 0)
    return index == slot[None]


def exchange_map(rows, devices, places):
    tokens = rows.shape[1]
    cap = places // devices
    target = rows // places
    to = lax.broadcasted_iota(jnp.int32, (devices, tokens), 0) == target
    first = lax.broadcasted_iota(jnp.int32, (tokens, tokens), 0)
    later = lax.broadcasted_iota(jnp.int32, (tokens, tokens), 1)
    earlier = jnp.where(first < later, 1.0, 0.0).astype(jnp.bfloat16)
    ahead = dot(jnp.where(to, 1.0, 0.0).astype(jnp.bfloat16), earlier, ((1,), (0,)))
    ahead = jnp.sum(jnp.where(to, ahead, 0.0), axis=0, keepdims=True).astype(jnp.int32)
    place = target * cap + ahead
    hit = lax.broadcasted_iota(jnp.int32, (places, tokens), 0) == place
    return jnp.where(hit, 1.0, 0.0).astype(jnp.bfloat16)


def hidden_kernel(devices, act, maps, rows, starts, out):
    sources, _, tokens = rows.shape
    rank, places = out.shape[0] // sources, out.shape[1]
    share = maps.shape[1]
    for k in range(sources):
        slot = slot_of(rows[k], starts[...])
        total = jnp.zeros((rank, tokens), jnp.float32)
        for part in slot_chunks(maps.shape[0] * share):
            size = part.stop - part.start
            some = maps[part.start // share : part.stop // share].reshape(size, -1)
            each = dot(some, act[k, :tokens, :], ((1,), (1,))).reshape(size // rank, rank, -1)
            total += jnp.sum(
                jnp.where(own_rows(slot, part.start, size, rank), each, 0.0), axis=0
            )
        high = total.astype(jnp.bfloat16)
        low = (total - high.astype(jnp.float32)).astype(jnp.bfloat16)
        place = exchange_map(rows[k], devices, places)
        out[k * rank : (k + 1) * rank, :] = dot(high, place, ((1,), (1,))) + dot(
            low, place, ((1,), (1,))
        )


def down_kernel(devices, act, grad, rows, starts, out, total):
    sources, _, tokens = rows.shape
    rank, places = grad.shape[0] // sources, grad.shape[1]
    step = pl.program_id(0)

    @pl.when(step == 0)
    def _():
        total[...] = jnp.zeros_like(total)

    for k in range(sources):
        slot = slot_of(rows[k], starts[...])
        place = exchange_map(rows[k], devices, places)
        wide = dot(grad[k * rank : (k + 1) * rank, :], place, ((1,), (0,)))[None]
        for part in slot_chunks(total.shape[0]):
            size = part.stop - part.start
            placed = jnp.where(own_rows(slot, part.start, size, rank), wide, 0.0)
            placed = placed.reshape(size, -1).astype(jnp.bfloat16)
            total[part, :] += dot(placed, act[k, :tokens, :], ((1,), (0,)))

    @pl.when(step == pl.num_programs(0) - 1)
    def _():
        out[...] = (adapter_scale * total[...]).astype(out.dtype)


def feature_calls(received, tokens, share, rank, places, starts):
    devices, packed, features = received.shape
    width = devices * share
    sources = 2
    grid = (devices // sources,)
    act = pl.BlockSpec((sources, packed, features), lambda j: (j, 0, 0))
    maps = pl.BlockSpec((devices, share, features), lambda j: (0, tokens // share, 0))
    rows = pl.BlockSpec((sources, 1, tokens), lambda j: (j, 0, 0))
    begin = pl.BlockSpec((starts, 1), lambda j: (0, 0))
    placed = pl.BlockSpec((sources * rank, places), lambda j: (j, 0))
    cost = pl.CostEstimate(
        flops=2 * devices * tokens * width * features,
        bytes_accessed=2 * devices * tokens * features,
        transcendentals=0,
    )
    params = pltpu.CompilerParams(vmem_limit_bytes=VMEM)
    hidden = pl.pallas_call(
        functools.partial(hidden_kernel, devices),
        grid=grid,
        in_specs=[act, maps, rows, begin],
        out_specs=placed,
        out_shape=jax.ShapeDtypeStruct((devices * rank, places), jnp.float32),
        cost_estimate=cost,
        compiler_params=params,
    )
    down = pl.pallas_call(
        functools.partial(down_kernel, devices),
        grid=grid,
        in_specs=[act, placed, rows, begin],
        out_specs=pl.BlockSpec((width, features), lambda j: (0, 0)),
        out_shape=jax.ShapeDtypeStruct((width, features), jnp.bfloat16),
        scratch_shapes=[pltpu.VMEM((width, features), jnp.float32)],
        cost_estimate=cost,
        compiler_params=params,
    )
    return hidden, down


def local(
    activations,
    cotangent,
    token_layout_row,
    tenant_first_row,
    frozen_value_weight,
    adapter_down_maps,
    adapter_up_maps,
):
    devices = lax.axis_size("blk")
    device = lax.axis_index("blk")
    tokens = activations.shape[0]
    resident, rank, width = adapter_down_maps.shape
    out_width = cotangent.shape[1]
    features = width // devices
    share = resident * rank
    resident_rows = resident * BLOCK
    cap = resident_rows // devices
    start_ids = tenant_first_row // BLOCK

    flat_maps = adapter_down_maps.reshape(share, width)
    packed = pack(token_layout_row, activations, flat_maps, cotangent, devices, cap)
    received = lax.all_to_all(packed, "blk", split_axis=0, concat_axis=0)
    recv_cot = [
        received[:, tokens + share + k * cap : tokens + share + (k + 1) * cap].reshape(
            resident_rows, features
        )
        for k in range(out_width // features)
    ]
    per_digit = -(-tokens // features)
    digits = received[:, tokens + 2 * share : tokens + 2 * share + 3 * per_digit]
    digits = digits.reshape(devices, 3, per_digit * features)[:, :, :tokens]
    rows_all = from_digits(digits)

    first_block = device * resident
    block_numbers = first_block + jnp.arange(resident, dtype=jnp.int32)
    begin = starts_of(block_numbers, start_ids)
    is_local = (begin >= first_block) & (begin <= block_numbers)
    home_slot = jnp.clip(begin - first_block, 0, resident - 1)
    both_maps = jnp.concatenate([adapter_down_maps, adapter_up_maps], axis=2)
    last_map = lax.dynamic_index_in_dim(both_maps, home_slot[resident - 1], 0, keepdims=False)
    carried = jnp.zeros_like(last_map)
    for step in range(1, HOPS + 1):
        home = (device - step) % devices
        carried = jnp.where(begin[0] // resident == home, moved(last_map, step), carried)
    block_maps = []
    for b in range(resident):
        own = carried
        for k in range(b + 1):
            own = jnp.where(is_local[b] & (home_slot[b] == k), both_maps[k], own)
        block_maps.append(own)
    block_maps = jnp.concatenate(block_maps, axis=0)
    down_blocks, up_blocks = block_maps[:, :width], block_maps[:, width:]

    order = jnp.arange(tokens, dtype=jnp.int32)
    mine = rows_all // resident_rows == device
    earlier = (order[:, None] < order[None, :]).astype(jnp.bfloat16)
    ahead = dot(mine.astype(jnp.bfloat16), earlier, ((1,), (0,))).astype(jnp.int32)
    hit = mine[:, None, :] & (ahead[:, None, :] == jnp.arange(cap)[None, :, None])
    row_in = rows_all - device * resident_rows + 1
    row_in = jnp.sum(jnp.where(hit, row_in[:, None, :], 0), axis=2).reshape(-1) - 1
    arrange = row_in[:, None] == jnp.arange(resident_rows, dtype=jnp.int32)[None, :]
    arrange = arrange.astype(jnp.bfloat16)
    in_block = row_in[:, None] // BLOCK == jnp.arange(share, dtype=jnp.int32)[None, :] // rank

    grad_in = sum(
        dot(part, up_blocks[:, k * features : (k + 1) * features], ((1,), (1,)))
        for k, part in enumerate(recv_cot)
    )
    grad_in = jnp.where(in_block, grad_in, 0.0).astype(jnp.bfloat16)
    grad_in = sum(grad_in[:, b * rank : (b + 1) * rank] for b in range(resident))
    grad_sent = grad_in.reshape(devices, cap, rank).transpose(1, 0, 2).reshape(cap, -1)
    grad_all = to_all(grad_sent).reshape(resident_rows, -1).T

    starts = start_ids[:, None]
    hidden_call, down_call = feature_calls(
        received, tokens, share, rank, resident_rows, starts.shape[0]
    )
    rows_all = rows_all[:, None, :]
    shares = hidden_call(received, received, rows_all, starts)
    down_f = down_call(received, grad_all, after(rows_all, shares), starts)
    hidden = shares.T.reshape(devices, cap, -1)
    hidden = lax.all_to_all(hidden, "blk", split_axis=0, concat_axis=0)
    hidden = jnp.sum(hidden, axis=0).astype(jnp.bfloat16)
    hidden = hidden.reshape(cap, devices, rank).transpose(1, 0, 2).reshape(-1, rank)
    down_home = lax.all_to_all(down_f, "blk", split_axis=0, concat_axis=1, tiled=True)
    down_map_gradient = down_home.astype(jnp.float32).reshape(resident, rank, width)

    cot_rows = jnp.concatenate(
        [dot(arrange, part, ((0,), (0,))).astype(jnp.bfloat16) for part in recv_cot], axis=1
    )
    grad_rows = dot(arrange, grad_in, ((0,), (0,))).astype(jnp.bfloat16)
    grad_rows = after(grad_rows, down_f)
    wide = jnp.where(in_block, jnp.concatenate([hidden] * resident, axis=1), 0)
    up_all = [dot(wide, part, ((0,), (0,))) for part in recv_cot]
    up_all = jnp.concatenate(up_all, axis=1).reshape(resident, rank, out_width)
    up_parts = [up_all[b] for b in range(resident)]

    tail = sum(jnp.where(is_local[b], 0.0, up_parts[b]) for b in range(resident))
    far = jnp.zeros_like(tail)
    for step in range(1, HOPS + 1):
        other = (device + step) % devices * resident
        theirs = starts_of(other[None], start_ids)[0]
        far = far + jnp.where(theirs // resident == device, moved(tail, -step), 0.0)
    up_grads = []
    for k in range(resident):
        total = jnp.where(begin[resident - 1] == first_block + k, far, 0.0)
        for b in range(resident):
            total = total + jnp.where(is_local[b] & (home_slot[b] == k), up_parts[b], 0.0)
        up_grads.append(adapter_scale * total)
    up_map_gradient = jnp.stack(up_grads)

    chips = devices // 2
    groups = ring_shards(
        frozen_value_weight, {chips // 2 - 2: shares, chips // 2 - 1: down_f}
    )
    if frozen_value_weight.shape[0] % (2 * LANES) == 0:
        out = None
        for group in groups:
            out = write_stripes(group, cot_rows, grad_rows, down_blocks, out)
    else:
        out = small_stripes(groups, cot_rows, grad_rows, down_blocks, rank)
    return (out, down_map_gradient, up_map_gradient)


def solution(mesh):
    return jax.shard_map(
        local,
        mesh=mesh,
        in_specs=(
            P(("groups", "blk"), None),
            P(("groups", "blk"), None),
            P(("groups", "blk")),
            P("groups"),
            P("blk", None),
            P(("groups", "blk"), None, None),
            P(("groups", "blk"), None, None),
        ),
        out_specs=(
            P(("groups", "blk"), None),
            P(("groups", "blk"), None, None),
            P(("groups", "blk"), None, None),
        ),
        check_vma=False,
    )
```

```python
import jax
import jax.numpy as jnp
from jax import lax
from jax.experimental import pallas as pl
from jax.experimental.pallas import tpu as pltpu
from jax.sharding import PartitionSpec as P

BLOCK = 128
HOPS = 4
LANES = 128
DIGIT = 64
VMEM = 56 << 20

adapter_scale = 2.0


def moved(value, steps):
    count = lax.axis_size("blk")
    return lax.ppermute(value, "blk", [(i, (i + steps) % count) for i in range(count)])


def to_all(value):
    count = lax.axis_size("blk")
    copies = jnp.broadcast_to(value[None], (count,) + value.shape)
    return lax.all_to_all(copies, "blk", split_axis=0, concat_axis=0)


def after(value, *others):
    anywhere = pl.BlockSpec(memory_space=pl.ANY)
    return pl.pallas_call(
        lambda *refs: None,
        in_specs=[anywhere] * (1 + len(others)),
        out_specs=anywhere,
        out_shape=jax.ShapeDtypeStruct(value.shape, value.dtype),
        input_output_aliases={0: 0},
        cost_estimate=pl.CostEstimate(flops=0, bytes_accessed=0, transcendentals=0),
    )(value, *others)


def dot(a, b, dims):
    return lax.dot_general(a, b, (dims, ((), ())), preferred_element_type=jnp.float32)


def starts_of(blocks, start_ids):
    latest = jnp.max(
        jnp.where(start_ids[None, :] <= blocks[:, None], start_ids[None, :], -1), axis=1
    )
    return jnp.where(latest >= 0, latest, jnp.max(start_ids))


def as_digits(rows, places):
    return (
        rows % DIGIT,
        rows // DIGIT % DIGIT,
        rows // (DIGIT * DIGIT),
        places % DIGIT,
        places // DIGIT,
    )


def from_digits(digits):
    low, middle, high, place, place_high = [digits[:, k].astype(jnp.int32) for k in range(5)]
    return (high * DIGIT + middle) * DIGIT + low, place_high * DIGIT + place


def pack_kernel(rows, act, maps, cot, out, place, digits):
    tokens, features = act.shape
    shared = maps.shape[0]
    cap = shared * features // cot.shape[1]
    devices = pl.num_programs(0)
    step = pl.program_id(0)

    @pl.when(step == 0)
    def _():
        target = rows[...] // (cap * devices)
        to = lax.broadcasted_iota(jnp.int32, (16, features), 0) == target
        first = lax.broadcasted_iota(jnp.int32, (features, features), 0)
        later = lax.broadcasted_iota(jnp.int32, (features, features), 1)
        earlier = jnp.where(first < later, 1.0, 0.0).astype(jnp.bfloat16)
        ahead = dot(jnp.where(to, 1.0, 0.0).astype(jnp.bfloat16), earlier, ((1,), (0,)))
        ahead = jnp.sum(jnp.where(to, ahead, 0.0), axis=0, keepdims=True)
        place[...] = target * cap + ahead.astype(jnp.int32)
        which = lax.broadcasted_iota(jnp.int32, (16, features), 0)
        values = jnp.zeros((16, features), jnp.int32)
        for k, digit in enumerate(as_digits(rows[...], place[...])):
            values = jnp.where(which == k, digit, values)
        digits[...] = values.astype(jnp.float32).astype(out.dtype)

    index = lax.broadcasted_iota(jnp.int32, (cap, tokens), 0) + step * cap
    send = jnp.where(index == place[:, :tokens], 1.0, 0.0).astype(jnp.bfloat16)
    sent = [
        dot(send, cot[:, k : k + features], ((1,), (0,)))
        for k in range(0, cot.shape[1], features)
    ]
    out[0, :tokens, :] = act[...]
    out[0, tokens : tokens + shared, :] = maps[...]
    out[0, tokens + shared : tokens + 2 * shared, :] = jnp.concatenate(sent, axis=0).astype(
        out.dtype
    )
    out[0, tokens + 2 * shared :, :] = digits[...]


def pack(rows, act, maps, cot, devices, cap):
    tokens, width = act.shape
    features = width // devices
    shared = maps.shape[0]
    total = tokens + 2 * shared + 16
    if features % LANES == 0 and cap % 8 == 0 and features >= tokens and devices <= 16:
        padding = jnp.full((features - tokens,), 16 * cap * devices, jnp.int32)
        return pl.pallas_call(
            pack_kernel,
            grid=(devices,),
            in_specs=[
                pl.BlockSpec((1, features), lambda j: (0, 0)),
                pl.BlockSpec((tokens, features), lambda j: (0, j)),
                pl.BlockSpec((shared, features), lambda j: (0, j)),
                pl.BlockSpec(cot.shape, lambda j: (0, 0)),
            ],
            out_specs=pl.BlockSpec((1, total, features), lambda j: (j, 0, 0)),
            out_shape=jax.ShapeDtypeStruct((devices, total, features), act.dtype),
            scratch_shapes=[
                pltpu.VMEM((1, features), jnp.int32),
                pltpu.VMEM((16, features), act.dtype),
            ],
            cost_estimate=pl.CostEstimate(
                flops=2 * devices * cap * tokens * cot.shape[1],
                bytes_accessed=4 * devices * total * features,
                transcendentals=0,
            ),
            compiler_params=pltpu.CompilerParams(vmem_limit_bytes=VMEM),
        )(jnp.concatenate([rows, padding])[None], act, maps, cot)
    target = rows // (cap * devices)
    order = jnp.arange(tokens, dtype=jnp.int32)
    before = (target[:, None] == target[None, :]) & (order[None, :] < order[:, None])
    place = target * cap + jnp.sum(before.astype(jnp.int32), axis=1)
    send = jnp.arange(cap * devices, dtype=jnp.int32)[:, None] == place[None, :]
    sent = dot(send.astype(jnp.bfloat16), cot, ((1,), (0,))).astype(jnp.bfloat16)
    sent = sent.reshape(devices, cap, cot.shape[1])
    digits = jnp.stack(as_digits(rows, place)).astype(jnp.bfloat16)
    digits = jnp.pad(digits, ((0, 0), (0, -tokens % features))).reshape(-1, features)
    digits = jnp.pad(digits, ((0, -digits.shape[0] % 16), (0, 0)))
    parts = [
        act.reshape(tokens, devices, features).transpose(1, 0, 2),
        maps.reshape(shared, devices, features).transpose(1, 0, 2),
    ]
    parts += [sent[:, :, k : k + features] for k in range(0, cot.shape[1], features)]
    parts += [jnp.broadcast_to(digits[None], (devices,) + digits.shape)]
    return jnp.concatenate(parts, axis=1)


def slot_chunks(width):
    size = min(width, 768)
    while width % size:
        size //= 2
    return [slice(k, k + size) for k in range(0, width, size)]


def slot_of(rows, starts):
    blocks = rows // BLOCK
    latest = jnp.max(jnp.where(starts <= blocks, starts, -1), axis=0, keepdims=True)
    return jnp.where(latest >= 0, latest, jnp.max(starts))


def own_rows(slot, first, size, rank):
    index = first // rank + lax.broadcasted_iota(jnp.int32, (size // rank, rank, 1), 0)
    return index == slot[None]


def placing(place, places):
    hit = lax.broadcasted_iota(jnp.int32, (places, place.shape[1]), 0) == place
    return jnp.where(hit, 1.0, 0.0).astype(jnp.bfloat16)


def hidden_kernel(act, maps, rows, spots, starts, out):
    sources, _, tokens = rows.shape
    rank, places = out.shape[0] // sources, out.shape[1]
    share = maps.shape[1]
    for k in range(sources):
        slot = slot_of(rows[k], starts[...])
        total = jnp.zeros((rank, tokens), jnp.float32)
        for part in slot_chunks(maps.shape[0] * share):
            size = part.stop - part.start
            some = maps[part.start // share : part.stop // share].reshape(size, -1)
            each = dot(some, act[k, :tokens, :], ((1,), (1,))).reshape(size // rank, rank, -1)
            total += jnp.sum(
                jnp.where(own_rows(slot, part.start, size, rank), each, 0.0), axis=0
            )
        high = total.astype(jnp.bfloat16)
        low = (total - high.astype(jnp.float32)).astype(jnp.bfloat16)
        place = placing(spots[k], places)
        out[k * rank : (k + 1) * rank, :] = dot(high, place, ((1,), (1,))) + dot(
            low, place, ((1,), (1,))
        )


def down_kernel(act, grad, rows, spots, starts, out, total):
    sources, _, tokens = rows.shape
    rank, places = grad.shape[0] // sources, grad.shape[1]
    step = pl.program_id(0)

    @pl.when(step == 0)
    def _():
        total[...] = jnp.zeros_like(total)

    for k in range(sources):
        slot = slot_of(rows[k], starts[...])
        place = placing(spots[k], places)
        wide = dot(grad[k * rank : (k + 1) * rank, :], place, ((1,), (0,)))[None]
        for part in slot_chunks(total.shape[0]):
            size = part.stop - part.start
            placed = jnp.where(own_rows(slot, part.start, size, rank), wide, 0.0)
            placed = placed.reshape(size, -1).astype(jnp.bfloat16)
            total[part, :] += dot(placed, act[k, :tokens, :], ((1,), (0,)))

    @pl.when(step == pl.num_programs(0) - 1)
    def _():
        out[...] = (adapter_scale * total[...]).astype(out.dtype)


def feature_calls(received, tokens, share, rank, places, starts):
    devices, packed, features = received.shape
    width = devices * share
    sources = 2
    grid = (devices // sources,)
    act = pl.BlockSpec((sources, packed, features), lambda j: (j, 0, 0))
    maps = pl.BlockSpec((devices, share, features), lambda j: (0, tokens // share, 0))
    rows = pl.BlockSpec((sources, 1, tokens), lambda j: (j, 0, 0))
    begin = pl.BlockSpec((starts, 1), lambda j: (0, 0))
    placed = pl.BlockSpec((sources * rank, places), lambda j: (j, 0))
    cost = pl.CostEstimate(
        flops=2 * devices * tokens * width * features,
        bytes_accessed=2 * devices * tokens * features,
        transcendentals=0,
    )
    params = pltpu.CompilerParams(vmem_limit_bytes=VMEM)
    hidden = pl.pallas_call(
        hidden_kernel,
        grid=grid,
        in_specs=[act, maps, rows, rows, begin],
        out_specs=placed,
        out_shape=jax.ShapeDtypeStruct((devices * rank, places), jnp.float32),
        cost_estimate=cost,
        compiler_params=params,
    )
    down = pl.pallas_call(
        down_kernel,
        grid=grid,
        in_specs=[act, placed, rows, rows, begin],
        out_specs=pl.BlockSpec((width, features), lambda j: (0, 0)),
        out_shape=jax.ShapeDtypeStruct((width, features), jnp.bfloat16),
        scratch_shapes=[pltpu.VMEM((width, features), jnp.float32)],
        cost_estimate=cost,
        compiler_params=params,
    )
    return hidden, down


def local(
    activations,
    cotangent,
    token_layout_row,
    tenant_first_row,
    frozen_value_weight,
    adapter_down_maps,
    adapter_up_maps,
):
    devices = lax.axis_size("blk")
    device = lax.axis_index("blk")
    tokens = activations.shape[0]
    resident, rank, width = adapter_down_maps.shape
    out_width = cotangent.shape[1]
    features = width // devices
    share = resident * rank
    resident_rows = resident * BLOCK
    cap = resident_rows // devices
    start_ids = tenant_first_row // BLOCK

    weight = lax.all_gather(frozen_value_weight, "blk", axis=0, tiled=True)

    flat_maps = adapter_down_maps.reshape(share, width)
    packed = pack(token_layout_row, activations, flat_maps, cotangent, devices, cap)
    received = lax.all_to_all(packed, "blk", split_axis=0, concat_axis=0)
    recv_cot = [
        received[:, tokens + share + k * cap : tokens + share + (k + 1) * cap].reshape(
            resident_rows, features
        )
        for k in range(out_width // features)
    ]
    per_digit = -(-tokens // features)
    digits = received[:, tokens + 2 * share : tokens + 2 * share + 5 * per_digit]
    digits = digits.reshape(devices, 5, per_digit * features)[:, :, :tokens]
    rows_all, place_all = from_digits(digits)

    first_block = device * resident
    block_numbers = first_block + jnp.arange(resident, dtype=jnp.int32)
    begin = starts_of(block_numbers, start_ids)
    is_local = (begin >= first_block) & (begin <= block_numbers)
    home_slot = jnp.clip(begin - first_block, 0, resident - 1)
    both_maps = jnp.concatenate([adapter_down_maps, adapter_up_maps], axis=2)
    last_map = lax.dynamic_index_in_dim(both_maps, home_slot[resident - 1], 0, keepdims=False)
    carried = jnp.zeros_like(last_map)
    for step in range(1, HOPS + 1):
        home = (device - step) % devices
        carried = jnp.where(begin[0] // resident == home, moved(last_map, step), carried)
    block_maps = []
    for b in range(resident):
        own = carried
        for k in range(b + 1):
            own = jnp.where(is_local[b] & (home_slot[b] == k), both_maps[k], own)
        block_maps.append(own)
    block_maps = jnp.concatenate(block_maps, axis=0)
    down_blocks, up_blocks = block_maps[:, :width], block_maps[:, width:]

    spots = device * cap + jnp.arange(cap, dtype=jnp.int32)
    hit = place_all[:, None, :] == spots[None, :, None]
    row_in = rows_all - device * resident_rows + 1
    row_in = jnp.sum(jnp.where(hit, row_in[:, None, :], 0), axis=2).reshape(-1) - 1
    arrange = row_in[:, None] == jnp.arange(resident_rows, dtype=jnp.int32)[None, :]
    arrange = arrange.astype(jnp.bfloat16)
    in_block = row_in[:, None] // BLOCK == jnp.arange(share, dtype=jnp.int32)[None, :] // rank

    grad_in = sum(
        dot(part, up_blocks[:, k * features : (k + 1) * features], ((1,), (1,)))
        for k, part in enumerate(recv_cot)
    )
    grad_in = jnp.where(in_block, grad_in, 0.0).astype(jnp.bfloat16)
    grad_in = sum(grad_in[:, b * rank : (b + 1) * rank] for b in range(resident))
    grad_sent = grad_in.reshape(devices, cap, rank).transpose(1, 0, 2).reshape(cap, -1)
    grad_all = to_all(grad_sent).reshape(resident_rows, -1).T

    starts = start_ids[:, None]
    hidden_call, down_call = feature_calls(
        received, tokens, share, rank, resident_rows, starts.shape[0]
    )
    rows_all = rows_all[:, None, :]
    place_all = place_all[:, None, :]
    shares = hidden_call(received, received, rows_all, place_all, starts)
    rows_all = after(rows_all, shares)
    down_f = down_call(received, grad_all, rows_all, place_all, starts)
    hidden = shares.T.reshape(devices, cap, -1)
    hidden = lax.all_to_all(hidden, "blk", split_axis=0, concat_axis=0)
    hidden = jnp.sum(hidden, axis=0).astype(jnp.bfloat16)
    hidden = hidden.reshape(cap, devices, rank).transpose(1, 0, 2).reshape(-1, rank)
    down_home = lax.all_to_all(down_f, "blk", split_axis=0, concat_axis=1, tiled=True)
    down_map_gradient = down_home.astype(jnp.float32).reshape(resident, rank, width)

    cot_rows = jnp.concatenate(
        [dot(arrange, part, ((0,), (0,))).astype(jnp.bfloat16) for part in recv_cot], axis=1
    )
    grad_rows = dot(arrange, grad_in, ((0,), (0,))).astype(jnp.bfloat16)
    lora = [
        dot(
            grad_rows[b * BLOCK : (b + 1) * BLOCK],
            down_blocks[b * rank : (b + 1) * rank],
            ((1,), (0,)),
        )
        for b in range(resident)
    ]
    lora = (adapter_scale * jnp.concatenate(lora, axis=0)).astype(jnp.bfloat16)
    wide = jnp.where(in_block, jnp.concatenate([hidden] * resident, axis=1), 0)
    up_all = [dot(wide, part, ((0,), (0,))) for part in recv_cot]
    up_all = jnp.concatenate(up_all, axis=1).reshape(resident, rank, out_width)
    up_parts = [up_all[b] for b in range(resident)]

    tail = sum(jnp.where(is_local[b], 0.0, up_parts[b]) for b in range(resident))
    far = jnp.zeros_like(tail)
    for step in range(1, HOPS + 1):
        other = (device + step) % devices * resident
        theirs = starts_of(other[None], start_ids)[0]
        far = far + jnp.where(theirs // resident == device, moved(tail, -step), 0.0)
    up_grads = []
    for k in range(resident):
        total = jnp.where(begin[resident - 1] == first_block + k, far, 0.0)
        for b in range(resident):
            total = total + jnp.where(is_local[b] & (home_slot[b] == k), up_parts[b], 0.0)
        up_grads.append(adapter_scale * total)
    up_map_gradient = jnp.stack(up_grads)

    out = dot(cot_rows, weight, ((1,), (1,))) + lora.astype(jnp.float32)
    out = out.astype(jnp.bfloat16)
    return (out, down_map_gradient, up_map_gradient)


def solution(mesh):
    return jax.shard_map(
        local,
        mesh=mesh,
        in_specs=(
            P(("groups", "blk"), None),
            P(("groups", "blk"), None),
            P(("groups", "blk")),
            P("groups"),
            P("blk", None),
            P(("groups", "blk"), None, None),
            P(("groups", "blk"), None, None),
        ),
        out_specs=(
            P(("groups", "blk"), None),
            P(("groups", "blk"), None, None),
            P(("groups", "blk"), None, None),
        ),
        check_vma=False,
    )
```

```python
import functools

import jax
import jax.numpy as jnp
from jax import lax
from jax.experimental import pallas as pl
from jax.experimental.pallas import tpu as pltpu
from jax.sharding import PartitionSpec as P

BLOCK = 128
HOPS = 4
LANES = 128
DIGIT = 64
VMEM = 56 << 20

adapter_scale = 2.0


def moved(value, steps):
    count = lax.axis_size("blk")
    return lax.ppermute(value, "blk", [(i, (i + steps) % count) for i in range(count)])


def to_all(value):
    count = lax.axis_size("blk")
    copies = jnp.broadcast_to(value[None], (count,) + value.shape)
    return lax.all_to_all(copies, "blk", split_axis=0, concat_axis=0)


def after(value, *others):
    anywhere = pl.BlockSpec(memory_space=pl.ANY)
    return pl.pallas_call(
        lambda *refs: None,
        in_specs=[anywhere] * (1 + len(others)),
        out_specs=anywhere,
        out_shape=jax.ShapeDtypeStruct(value.shape, value.dtype),
        input_output_aliases={0: 0},
        cost_estimate=pl.CostEstimate(flops=0, bytes_accessed=0, transcendentals=0),
    )(value, *others)


def dot(a, b, dims):
    return lax.dot_general(a, b, (dims, ((), ())), preferred_element_type=jnp.float32)


def starts_of(blocks, start_ids):
    latest = jnp.max(
        jnp.where(start_ids[None, :] <= blocks[:, None], start_ids[None, :], -1), axis=1
    )
    return jnp.where(latest >= 0, latest, jnp.max(start_ids))


def as_digits(rows, places):
    return (
        rows % DIGIT,
        rows // DIGIT % DIGIT,
        rows // (DIGIT * DIGIT),
        places % DIGIT,
        places // DIGIT,
    )


def from_digits(digits):
    low, middle, high, place, place_high = [digits[:, k].astype(jnp.int32) for k in range(5)]
    return (high * DIGIT + middle) * DIGIT + low, place_high * DIGIT + place


def weight_pieces(weight):
    count = lax.axis_size("blk")
    half = weight.shape[0] // 2
    group = lax.axis_index("groups")
    mine = lax.dynamic_slice_in_dim(weight, group * half, half, 0)
    lines = [list(range(k, count, 4)) for k in range(4)]
    column = lax.all_gather(mine, "blk", axis_index_groups=lines)

    def over(piece, bit):
        return lax.ppermute(piece, "blk", [(i, i ^ bit) for i in range(count)])

    def groups(piece):
        return lax.ppermute(piece, "groups", [(0, 1), (1, 0)])

    across = over(column, 2)
    pieces = []
    for piece in (column, across):
        theirs = groups(piece)
        pieces.append((piece, theirs))
        pieces.append((over(piece, 1), over(theirs, 1)))
    return pieces


def quarter_kernel(where, cot, grad, down, mine, theirs, *rest):
    out = rest[-1]
    rank = grad.shape[1]
    half = mine.shape[1]
    lora = [
        adapter_scale
        * dot(
            grad[b * BLOCK : (b + 1) * BLOCK, :],
            down[b * rank : (b + 1) * rank, :],
            ((1,), (0,)),
        )
        for b in range(cot.shape[0] // BLOCK)
    ]
    lora = jnp.concatenate(lora, axis=0).astype(jnp.bfloat16).astype(jnp.float32)

    def product(group):
        for k, piece in enumerate((mine, theirs) if group == 0 else (theirs, mine)):
            part = slice(k * half, (k + 1) * half)
            frozen = dot(cot[...], piece[0], ((1,), (1,)))
            out[:, part] = (frozen + lora[:, part]).astype(jnp.bfloat16)

    for group in range(2):
        pl.when(where[1] == group)(functools.partial(product, group))


def write_quarter(quarter, first, group, cot, grad, down, out=None):
    mine, theirs = quarter
    rows, depth = cot.shape
    width = down.shape[1]
    shards, half, _ = mine.shape
    where = jnp.stack([first, group]).astype(jnp.int32)
    piece = pl.BlockSpec((1, half, depth), lambda j, where: (j, 0, 0))
    specs = [
        pl.BlockSpec((rows, depth), lambda j, where: (0, 0)),
        pl.BlockSpec(grad.shape, lambda j, where: (0, 0)),
        pl.BlockSpec((down.shape[0], 2 * half), lambda j, where: (0, 4 * j + where[0])),
        piece,
        piece,
    ]
    args = [where, cot, grad, down, mine, theirs]
    alias = {}
    if out is not None:
        specs.append(pl.BlockSpec(memory_space=pl.ANY))
        args.append(out)
        alias = {len(args) - 1: 0}
    return pl.pallas_call(
        quarter_kernel,
        grid_spec=pltpu.PrefetchScalarGridSpec(
            num_scalar_prefetch=1,
            grid=(shards,),
            in_specs=specs,
            out_specs=pl.BlockSpec((rows, 2 * half), lambda j, where: (0, 4 * j + where[0])),
        ),
        out_shape=jax.ShapeDtypeStruct((rows, width), jnp.bfloat16),
        input_output_aliases=alias,
        cost_estimate=pl.CostEstimate(
            flops=4 * rows * depth * half * shards,
            bytes_accessed=4 * (depth + rows) * half * shards,
            transcendentals=0,
        ),
        compiler_params=pltpu.CompilerParams(vmem_limit_bytes=VMEM),
    )(*args)


def together(pieces, firsts, group):
    shards, half, depth = pieces[0][0].shape
    weight = jnp.zeros((shards, 4, 2, half, depth), jnp.bfloat16)
    for quarter, first in zip(pieces, firsts):
        for k, piece in enumerate(quarter):
            place = (0, first, group if k == 0 else 1 - group, 0, 0)
            weight = lax.dynamic_update_slice(weight, piece[:, None, None], place)
    return weight.reshape(-1, depth)


def pack_kernel(rows, act, maps, cot, out, place, digits):
    targets, packed, features = out.shape
    tokens, shared = act.shape[0], maps.shape[0]
    cap = shared * features // cot.shape[1]
    devices = targets * pl.num_programs(0)
    step = pl.program_id(0)

    @pl.when(step == 0)
    def _():
        target = rows[...] // (cap * devices)
        to = lax.broadcasted_iota(jnp.int32, (16, features), 0) == target
        first = lax.broadcasted_iota(jnp.int32, (features, features), 0)
        later = lax.broadcasted_iota(jnp.int32, (features, features), 1)
        earlier = jnp.where(first < later, 1.0, 0.0).astype(jnp.bfloat16)
        ahead = dot(jnp.where(to, 1.0, 0.0).astype(jnp.bfloat16), earlier, ((1,), (0,)))
        ahead = jnp.sum(jnp.where(to, ahead, 0.0), axis=0, keepdims=True)
        place[...] = target * cap + ahead.astype(jnp.int32)
        which = lax.broadcasted_iota(jnp.int32, (16, features), 0)
        values = jnp.zeros((16, features), jnp.int32)
        for k, digit in enumerate(as_digits(rows[...], place[...])):
            values = jnp.where(which == k, digit, values)
        digits[...] = values.astype(jnp.float32).astype(out.dtype)

    index = lax.broadcasted_iota(jnp.int32, (targets * cap, tokens), 0) + step * targets * cap
    send = jnp.where(index == place[:, :tokens], 1.0, 0.0).astype(jnp.bfloat16)
    sent = dot(send, cot[...], ((1,), (0,)))
    for k in range(targets):
        part = slice(k * features, (k + 1) * features)
        some = sent[k * cap : (k + 1) * cap]
        folds = [some[:, f : f + features] for f in range(0, cot.shape[1], features)]
        out[k, :tokens, :] = act[:, part]
        out[k, tokens : tokens + shared, :] = maps[:, part]
        out[k, tokens + shared : tokens + 2 * shared, :] = jnp.concatenate(
            folds, axis=0
        ).astype(out.dtype)
        out[k, tokens + 2 * shared :, :] = digits[...]


def pack(rows, act, maps, cot, devices, cap):
    tokens, width = act.shape
    features = width // devices
    shared = maps.shape[0]
    total = tokens + 2 * shared + 16
    targets = 4
    if features % LANES == 0 and cap % 8 == 0 and features >= tokens and devices <= 16:
        padding = jnp.full((features - tokens,), 16 * cap * devices, jnp.int32)
        return pl.pallas_call(
            pack_kernel,
            grid=(devices // targets,),
            in_specs=[
                pl.BlockSpec((1, features), lambda j: (0, 0)),
                pl.BlockSpec((tokens, targets * features), lambda j: (0, j)),
                pl.BlockSpec((shared, targets * features), lambda j: (0, j)),
                pl.BlockSpec(cot.shape, lambda j: (0, 0)),
            ],
            out_specs=pl.BlockSpec((targets, total, features), lambda j: (j, 0, 0)),
            out_shape=jax.ShapeDtypeStruct((devices, total, features), act.dtype),
            scratch_shapes=[
                pltpu.VMEM((1, features), jnp.int32),
                pltpu.VMEM((16, features), act.dtype),
            ],
            cost_estimate=pl.CostEstimate(
                flops=2 * devices * cap * tokens * cot.shape[1],
                bytes_accessed=4 * devices * total * features,
                transcendentals=0,
            ),
            compiler_params=pltpu.CompilerParams(vmem_limit_bytes=VMEM),
        )(jnp.concatenate([rows, padding])[None], act, maps, cot)
    target = rows // (cap * devices)
    order = jnp.arange(tokens, dtype=jnp.int32)
    before = (target[:, None] == target[None, :]) & (order[None, :] < order[:, None])
    place = target * cap + jnp.sum(before.astype(jnp.int32), axis=1)
    send = jnp.arange(cap * devices, dtype=jnp.int32)[:, None] == place[None, :]
    sent = dot(send.astype(jnp.bfloat16), cot, ((1,), (0,))).astype(jnp.bfloat16)
    sent = sent.reshape(devices, cap, cot.shape[1])
    digits = jnp.stack(as_digits(rows, place)).astype(jnp.bfloat16)
    digits = jnp.pad(digits, ((0, 0), (0, -tokens % features))).reshape(-1, features)
    digits = jnp.pad(digits, ((0, -digits.shape[0] % 16), (0, 0)))
    parts = [
        act.reshape(tokens, devices, features).transpose(1, 0, 2),
        maps.reshape(shared, devices, features).transpose(1, 0, 2),
    ]
    parts += [sent[:, :, k : k + features] for k in range(0, cot.shape[1], features)]
    parts += [jnp.broadcast_to(digits[None], (devices,) + digits.shape)]
    return jnp.concatenate(parts, axis=1)


def slot_chunks(width):
    size = min(width, 768)
    while width % size:
        size //= 2
    return [slice(k, k + size) for k in range(0, width, size)]


def slot_of(rows, starts):
    blocks = rows // BLOCK
    latest = jnp.max(jnp.where(starts <= blocks, starts, -1), axis=0, keepdims=True)
    return jnp.where(latest >= 0, latest, jnp.max(starts))


def own_rows(slot, first, size, rank):
    index = first // rank + lax.broadcasted_iota(jnp.int32, (size // rank, rank, 1), 0)
    return index == slot[None]


def placing(place, places):
    hit = lax.broadcasted_iota(jnp.int32, (places, place.shape[1]), 0) == place
    return jnp.where(hit, 1.0, 0.0).astype(jnp.bfloat16)


def all_rows(act, tokens):
    return jnp.concatenate([act[k, :tokens, :] for k in range(act.shape[0])], axis=0)


def of_source(sources, width):
    lane = lax.broadcasted_iota(jnp.int32, (sources, 1, width), 2)
    return lane // (width // sources) == lax.broadcasted_iota(
        jnp.int32, (sources, 1, width), 0
    )


def hidden_kernel(act, maps, rows, spots, starts, out):
    sources, share, width = act.shape[0], maps.shape[1], rows.shape[1]
    rank, places = out.shape[0] // sources, out.shape[1]
    slot = slot_of(rows[...], starts[...])
    every = all_rows(act, width // sources)
    total = jnp.zeros((rank, width), jnp.float32)
    for part in slot_chunks(maps.shape[0] * share):
        size = part.stop - part.start
        some = maps[part.start // share : part.stop // share].reshape(size, -1)
        each = dot(some, every, ((1,), (1,))).reshape(size // rank, rank, -1)
        total += jnp.sum(jnp.where(own_rows(slot, part.start, size, rank), each, 0.0), axis=0)
    total = jnp.where(of_source(sources, width), total[None], 0.0).reshape(out.shape[0], width)
    high = total.astype(jnp.bfloat16)
    low = (total - high.astype(jnp.float32)).astype(jnp.bfloat16)
    place = placing(spots[...], places)
    out[...] = dot(high, place, ((1,), (1,))) + dot(low, place, ((1,), (1,)))


def down_kernel(act, grad, rows, spots, starts, out, total):
    sources, width = act.shape[0], rows.shape[1]
    rank, places = grad.shape[0] // sources, grad.shape[1]
    step = pl.program_id(0)

    @pl.when(step == 0)
    def _():
        total[...] = jnp.zeros_like(total)

    slot = slot_of(rows[...], starts[...])
    every = all_rows(act, width // sources)
    wide = dot(grad[...], placing(spots[...], places), ((1,), (0,)))
    wide = wide.reshape(sources, rank, width)
    wide = jnp.sum(jnp.where(of_source(sources, width), wide, 0.0), axis=0, keepdims=True)
    for part in slot_chunks(total.shape[0]):
        size = part.stop - part.start
        placed = jnp.where(own_rows(slot, part.start, size, rank), wide, 0.0)
        placed = placed.reshape(size, -1).astype(jnp.bfloat16)
        total[part, :] += dot(placed, every, ((1,), (0,)))

    @pl.when(step == pl.num_programs(0) - 1)
    def _():
        out[...] = (adapter_scale * total[...]).astype(out.dtype)


def feature_calls(received, tokens, share, rank, places, starts):
    devices, packed, features = received.shape
    width = devices * share
    sources = 4
    grid = (devices // sources,)
    act = pl.BlockSpec((sources, packed, features), lambda j: (j, 0, 0))
    maps = pl.BlockSpec((devices, share, features), lambda j: (0, tokens // share, 0))
    rows = pl.BlockSpec((1, sources * tokens), lambda j: (0, j))
    begin = pl.BlockSpec((starts, 1), lambda j: (0, 0))
    placed = pl.BlockSpec((sources * rank, places), lambda j: (j, 0))
    cost = pl.CostEstimate(
        flops=2 * devices * tokens * width * features,
        bytes_accessed=2 * devices * tokens * features,
        transcendentals=0,
    )
    params = pltpu.CompilerParams(vmem_limit_bytes=VMEM)
    hidden = pl.pallas_call(
        hidden_kernel,
        grid=grid,
        in_specs=[act, maps, rows, rows, begin],
        out_specs=placed,
        out_shape=jax.ShapeDtypeStruct((devices * rank, places), jnp.float32),
        cost_estimate=cost,
        compiler_params=params,
    )
    down = pl.pallas_call(
        down_kernel,
        grid=grid,
        in_specs=[act, placed, rows, rows, begin],
        out_specs=pl.BlockSpec((width, features), lambda j: (0, 0)),
        out_shape=jax.ShapeDtypeStruct((width, features), jnp.bfloat16),
        scratch_shapes=[pltpu.VMEM((width, features), jnp.float32)],
        cost_estimate=cost,
        compiler_params=params,
    )
    return hidden, down


def local(
    activations,
    cotangent,
    token_layout_row,
    tenant_first_row,
    frozen_value_weight,
    adapter_down_maps,
    adapter_up_maps,
):
    devices = lax.axis_size("blk")
    device = lax.axis_index("blk")
    tokens = activations.shape[0]
    resident, rank, width = adapter_down_maps.shape
    out_width = cotangent.shape[1]
    features = width // devices
    share = resident * rank
    resident_rows = resident * BLOCK
    cap = resident_rows // devices
    start_ids = tenant_first_row // BLOCK

    pieces = weight_pieces(frozen_value_weight)

    first_block = device * resident
    block_numbers = first_block + jnp.arange(resident, dtype=jnp.int32)
    begin = starts_of(block_numbers, start_ids)
    is_local = (begin >= first_block) & (begin <= block_numbers)
    home_slot = jnp.clip(begin - first_block, 0, resident - 1)
    both_maps = jnp.concatenate([adapter_down_maps, adapter_up_maps], axis=2)
    last_map = lax.dynamic_index_in_dim(both_maps, home_slot[resident - 1], 0, keepdims=False)
    carried = jnp.zeros_like(last_map)
    for step in range(1, HOPS + 1):
        home = (device - step) % devices
        carried = jnp.where(begin[0] // resident == home, moved(last_map, step), carried)
    block_maps = []
    for b in range(resident):
        own = carried
        for k in range(b + 1):
            own = jnp.where(is_local[b] & (home_slot[b] == k), both_maps[k], own)
        block_maps.append(own)
    block_maps = jnp.concatenate(block_maps, axis=0)
    down_blocks, up_blocks = block_maps[:, :width], block_maps[:, width:]

    flat_maps = adapter_down_maps.reshape(share, width)
    packed = pack(token_layout_row, activations, flat_maps, cotangent, devices, cap)
    packed = after(packed, carried)
    received = lax.all_to_all(packed, "blk", split_axis=0, concat_axis=0)
    recv_cot = [
        received[:, tokens + share + k * cap : tokens + share + (k + 1) * cap].reshape(
            resident_rows, features
        )
        for k in range(out_width // features)
    ]
    per_digit = -(-tokens // features)
    digits = received[:, tokens + 2 * share : tokens + 2 * share + 5 * per_digit]
    digits = digits.reshape(devices, 5, per_digit * features)[:, :, :tokens]
    rows_all, place_all = from_digits(digits)

    spots = device * cap + jnp.arange(cap, dtype=jnp.int32)
    hit = place_all[:, None, :] == spots[None, :, None]
    row_in = rows_all - device * resident_rows + 1
    row_in = jnp.sum(jnp.where(hit, row_in[:, None, :], 0), axis=2).reshape(-1) - 1
    arrange = row_in[:, None] == jnp.arange(resident_rows, dtype=jnp.int32)[None, :]
    arrange = arrange.astype(jnp.bfloat16)
    in_block = row_in[:, None] // BLOCK == jnp.arange(share, dtype=jnp.int32)[None, :] // rank

    grad_in = sum(
        dot(part, up_blocks[:, k * features : (k + 1) * features], ((1,), (1,)))
        for k, part in enumerate(recv_cot)
    )
    grad_in = jnp.where(in_block, grad_in, 0.0).astype(jnp.bfloat16)
    grad_in = sum(grad_in[:, b * rank : (b + 1) * rank] for b in range(resident))
    grad_sent = grad_in.reshape(devices, cap, rank).transpose(1, 0, 2).reshape(cap, -1)
    grad_all = to_all(grad_sent).reshape(resident_rows, -1).T

    starts = start_ids[:, None]
    hidden_call, down_call = feature_calls(
        received, tokens, share, rank, resident_rows, starts.shape[0]
    )
    rows_all, place_all = rows_all.reshape(1, -1), place_all.reshape(1, -1)
    place_all = after(place_all, pieces[2][0])
    shares = hidden_call(received, received, rows_all, place_all, starts)
    rows_all = after(rows_all, shares)
    down_f = down_call(received, grad_all, rows_all, place_all, starts)
    hidden = shares.T.reshape(devices, cap, -1)
    hidden = lax.all_to_all(hidden, "blk", split_axis=0, concat_axis=0)
    hidden = jnp.sum(hidden, axis=0).astype(jnp.bfloat16)
    hidden = hidden.reshape(cap, devices, rank).transpose(1, 0, 2).reshape(-1, rank)
    down_home = lax.all_to_all(down_f, "blk", split_axis=0, concat_axis=1, tiled=True)
    down_map_gradient = down_home.astype(jnp.float32).reshape(resident, rank, width)

    cot_rows = jnp.concatenate(
        [dot(arrange, part, ((0,), (0,))).astype(jnp.bfloat16) for part in recv_cot], axis=1
    )
    grad_rows = dot(arrange, grad_in, ((0,), (0,))).astype(jnp.bfloat16)
    grad_rows = after(grad_rows, down_f)
    wide = jnp.where(in_block, jnp.concatenate([hidden] * resident, axis=1), 0)
    up_all = [dot(wide, part, ((0,), (0,))) for part in recv_cot]
    up_all = jnp.concatenate(up_all, axis=1).reshape(resident, rank, out_width)
    up_parts = [up_all[b] for b in range(resident)]

    tail = sum(jnp.where(is_local[b], 0.0, up_parts[b]) for b in range(resident))
    far = jnp.zeros_like(tail)
    for step in range(1, HOPS + 1):
        other = (device + step) % devices * resident
        theirs = starts_of(other[None], start_ids)[0]
        far = far + jnp.where(theirs // resident == device, moved(tail, -step), 0.0)
    up_grads = []
    for k in range(resident):
        total = jnp.where(begin[resident - 1] == first_block + k, far, 0.0)
        for b in range(resident):
            total = total + jnp.where(is_local[b] & (home_slot[b] == k), up_parts[b], 0.0)
        up_grads.append(adapter_scale * total)
    up_map_gradient = jnp.stack(up_grads)

    group = lax.axis_index("groups")
    quarter = device % 4
    firsts = [quarter, quarter ^ 1, quarter ^ 2, quarter ^ 3]
    if pieces[0][0].shape[1] % LANES == 0:
        out = None
        for piece, first in zip(pieces, firsts):
            out = write_quarter(piece, first, group, cot_rows, grad_rows, down_blocks, out)
    else:
        weight = together(pieces, firsts, group)
        lora = [
            dot(
                grad_rows[b * BLOCK : (b + 1) * BLOCK],
                down_blocks[b * rank : (b + 1) * rank],
                ((1,), (0,)),
            )
            for b in range(resident)
        ]
        lora = (adapter_scale * jnp.concatenate(lora, axis=0)).astype(jnp.bfloat16)
        out = dot(cot_rows, weight, ((1,), (1,))) + lora.astype(jnp.float32)
        out = out.astype(jnp.bfloat16)
    return (out, down_map_gradient, up_map_gradient)


def solution(mesh):
    return jax.shard_map(
        local,
        mesh=mesh,
        in_specs=(
            P(("groups", "blk"), None),
            P(("groups", "blk"), None),
            P(("groups", "blk")),
            P("groups"),
            P("blk", None),
            P(("groups", "blk"), None, None),
            P(("groups", "blk"), None, None),
        ),
        out_specs=(
            P(("groups", "blk"), None),
            P(("groups", "blk"), None, None),
            P(("groups", "blk"), None, None),
        ),
        check_vma=False,
    )
```

```python
import functools

import jax
import jax.numpy as jnp
from jax import lax
from jax.experimental import pallas as pl
from jax.experimental.pallas import tpu as pltpu
from jax.sharding import PartitionSpec as P

BLOCK = 128
HOPS = 4
LANES = 128
DIGIT = 64
VMEM = 56 << 20

adapter_scale = 2.0


def moved(value, steps):
    count = lax.axis_size("blk")
    return lax.ppermute(value, "blk", [(i, (i + steps) % count) for i in range(count)])


def to_all(value):
    count = lax.axis_size("blk")
    copies = jnp.broadcast_to(value[None], (count,) + value.shape)
    return lax.all_to_all(copies, "blk", split_axis=0, concat_axis=0)


def after(value, *others):
    anywhere = pl.BlockSpec(memory_space=pl.ANY)
    return pl.pallas_call(
        lambda *refs: None,
        in_specs=[anywhere] * (1 + len(others)),
        out_specs=anywhere,
        out_shape=jax.ShapeDtypeStruct(value.shape, value.dtype),
        input_output_aliases={0: 0},
        cost_estimate=pl.CostEstimate(flops=0, bytes_accessed=0, transcendentals=0),
        compiler_params=pltpu.CompilerParams(vmem_limit_bytes=VMEM),
    )(value, *others)


def dot(a, b, dims):
    return lax.dot_general(a, b, (dims, ((), ())), preferred_element_type=jnp.float32)


def starts_of(blocks, start_ids):
    latest = jnp.max(
        jnp.where(start_ids[None, :] <= blocks[:, None], start_ids[None, :], -1), axis=1
    )
    return jnp.where(latest >= 0, latest, jnp.max(start_ids))


def as_digits(rows, places):
    return (
        rows % DIGIT,
        rows // DIGIT % DIGIT,
        rows // (DIGIT * DIGIT),
        places % DIGIT,
        places // DIGIT,
    )


def from_digits(digits):
    low, middle, high, place, place_high = [digits[:, k].astype(jnp.int32) for k in range(5)]
    return (high * DIGIT + middle) * DIGIT + low, place_high * DIGIT + place


def weight_pieces(weight):
    count = lax.axis_size("blk")
    half = weight.shape[0] // 2
    group = lax.axis_index("groups")
    mine = lax.dynamic_slice_in_dim(weight, group * half, half, 0)
    lines = [list(range(k, count, 4)) for k in range(4)]
    column = lax.all_gather(mine, "blk", axis_index_groups=lines)

    def over(piece, bit):
        return lax.ppermute(piece, "blk", [(i, i ^ bit) for i in range(count)])

    def groups(piece):
        return lax.ppermute(piece, "groups", [(0, 1), (1, 0)])

    across = over(column, 2)
    pieces = []
    for piece in (column, across):
        theirs = groups(piece)
        pieces.append((piece, theirs))
        pieces.append((over(piece, 1), over(theirs, 1)))
    return pieces


def quarter_kernel(where, cot, grad, down, mine, theirs, *rest):
    out, token = rest[-2:]
    token[...] = jnp.zeros_like(token)
    rank = grad.shape[1]
    half = mine.shape[1]
    lora = [
        adapter_scale
        * dot(
            grad[b * BLOCK : (b + 1) * BLOCK, :],
            down[b * rank : (b + 1) * rank, :],
            ((1,), (0,)),
        )
        for b in range(cot.shape[0] // BLOCK)
    ]
    lora = jnp.concatenate(lora, axis=0).astype(jnp.bfloat16).astype(jnp.float32)

    def product(group):
        for k, piece in enumerate((mine, theirs) if group == 0 else (theirs, mine)):
            part = slice(k * half, (k + 1) * half)
            frozen = dot(cot[...], piece[0], ((1,), (1,)))
            out[:, part] = (frozen + lora[:, part]).astype(jnp.bfloat16)

    for group in range(2):
        pl.when(where[1] == group)(functools.partial(product, group))


def write_quarter(quarter, first, group, cot, grad, down, out=None):
    mine, theirs = quarter
    rows, depth = cot.shape
    width = down.shape[1]
    shards, half, _ = mine.shape
    where = jnp.stack([first, group]).astype(jnp.int32)
    piece = pl.BlockSpec((1, half, depth), lambda j, where: (j, 0, 0))
    specs = [
        pl.BlockSpec((rows, depth), lambda j, where: (0, 0)),
        pl.BlockSpec(grad.shape, lambda j, where: (0, 0)),
        pl.BlockSpec((down.shape[0], 2 * half), lambda j, where: (0, 4 * j + where[0])),
        piece,
        piece,
    ]
    args = [where, cot, grad, down, mine, theirs]
    alias = {}
    if out is not None:
        specs.append(pl.BlockSpec(memory_space=pl.ANY))
        args.append(out)
        alias = {len(args) - 1: 0}
    return pl.pallas_call(
        quarter_kernel,
        grid_spec=pltpu.PrefetchScalarGridSpec(
            num_scalar_prefetch=1,
            grid=(shards,),
            in_specs=specs,
            out_specs=[
                pl.BlockSpec((rows, 2 * half), lambda j, where: (0, 4 * j + where[0])),
                pl.BlockSpec((8, LANES), lambda j, where: (0, 0)),
            ],
        ),
        out_shape=[
            jax.ShapeDtypeStruct((rows, width), jnp.bfloat16),
            jax.ShapeDtypeStruct((8, LANES), jnp.float32),
        ],
        input_output_aliases=alias,
        cost_estimate=pl.CostEstimate(
            flops=4 * rows * depth * half * shards,
            bytes_accessed=4 * (depth + rows) * half * shards,
            transcendentals=0,
        ),
        compiler_params=pltpu.CompilerParams(vmem_limit_bytes=VMEM),
    )(*args)


def together(pieces, firsts, group):
    shards, half, depth = pieces[0][0].shape
    weight = jnp.zeros((shards, 4, 2, half, depth), jnp.bfloat16)
    for quarter, first in zip(pieces, firsts):
        for k, piece in enumerate(quarter):
            place = (0, first, group if k == 0 else 1 - group, 0, 0)
            weight = lax.dynamic_update_slice(weight, piece[:, None, None], place)
    return weight.reshape(-1, depth)


def rows_kernel(rows, cot, out, place):
    devices, packed, features = out.shape
    shared = packed - 16
    folds = cot.shape[1] // features
    cap = shared // folds
    target = rows[...] // (cap * devices)
    to = lax.broadcasted_iota(jnp.int32, (16, features), 0) == target
    first = lax.broadcasted_iota(jnp.int32, (features, features), 0)
    later = lax.broadcasted_iota(jnp.int32, (features, features), 1)
    earlier = jnp.where(first < later, 1.0, 0.0).astype(jnp.bfloat16)
    ahead = dot(jnp.where(to, 1.0, 0.0).astype(jnp.bfloat16), earlier, ((1,), (0,)))
    ahead = jnp.sum(jnp.where(to, ahead, 0.0), axis=0, keepdims=True)
    place[...] = target * cap + ahead.astype(jnp.int32)
    which = lax.broadcasted_iota(jnp.int32, (16, features), 0)
    digits = jnp.zeros((16, features), jnp.int32)
    for k, digit in enumerate(as_digits(rows[...], place[...])):
        digits = jnp.where(which == k, digit, digits)
    digits = digits.astype(jnp.float32).astype(out.dtype)
    send = placing(place[:, : cot.shape[0]], cap * devices)
    for f in range(folds):
        sent = dot(send, cot[:, f * features : (f + 1) * features], ((1,), (0,)))
        for k in range(devices):
            some = sent[k * cap : (k + 1) * cap].astype(out.dtype)
            out[k, f * cap : (f + 1) * cap, :] = some
    for k in range(devices):
        out[k, shared:, :] = digits


def pack_rows(rows, cot, devices, cap, features):
    tokens = rows.shape[0]
    folds = cot.shape[1] // features
    if features % LANES == 0 and cap % 8 == 0 and features >= tokens and devices <= 16:
        padding = jnp.full((features - tokens,), 16 * cap * devices, jnp.int32)
        return pl.pallas_call(
            rows_kernel,
            out_shape=jax.ShapeDtypeStruct((devices, folds * cap + 16, features), cot.dtype),
            scratch_shapes=[pltpu.VMEM((1, features), jnp.int32)],
            cost_estimate=pl.CostEstimate(
                flops=2 * devices * cap * tokens * cot.shape[1],
                bytes_accessed=6 * cot.size,
                transcendentals=0,
            ),
            compiler_params=pltpu.CompilerParams(vmem_limit_bytes=VMEM),
        )(jnp.concatenate([rows, padding])[None], cot)
    target = rows // (cap * devices)
    order = jnp.arange(tokens, dtype=jnp.int32)
    before = (target[:, None] == target[None, :]) & (order[None, :] < order[:, None])
    place = target * cap + jnp.sum(before.astype(jnp.int32), axis=1)
    send = jnp.arange(cap * devices, dtype=jnp.int32)[:, None] == place[None, :]
    sent = dot(send.astype(jnp.bfloat16), cot, ((1,), (0,))).astype(jnp.bfloat16)
    sent = sent.reshape(devices, cap, cot.shape[1])
    digits = jnp.stack(as_digits(rows, place)).astype(jnp.bfloat16)
    digits = jnp.pad(digits, ((0, 0), (0, -tokens % features))).reshape(-1, features)
    digits = jnp.pad(digits, ((0, -digits.shape[0] % 16), (0, 0)))
    parts = [sent[:, :, k : k + features] for k in range(0, cot.shape[1], features)]
    parts += [jnp.broadcast_to(digits[None], (devices,) + digits.shape)]
    return jnp.concatenate(parts, axis=1)


def features_kernel(act, maps, out):
    targets, _, features = out.shape
    tokens = act.shape[0]
    for k in range(targets):
        part = slice(k * features, (k + 1) * features)
        out[k, :tokens, :] = act[:, part]
        out[k, tokens:, :] = maps[:, part]


def pack_features(act, maps, devices):
    tokens, width = act.shape
    features = width // devices
    shared = maps.shape[0]
    targets = 4
    if features % LANES == 0:
        return pl.pallas_call(
            features_kernel,
            grid=(devices // targets,),
            in_specs=[
                pl.BlockSpec((tokens, targets * features), lambda j: (0, j)),
                pl.BlockSpec((shared, targets * features), lambda j: (0, j)),
            ],
            out_specs=pl.BlockSpec((targets, tokens + shared, features), lambda j: (j, 0, 0)),
            out_shape=jax.ShapeDtypeStruct((devices, tokens + shared, features), act.dtype),
            cost_estimate=pl.CostEstimate(
                flops=0, bytes_accessed=4 * (tokens + shared) * width, transcendentals=0
            ),
            compiler_params=pltpu.CompilerParams(vmem_limit_bytes=VMEM),
        )(act, maps)
    both = jnp.concatenate([act, maps], axis=0)
    return both.reshape(tokens + shared, devices, features).transpose(1, 0, 2)


def slot_chunks(width):
    size = min(width, 768)
    while width % size:
        size //= 2
    return [slice(k, k + size) for k in range(0, width, size)]


def slot_of(rows, starts):
    blocks = rows // BLOCK
    latest = jnp.max(jnp.where(starts <= blocks, starts, -1), axis=0, keepdims=True)
    return jnp.where(latest >= 0, latest, jnp.max(starts))


def own_rows(slot, first, size, rank):
    index = first // rank + lax.broadcasted_iota(jnp.int32, (size // rank, rank, 1), 0)
    return index == slot[None]


def placing(place, places):
    hit = lax.broadcasted_iota(jnp.int32, (places, place.shape[1]), 0) == place
    return jnp.where(hit, 1.0, 0.0).astype(jnp.bfloat16)


def all_rows(act, tokens):
    return jnp.concatenate([act[k, :tokens, :] for k in range(act.shape[0])], axis=0)


def of_source(sources, width):
    lane = lax.broadcasted_iota(jnp.int32, (sources, 1, width), 2)
    return lane // (width // sources) == lax.broadcasted_iota(
        jnp.int32, (sources, 1, width), 0
    )


def hidden_kernel(act, maps, rows, spots, starts, out):
    sources, share, width = act.shape[0], maps.shape[1], rows.shape[1]
    rank, places = out.shape[0] // sources, out.shape[1]
    slot = slot_of(rows[...], starts[...])
    every = all_rows(act, width // sources)
    total = jnp.zeros((rank, width), jnp.float32)
    for part in slot_chunks(maps.shape[0] * share):
        size = part.stop - part.start
        some = maps[part.start // share : part.stop // share].reshape(size, -1)
        each = dot(some, every, ((1,), (1,))).reshape(size // rank, rank, -1)
        total += jnp.sum(jnp.where(own_rows(slot, part.start, size, rank), each, 0.0), axis=0)
    total = jnp.where(of_source(sources, width), total[None], 0.0).reshape(out.shape[0], width)
    high = total.astype(jnp.bfloat16)
    low = (total - high.astype(jnp.float32)).astype(jnp.bfloat16)
    place = placing(spots[...], places)
    out[...] = dot(high, place, ((1,), (1,))) + dot(low, place, ((1,), (1,)))


def down_kernel(act, grad, rows, spots, starts, out, total):
    sources, width = act.shape[0], rows.shape[1]
    rank, places = grad.shape[0] // sources, grad.shape[1]
    step = pl.program_id(0)

    @pl.when(step == 0)
    def _():
        total[...] = jnp.zeros_like(total)

    slot = slot_of(rows[...], starts[...])
    every = all_rows(act, width // sources)
    wide = dot(grad[...], placing(spots[...], places), ((1,), (0,)))
    wide = wide.reshape(sources, rank, width)
    wide = jnp.sum(jnp.where(of_source(sources, width), wide, 0.0), axis=0, keepdims=True)
    for part in slot_chunks(total.shape[0]):
        size = part.stop - part.start
        placed = jnp.where(own_rows(slot, part.start, size, rank), wide, 0.0)
        placed = placed.reshape(size, -1).astype(jnp.bfloat16)
        total[part, :] += dot(placed, every, ((1,), (0,)))

    @pl.when(step == pl.num_programs(0) - 1)
    def _():
        out[...] = (adapter_scale * total[...]).astype(out.dtype)


def feature_calls(received, tokens, share, rank, places, starts):
    devices, packed, features = received.shape
    width = devices * share
    sources = 4
    grid = (devices // sources,)
    act = pl.BlockSpec((sources, packed, features), lambda j: (j, 0, 0))
    maps = pl.BlockSpec((devices, share, features), lambda j: (0, tokens // share, 0))
    rows = pl.BlockSpec((1, sources * tokens), lambda j: (0, j))
    begin = pl.BlockSpec((starts, 1), lambda j: (0, 0))
    placed = pl.BlockSpec((sources * rank, places), lambda j: (j, 0))
    cost = pl.CostEstimate(
        flops=2 * devices * tokens * width * features,
        bytes_accessed=2 * devices * tokens * features,
        transcendentals=0,
    )
    params = pltpu.CompilerParams(vmem_limit_bytes=VMEM)
    hidden = pl.pallas_call(
        hidden_kernel,
        grid=grid,
        in_specs=[act, maps, rows, rows, begin],
        out_specs=placed,
        out_shape=jax.ShapeDtypeStruct((devices * rank, places), jnp.float32),
        cost_estimate=cost,
        compiler_params=params,
    )
    down = pl.pallas_call(
        down_kernel,
        grid=grid,
        in_specs=[act, placed, rows, rows, begin],
        out_specs=pl.BlockSpec((width, features), lambda j: (0, 0)),
        out_shape=jax.ShapeDtypeStruct((width, features), jnp.bfloat16),
        scratch_shapes=[pltpu.VMEM((width, features), jnp.float32)],
        cost_estimate=cost,
        compiler_params=params,
    )
    return hidden, down


def local(
    activations,
    cotangent,
    token_layout_row,
    tenant_first_row,
    frozen_value_weight,
    adapter_down_maps,
    adapter_up_maps,
):
    devices = lax.axis_size("blk")
    device = lax.axis_index("blk")
    tokens = activations.shape[0]
    resident, rank, width = adapter_down_maps.shape
    out_width = cotangent.shape[1]
    features = width // devices
    share = resident * rank
    resident_rows = resident * BLOCK
    cap = resident_rows // devices
    start_ids = tenant_first_row // BLOCK

    pieces = weight_pieces(frozen_value_weight)

    sent_rows = pack_rows(token_layout_row, cotangent, devices, cap, features)
    got_rows = lax.all_to_all(sent_rows, "blk", split_axis=0, concat_axis=0)
    recv_cot = [
        got_rows[:, k * cap : (k + 1) * cap].reshape(resident_rows, features)
        for k in range(out_width // features)
    ]
    per_digit = -(-tokens // features)
    digits = got_rows[:, share : share + 5 * per_digit]
    digits = digits.reshape(devices, 5, per_digit * features)[:, :, :tokens]
    rows_all, place_all = from_digits(digits)

    first_block = device * resident
    block_numbers = first_block + jnp.arange(resident, dtype=jnp.int32)
    begin = starts_of(block_numbers, start_ids)
    is_local = (begin >= first_block) & (begin <= block_numbers)
    home_slot = jnp.clip(begin - first_block, 0, resident - 1)
    last_map = jnp.concatenate(
        [
            lax.dynamic_index_in_dim(maps, home_slot[resident - 1], 0, keepdims=False)
            for maps in (adapter_down_maps, adapter_up_maps)
        ],
        axis=1,
    )
    carried = jnp.zeros_like(last_map)
    for step in range(1, HOPS + 1):
        home = (device - step) % devices
        carried = jnp.where(begin[0] // resident == home, moved(last_map, step), carried)

    def of_blocks(maps, own):
        blocks = []
        for b in range(resident):
            chosen = own
            for k in range(b + 1):
                chosen = jnp.where(is_local[b] & (home_slot[b] == k), maps[k], chosen)
            blocks.append(chosen)
        return jnp.concatenate(blocks, axis=0)

    down_blocks = of_blocks(adapter_down_maps, carried[:, :width])
    up_blocks = of_blocks(adapter_up_maps, carried[:, width:])

    spots = device * cap + jnp.arange(cap, dtype=jnp.int32)
    hit = place_all[:, None, :] == spots[None, :, None]
    row_in = rows_all - device * resident_rows + 1
    row_in = jnp.sum(jnp.where(hit, row_in[:, None, :], 0), axis=2).reshape(-1) - 1
    arrange = row_in[:, None] == jnp.arange(resident_rows, dtype=jnp.int32)[None, :]
    arrange = arrange.astype(jnp.bfloat16)
    in_block = row_in[:, None] // BLOCK == jnp.arange(share, dtype=jnp.int32)[None, :] // rank

    grad_in = sum(
        dot(part, up_blocks[:, k * features : (k + 1) * features], ((1,), (1,)))
        for k, part in enumerate(recv_cot)
    )
    grad_in = jnp.where(in_block, grad_in, 0.0).astype(jnp.bfloat16)
    grad_in = sum(grad_in[:, b * rank : (b + 1) * rank] for b in range(resident))
    grad_sent = grad_in.reshape(devices, cap, rank).transpose(1, 0, 2).reshape(cap, -1)
    grad_all = to_all(after(grad_sent, pieces[0][0])).reshape(resident_rows, -1).T

    flat_maps = adapter_down_maps.reshape(share, width)
    received = after(pack_features(activations, flat_maps, devices), grad_all)
    received = lax.all_to_all(received, "blk", split_axis=0, concat_axis=0)

    rows_all, place_all = rows_all.reshape(1, -1), place_all.reshape(1, -1)

    cot_rows = jnp.concatenate(
        [dot(arrange, part, ((0,), (0,))).astype(jnp.bfloat16) for part in recv_cot], axis=1
    )
    grad_rows = dot(arrange, grad_in, ((0,), (0,))).astype(jnp.bfloat16)
    group = lax.axis_index("groups")
    quarter = device % 4
    firsts = [quarter, quarter ^ 1, quarter ^ 2, quarter ^ 3]
    if pieces[0][0].shape[1] % LANES == 0:
        out = None
        for number, (piece, first) in enumerate(zip(pieces, firsts)):
            out, token = write_quarter(
                piece, first, group, cot_rows, grad_rows, down_blocks, out
            )
            if number == 1:
                place_all = after(place_all, token)
    else:
        weight = together(pieces, firsts, group)
        lora = [
            dot(
                grad_rows[b * BLOCK : (b + 1) * BLOCK],
                down_blocks[b * rank : (b + 1) * rank],
                ((1,), (0,)),
            )
            for b in range(resident)
        ]
        lora = (adapter_scale * jnp.concatenate(lora, axis=0)).astype(jnp.bfloat16)
        out = dot(cot_rows, weight, ((1,), (1,))) + lora.astype(jnp.float32)
        out = out.astype(jnp.bfloat16)

    starts = start_ids[:, None]
    hidden_call, down_call = feature_calls(
        received, tokens, share, rank, resident_rows, starts.shape[0]
    )
    shares = hidden_call(received, received, rows_all, place_all, starts)
    rows_all = after(rows_all, shares)
    down_f = down_call(received, grad_all, rows_all, place_all, starts)
    hidden = shares.T.reshape(devices, cap, -1)
    hidden = lax.all_to_all(hidden, "blk", split_axis=0, concat_axis=0)
    hidden = jnp.sum(hidden, axis=0).astype(jnp.bfloat16)
    hidden = hidden.reshape(cap, devices, rank).transpose(1, 0, 2).reshape(-1, rank)
    down_home = lax.all_to_all(down_f, "blk", split_axis=0, concat_axis=1, tiled=True)
    down_map_gradient = down_home.astype(jnp.float32).reshape(resident, rank, width)

    wide = jnp.where(in_block, jnp.concatenate([hidden] * resident, axis=1), 0)
    up_all = [dot(wide, part, ((0,), (0,))) for part in recv_cot]
    up_all = jnp.concatenate(up_all, axis=1).reshape(resident, rank, out_width)
    up_parts = [up_all[b] for b in range(resident)]

    tail = sum(jnp.where(is_local[b], 0.0, up_parts[b]) for b in range(resident))
    far = jnp.zeros_like(tail)
    for step in range(1, HOPS + 1):
        other = (device + step) % devices * resident
        theirs = starts_of(other[None], start_ids)[0]
        far = far + jnp.where(theirs // resident == device, moved(tail, -step), 0.0)
    up_grads = []
    for k in range(resident):
        total = jnp.where(begin[resident - 1] == first_block + k, far, 0.0)
        for b in range(resident):
            total = total + jnp.where(is_local[b] & (home_slot[b] == k), up_parts[b], 0.0)
        up_grads.append(adapter_scale * total)
    up_map_gradient = jnp.stack(up_grads)

    return (out, down_map_gradient, up_map_gradient)


def solution(mesh):
    return jax.shard_map(
        local,
        mesh=mesh,
        in_specs=(
            P(("groups", "blk"), None),
            P(("groups", "blk"), None),
            P(("groups", "blk")),
            P("groups"),
            P("blk", None),
            P(("groups", "blk"), None, None),
            P(("groups", "blk"), None, None),
        ),
        out_specs=(
            P(("groups", "blk"), None),
            P(("groups", "blk"), None, None),
            P(("groups", "blk"), None, None),
        ),
        check_vma=False,
    )
```

```python
import functools

import jax
import jax.numpy as jnp
from jax import lax
from jax.experimental import pallas as pl
from jax.experimental.pallas import tpu as pltpu
from jax.sharding import PartitionSpec as P

BLOCK = 128
HOPS = 4
LANES = 128
DIGIT = 64
VMEM = 56 << 20

adapter_scale = 2.0


def moved(value, steps):
    count = lax.axis_size("blk")
    return lax.ppermute(value, "blk", [(i, (i + steps) % count) for i in range(count)])


def to_all(value):
    count = lax.axis_size("blk")
    copies = jnp.broadcast_to(value[None], (count,) + value.shape)
    return lax.all_to_all(copies, "blk", split_axis=0, concat_axis=0)


def after(value, *others):
    anywhere = pl.BlockSpec(memory_space=pl.ANY)
    return pl.pallas_call(
        lambda *refs: None,
        in_specs=[anywhere] * (1 + len(others)),
        out_specs=anywhere,
        out_shape=jax.ShapeDtypeStruct(value.shape, value.dtype),
        input_output_aliases={0: 0},
        cost_estimate=pl.CostEstimate(flops=0, bytes_accessed=0, transcendentals=0),
        compiler_params=pltpu.CompilerParams(vmem_limit_bytes=VMEM),
    )(value, *others)


def dot(a, b, dims):
    return lax.dot_general(a, b, (dims, ((), ())), preferred_element_type=jnp.float32)


def starts_of(blocks, start_ids):
    latest = jnp.max(
        jnp.where(start_ids[None, :] <= blocks[:, None], start_ids[None, :], -1), axis=1
    )
    return jnp.where(latest >= 0, latest, jnp.max(start_ids))


def as_digits(rows, places):
    return (
        rows % DIGIT,
        rows // DIGIT % DIGIT,
        rows // (DIGIT * DIGIT),
        places % DIGIT,
        places // DIGIT,
    )


def from_digits(digits):
    low, middle, high, place, place_high = [digits[:, k].astype(jnp.int32) for k in range(5)]
    return (high * DIGIT + middle) * DIGIT + low, place_high * DIGIT + place


def weight_pieces(weight):
    count = lax.axis_size("blk")
    half = weight.shape[0] // 2
    group = lax.axis_index("groups")
    mine = lax.dynamic_slice_in_dim(weight, group * half, half, 0)
    lines = [list(range(k, count, 4)) for k in range(4)]
    column = lax.all_gather(mine, "blk", axis_index_groups=lines)

    def over(piece, bit):
        return lax.ppermute(piece, "blk", [(i, i ^ bit) for i in range(count)])

    def groups(piece):
        return lax.ppermute(piece, "groups", [(0, 1), (1, 0)])

    across = over(column, 2)
    pieces = []
    for piece in (column, across):
        theirs = groups(piece)
        pieces.append((piece, theirs))
        pieces.append((over(piece, 1), over(theirs, 1)))
    return pieces


def quarter_kernel(where, cot, grad, down, mine, theirs, *rest):
    out, token = rest[-2:]
    token[...] = jnp.zeros_like(token)
    rank = grad.shape[1]
    half = mine.shape[1]
    lora = [
        adapter_scale
        * dot(
            grad[b * BLOCK : (b + 1) * BLOCK, :],
            down[b * rank : (b + 1) * rank, :],
            ((1,), (0,)),
        )
        for b in range(cot.shape[0] // BLOCK)
    ]
    lora = jnp.concatenate(lora, axis=0).astype(jnp.bfloat16).astype(jnp.float32)

    def product(group):
        for k, piece in enumerate((mine, theirs) if group == 0 else (theirs, mine)):
            part = slice(k * half, (k + 1) * half)
            frozen = dot(cot[...], piece[0], ((1,), (1,)))
            out[:, part] = (frozen + lora[:, part]).astype(jnp.bfloat16)

    for group in range(2):
        pl.when(where[1] == group)(functools.partial(product, group))


def write_quarter(quarter, first, group, cot, grad, down, out=None):
    mine, theirs = quarter
    rows, depth = cot.shape
    width = down.shape[1]
    shards, half, _ = mine.shape
    where = jnp.stack([first, group]).astype(jnp.int32)
    piece = pl.BlockSpec((1, half, depth), lambda j, where: (j, 0, 0))
    specs = [
        pl.BlockSpec((rows, depth), lambda j, where: (0, 0)),
        pl.BlockSpec(grad.shape, lambda j, where: (0, 0)),
        pl.BlockSpec((down.shape[0], 2 * half), lambda j, where: (0, 4 * j + where[0])),
        piece,
        piece,
    ]
    args = [where, cot, grad, down, mine, theirs]
    alias = {}
    if out is not None:
        specs.append(pl.BlockSpec(memory_space=pl.ANY))
        args.append(out)
        alias = {len(args) - 1: 0}
    return pl.pallas_call(
        quarter_kernel,
        grid_spec=pltpu.PrefetchScalarGridSpec(
            num_scalar_prefetch=1,
            grid=(shards,),
            in_specs=specs,
            out_specs=[
                pl.BlockSpec((rows, 2 * half), lambda j, where: (0, 4 * j + where[0])),
                pl.BlockSpec((8, LANES), lambda j, where: (0, 0)),
            ],
        ),
        out_shape=[
            jax.ShapeDtypeStruct((rows, width), jnp.bfloat16),
            jax.ShapeDtypeStruct((8, LANES), jnp.float32),
        ],
        input_output_aliases=alias,
        cost_estimate=pl.CostEstimate(
            flops=4 * rows * depth * half * shards,
            bytes_accessed=4 * (depth + rows) * half * shards,
            transcendentals=0,
        ),
        compiler_params=pltpu.CompilerParams(vmem_limit_bytes=VMEM),
    )(*args)


def together(pieces, firsts, group):
    shards, half, depth = pieces[0][0].shape
    weight = jnp.zeros((shards, 4, 2, half, depth), jnp.bfloat16)
    for quarter, first in zip(pieces, firsts):
        for k, piece in enumerate(quarter):
            place = (0, first, group if k == 0 else 1 - group, 0, 0)
            weight = lax.dynamic_update_slice(weight, piece[:, None, None], place)
    return weight.reshape(-1, depth)


def rows_kernel(rows, cot, out, place):
    devices, packed, features = out.shape
    shared = packed - 16
    folds = cot.shape[1] // features
    cap = shared // folds
    target = rows[...] // (cap * devices)
    to = lax.broadcasted_iota(jnp.int32, (16, features), 0) == target
    first = lax.broadcasted_iota(jnp.int32, (features, features), 0)
    later = lax.broadcasted_iota(jnp.int32, (features, features), 1)
    earlier = jnp.where(first < later, 1.0, 0.0).astype(jnp.bfloat16)
    ahead = dot(jnp.where(to, 1.0, 0.0).astype(jnp.bfloat16), earlier, ((1,), (0,)))
    ahead = jnp.sum(jnp.where(to, ahead, 0.0), axis=0, keepdims=True)
    place[...] = target * cap + ahead.astype(jnp.int32)
    which = lax.broadcasted_iota(jnp.int32, (16, features), 0)
    digits = jnp.zeros((16, features), jnp.int32)
    for k, digit in enumerate(as_digits(rows[...], place[...])):
        digits = jnp.where(which == k, digit, digits)
    digits = digits.astype(jnp.float32).astype(out.dtype)
    send = placing(place[:, : cot.shape[0]], cap * devices)
    for f in range(folds):
        sent = dot(send, cot[:, f * features : (f + 1) * features], ((1,), (0,)))
        for k in range(devices):
            some = sent[k * cap : (k + 1) * cap].astype(out.dtype)
            out[k, f * cap : (f + 1) * cap, :] = some
    for k in range(devices):
        out[k, shared:, :] = digits


def pack_rows(rows, cot, devices, cap, features):
    tokens = rows.shape[0]
    folds = cot.shape[1] // features
    if features % LANES == 0 and cap % 8 == 0 and features >= tokens and devices <= 16:
        padding = jnp.full((features - tokens,), 16 * cap * devices, jnp.int32)
        return pl.pallas_call(
            rows_kernel,
            out_shape=jax.ShapeDtypeStruct((devices, folds * cap + 16, features), cot.dtype),
            scratch_shapes=[pltpu.VMEM((1, features), jnp.int32)],
            cost_estimate=pl.CostEstimate(
                flops=2 * devices * cap * tokens * cot.shape[1],
                bytes_accessed=6 * cot.size,
                transcendentals=0,
            ),
            compiler_params=pltpu.CompilerParams(vmem_limit_bytes=VMEM),
        )(jnp.concatenate([rows, padding])[None], cot)
    target = rows // (cap * devices)
    order = jnp.arange(tokens, dtype=jnp.int32)
    before = (target[:, None] == target[None, :]) & (order[None, :] < order[:, None])
    place = target * cap + jnp.sum(before.astype(jnp.int32), axis=1)
    send = jnp.arange(cap * devices, dtype=jnp.int32)[:, None] == place[None, :]
    sent = dot(send.astype(jnp.bfloat16), cot, ((1,), (0,))).astype(jnp.bfloat16)
    sent = sent.reshape(devices, cap, cot.shape[1])
    digits = jnp.stack(as_digits(rows, place)).astype(jnp.bfloat16)
    digits = jnp.pad(digits, ((0, 0), (0, -tokens % features))).reshape(-1, features)
    digits = jnp.pad(digits, ((0, -digits.shape[0] % 16), (0, 0)))
    parts = [sent[:, :, k : k + features] for k in range(0, cot.shape[1], features)]
    parts += [jnp.broadcast_to(digits[None], (devices,) + digits.shape)]
    return jnp.concatenate(parts, axis=1)


def features_kernel(act, maps, out):
    targets, _, features = out.shape
    tokens = act.shape[0]
    for k in range(targets):
        part = slice(k * features, (k + 1) * features)
        out[k, :tokens, :] = act[:, part]
        out[k, tokens:, :] = maps[:, part]


def pack_features(act, maps, devices):
    tokens, width = act.shape
    features = width // devices
    shared = maps.shape[0]
    targets = 4
    if features % LANES == 0:
        return pl.pallas_call(
            features_kernel,
            grid=(devices // targets,),
            in_specs=[
                pl.BlockSpec((tokens, targets * features), lambda j: (0, j)),
                pl.BlockSpec((shared, targets * features), lambda j: (0, j)),
            ],
            out_specs=pl.BlockSpec((targets, tokens + shared, features), lambda j: (j, 0, 0)),
            out_shape=jax.ShapeDtypeStruct((devices, tokens + shared, features), act.dtype),
            cost_estimate=pl.CostEstimate(
                flops=0, bytes_accessed=4 * (tokens + shared) * width, transcendentals=0
            ),
            compiler_params=pltpu.CompilerParams(vmem_limit_bytes=VMEM),
        )(act, maps)
    both = jnp.concatenate([act, maps], axis=0)
    return both.reshape(tokens + shared, devices, features).transpose(1, 0, 2)


def slot_chunks(width):
    size = min(width, 768)
    while width % size:
        size //= 2
    return [slice(k, k + size) for k in range(0, width, size)]


def slot_of(rows, starts):
    blocks = rows // BLOCK
    latest = jnp.max(jnp.where(starts <= blocks, starts, -1), axis=0, keepdims=True)
    return jnp.where(latest >= 0, latest, jnp.max(starts))


def own_rows(slot, first, size, rank):
    index = first // rank + lax.broadcasted_iota(jnp.int32, (size // rank, rank, 1), 0)
    return index == slot[None]


def placing(place, places):
    hit = lax.broadcasted_iota(jnp.int32, (places, place.shape[1]), 0) == place
    return jnp.where(hit, 1.0, 0.0).astype(jnp.bfloat16)


def all_rows(act, tokens):
    return jnp.concatenate([act[k, :tokens, :] for k in range(act.shape[0])], axis=0)


def of_source(sources, width):
    lane = lax.broadcasted_iota(jnp.int32, (sources, 1, width), 2)
    return lane // (width // sources) == lax.broadcasted_iota(
        jnp.int32, (sources, 1, width), 0
    )


def hidden_kernel(act, maps, rows, spots, starts, out):
    sources, share, width = act.shape[0], maps.shape[1], rows.shape[1]
    rank, places = out.shape[0] // sources, out.shape[1]
    slot = slot_of(rows[...], starts[...])
    every = all_rows(act, width // sources)
    total = jnp.zeros((rank, width), jnp.float32)
    for part in slot_chunks(maps.shape[0] * share):
        size = part.stop - part.start
        some = maps[part.start // share : part.stop // share].reshape(size, -1)
        each = dot(some, every, ((1,), (1,))).reshape(size // rank, rank, -1)
        total += jnp.sum(jnp.where(own_rows(slot, part.start, size, rank), each, 0.0), axis=0)
    total = jnp.where(of_source(sources, width), total[None], 0.0).reshape(out.shape[0], width)
    high = total.astype(jnp.bfloat16)
    low = (total - high.astype(jnp.float32)).astype(jnp.bfloat16)
    place = placing(spots[...], places)
    out[...] = dot(high, place, ((1,), (1,))) + dot(low, place, ((1,), (1,)))


def down_kernel(act, grad, rows, spots, starts, out, total):
    sources, width = act.shape[0], rows.shape[1]
    rank, places = grad.shape[0] // sources, grad.shape[1]
    step = pl.program_id(0)

    @pl.when(step == 0)
    def _():
        total[...] = jnp.zeros_like(total)

    slot = slot_of(rows[...], starts[...])
    every = all_rows(act, width // sources)
    wide = dot(grad[...], placing(spots[...], places), ((1,), (0,)))
    wide = wide.reshape(sources, rank, width)
    wide = jnp.sum(jnp.where(of_source(sources, width), wide, 0.0), axis=0, keepdims=True)
    for part in slot_chunks(total.shape[0]):
        size = part.stop - part.start
        placed = jnp.where(own_rows(slot, part.start, size, rank), wide, 0.0)
        placed = placed.reshape(size, -1).astype(jnp.bfloat16)
        total[part, :] += dot(placed, every, ((1,), (0,)))

    @pl.when(step == pl.num_programs(0) - 1)
    def _():
        out[...] = (adapter_scale * total[...]).astype(out.dtype)


def feature_calls(received, tokens, share, rank, places, starts):
    devices, packed, features = received.shape
    width = devices * share
    sources = 4
    grid = (devices // sources,)
    act = pl.BlockSpec((sources, packed, features), lambda j: (j, 0, 0))
    maps = pl.BlockSpec((devices, share, features), lambda j: (0, tokens // share, 0))
    rows = pl.BlockSpec((1, sources * tokens), lambda j: (0, j))
    begin = pl.BlockSpec((starts, 1), lambda j: (0, 0))
    placed = pl.BlockSpec((sources * rank, places), lambda j: (j, 0))
    cost = pl.CostEstimate(
        flops=2 * devices * tokens * width * features,
        bytes_accessed=2 * devices * tokens * features,
        transcendentals=0,
    )
    params = pltpu.CompilerParams(vmem_limit_bytes=VMEM)
    hidden = pl.pallas_call(
        hidden_kernel,
        grid=grid,
        in_specs=[act, maps, rows, rows, begin],
        out_specs=placed,
        out_shape=jax.ShapeDtypeStruct((devices * rank, places), jnp.float32),
        cost_estimate=cost,
        compiler_params=params,
    )
    down = pl.pallas_call(
        down_kernel,
        grid=grid,
        in_specs=[act, placed, rows, rows, begin],
        out_specs=pl.BlockSpec((width, features), lambda j: (0, 0)),
        out_shape=jax.ShapeDtypeStruct((width, features), jnp.bfloat16),
        scratch_shapes=[pltpu.VMEM((width, features), jnp.float32)],
        cost_estimate=cost,
        compiler_params=params,
    )
    return hidden, down


def local(
    activations,
    cotangent,
    token_layout_row,
    tenant_first_row,
    frozen_value_weight,
    adapter_down_maps,
    adapter_up_maps,
):
    devices = lax.axis_size("blk")
    device = lax.axis_index("blk")
    tokens = activations.shape[0]
    resident, rank, width = adapter_down_maps.shape
    out_width = cotangent.shape[1]
    features = width // devices
    share = resident * rank
    resident_rows = resident * BLOCK
    cap = resident_rows // devices
    start_ids = tenant_first_row // BLOCK

    pieces = weight_pieces(frozen_value_weight)

    sent_rows = pack_rows(token_layout_row, cotangent, devices, cap, features)
    sent_rows = after(sent_rows, pieces[0][0])
    got_rows = lax.all_to_all(sent_rows, "blk", split_axis=0, concat_axis=0)
    recv_cot = [
        got_rows[:, k * cap : (k + 1) * cap].reshape(resident_rows, features)
        for k in range(out_width // features)
    ]
    per_digit = -(-tokens // features)
    digits = got_rows[:, share : share + 5 * per_digit]
    digits = digits.reshape(devices, 5, per_digit * features)[:, :, :tokens]
    rows_all, place_all = from_digits(digits)

    first_block = device * resident
    block_numbers = first_block + jnp.arange(resident, dtype=jnp.int32)
    begin = starts_of(block_numbers, start_ids)
    is_local = (begin >= first_block) & (begin <= block_numbers)
    home_slot = jnp.clip(begin - first_block, 0, resident - 1)
    last_map = jnp.concatenate(
        [
            lax.dynamic_index_in_dim(maps, home_slot[resident - 1], 0, keepdims=False)
            for maps in (adapter_down_maps, adapter_up_maps)
        ],
        axis=1,
    )
    carried = jnp.zeros_like(last_map)
    for step in range(1, HOPS + 1):
        home = (device - step) % devices
        carried = jnp.where(begin[0] // resident == home, moved(last_map, step), carried)

    def of_blocks(maps, own):
        blocks = []
        for b in range(resident):
            chosen = own
            for k in range(b + 1):
                chosen = jnp.where(is_local[b] & (home_slot[b] == k), maps[k], chosen)
            blocks.append(chosen)
        return jnp.concatenate(blocks, axis=0)

    down_blocks = of_blocks(adapter_down_maps, carried[:, :width])
    up_blocks = of_blocks(adapter_up_maps, carried[:, width:])

    spots = device * cap + jnp.arange(cap, dtype=jnp.int32)
    hit = place_all[:, None, :] == spots[None, :, None]
    row_in = rows_all - device * resident_rows + 1
    row_in = jnp.sum(jnp.where(hit, row_in[:, None, :], 0), axis=2).reshape(-1) - 1
    arrange = row_in[:, None] == jnp.arange(resident_rows, dtype=jnp.int32)[None, :]
    arrange = arrange.astype(jnp.bfloat16)
    in_block = row_in[:, None] // BLOCK == jnp.arange(share, dtype=jnp.int32)[None, :] // rank

    grad_in = sum(
        dot(part, up_blocks[:, k * features : (k + 1) * features], ((1,), (1,)))
        for k, part in enumerate(recv_cot)
    )
    grad_in = jnp.where(in_block, grad_in, 0.0).astype(jnp.bfloat16)
    grad_in = sum(grad_in[:, b * rank : (b + 1) * rank] for b in range(resident))
    grad_sent = grad_in.reshape(devices, cap, rank).transpose(1, 0, 2).reshape(cap, -1)

    flat_maps = adapter_down_maps.reshape(share, width)
    received = after(pack_features(activations, flat_maps, devices), got_rows)
    received = lax.all_to_all(received, "blk", split_axis=0, concat_axis=0)
    grad_all = to_all(after(grad_sent, received)).reshape(resident_rows, -1).T

    rows_all, place_all = rows_all.reshape(1, -1), place_all.reshape(1, -1)

    cot_rows = jnp.concatenate(
        [dot(arrange, part, ((0,), (0,))).astype(jnp.bfloat16) for part in recv_cot], axis=1
    )
    grad_rows = dot(arrange, grad_in, ((0,), (0,))).astype(jnp.bfloat16)
    group = lax.axis_index("groups")
    quarter = device % 4
    firsts = [quarter, quarter ^ 1, quarter ^ 2, quarter ^ 3]
    if pieces[0][0].shape[1] % LANES == 0:
        out = None
        for number, (piece, first) in enumerate(zip(pieces, firsts)):
            out, token = write_quarter(
                piece, first, group, cot_rows, grad_rows, down_blocks, out
            )
            if number == 3:
                place_all = after(place_all, token)
    else:
        weight = together(pieces, firsts, group)
        lora = [
            dot(
                grad_rows[b * BLOCK : (b + 1) * BLOCK],
                down_blocks[b * rank : (b + 1) * rank],
                ((1,), (0,)),
            )
            for b in range(resident)
        ]
        lora = (adapter_scale * jnp.concatenate(lora, axis=0)).astype(jnp.bfloat16)
        out = dot(cot_rows, weight, ((1,), (1,))) + lora.astype(jnp.float32)
        out = out.astype(jnp.bfloat16)

    starts = start_ids[:, None]
    hidden_call, down_call = feature_calls(
        received, tokens, share, rank, resident_rows, starts.shape[0]
    )
    shares = hidden_call(received, received, rows_all, place_all, starts)
    rows_all = after(rows_all, shares)
    down_f = down_call(received, grad_all, rows_all, place_all, starts)
    hidden = shares.T.reshape(devices, cap, -1)
    hidden = lax.all_to_all(hidden, "blk", split_axis=0, concat_axis=0)
    hidden = jnp.sum(hidden, axis=0).astype(jnp.bfloat16)
    hidden = hidden.reshape(cap, devices, rank).transpose(1, 0, 2).reshape(-1, rank)
    down_home = lax.all_to_all(down_f, "blk", split_axis=0, concat_axis=1, tiled=True)
    down_map_gradient = down_home.astype(jnp.float32).reshape(resident, rank, width)

    wide = jnp.where(in_block, jnp.concatenate([hidden] * resident, axis=1), 0)
    up_all = [dot(wide, part, ((0,), (0,))) for part in recv_cot]
    up_all = jnp.concatenate(up_all, axis=1).reshape(resident, rank, out_width)
    up_parts = [up_all[b] for b in range(resident)]

    tail = sum(jnp.where(is_local[b], 0.0, up_parts[b]) for b in range(resident))
    far = jnp.zeros_like(tail)
    for step in range(1, HOPS + 1):
        other = (device + step) % devices * resident
        theirs = starts_of(other[None], start_ids)[0]
        far = far + jnp.where(theirs // resident == device, moved(tail, -step), 0.0)
    up_grads = []
    for k in range(resident):
        total = jnp.where(begin[resident - 1] == first_block + k, far, 0.0)
        for b in range(resident):
            total = total + jnp.where(is_local[b] & (home_slot[b] == k), up_parts[b], 0.0)
        up_grads.append(adapter_scale * total)
    up_map_gradient = jnp.stack(up_grads)

    return (out, down_map_gradient, up_map_gradient)


def solution(mesh):
    return jax.shard_map(
        local,
        mesh=mesh,
        in_specs=(
            P(("groups", "blk"), None),
            P(("groups", "blk"), None),
            P(("groups", "blk")),
            P("groups"),
            P("blk", None),
            P(("groups", "blk"), None, None),
            P(("groups", "blk"), None, None),
        ),
        out_specs=(
            P(("groups", "blk"), None),
            P(("groups", "blk"), None, None),
            P(("groups", "blk"), None, None),
        ),
        check_vma=False,
    )
```

```python
import functools

import jax
import jax.numpy as jnp
from jax import lax
from jax.experimental import pallas as pl
from jax.experimental.pallas import tpu as pltpu
from jax.sharding import PartitionSpec as P

BLOCK = 128
HOPS = 4
LANES = 128
DIGIT = 64
VMEM = 56 << 20

adapter_scale = 2.0


def moved(value, steps):
    count = lax.axis_size("blk")
    return lax.ppermute(value, "blk", [(i, (i + steps) % count) for i in range(count)])


def to_all(value):
    count = lax.axis_size("blk")
    copies = jnp.broadcast_to(value[None], (count,) + value.shape)
    return lax.all_to_all(copies, "blk", split_axis=0, concat_axis=0)


def after(value, *others):
    anywhere = pl.BlockSpec(memory_space=pl.ANY)
    return pl.pallas_call(
        lambda *refs: None,
        in_specs=[anywhere] * (1 + len(others)),
        out_specs=anywhere,
        out_shape=jax.ShapeDtypeStruct(value.shape, value.dtype),
        input_output_aliases={0: 0},
        cost_estimate=pl.CostEstimate(flops=0, bytes_accessed=0, transcendentals=0),
        compiler_params=pltpu.CompilerParams(vmem_limit_bytes=VMEM),
    )(value, *others)


def dot(a, b, dims):
    return lax.dot_general(a, b, (dims, ((), ())), preferred_element_type=jnp.float32)


def starts_of(blocks, start_ids):
    latest = jnp.max(
        jnp.where(start_ids[None, :] <= blocks[:, None], start_ids[None, :], -1), axis=1
    )
    return jnp.where(latest >= 0, latest, jnp.max(start_ids))


def as_digits(rows, places):
    return (
        rows % DIGIT,
        rows // DIGIT % DIGIT,
        rows // (DIGIT * DIGIT),
        places % DIGIT,
        places // DIGIT,
    )


def from_digits(digits):
    low, middle, high, place, place_high = [digits[:, k].astype(jnp.int32) for k in range(5)]
    return (high * DIGIT + middle) * DIGIT + low, place_high * DIGIT + place


CHUNKS = 2


def weight_pieces(weight):
    count = lax.axis_size("blk")
    half = weight.shape[0] // 2
    size = half // CHUNKS
    first = lax.axis_index("groups") * half
    lines = [list(range(k, count, 4)) for k in range(4)]

    def over(piece, bit):
        return lax.ppermute(piece, "blk", [(i, i ^ bit) for i in range(count)])

    def groups(piece):
        return lax.ppermute(piece, "groups", [(0, 1), (1, 0)])

    columns = [
        lax.all_gather(
            lax.dynamic_slice_in_dim(weight, first + k * size, size, 0),
            "blk",
            axis_index_groups=lines,
        )
        for k in range(CHUNKS)
    ]
    pieces = []
    for mine in (columns, [over(column, 2) for column in columns]):
        both = mine + [groups(piece) for piece in mine]
        pieces += [both, [over(piece, 1) for piece in both]]
    return pieces


def quarter_kernel(where, cot, grad, down, *rest):
    pieces = rest[: 2 * CHUNKS]
    out, token = rest[-2:]
    token[...] = jnp.zeros_like(token)
    rank = grad.shape[1]
    lora = [
        adapter_scale
        * dot(
            grad[b * BLOCK : (b + 1) * BLOCK, :],
            down[b * rank : (b + 1) * rank, :],
            ((1,), (0,)),
        )
        for b in range(cot.shape[0] // BLOCK)
    ]
    lora = jnp.concatenate(lora, axis=0).astype(jnp.bfloat16).astype(jnp.float32)

    def product(group):
        order = pieces[group * CHUNKS :] + pieces[: group * CHUNKS]
        weight = jnp.concatenate([piece[0] for piece in order], axis=0)
        frozen = dot(cot[...], weight, ((1,), (1,)))
        out[...] = (frozen + lora).astype(jnp.bfloat16)

    for group in range(2):
        pl.when(where[1] == group)(functools.partial(product, group))


def write_quarter(quarter, first, group, cot, grad, down, out=None):
    rows, depth = cot.shape
    width = down.shape[1]
    shards, part, _ = quarter[0].shape
    stripe = part * len(quarter)
    where = jnp.stack([first, group]).astype(jnp.int32)
    specs = [
        pl.BlockSpec((rows, depth), lambda j, where: (0, 0)),
        pl.BlockSpec(grad.shape, lambda j, where: (0, 0)),
        pl.BlockSpec((down.shape[0], stripe), lambda j, where: (0, 4 * j + where[0])),
    ] + [pl.BlockSpec((1, part, depth), lambda j, where: (j, 0, 0)) for _ in quarter]
    args = [where, cot, grad, down] + quarter
    alias = {}
    if out is not None:
        specs.append(pl.BlockSpec(memory_space=pl.ANY))
        args.append(out)
        alias = {len(args) - 1: 0}
    return pl.pallas_call(
        quarter_kernel,
        grid_spec=pltpu.PrefetchScalarGridSpec(
            num_scalar_prefetch=1,
            grid=(shards,),
            in_specs=specs,
            out_specs=[
                pl.BlockSpec((rows, stripe), lambda j, where: (0, 4 * j + where[0])),
                pl.BlockSpec((8, LANES), lambda j, where: (0, 0)),
            ],
        ),
        out_shape=[
            jax.ShapeDtypeStruct((rows, width), jnp.bfloat16),
            jax.ShapeDtypeStruct((8, LANES), jnp.float32),
        ],
        input_output_aliases=alias,
        cost_estimate=pl.CostEstimate(
            flops=2 * rows * depth * stripe * shards,
            bytes_accessed=2 * (depth + rows) * stripe * shards,
            transcendentals=0,
        ),
        compiler_params=pltpu.CompilerParams(vmem_limit_bytes=VMEM),
    )(*args)


def together(pieces, firsts, group):
    shards, part, depth = pieces[0][0].shape
    weight = jnp.zeros((shards, 4, 2, CHUNKS, part, depth), jnp.bfloat16)
    for quarter, first in zip(pieces, firsts):
        for k, piece in enumerate(quarter):
            half = group if k < CHUNKS else 1 - group
            place = (0, first, half, k % CHUNKS, 0, 0)
            weight = lax.dynamic_update_slice(weight, piece[:, None, None, None], place)
    return weight.reshape(-1, depth)


def rows_kernel(rows, cot, out, place):
    devices, packed, features = out.shape
    shared = packed - 16
    folds = cot.shape[1] // features
    cap = shared // folds
    target = rows[...] // (cap * devices)
    to = lax.broadcasted_iota(jnp.int32, (16, features), 0) == target
    first = lax.broadcasted_iota(jnp.int32, (features, features), 0)
    later = lax.broadcasted_iota(jnp.int32, (features, features), 1)
    earlier = jnp.where(first < later, 1.0, 0.0).astype(jnp.bfloat16)
    ahead = dot(jnp.where(to, 1.0, 0.0).astype(jnp.bfloat16), earlier, ((1,), (0,)))
    ahead = jnp.sum(jnp.where(to, ahead, 0.0), axis=0, keepdims=True)
    place[...] = target * cap + ahead.astype(jnp.int32)
    which = lax.broadcasted_iota(jnp.int32, (16, features), 0)
    digits = jnp.zeros((16, features), jnp.int32)
    for k, digit in enumerate(as_digits(rows[...], place[...])):
        digits = jnp.where(which == k, digit, digits)
    digits = digits.astype(jnp.float32).astype(out.dtype)
    send = placing(place[:, : cot.shape[0]], cap * devices)
    for f in range(folds):
        sent = dot(send, cot[:, f * features : (f + 1) * features], ((1,), (0,)))
        for k in range(devices):
            some = sent[k * cap : (k + 1) * cap].astype(out.dtype)
            out[k, f * cap : (f + 1) * cap, :] = some
    for k in range(devices):
        out[k, shared:, :] = digits


def pack_rows(rows, cot, devices, cap, features):
    tokens = rows.shape[0]
    folds = cot.shape[1] // features
    if features % LANES == 0 and cap % 8 == 0 and features >= tokens and devices <= 16:
        padding = jnp.full((features - tokens,), 16 * cap * devices, jnp.int32)
        return pl.pallas_call(
            rows_kernel,
            out_shape=jax.ShapeDtypeStruct((devices, folds * cap + 16, features), cot.dtype),
            scratch_shapes=[pltpu.VMEM((1, features), jnp.int32)],
            cost_estimate=pl.CostEstimate(
                flops=2 * devices * cap * tokens * cot.shape[1],
                bytes_accessed=6 * cot.size,
                transcendentals=0,
            ),
            compiler_params=pltpu.CompilerParams(vmem_limit_bytes=VMEM),
        )(jnp.concatenate([rows, padding])[None], cot)
    target = rows // (cap * devices)
    order = jnp.arange(tokens, dtype=jnp.int32)
    before = (target[:, None] == target[None, :]) & (order[None, :] < order[:, None])
    place = target * cap + jnp.sum(before.astype(jnp.int32), axis=1)
    send = jnp.arange(cap * devices, dtype=jnp.int32)[:, None] == place[None, :]
    sent = dot(send.astype(jnp.bfloat16), cot, ((1,), (0,))).astype(jnp.bfloat16)
    sent = sent.reshape(devices, cap, cot.shape[1])
    digits = jnp.stack(as_digits(rows, place)).astype(jnp.bfloat16)
    digits = jnp.pad(digits, ((0, 0), (0, -tokens % features))).reshape(-1, features)
    digits = jnp.pad(digits, ((0, -digits.shape[0] % 16), (0, 0)))
    parts = [sent[:, :, k : k + features] for k in range(0, cot.shape[1], features)]
    parts += [jnp.broadcast_to(digits[None], (devices,) + digits.shape)]
    return jnp.concatenate(parts, axis=1)


def features_kernel(act, maps, out):
    targets, _, features = out.shape
    tokens = act.shape[0]
    for k in range(targets):
        part = slice(k * features, (k + 1) * features)
        out[k, :tokens, :] = act[:, part]
        out[k, tokens:, :] = maps[:, part]


def pack_features(act, maps, devices):
    tokens, width = act.shape
    features = width // devices
    shared = maps.shape[0]
    targets = 4
    if features % LANES == 0:
        return pl.pallas_call(
            features_kernel,
            grid=(devices // targets,),
            in_specs=[
                pl.BlockSpec((tokens, targets * features), lambda j: (0, j)),
                pl.BlockSpec((shared, targets * features), lambda j: (0, j)),
            ],
            out_specs=pl.BlockSpec((targets, tokens + shared, features), lambda j: (j, 0, 0)),
            out_shape=jax.ShapeDtypeStruct((devices, tokens + shared, features), act.dtype),
            cost_estimate=pl.CostEstimate(
                flops=0, bytes_accessed=4 * (tokens + shared) * width, transcendentals=0
            ),
            compiler_params=pltpu.CompilerParams(vmem_limit_bytes=VMEM),
        )(act, maps)
    both = jnp.concatenate([act, maps], axis=0)
    return both.reshape(tokens + shared, devices, features).transpose(1, 0, 2)


def slot_chunks(width):
    size = min(width, 768)
    while width % size:
        size //= 2
    return [slice(k, k + size) for k in range(0, width, size)]


def slot_of(rows, starts):
    blocks = rows // BLOCK
    latest = jnp.max(jnp.where(starts <= blocks, starts, -1), axis=0, keepdims=True)
    return jnp.where(latest >= 0, latest, jnp.max(starts))


def own_rows(slot, first, size, rank):
    index = first // rank + lax.broadcasted_iota(jnp.int32, (size // rank, rank, 1), 0)
    return index == slot[None]


def placing(place, places):
    hit = lax.broadcasted_iota(jnp.int32, (places, place.shape[1]), 0) == place
    return jnp.where(hit, 1.0, 0.0).astype(jnp.bfloat16)


def all_rows(act, tokens):
    return jnp.concatenate([act[k, :tokens, :] for k in range(act.shape[0])], axis=0)


def of_source(sources, width):
    lane = lax.broadcasted_iota(jnp.int32, (sources, 1, width), 2)
    return lane // (width // sources) == lax.broadcasted_iota(
        jnp.int32, (sources, 1, width), 0
    )


def hidden_kernel(act, maps, rows, spots, starts, out):
    sources, share, width = act.shape[0], maps.shape[1], rows.shape[1]
    rank, places = out.shape[0] // sources, out.shape[1]
    slot = slot_of(rows[...], starts[...])
    every = all_rows(act, width // sources)
    total = jnp.zeros((rank, width), jnp.float32)
    for part in slot_chunks(maps.shape[0] * share):
        size = part.stop - part.start
        some = maps[part.start // share : part.stop // share].reshape(size, -1)
        each = dot(some, every, ((1,), (1,))).reshape(size // rank, rank, -1)
        total += jnp.sum(jnp.where(own_rows(slot, part.start, size, rank), each, 0.0), axis=0)
    total = jnp.where(of_source(sources, width), total[None], 0.0).reshape(out.shape[0], width)
    high = total.astype(jnp.bfloat16)
    low = (total - high.astype(jnp.float32)).astype(jnp.bfloat16)
    place = placing(spots[...], places)
    out[...] = dot(high, place, ((1,), (1,))) + dot(low, place, ((1,), (1,)))


def down_kernel(act, grad, rows, spots, starts, out, total):
    sources, width = act.shape[0], rows.shape[1]
    rank, places = grad.shape[0] // sources, grad.shape[1]
    step = pl.program_id(0)

    @pl.when(step == 0)
    def _():
        total[...] = jnp.zeros_like(total)

    slot = slot_of(rows[...], starts[...])
    every = all_rows(act, width // sources)
    wide = dot(grad[...], placing(spots[...], places), ((1,), (0,)))
    wide = wide.reshape(sources, rank, width)
    wide = jnp.sum(jnp.where(of_source(sources, width), wide, 0.0), axis=0, keepdims=True)
    for part in slot_chunks(total.shape[0]):
        size = part.stop - part.start
        placed = jnp.where(own_rows(slot, part.start, size, rank), wide, 0.0)
        placed = placed.reshape(size, -1).astype(jnp.bfloat16)
        total[part, :] += dot(placed, every, ((1,), (0,)))

    @pl.when(step == pl.num_programs(0) - 1)
    def _():
        out[...] = (adapter_scale * total[...]).astype(out.dtype)


def feature_calls(received, tokens, share, rank, places, starts):
    devices, packed, features = received.shape
    width = devices * share
    sources = 4
    grid = (devices // sources,)
    act = pl.BlockSpec((sources, packed, features), lambda j: (j, 0, 0))
    maps = pl.BlockSpec((devices, share, features), lambda j: (0, tokens // share, 0))
    rows = pl.BlockSpec((1, sources * tokens), lambda j: (0, j))
    begin = pl.BlockSpec((starts, 1), lambda j: (0, 0))
    placed = pl.BlockSpec((sources * rank, places), lambda j: (j, 0))
    cost = pl.CostEstimate(
        flops=2 * devices * tokens * width * features,
        bytes_accessed=2 * devices * tokens * features,
        transcendentals=0,
    )
    params = pltpu.CompilerParams(vmem_limit_bytes=VMEM)
    hidden = pl.pallas_call(
        hidden_kernel,
        grid=grid,
        in_specs=[act, maps, rows, rows, begin],
        out_specs=placed,
        out_shape=jax.ShapeDtypeStruct((devices * rank, places), jnp.float32),
        cost_estimate=cost,
        compiler_params=params,
    )
    down = pl.pallas_call(
        down_kernel,
        grid=grid,
        in_specs=[act, placed, rows, rows, begin],
        out_specs=pl.BlockSpec((width, features), lambda j: (0, 0)),
        out_shape=jax.ShapeDtypeStruct((width, features), jnp.bfloat16),
        scratch_shapes=[pltpu.VMEM((width, features), jnp.float32)],
        cost_estimate=cost,
        compiler_params=params,
    )
    return hidden, down


def local(
    activations,
    cotangent,
    token_layout_row,
    tenant_first_row,
    frozen_value_weight,
    adapter_down_maps,
    adapter_up_maps,
):
    devices = lax.axis_size("blk")
    device = lax.axis_index("blk")
    tokens = activations.shape[0]
    resident, rank, width = adapter_down_maps.shape
    out_width = cotangent.shape[1]
    features = width // devices
    share = resident * rank
    resident_rows = resident * BLOCK
    cap = resident_rows // devices
    start_ids = tenant_first_row // BLOCK

    pieces = weight_pieces(frozen_value_weight)

    first_block = device * resident
    block_numbers = first_block + jnp.arange(resident, dtype=jnp.int32)
    begin = starts_of(block_numbers, start_ids)
    is_local = (begin >= first_block) & (begin <= block_numbers)
    home_slot = jnp.clip(begin - first_block, 0, resident - 1)
    last_map = jnp.concatenate(
        [
            lax.dynamic_index_in_dim(maps, home_slot[resident - 1], 0, keepdims=False)
            for maps in (adapter_down_maps, adapter_up_maps)
        ],
        axis=1,
    )
    carried = jnp.zeros_like(last_map)
    for step in range(1, HOPS + 1):
        home = (device - step) % devices
        carried = jnp.where(begin[0] // resident == home, moved(last_map, step), carried)

    def of_blocks(maps, own):
        blocks = []
        for b in range(resident):
            chosen = own
            for k in range(b + 1):
                chosen = jnp.where(is_local[b] & (home_slot[b] == k), maps[k], chosen)
            blocks.append(chosen)
        return jnp.concatenate(blocks, axis=0)

    down_blocks = of_blocks(adapter_down_maps, carried[:, :width])
    up_blocks = of_blocks(adapter_up_maps, carried[:, width:])

    sent_rows = pack_rows(token_layout_row, cotangent, devices, cap, features)
    own, _, across, _ = pieces
    early = [own[CHUNKS - 1], own[CHUNKS], across[0], carried]
    sent_rows = after(sent_rows, *early)
    got_rows = lax.all_to_all(sent_rows, "blk", split_axis=0, concat_axis=0)
    recv_cot = [
        got_rows[:, k * cap : (k + 1) * cap].reshape(resident_rows, features)
        for k in range(out_width // features)
    ]
    per_digit = -(-tokens // features)
    digits = got_rows[:, share : share + 5 * per_digit]
    digits = digits.reshape(devices, 5, per_digit * features)[:, :, :tokens]
    rows_all, place_all = from_digits(digits)

    spots = device * cap + jnp.arange(cap, dtype=jnp.int32)
    hit = place_all[:, None, :] == spots[None, :, None]
    row_in = rows_all - device * resident_rows + 1
    row_in = jnp.sum(jnp.where(hit, row_in[:, None, :], 0), axis=2).reshape(-1) - 1
    arrange = row_in[:, None] == jnp.arange(resident_rows, dtype=jnp.int32)[None, :]
    arrange = arrange.astype(jnp.bfloat16)
    in_block = row_in[:, None] // BLOCK == jnp.arange(share, dtype=jnp.int32)[None, :] // rank

    grad_in = sum(
        dot(part, up_blocks[:, k * features : (k + 1) * features], ((1,), (1,)))
        for k, part in enumerate(recv_cot)
    )
    grad_in = jnp.where(in_block, grad_in, 0.0).astype(jnp.bfloat16)
    grad_in = sum(grad_in[:, b * rank : (b + 1) * rank] for b in range(resident))
    grad_sent = grad_in.reshape(devices, cap, rank).transpose(1, 0, 2).reshape(cap, -1)

    flat_maps = adapter_down_maps.reshape(share, width)
    received = pack_features(activations, flat_maps, devices)
    received = after(received, got_rows, own[-1], across[CHUNKS - 1])
    received = lax.all_to_all(received, "blk", split_axis=0, concat_axis=0)
    grad_all = to_all(after(grad_sent, received)).reshape(resident_rows, -1).T

    rows_all, place_all = rows_all.reshape(1, -1), place_all.reshape(1, -1)

    cot_rows = jnp.concatenate(
        [dot(arrange, part, ((0,), (0,))).astype(jnp.bfloat16) for part in recv_cot], axis=1
    )
    grad_rows = dot(arrange, grad_in, ((0,), (0,))).astype(jnp.bfloat16)
    group = lax.axis_index("groups")
    quarter = device % 4
    firsts = [quarter, quarter ^ 1, quarter ^ 2, quarter ^ 3]
    if own[0].shape[1] % LANES == 0:
        out = None
        for number, (piece, first) in enumerate(zip(pieces, firsts)):
            out, token = write_quarter(
                piece, first, group, cot_rows, grad_rows, down_blocks, out
            )
            if number == 3:
                place_all = after(place_all, token)
    else:
        weight = together(pieces, firsts, group)
        lora = [
            dot(
                grad_rows[b * BLOCK : (b + 1) * BLOCK],
                down_blocks[b * rank : (b + 1) * rank],
                ((1,), (0,)),
            )
            for b in range(resident)
        ]
        lora = (adapter_scale * jnp.concatenate(lora, axis=0)).astype(jnp.bfloat16)
        out = dot(cot_rows, weight, ((1,), (1,))) + lora.astype(jnp.float32)
        out = out.astype(jnp.bfloat16)

    starts = start_ids[:, None]
    hidden_call, down_call = feature_calls(
        received, tokens, share, rank, resident_rows, starts.shape[0]
    )
    shares = hidden_call(received, received, rows_all, place_all, starts)
    rows_all = after(rows_all, shares)
    down_f = down_call(received, grad_all, rows_all, place_all, starts)
    hidden = shares.T.reshape(devices, cap, -1)
    hidden = lax.all_to_all(hidden, "blk", split_axis=0, concat_axis=0)
    hidden = jnp.sum(hidden, axis=0).astype(jnp.bfloat16)
    hidden = hidden.reshape(cap, devices, rank).transpose(1, 0, 2).reshape(-1, rank)
    down_home = lax.all_to_all(down_f, "blk", split_axis=0, concat_axis=1, tiled=True)
    down_map_gradient = down_home.astype(jnp.float32).reshape(resident, rank, width)

    wide = jnp.where(in_block, jnp.concatenate([hidden] * resident, axis=1), 0)
    up_all = [dot(wide, part, ((0,), (0,))) for part in recv_cot]
    up_all = jnp.concatenate(up_all, axis=1).reshape(resident, rank, out_width)
    up_parts = [up_all[b] for b in range(resident)]

    tail = sum(jnp.where(is_local[b], 0.0, up_parts[b]) for b in range(resident))
    far = jnp.zeros_like(tail)
    for step in range(1, HOPS + 1):
        other = (device + step) % devices * resident
        theirs = starts_of(other[None], start_ids)[0]
        far = far + jnp.where(theirs // resident == device, moved(tail, -step), 0.0)
    up_grads = []
    for k in range(resident):
        total = jnp.where(begin[resident - 1] == first_block + k, far, 0.0)
        for b in range(resident):
            total = total + jnp.where(is_local[b] & (home_slot[b] == k), up_parts[b], 0.0)
        up_grads.append(adapter_scale * total)
    up_map_gradient = jnp.stack(up_grads)

    return (out, down_map_gradient, up_map_gradient)


def solution(mesh):
    return jax.shard_map(
        local,
        mesh=mesh,
        in_specs=(
            P(("groups", "blk"), None),
            P(("groups", "blk"), None),
            P(("groups", "blk")),
            P("groups"),
            P("blk", None),
            P(("groups", "blk"), None, None),
            P(("groups", "blk"), None, None),
        ),
        out_specs=(
            P(("groups", "blk"), None),
            P(("groups", "blk"), None, None),
            P(("groups", "blk"), None, None),
        ),
        check_vma=False,
    )
```

```python
import functools

import jax
import jax.numpy as jnp
from jax import lax
from jax.experimental import pallas as pl
from jax.experimental.pallas import tpu as pltpu
from jax.sharding import PartitionSpec as P

BLOCK = 128
HOPS = 4
LANES = 128
DIGIT = 64
VMEM = 56 << 20

adapter_scale = 2.0


def moved(value, steps):
    count = lax.axis_size("blk")
    return lax.ppermute(value, "blk", [(i, (i + steps) % count) for i in range(count)])


def to_all(value):
    count = lax.axis_size("blk")
    copies = jnp.broadcast_to(value[None], (count,) + value.shape)
    return lax.all_to_all(copies, "blk", split_axis=0, concat_axis=0)


def after(value, *others):
    anywhere = pl.BlockSpec(memory_space=pl.ANY)
    return pl.pallas_call(
        lambda *refs: None,
        in_specs=[anywhere] * (1 + len(others)),
        out_specs=anywhere,
        out_shape=jax.ShapeDtypeStruct(value.shape, value.dtype),
        input_output_aliases={0: 0},
        cost_estimate=pl.CostEstimate(flops=0, bytes_accessed=0, transcendentals=0),
        compiler_params=pltpu.CompilerParams(vmem_limit_bytes=VMEM),
    )(value, *others)


def dot(a, b, dims):
    return lax.dot_general(a, b, (dims, ((), ())), preferred_element_type=jnp.float32)


def starts_of(blocks, start_ids):
    latest = jnp.max(
        jnp.where(start_ids[None, :] <= blocks[:, None], start_ids[None, :], -1), axis=1
    )
    return jnp.where(latest >= 0, latest, jnp.max(start_ids))


def as_digits(rows, places):
    return (
        rows % DIGIT,
        rows // DIGIT % DIGIT,
        rows // (DIGIT * DIGIT),
        places % DIGIT,
        places // DIGIT,
    )


def from_digits(digits):
    low, middle, high, place, place_high = [digits[:, k].astype(jnp.int32) for k in range(5)]
    return (high * DIGIT + middle) * DIGIT + low, place_high * DIGIT + place


CHUNKS = 2


def weight_pieces(weight):
    count = lax.axis_size("blk")
    half = weight.shape[0] // 2
    size = half // CHUNKS
    first = lax.axis_index("groups") * half
    lines = [list(range(k, count, 4)) for k in range(4)]

    def over(piece, bit):
        return lax.ppermute(piece, "blk", [(i, i ^ bit) for i in range(count)])

    def groups(piece):
        return lax.ppermute(piece, "groups", [(0, 1), (1, 0)])

    column = lax.all_gather(
        lax.dynamic_slice_in_dim(weight, first, half, 0), "blk", axis_index_groups=lines
    )
    columns = [column[:, k * size : (k + 1) * size] for k in range(CHUNKS)]
    pieces = []
    for mine in (columns, [over(column, 2) for column in columns]):
        both = mine + [groups(piece) for piece in mine]
        pieces += [both, [over(piece, 1) for piece in both]]
    return pieces


def quarter_kernel(where, cot, grad, down, *rest):
    pieces = rest[: 2 * CHUNKS]
    out, token = rest[-2:]
    token[...] = jnp.zeros_like(token)
    rank = grad.shape[1]
    lora = [
        adapter_scale
        * dot(
            grad[b * BLOCK : (b + 1) * BLOCK, :],
            down[b * rank : (b + 1) * rank, :],
            ((1,), (0,)),
        )
        for b in range(cot.shape[0] // BLOCK)
    ]
    lora = jnp.concatenate(lora, axis=0).astype(jnp.bfloat16).astype(jnp.float32)

    def product(group):
        order = pieces[group * CHUNKS :] + pieces[: group * CHUNKS]
        weight = jnp.concatenate([piece[0] for piece in order], axis=0)
        frozen = dot(cot[...], weight, ((1,), (1,)))
        out[...] = (frozen + lora).astype(jnp.bfloat16)

    for group in range(2):
        pl.when(where[1] == group)(functools.partial(product, group))


def write_quarter(quarter, first, group, cot, grad, down, out=None):
    rows, depth = cot.shape
    width = down.shape[1]
    shards, part, _ = quarter[0].shape
    stripe = part * len(quarter)
    where = jnp.stack([first, group]).astype(jnp.int32)
    specs = [
        pl.BlockSpec((rows, depth), lambda j, where: (0, 0)),
        pl.BlockSpec(grad.shape, lambda j, where: (0, 0)),
        pl.BlockSpec((down.shape[0], stripe), lambda j, where: (0, 4 * j + where[0])),
    ] + [pl.BlockSpec((1, part, depth), lambda j, where: (j, 0, 0)) for _ in quarter]
    args = [where, cot, grad, down] + quarter
    alias = {}
    if out is not None:
        specs.append(pl.BlockSpec(memory_space=pl.ANY))
        args.append(out)
        alias = {len(args) - 1: 0}
    return pl.pallas_call(
        quarter_kernel,
        grid_spec=pltpu.PrefetchScalarGridSpec(
            num_scalar_prefetch=1,
            grid=(shards,),
            in_specs=specs,
            out_specs=[
                pl.BlockSpec((rows, stripe), lambda j, where: (0, 4 * j + where[0])),
                pl.BlockSpec((8, LANES), lambda j, where: (0, 0)),
            ],
        ),
        out_shape=[
            jax.ShapeDtypeStruct((rows, width), jnp.bfloat16),
            jax.ShapeDtypeStruct((8, LANES), jnp.float32),
        ],
        input_output_aliases=alias,
        cost_estimate=pl.CostEstimate(
            flops=2 * rows * depth * stripe * shards,
            bytes_accessed=2 * (depth + rows) * stripe * shards,
            transcendentals=0,
        ),
        compiler_params=pltpu.CompilerParams(vmem_limit_bytes=VMEM),
    )(*args)


def together(pieces, firsts, group):
    shards, part, depth = pieces[0][0].shape
    weight = jnp.zeros((shards, 4, 2, CHUNKS, part, depth), jnp.bfloat16)
    for quarter, first in zip(pieces, firsts):
        for k, piece in enumerate(quarter):
            half = group if k < CHUNKS else 1 - group
            place = (0, first, half, k % CHUNKS, 0, 0)
            weight = lax.dynamic_update_slice(weight, piece[:, None, None, None], place)
    return weight.reshape(-1, depth)


def rows_kernel(rows, cot, out, place):
    devices, packed, features = out.shape
    shared = packed - 16
    folds = cot.shape[1] // features
    cap = shared // folds
    target = rows[...] // (cap * devices)
    to = lax.broadcasted_iota(jnp.int32, (16, features), 0) == target
    first = lax.broadcasted_iota(jnp.int32, (features, features), 0)
    later = lax.broadcasted_iota(jnp.int32, (features, features), 1)
    earlier = jnp.where(first < later, 1.0, 0.0).astype(jnp.bfloat16)
    ahead = dot(jnp.where(to, 1.0, 0.0).astype(jnp.bfloat16), earlier, ((1,), (0,)))
    ahead = jnp.sum(jnp.where(to, ahead, 0.0), axis=0, keepdims=True)
    place[...] = target * cap + ahead.astype(jnp.int32)
    which = lax.broadcasted_iota(jnp.int32, (16, features), 0)
    digits = jnp.zeros((16, features), jnp.int32)
    for k, digit in enumerate(as_digits(rows[...], place[...])):
        digits = jnp.where(which == k, digit, digits)
    digits = digits.astype(jnp.float32).astype(out.dtype)
    send = placing(place[:, : cot.shape[0]], cap * devices)
    for f in range(folds):
        sent = dot(send, cot[:, f * features : (f + 1) * features], ((1,), (0,)))
        for k in range(devices):
            some = sent[k * cap : (k + 1) * cap].astype(out.dtype)
            out[k, f * cap : (f + 1) * cap, :] = some
    for k in range(devices):
        out[k, shared:, :] = digits


def pack_rows(rows, cot, devices, cap, features):
    tokens = rows.shape[0]
    folds = cot.shape[1] // features
    if features % LANES == 0 and cap % 8 == 0 and features >= tokens and devices <= 16:
        padding = jnp.full((features - tokens,), 16 * cap * devices, jnp.int32)
        return pl.pallas_call(
            rows_kernel,
            out_shape=jax.ShapeDtypeStruct((devices, folds * cap + 16, features), cot.dtype),
            scratch_shapes=[pltpu.VMEM((1, features), jnp.int32)],
            cost_estimate=pl.CostEstimate(
                flops=2 * devices * cap * tokens * cot.shape[1],
                bytes_accessed=6 * cot.size,
                transcendentals=0,
            ),
            compiler_params=pltpu.CompilerParams(vmem_limit_bytes=VMEM),
        )(jnp.concatenate([rows, padding])[None], cot)
    target = rows // (cap * devices)
    order = jnp.arange(tokens, dtype=jnp.int32)
    before = (target[:, None] == target[None, :]) & (order[None, :] < order[:, None])
    place = target * cap + jnp.sum(before.astype(jnp.int32), axis=1)
    send = jnp.arange(cap * devices, dtype=jnp.int32)[:, None] == place[None, :]
    sent = dot(send.astype(jnp.bfloat16), cot, ((1,), (0,))).astype(jnp.bfloat16)
    sent = sent.reshape(devices, cap, cot.shape[1])
    digits = jnp.stack(as_digits(rows, place)).astype(jnp.bfloat16)
    digits = jnp.pad(digits, ((0, 0), (0, -tokens % features))).reshape(-1, features)
    digits = jnp.pad(digits, ((0, -digits.shape[0] % 16), (0, 0)))
    parts = [sent[:, :, k : k + features] for k in range(0, cot.shape[1], features)]
    parts += [jnp.broadcast_to(digits[None], (devices,) + digits.shape)]
    return jnp.concatenate(parts, axis=1)


def features_kernel(act, maps, out):
    targets, _, features = out.shape
    tokens = act.shape[0]
    for k in range(targets):
        part = slice(k * features, (k + 1) * features)
        out[k, :tokens, :] = act[:, part]
        out[k, tokens:, :] = maps[:, part]


def pack_features(act, maps, devices):
    tokens, width = act.shape
    features = width // devices
    shared = maps.shape[0]
    targets = 4
    if features % LANES == 0:
        return pl.pallas_call(
            features_kernel,
            grid=(devices // targets,),
            in_specs=[
                pl.BlockSpec((tokens, targets * features), lambda j: (0, j)),
                pl.BlockSpec((shared, targets * features), lambda j: (0, j)),
            ],
            out_specs=pl.BlockSpec((targets, tokens + shared, features), lambda j: (j, 0, 0)),
            out_shape=jax.ShapeDtypeStruct((devices, tokens + shared, features), act.dtype),
            cost_estimate=pl.CostEstimate(
                flops=0, bytes_accessed=4 * (tokens + shared) * width, transcendentals=0
            ),
            compiler_params=pltpu.CompilerParams(vmem_limit_bytes=VMEM),
        )(act, maps)
    both = jnp.concatenate([act, maps], axis=0)
    return both.reshape(tokens + shared, devices, features).transpose(1, 0, 2)


def slot_chunks(width):
    size = min(width, 768)
    while width % size:
        size //= 2
    return [slice(k, k + size) for k in range(0, width, size)]


def slot_of(rows, starts):
    blocks = rows // BLOCK
    latest = jnp.max(jnp.where(starts <= blocks, starts, -1), axis=0, keepdims=True)
    return jnp.where(latest >= 0, latest, jnp.max(starts))


def own_rows(slot, first, size, rank):
    index = first // rank + lax.broadcasted_iota(jnp.int32, (size // rank, rank, 1), 0)
    return index == slot[None]


def placing(place, places):
    hit = lax.broadcasted_iota(jnp.int32, (places, place.shape[1]), 0) == place
    return jnp.where(hit, 1.0, 0.0).astype(jnp.bfloat16)


def all_rows(act, tokens):
    return jnp.concatenate([act[k, :tokens, :] for k in range(act.shape[0])], axis=0)


def of_source(sources, width):
    lane = lax.broadcasted_iota(jnp.int32, (sources, 1, width), 2)
    return lane // (width // sources) == lax.broadcasted_iota(
        jnp.int32, (sources, 1, width), 0
    )


def hidden_kernel(act, maps, rows, spots, starts, out):
    sources, share, width = act.shape[0], maps.shape[1], rows.shape[1]
    rank, places = out.shape[0] // sources, out.shape[1]
    slot = slot_of(rows[...], starts[...])
    every = all_rows(act, width // sources)
    total = jnp.zeros((rank, width), jnp.float32)
    for part in slot_chunks(maps.shape[0] * share):
        size = part.stop - part.start
        some = maps[part.start // share : part.stop // share].reshape(size, -1)
        each = dot(some, every, ((1,), (1,))).reshape(size // rank, rank, -1)
        total += jnp.sum(jnp.where(own_rows(slot, part.start, size, rank), each, 0.0), axis=0)
    total = jnp.where(of_source(sources, width), total[None], 0.0).reshape(out.shape[0], width)
    high = total.astype(jnp.bfloat16)
    low = (total - high.astype(jnp.float32)).astype(jnp.bfloat16)
    place = placing(spots[...], places)
    out[...] = dot(high, place, ((1,), (1,))) + dot(low, place, ((1,), (1,)))


def down_kernel(act, grad, rows, spots, starts, out, total):
    sources, width = act.shape[0], rows.shape[1]
    rank, places = grad.shape[0] // sources, grad.shape[1]
    step = pl.program_id(0)

    @pl.when(step == 0)
    def _():
        total[...] = jnp.zeros_like(total)

    slot = slot_of(rows[...], starts[...])
    every = all_rows(act, width // sources)
    wide = dot(grad[...], placing(spots[...], places), ((1,), (0,)))
    wide = wide.reshape(sources, rank, width)
    wide = jnp.sum(jnp.where(of_source(sources, width), wide, 0.0), axis=0, keepdims=True)
    for part in slot_chunks(total.shape[0]):
        size = part.stop - part.start
        placed = jnp.where(own_rows(slot, part.start, size, rank), wide, 0.0)
        placed = placed.reshape(size, -1).astype(jnp.bfloat16)
        total[part, :] += dot(placed, every, ((1,), (0,)))

    @pl.when(step == pl.num_programs(0) - 1)
    def _():
        out[...] = (adapter_scale * total[...]).astype(out.dtype)


def feature_calls(received, tokens, share, rank, places, starts):
    devices, packed, features = received.shape
    width = devices * share
    sources = 4
    grid = (devices // sources,)
    act = pl.BlockSpec((sources, packed, features), lambda j: (j, 0, 0))
    maps = pl.BlockSpec((devices, share, features), lambda j: (0, tokens // share, 0))
    rows = pl.BlockSpec((1, sources * tokens), lambda j: (0, j))
    begin = pl.BlockSpec((starts, 1), lambda j: (0, 0))
    placed = pl.BlockSpec((sources * rank, places), lambda j: (j, 0))
    cost = pl.CostEstimate(
        flops=2 * devices * tokens * width * features,
        bytes_accessed=2 * devices * tokens * features,
        transcendentals=0,
    )
    params = pltpu.CompilerParams(vmem_limit_bytes=VMEM)
    hidden = pl.pallas_call(
        hidden_kernel,
        grid=grid,
        in_specs=[act, maps, rows, rows, begin],
        out_specs=placed,
        out_shape=jax.ShapeDtypeStruct((devices * rank, places), jnp.float32),
        cost_estimate=cost,
        compiler_params=params,
    )
    down = pl.pallas_call(
        down_kernel,
        grid=grid,
        in_specs=[act, placed, rows, rows, begin],
        out_specs=pl.BlockSpec((width, features), lambda j: (0, 0)),
        out_shape=jax.ShapeDtypeStruct((width, features), jnp.bfloat16),
        scratch_shapes=[pltpu.VMEM((width, features), jnp.float32)],
        cost_estimate=cost,
        compiler_params=params,
    )
    return hidden, down


def local(
    activations,
    cotangent,
    token_layout_row,
    tenant_first_row,
    frozen_value_weight,
    adapter_down_maps,
    adapter_up_maps,
):
    devices = lax.axis_size("blk")
    device = lax.axis_index("blk")
    tokens = activations.shape[0]
    resident, rank, width = adapter_down_maps.shape
    out_width = cotangent.shape[1]
    features = width // devices
    share = resident * rank
    resident_rows = resident * BLOCK
    cap = resident_rows // devices
    start_ids = tenant_first_row // BLOCK

    pieces = weight_pieces(frozen_value_weight)

    first_block = device * resident
    block_numbers = first_block + jnp.arange(resident, dtype=jnp.int32)
    begin = starts_of(block_numbers, start_ids)
    is_local = (begin >= first_block) & (begin <= block_numbers)
    home_slot = jnp.clip(begin - first_block, 0, resident - 1)
    last_map = jnp.concatenate(
        [
            lax.dynamic_index_in_dim(maps, home_slot[resident - 1], 0, keepdims=False)
            for maps in (adapter_down_maps, adapter_up_maps)
        ],
        axis=1,
    )
    carried = jnp.zeros_like(last_map)
    for step in range(1, HOPS + 1):
        home = (device - step) % devices
        carried = jnp.where(begin[0] // resident == home, moved(last_map, step), carried)

    def of_blocks(maps, own):
        blocks = []
        for b in range(resident):
            chosen = own
            for k in range(b + 1):
                chosen = jnp.where(is_local[b] & (home_slot[b] == k), maps[k], chosen)
            blocks.append(chosen)
        return jnp.concatenate(blocks, axis=0)

    down_blocks = of_blocks(adapter_down_maps, carried[:, :width])
    up_blocks = of_blocks(adapter_up_maps, carried[:, width:])

    sent_rows = pack_rows(token_layout_row, cotangent, devices, cap, features)
    own, _, across, _ = pieces
    sent_rows = after(sent_rows, own[0], own[1], carried)
    got_rows = lax.all_to_all(sent_rows, "blk", split_axis=0, concat_axis=0)
    recv_cot = [
        got_rows[:, k * cap : (k + 1) * cap].reshape(resident_rows, features)
        for k in range(out_width // features)
    ]
    per_digit = -(-tokens // features)
    digits = got_rows[:, share : share + 5 * per_digit]
    digits = digits.reshape(devices, 5, per_digit * features)[:, :, :tokens]
    rows_all, place_all = from_digits(digits)

    spots = device * cap + jnp.arange(cap, dtype=jnp.int32)
    hit = place_all[:, None, :] == spots[None, :, None]
    row_in = rows_all - device * resident_rows + 1
    row_in = jnp.sum(jnp.where(hit, row_in[:, None, :], 0), axis=2).reshape(-1) - 1
    arrange = row_in[:, None] == jnp.arange(resident_rows, dtype=jnp.int32)[None, :]
    arrange = arrange.astype(jnp.bfloat16)
    in_block = row_in[:, None] // BLOCK == jnp.arange(share, dtype=jnp.int32)[None, :] // rank

    grad_in = sum(
        dot(part, up_blocks[:, k * features : (k + 1) * features], ((1,), (1,)))
        for k, part in enumerate(recv_cot)
    )
    grad_in = jnp.where(in_block, grad_in, 0.0).astype(jnp.bfloat16)
    grad_in = sum(grad_in[:, b * rank : (b + 1) * rank] for b in range(resident))
    grad_sent = grad_in.reshape(devices, cap, rank).transpose(1, 0, 2).reshape(cap, -1)

    flat_maps = adapter_down_maps.reshape(share, width)
    received = pack_features(activations, flat_maps, devices)
    received = after(received, got_rows, own[CHUNKS], across[0])
    received = lax.all_to_all(received, "blk", split_axis=0, concat_axis=0)
    grad_all = to_all(after(grad_sent, received)).reshape(resident_rows, -1).T

    rows_all, place_all = rows_all.reshape(1, -1), place_all.reshape(1, -1)

    cot_rows = jnp.concatenate(
        [dot(arrange, part, ((0,), (0,))).astype(jnp.bfloat16) for part in recv_cot], axis=1
    )
    grad_rows = dot(arrange, grad_in, ((0,), (0,))).astype(jnp.bfloat16)
    group = lax.axis_index("groups")
    quarter = device % 4
    firsts = [quarter, quarter ^ 1, quarter ^ 2, quarter ^ 3]
    if own[0].shape[1] % LANES == 0:
        out = None
        for number, (piece, first) in enumerate(zip(pieces, firsts)):
            out, token = write_quarter(
                piece, first, group, cot_rows, grad_rows, down_blocks, out
            )
            if number == 3:
                place_all = after(place_all, token)
    else:
        weight = together(pieces, firsts, group)
        lora = [
            dot(
                grad_rows[b * BLOCK : (b + 1) * BLOCK],
                down_blocks[b * rank : (b + 1) * rank],
                ((1,), (0,)),
            )
            for b in range(resident)
        ]
        lora = (adapter_scale * jnp.concatenate(lora, axis=0)).astype(jnp.bfloat16)
        out = dot(cot_rows, weight, ((1,), (1,))) + lora.astype(jnp.float32)
        out = out.astype(jnp.bfloat16)

    starts = start_ids[:, None]
    hidden_call, down_call = feature_calls(
        received, tokens, share, rank, resident_rows, starts.shape[0]
    )
    shares = hidden_call(received, received, rows_all, place_all, starts)
    rows_all = after(rows_all, shares)
    down_f = down_call(received, grad_all, rows_all, place_all, starts)
    hidden = shares.T.reshape(devices, cap, -1)
    hidden = lax.all_to_all(hidden, "blk", split_axis=0, concat_axis=0)
    hidden = jnp.sum(hidden, axis=0).astype(jnp.bfloat16)
    hidden = hidden.reshape(cap, devices, rank).transpose(1, 0, 2).reshape(-1, rank)
    down_home = lax.all_to_all(down_f, "blk", split_axis=0, concat_axis=1, tiled=True)
    down_map_gradient = down_home.astype(jnp.float32).reshape(resident, rank, width)

    wide = jnp.where(in_block, jnp.concatenate([hidden] * resident, axis=1), 0)
    up_all = [dot(wide, part, ((0,), (0,))) for part in recv_cot]
    up_all = jnp.concatenate(up_all, axis=1).reshape(resident, rank, out_width)
    up_parts = [up_all[b] for b in range(resident)]

    tail = sum(jnp.where(is_local[b], 0.0, up_parts[b]) for b in range(resident))
    far = jnp.zeros_like(tail)
    for step in range(1, HOPS + 1):
        other = (device + step) % devices * resident
        theirs = starts_of(other[None], start_ids)[0]
        far = far + jnp.where(theirs // resident == device, moved(tail, -step), 0.0)
    up_grads = []
    for k in range(resident):
        total = jnp.where(begin[resident - 1] == first_block + k, far, 0.0)
        for b in range(resident):
            total = total + jnp.where(is_local[b] & (home_slot[b] == k), up_parts[b], 0.0)
        up_grads.append(adapter_scale * total)
    up_map_gradient = jnp.stack(up_grads)

    return (out, down_map_gradient, up_map_gradient)


def solution(mesh):
    return jax.shard_map(
        local,
        mesh=mesh,
        in_specs=(
            P(("groups", "blk"), None),
            P(("groups", "blk"), None),
            P(("groups", "blk")),
            P("groups"),
            P("blk", None),
            P(("groups", "blk"), None, None),
            P(("groups", "blk"), None, None),
        ),
        out_specs=(
            P(("groups", "blk"), None),
            P(("groups", "blk"), None, None),
            P(("groups", "blk"), None, None),
        ),
        check_vma=False,
    )
```

```python
import functools

import jax
import jax.numpy as jnp
from jax import lax
from jax.experimental import pallas as pl
from jax.experimental.pallas import tpu as pltpu
from jax.sharding import PartitionSpec as P

BLOCK = 128
HOPS = 4
LANES = 128
DIGIT = 64
VMEM = 56 << 20

adapter_scale = 2.0


def moved(value, steps):
    count = lax.axis_size("blk")
    return lax.ppermute(value, "blk", [(i, (i + steps) % count) for i in range(count)])


def to_all(value):
    count = lax.axis_size("blk")
    copies = jnp.broadcast_to(value[None], (count,) + value.shape)
    return lax.all_to_all(copies, "blk", split_axis=0, concat_axis=0)


def after(value, *others):
    anywhere = pl.BlockSpec(memory_space=pl.ANY)
    return pl.pallas_call(
        lambda *refs: None,
        in_specs=[anywhere] * (1 + len(others)),
        out_specs=anywhere,
        out_shape=jax.ShapeDtypeStruct(value.shape, value.dtype),
        input_output_aliases={0: 0},
        cost_estimate=pl.CostEstimate(flops=0, bytes_accessed=0, transcendentals=0),
        compiler_params=pltpu.CompilerParams(vmem_limit_bytes=VMEM),
    )(value, *others)


def dot(a, b, dims):
    return lax.dot_general(a, b, (dims, ((), ())), preferred_element_type=jnp.float32)


def starts_of(blocks, start_ids):
    latest = jnp.max(
        jnp.where(start_ids[None, :] <= blocks[:, None], start_ids[None, :], -1), axis=1
    )
    return jnp.where(latest >= 0, latest, jnp.max(start_ids))


def as_digits(rows, places):
    return (
        rows % DIGIT,
        rows // DIGIT % DIGIT,
        rows // (DIGIT * DIGIT),
        places % DIGIT,
        places // DIGIT,
    )


def from_digits(digits):
    low, middle, high, place, place_high = [digits[:, k].astype(jnp.int32) for k in range(5)]
    return (high * DIGIT + middle) * DIGIT + low, place_high * DIGIT + place


CHUNKS = 1


def weight_pieces(weight):
    count = lax.axis_size("blk")
    half = weight.shape[0] // 2
    size = half // CHUNKS
    first = lax.axis_index("groups") * half
    lines = [list(range(k, count, 4)) for k in range(4)]

    def over(piece, bit):
        return lax.ppermute(piece, "blk", [(i, i ^ bit) for i in range(count)])

    def groups(piece):
        return lax.ppermute(piece, "groups", [(0, 1), (1, 0)])

    column = lax.all_gather(
        lax.dynamic_slice_in_dim(weight, first, half, 0), "blk", axis_index_groups=lines
    )
    columns = [column[:, k * size : (k + 1) * size] for k in range(CHUNKS)]
    pieces = []
    for mine in (columns, [over(column, 2) for column in columns]):
        both = mine + [groups(piece) for piece in mine]
        pieces += [both, [over(piece, 1) for piece in both]]
    return pieces


def quarter_kernel(where, cot, grad, down, *rest):
    pieces = rest[: 2 * CHUNKS]
    out = rest[-1]
    rank = grad.shape[1]
    lora = [
        adapter_scale
        * dot(
            grad[b * BLOCK : (b + 1) * BLOCK, :],
            down[b * rank : (b + 1) * rank, :],
            ((1,), (0,)),
        )
        for b in range(cot.shape[0] // BLOCK)
    ]
    lora = jnp.concatenate(lora, axis=0).astype(jnp.bfloat16).astype(jnp.float32)

    def product(group):
        order = pieces[group * CHUNKS :] + pieces[: group * CHUNKS]
        weight = jnp.concatenate([piece[0] for piece in order], axis=0)
        frozen = dot(cot[...], weight, ((1,), (1,)))
        out[...] = (frozen + lora).astype(jnp.bfloat16)

    for group in range(2):
        pl.when(where[1] == group)(functools.partial(product, group))


def write_quarter(quarter, first, group, cot, grad, down, out=None):
    rows, depth = cot.shape
    width = down.shape[1]
    shards, part, _ = quarter[0].shape
    stripe = part * len(quarter)
    where = jnp.stack([first, group]).astype(jnp.int32)
    specs = [
        pl.BlockSpec((rows, depth), lambda j, where: (0, 0)),
        pl.BlockSpec(grad.shape, lambda j, where: (0, 0)),
        pl.BlockSpec((down.shape[0], stripe), lambda j, where: (0, 4 * j + where[0])),
    ] + [pl.BlockSpec((1, part, depth), lambda j, where: (j, 0, 0)) for _ in quarter]
    args = [where, cot, grad, down] + quarter
    alias = {}
    if out is not None:
        specs.append(pl.BlockSpec(memory_space=pl.ANY))
        args.append(out)
        alias = {len(args) - 1: 0}
    return pl.pallas_call(
        quarter_kernel,
        grid_spec=pltpu.PrefetchScalarGridSpec(
            num_scalar_prefetch=1,
            grid=(shards,),
            in_specs=specs,
            out_specs=pl.BlockSpec((rows, stripe), lambda j, where: (0, 4 * j + where[0])),
        ),
        out_shape=jax.ShapeDtypeStruct((rows, width), jnp.bfloat16),
        input_output_aliases=alias,
        cost_estimate=pl.CostEstimate(
            flops=2 * rows * depth * stripe * shards,
            bytes_accessed=2 * (depth + rows) * stripe * shards,
            transcendentals=0,
        ),
        compiler_params=pltpu.CompilerParams(vmem_limit_bytes=VMEM),
    )(*args)


def together(pieces, firsts, group):
    shards, part, depth = pieces[0][0].shape
    weight = jnp.zeros((shards, 4, 2, CHUNKS, part, depth), jnp.bfloat16)
    for quarter, first in zip(pieces, firsts):
        for k, piece in enumerate(quarter):
            half = group if k < CHUNKS else 1 - group
            place = (0, first, half, k % CHUNKS, 0, 0)
            weight = lax.dynamic_update_slice(weight, piece[:, None, None, None], place)
    return weight.reshape(-1, depth)


def rows_kernel(rows, cot, out, digits_out, place):
    devices, shared, features = out.shape
    folds = cot.shape[1] // features
    cap = shared // folds
    target = rows[...] // (cap * devices)
    to = lax.broadcasted_iota(jnp.int32, (16, features), 0) == target
    first = lax.broadcasted_iota(jnp.int32, (features, features), 0)
    later = lax.broadcasted_iota(jnp.int32, (features, features), 1)
    earlier = jnp.where(first < later, 1.0, 0.0).astype(jnp.bfloat16)
    ahead = dot(jnp.where(to, 1.0, 0.0).astype(jnp.bfloat16), earlier, ((1,), (0,)))
    ahead = jnp.sum(jnp.where(to, ahead, 0.0), axis=0, keepdims=True)
    place[...] = target * cap + ahead.astype(jnp.int32)
    which = lax.broadcasted_iota(jnp.int32, (16, features), 0)
    digits = jnp.zeros((16, features), jnp.int32)
    for k, digit in enumerate(as_digits(rows[...], place[...])):
        digits = jnp.where(which == k, digit, digits)
    digits_out[...] = digits.astype(jnp.float32).astype(out.dtype)
    send = placing(place[:, : cot.shape[0]], cap * devices)
    for f in range(folds):
        sent = dot(send, cot[:, f * features : (f + 1) * features], ((1,), (0,)))
        for k in range(devices):
            some = sent[k * cap : (k + 1) * cap].astype(out.dtype)
            out[k, f * cap : (f + 1) * cap, :] = some


def pack_rows(rows, cot, devices, cap, features):
    tokens = rows.shape[0]
    folds = cot.shape[1] // features
    if features % LANES == 0 and cap % 8 == 0 and features >= tokens and devices <= 16:
        padding = jnp.full((features - tokens,), 16 * cap * devices, jnp.int32)
        return pl.pallas_call(
            rows_kernel,
            out_shape=[
                jax.ShapeDtypeStruct((devices, folds * cap, features), cot.dtype),
                jax.ShapeDtypeStruct((16, features), cot.dtype),
            ],
            scratch_shapes=[pltpu.VMEM((1, features), jnp.int32)],
            cost_estimate=pl.CostEstimate(
                flops=2 * devices * cap * tokens * cot.shape[1],
                bytes_accessed=6 * cot.size,
                transcendentals=0,
            ),
            compiler_params=pltpu.CompilerParams(vmem_limit_bytes=VMEM),
        )(jnp.concatenate([rows, padding])[None], cot)
    target = rows // (cap * devices)
    order = jnp.arange(tokens, dtype=jnp.int32)
    before = (target[:, None] == target[None, :]) & (order[None, :] < order[:, None])
    place = target * cap + jnp.sum(before.astype(jnp.int32), axis=1)
    send = jnp.arange(cap * devices, dtype=jnp.int32)[:, None] == place[None, :]
    sent = dot(send.astype(jnp.bfloat16), cot, ((1,), (0,))).astype(jnp.bfloat16)
    sent = sent.reshape(devices, cap, cot.shape[1])
    digits = jnp.stack(as_digits(rows, place)).astype(jnp.bfloat16)
    digits = jnp.pad(digits, ((0, 0), (0, -tokens % features))).reshape(-1, features)
    digits = jnp.pad(digits, ((0, -digits.shape[0] % 16), (0, 0)))
    parts = [sent[:, :, k : k + features] for k in range(0, cot.shape[1], features)]
    return jnp.concatenate(parts, axis=1), digits


def features_kernel(act, maps, digits, out):
    targets, _, features = out.shape
    tokens, shared = act.shape[0], maps.shape[0]
    for k in range(targets):
        part = slice(k * features, (k + 1) * features)
        out[k, :tokens, :] = act[:, part]
        out[k, tokens : tokens + shared, :] = maps[:, part]
        out[k, tokens + shared :, :] = digits[...]


def pack_features(act, maps, digits, devices):
    tokens, width = act.shape
    features = width // devices
    shared = maps.shape[0]
    total = tokens + shared + digits.shape[0]
    targets = 4
    if features % LANES == 0:
        return pl.pallas_call(
            features_kernel,
            grid=(devices // targets,),
            in_specs=[
                pl.BlockSpec((tokens, targets * features), lambda j: (0, j)),
                pl.BlockSpec((shared, targets * features), lambda j: (0, j)),
                pl.BlockSpec(digits.shape, lambda j: (0, 0)),
            ],
            out_specs=pl.BlockSpec((targets, total, features), lambda j: (j, 0, 0)),
            out_shape=jax.ShapeDtypeStruct((devices, total, features), act.dtype),
            cost_estimate=pl.CostEstimate(
                flops=0, bytes_accessed=4 * total * width, transcendentals=0
            ),
            compiler_params=pltpu.CompilerParams(vmem_limit_bytes=VMEM),
        )(act, maps, digits)
    both = jnp.concatenate([act, maps], axis=0)
    both = both.reshape(tokens + shared, devices, features).transpose(1, 0, 2)
    copies = jnp.broadcast_to(digits[None], (devices,) + digits.shape)
    return jnp.concatenate([both, copies], axis=1)


def slot_chunks(width):
    size = min(width, 768)
    while width % size:
        size //= 2
    return [slice(k, k + size) for k in range(0, width, size)]


def slot_of(rows, starts):
    blocks = rows // BLOCK
    latest = jnp.max(jnp.where(starts <= blocks, starts, -1), axis=0, keepdims=True)
    return jnp.where(latest >= 0, latest, jnp.max(starts))


def own_rows(slot, first, size, rank):
    index = first // rank + lax.broadcasted_iota(jnp.int32, (size // rank, rank, 1), 0)
    return index == slot[None]


def placing(place, places):
    hit = lax.broadcasted_iota(jnp.int32, (places, place.shape[1]), 0) == place
    return jnp.where(hit, 1.0, 0.0).astype(jnp.bfloat16)


def all_rows(act, tokens):
    return jnp.concatenate([act[k, :tokens, :] for k in range(act.shape[0])], axis=0)


def of_source(sources, width):
    lane = lax.broadcasted_iota(jnp.int32, (sources, 1, width), 2)
    return lane // (width // sources) == lax.broadcasted_iota(
        jnp.int32, (sources, 1, width), 0
    )


def hidden_kernel(act, maps, rows, spots, starts, out):
    sources, share, width = act.shape[0], maps.shape[1], rows.shape[1]
    _, height, places = out.shape
    rank = height // sources
    slot = slot_of(rows[...], starts[...])
    every = all_rows(act, width // sources)
    total = jnp.zeros((rank, width), jnp.float32)
    for part in slot_chunks(maps.shape[0] * share):
        size = part.stop - part.start
        some = maps[part.start // share : part.stop // share].reshape(size, -1)
        each = dot(some, every, ((1,), (1,))).reshape(size // rank, rank, -1)
        total += jnp.sum(jnp.where(own_rows(slot, part.start, size, rank), each, 0.0), axis=0)
    total = jnp.where(of_source(sources, width), total[None], 0.0).reshape(height, width)
    high = total.astype(jnp.bfloat16)
    low = (total - high.astype(jnp.float32)).astype(jnp.bfloat16)
    place = placing(spots[...], places)
    for k, part in enumerate((high, low)):
        out[k] = dot(part, place, ((1,), (1,))).astype(out.dtype)


def down_kernel(act, grad, rows, spots, starts, out, total):
    sources, width = act.shape[0], rows.shape[1]
    rank, places = grad.shape[0] // sources, grad.shape[1]
    step = pl.program_id(0)

    @pl.when(step == 0)
    def _():
        total[...] = jnp.zeros_like(total)

    slot = slot_of(rows[...], starts[...])
    every = all_rows(act, width // sources)
    wide = dot(grad[...], placing(spots[...], places), ((1,), (0,)))
    wide = wide.reshape(sources, rank, width)
    wide = jnp.sum(jnp.where(of_source(sources, width), wide, 0.0), axis=0, keepdims=True)
    for part in slot_chunks(total.shape[0]):
        size = part.stop - part.start
        placed = jnp.where(own_rows(slot, part.start, size, rank), wide, 0.0)
        placed = placed.reshape(size, -1).astype(jnp.bfloat16)
        total[part, :] += dot(placed, every, ((1,), (0,)))

    @pl.when(step == pl.num_programs(0) - 1)
    def _():
        out[...] = (adapter_scale * total[...]).astype(out.dtype)


def feature_calls(received, tokens, share, rank, places, starts):
    devices, packed, features = received.shape
    width = devices * share
    sources = 4
    grid = (devices // sources,)
    act = pl.BlockSpec((sources, packed, features), lambda j: (j, 0, 0))
    maps = pl.BlockSpec((devices, share, features), lambda j: (0, tokens // share, 0))
    rows = pl.BlockSpec((1, sources * tokens), lambda j: (0, j))
    begin = pl.BlockSpec((starts, 1), lambda j: (0, 0))
    placed = pl.BlockSpec((sources * rank, places), lambda j: (j, 0))
    cost = pl.CostEstimate(
        flops=2 * devices * tokens * width * features,
        bytes_accessed=2 * devices * tokens * features,
        transcendentals=0,
    )
    params = pltpu.CompilerParams(vmem_limit_bytes=VMEM)
    hidden = pl.pallas_call(
        hidden_kernel,
        grid=grid,
        in_specs=[act, maps, rows, rows, begin],
        out_specs=pl.BlockSpec((2, sources * rank, places), lambda j: (0, j, 0)),
        out_shape=jax.ShapeDtypeStruct((2, devices * rank, places), received.dtype),
        cost_estimate=cost,
        compiler_params=params,
    )
    down = pl.pallas_call(
        down_kernel,
        grid=grid,
        in_specs=[act, placed, rows, rows, begin],
        out_specs=pl.BlockSpec((width, features), lambda j: (0, 0)),
        out_shape=jax.ShapeDtypeStruct((width, features), jnp.bfloat16),
        scratch_shapes=[pltpu.VMEM((width, features), jnp.float32)],
        cost_estimate=cost,
        compiler_params=params,
    )
    return hidden, down


def local(
    activations,
    cotangent,
    token_layout_row,
    tenant_first_row,
    frozen_value_weight,
    adapter_down_maps,
    adapter_up_maps,
):
    devices = lax.axis_size("blk")
    device = lax.axis_index("blk")
    tokens = activations.shape[0]
    resident, rank, width = adapter_down_maps.shape
    out_width = cotangent.shape[1]
    features = width // devices
    share = resident * rank
    resident_rows = resident * BLOCK
    cap = resident_rows // devices
    start_ids = tenant_first_row // BLOCK

    pieces = weight_pieces(frozen_value_weight)

    first_block = device * resident
    block_numbers = first_block + jnp.arange(resident, dtype=jnp.int32)
    begin = starts_of(block_numbers, start_ids)
    is_local = (begin >= first_block) & (begin <= block_numbers)
    home_slot = jnp.clip(begin - first_block, 0, resident - 1)
    last_map = jnp.concatenate(
        [
            lax.dynamic_index_in_dim(maps, home_slot[resident - 1], 0, keepdims=False)
            for maps in (adapter_down_maps, adapter_up_maps)
        ],
        axis=1,
    )
    carried = jnp.zeros_like(last_map)
    for step in range(1, HOPS + 1):
        home = (device - step) % devices
        carried = jnp.where(begin[0] // resident == home, moved(last_map, step), carried)

    def of_blocks(maps, own):
        blocks = []
        for b in range(resident):
            chosen = own
            for k in range(b + 1):
                chosen = jnp.where(is_local[b] & (home_slot[b] == k), maps[k], chosen)
            blocks.append(chosen)
        return jnp.concatenate(blocks, axis=0)

    down_blocks = of_blocks(adapter_down_maps, carried[:, :width])
    up_blocks = of_blocks(adapter_up_maps, carried[:, width:])

    sent_cot, digits = pack_rows(token_layout_row, cotangent, devices, cap, features)
    flat_maps = adapter_down_maps.reshape(share, width)
    received = pack_features(activations, flat_maps, digits, devices)
    received = lax.all_to_all(received, "blk", split_axis=0, concat_axis=0)
    per_digit = -(-tokens // features)
    digits = received[:, tokens + share : tokens + share + 5 * per_digit]
    digits = digits.reshape(devices, 5, per_digit * features)[:, :, :tokens]
    rows_all, place_all = from_digits(digits)

    own, _, across, _ = pieces
    sent_cot = after(sent_cot, received, own[CHUNKS], across[0])
    got_cot = lax.all_to_all(sent_cot, "blk", split_axis=0, concat_axis=0)
    recv_cot = [
        got_cot[:, k * cap : (k + 1) * cap].reshape(resident_rows, features)
        for k in range(out_width // features)
    ]

    spots = device * cap + jnp.arange(cap, dtype=jnp.int32)
    hit = place_all[:, None, :] == spots[None, :, None]
    row_in = rows_all - device * resident_rows + 1
    row_in = jnp.sum(jnp.where(hit, row_in[:, None, :], 0), axis=2).reshape(-1) - 1
    arrange = row_in[:, None] == jnp.arange(resident_rows, dtype=jnp.int32)[None, :]
    arrange = arrange.astype(jnp.bfloat16)
    in_block = row_in[:, None] // BLOCK == jnp.arange(share, dtype=jnp.int32)[None, :] // rank

    grad_in = sum(
        dot(part, up_blocks[:, k * features : (k + 1) * features], ((1,), (1,)))
        for k, part in enumerate(recv_cot)
    )
    grad_in = jnp.where(in_block, grad_in, 0.0).astype(jnp.bfloat16)
    grad_in = sum(grad_in[:, b * rank : (b + 1) * rank] for b in range(resident))
    grad_sent = grad_in.reshape(devices, cap, rank).transpose(1, 0, 2).reshape(cap, -1)

    rows_all, place_all = rows_all.reshape(1, -1), place_all.reshape(1, -1)

    cot_rows = jnp.concatenate(
        [dot(arrange, part, ((0,), (0,))).astype(jnp.bfloat16) for part in recv_cot], axis=1
    )
    grad_rows = dot(arrange, grad_in, ((0,), (0,))).astype(jnp.bfloat16)
    group = lax.axis_index("groups")
    quarter = device % 4
    firsts = [quarter, quarter ^ 1, quarter ^ 2, quarter ^ 3]
    if own[0].shape[1] % LANES == 0:
        out = None
        for piece, first in zip(pieces, firsts):
            out = write_quarter(piece, first, group, cot_rows, grad_rows, down_blocks, out)
    else:
        weight = together(pieces, firsts, group)
        lora = [
            dot(
                grad_rows[b * BLOCK : (b + 1) * BLOCK],
                down_blocks[b * rank : (b + 1) * rank],
                ((1,), (0,)),
            )
            for b in range(resident)
        ]
        lora = (adapter_scale * jnp.concatenate(lora, axis=0)).astype(jnp.bfloat16)
        out = dot(cot_rows, weight, ((1,), (1,))) + lora.astype(jnp.float32)
        out = out.astype(jnp.bfloat16)

    starts = start_ids[:, None]
    hidden_call, down_call = feature_calls(
        received, tokens, share, rank, resident_rows, starts.shape[0]
    )
    shares = hidden_call(received, received, rows_all, place_all, starts)

    shares = shares.reshape(-1, resident_rows).T.reshape(devices, cap, -1)
    copies = jnp.broadcast_to(grad_sent[None], (devices,) + grad_sent.shape)
    small = jnp.concatenate([copies, shares], axis=2)
    small = lax.all_to_all(small, "blk", split_axis=0, concat_axis=0)
    each = devices * rank
    grad_all = small[:, :, :each].reshape(resident_rows, each).T
    hidden = jnp.sum(small[:, :, each:].astype(jnp.float32), axis=0)
    hidden = (hidden[:, :each] + hidden[:, each:]).astype(jnp.bfloat16)
    hidden = hidden.reshape(cap, devices, rank).transpose(1, 0, 2).reshape(-1, rank)

    down_f = down_call(received, grad_all, rows_all, place_all, starts)
    down_home = lax.all_to_all(down_f, "blk", split_axis=0, concat_axis=1, tiled=True)
    down_map_gradient = down_home.astype(jnp.float32).reshape(resident, rank, width)

    wide = jnp.where(in_block, jnp.concatenate([hidden] * resident, axis=1), 0)
    up_all = [dot(wide, part, ((0,), (0,))) for part in recv_cot]
    up_all = jnp.concatenate(up_all, axis=1).reshape(resident, rank, out_width)
    up_parts = [up_all[b] for b in range(resident)]

    tail = sum(jnp.where(is_local[b], 0.0, up_parts[b]) for b in range(resident))
    far = jnp.zeros_like(tail)
    for step in range(1, HOPS + 1):
        other = (device + step) % devices * resident
        theirs = starts_of(other[None], start_ids)[0]
        far = far + jnp.where(theirs // resident == device, moved(tail, -step), 0.0)
    up_grads = []
    for k in range(resident):
        total = jnp.where(begin[resident - 1] == first_block + k, far, 0.0)
        for b in range(resident):
            total = total + jnp.where(is_local[b] & (home_slot[b] == k), up_parts[b], 0.0)
        up_grads.append(adapter_scale * total)
    up_map_gradient = jnp.stack(up_grads)

    return (out, down_map_gradient, up_map_gradient)


def solution(mesh):
    return jax.shard_map(
        local,
        mesh=mesh,
        in_specs=(
            P(("groups", "blk"), None),
            P(("groups", "blk"), None),
            P(("groups", "blk")),
            P("groups"),
            P("blk", None),
            P(("groups", "blk"), None, None),
            P(("groups", "blk"), None, None),
        ),
        out_specs=(
            P(("groups", "blk"), None),
            P(("groups", "blk"), None, None),
            P(("groups", "blk"), None, None),
        ),
        check_vma=False,
    )
```

```python
import functools

import jax
import jax.numpy as jnp
from jax import lax
from jax.experimental import pallas as pl
from jax.experimental.pallas import tpu as pltpu
from jax.sharding import PartitionSpec as P

BLOCK = 128
HOPS = 4
LANES = 128
DIGIT = 64
VMEM = 56 << 20

adapter_scale = 2.0


def moved(value, steps):
    count = lax.axis_size("blk")
    return lax.ppermute(value, "blk", [(i, (i + steps) % count) for i in range(count)])


def to_all(value):
    count = lax.axis_size("blk")
    copies = jnp.broadcast_to(value[None], (count,) + value.shape)
    return lax.all_to_all(copies, "blk", split_axis=0, concat_axis=0)


def after(value, *others):
    anywhere = pl.BlockSpec(memory_space=pl.ANY)
    return pl.pallas_call(
        lambda *refs: None,
        in_specs=[anywhere] * (1 + len(others)),
        out_specs=anywhere,
        out_shape=jax.ShapeDtypeStruct(value.shape, value.dtype),
        input_output_aliases={0: 0},
        cost_estimate=pl.CostEstimate(flops=0, bytes_accessed=0, transcendentals=0),
        compiler_params=pltpu.CompilerParams(vmem_limit_bytes=VMEM),
    )(value, *others)


def dot(a, b, dims):
    return lax.dot_general(a, b, (dims, ((), ())), preferred_element_type=jnp.float32)


def starts_of(blocks, start_ids):
    latest = jnp.max(
        jnp.where(start_ids[None, :] <= blocks[:, None], start_ids[None, :], -1), axis=1
    )
    return jnp.where(latest >= 0, latest, jnp.max(start_ids))


def as_digits(rows, places):
    return (
        rows % DIGIT,
        rows // DIGIT % DIGIT,
        rows // (DIGIT * DIGIT),
        places % DIGIT,
        places // DIGIT,
    )


def from_digits(digits):
    low, middle, high, place, place_high = [digits[:, k].astype(jnp.int32) for k in range(5)]
    return (high * DIGIT + middle) * DIGIT + low, place_high * DIGIT + place


def weight_column(weight):
    count = lax.axis_size("blk")
    half = weight.shape[0] // 2
    lines = [list(range(k, count, 4)) for k in range(4)]
    mine = lax.dynamic_slice_in_dim(weight, lax.axis_index("groups") * half, half, 0)
    return lax.all_gather(mine, "blk", axis_index_groups=lines)


def weight_quarters(column, late):
    count = lax.axis_size("blk")

    def over(piece, bit):
        return lax.ppermute(piece, "blk", [(i, i ^ bit) for i in range(count)])

    def groups(piece):
        return lax.ppermute(piece, "groups", [(0, 1), (1, 0)])

    theirs = groups(column)
    across = over(column, 2)
    across_theirs = groups(across)
    return [
        [column, theirs],
        [over(column, 1), over(theirs, 1)],
        [across, across_theirs],
        [over(across, 1), over(after(across_theirs, late), 1)],
    ]


def quarter_kernel(where, cot, grad, down, *rest):
    pieces = rest[:2]
    out = rest[-1]
    rank = grad.shape[1]
    lora = [
        adapter_scale
        * dot(
            grad[b * BLOCK : (b + 1) * BLOCK, :],
            down[b * rank : (b + 1) * rank, :],
            ((1,), (0,)),
        )
        for b in range(cot.shape[0] // BLOCK)
    ]
    lora = jnp.concatenate(lora, axis=0).astype(jnp.bfloat16).astype(jnp.float32)

    def product(group):
        order = pieces[group:] + pieces[:group]
        weight = jnp.concatenate([piece[0] for piece in order], axis=0)
        frozen = dot(cot[...], weight, ((1,), (1,)))
        out[...] = (frozen + lora).astype(jnp.bfloat16)

    for group in range(2):
        pl.when(where[1] == group)(functools.partial(product, group))


def write_quarter(quarter, first, group, cot, grad, down, out=None):
    rows, depth = cot.shape
    width = down.shape[1]
    shards, part, _ = quarter[0].shape
    stripe = part * len(quarter)
    where = jnp.stack([first, group]).astype(jnp.int32)
    specs = [
        pl.BlockSpec((rows, depth), lambda j, where: (0, 0)),
        pl.BlockSpec(grad.shape, lambda j, where: (0, 0)),
        pl.BlockSpec((down.shape[0], stripe), lambda j, where: (0, 4 * j + where[0])),
    ] + [pl.BlockSpec((1, part, depth), lambda j, where: (j, 0, 0)) for _ in quarter]
    args = [where, cot, grad, down] + quarter
    alias = {}
    if out is not None:
        specs.append(pl.BlockSpec(memory_space=pl.ANY))
        args.append(out)
        alias = {len(args) - 1: 0}
    return pl.pallas_call(
        quarter_kernel,
        grid_spec=pltpu.PrefetchScalarGridSpec(
            num_scalar_prefetch=1,
            grid=(shards,),
            in_specs=specs,
            out_specs=pl.BlockSpec((rows, stripe), lambda j, where: (0, 4 * j + where[0])),
        ),
        out_shape=jax.ShapeDtypeStruct((rows, width), jnp.bfloat16),
        input_output_aliases=alias,
        cost_estimate=pl.CostEstimate(
            flops=2 * rows * depth * stripe * shards,
            bytes_accessed=2 * (depth + rows) * stripe * shards,
            transcendentals=0,
        ),
        compiler_params=pltpu.CompilerParams(vmem_limit_bytes=VMEM),
    )(*args)


def together(pieces, firsts, group):
    shards, part, depth = pieces[0][0].shape
    weight = jnp.zeros((shards, 4, 2, part, depth), jnp.bfloat16)
    for quarter, first in zip(pieces, firsts):
        for k, piece in enumerate(quarter):
            place = (0, first, group if k == 0 else 1 - group, 0, 0)
            weight = lax.dynamic_update_slice(weight, piece[:, None, None], place)
    return weight.reshape(-1, depth)


def rows_kernel(rows, cot, out, digits_out, place):
    devices, shared, features = out.shape
    folds = cot.shape[1] // features
    cap = shared // folds
    target = rows[...] // (cap * devices)
    to = lax.broadcasted_iota(jnp.int32, (16, features), 0) == target
    first = lax.broadcasted_iota(jnp.int32, (features, features), 0)
    later = lax.broadcasted_iota(jnp.int32, (features, features), 1)
    earlier = jnp.where(first < later, 1.0, 0.0).astype(jnp.bfloat16)
    ahead = dot(jnp.where(to, 1.0, 0.0).astype(jnp.bfloat16), earlier, ((1,), (0,)))
    ahead = jnp.sum(jnp.where(to, ahead, 0.0), axis=0, keepdims=True)
    place[...] = target * cap + ahead.astype(jnp.int32)
    which = lax.broadcasted_iota(jnp.int32, (16, features), 0)
    digits = jnp.zeros((16, features), jnp.int32)
    for k, digit in enumerate(as_digits(rows[...], place[...])):
        digits = jnp.where(which == k, digit, digits)
    digits_out[...] = digits.astype(jnp.float32).astype(out.dtype)
    send = placing(place[:, : cot.shape[0]], cap * devices)
    for f in range(folds):
        sent = dot(send, cot[:, f * features : (f + 1) * features], ((1,), (0,)))
        for k in range(devices):
            some = sent[k * cap : (k + 1) * cap].astype(out.dtype)
            out[k, f * cap : (f + 1) * cap, :] = some


def pack_rows(rows, cot, devices, cap, features):
    tokens = rows.shape[0]
    folds = cot.shape[1] // features
    if features % LANES == 0 and cap % 8 == 0 and features >= tokens and devices <= 16:
        padding = jnp.full((features - tokens,), 16 * cap * devices, jnp.int32)
        return pl.pallas_call(
            rows_kernel,
            out_shape=[
                jax.ShapeDtypeStruct((devices, folds * cap, features), cot.dtype),
                jax.ShapeDtypeStruct((16, features), cot.dtype),
            ],
            scratch_shapes=[pltpu.VMEM((1, features), jnp.int32)],
            cost_estimate=pl.CostEstimate(
                flops=2 * devices * cap * tokens * cot.shape[1],
                bytes_accessed=6 * cot.size,
                transcendentals=0,
            ),
            compiler_params=pltpu.CompilerParams(vmem_limit_bytes=VMEM),
        )(jnp.concatenate([rows, padding])[None], cot)
    target = rows // (cap * devices)
    order = jnp.arange(tokens, dtype=jnp.int32)
    before = (target[:, None] == target[None, :]) & (order[None, :] < order[:, None])
    place = target * cap + jnp.sum(before.astype(jnp.int32), axis=1)
    send = jnp.arange(cap * devices, dtype=jnp.int32)[:, None] == place[None, :]
    sent = dot(send.astype(jnp.bfloat16), cot, ((1,), (0,))).astype(jnp.bfloat16)
    sent = sent.reshape(devices, cap, cot.shape[1])
    digits = jnp.stack(as_digits(rows, place)).astype(jnp.bfloat16)
    digits = jnp.pad(digits, ((0, 0), (0, -tokens % features))).reshape(-1, features)
    digits = jnp.pad(digits, ((0, -digits.shape[0] % 16), (0, 0)))
    parts = [sent[:, :, k : k + features] for k in range(0, cot.shape[1], features)]
    return jnp.concatenate(parts, axis=1), digits


def features_kernel(act, maps, cot, digits, out):
    targets, _, features = out.shape
    tokens, shared = act.shape[0], maps.shape[0]
    for k in range(targets):
        part = slice(k * features, (k + 1) * features)
        out[k, :tokens, :] = act[:, part]
        out[k, tokens : tokens + shared, :] = maps[:, part]
        out[k, tokens + shared : tokens + 2 * shared, :] = cot[k]
        out[k, tokens + 2 * shared :, :] = digits[...]


def pack_features(act, maps, cot, digits, devices):
    tokens, width = act.shape
    features = width // devices
    shared = maps.shape[0]
    total = tokens + 2 * shared + digits.shape[0]
    targets = 4
    if features % LANES == 0:
        return pl.pallas_call(
            features_kernel,
            grid=(devices // targets,),
            in_specs=[
                pl.BlockSpec((tokens, targets * features), lambda j: (0, j)),
                pl.BlockSpec((shared, targets * features), lambda j: (0, j)),
                pl.BlockSpec((targets, shared, features), lambda j: (j, 0, 0)),
                pl.BlockSpec(digits.shape, lambda j: (0, 0)),
            ],
            out_specs=pl.BlockSpec((targets, total, features), lambda j: (j, 0, 0)),
            out_shape=jax.ShapeDtypeStruct((devices, total, features), act.dtype),
            cost_estimate=pl.CostEstimate(
                flops=0, bytes_accessed=4 * total * width, transcendentals=0
            ),
            compiler_params=pltpu.CompilerParams(vmem_limit_bytes=VMEM),
        )(act, maps, cot, digits)
    both = jnp.concatenate([act, maps], axis=0)
    both = both.reshape(tokens + shared, devices, features).transpose(1, 0, 2)
    copies = jnp.broadcast_to(digits[None], (devices,) + digits.shape)
    return jnp.concatenate([both, cot, copies], axis=1)


def slot_chunks(width):
    size = min(width, 768)
    while width % size:
        size //= 2
    return [slice(k, k + size) for k in range(0, width, size)]


def slot_of(rows, starts):
    blocks = rows // BLOCK
    latest = jnp.max(jnp.where(starts <= blocks, starts, -1), axis=0, keepdims=True)
    return jnp.where(latest >= 0, latest, jnp.max(starts))


def own_rows(slot, first, size, rank):
    index = first // rank + lax.broadcasted_iota(jnp.int32, (size // rank, rank, 1), 0)
    return index == slot[None]


def placing(place, places):
    hit = lax.broadcasted_iota(jnp.int32, (places, place.shape[1]), 0) == place
    return jnp.where(hit, 1.0, 0.0).astype(jnp.bfloat16)


def all_rows(act, tokens):
    return jnp.concatenate([act[k, :tokens, :] for k in range(act.shape[0])], axis=0)


def of_source(sources, width):
    lane = lax.broadcasted_iota(jnp.int32, (sources, 1, width), 2)
    return lane // (width // sources) == lax.broadcasted_iota(
        jnp.int32, (sources, 1, width), 0
    )


def hidden_kernel(act, maps, rows, spots, starts, out):
    sources, share, width = act.shape[0], maps.shape[1], rows.shape[1]
    _, height, places = out.shape
    rank = height // sources
    slot = slot_of(rows[...], starts[...])
    every = all_rows(act, width // sources)
    total = jnp.zeros((rank, width), jnp.float32)
    for part in slot_chunks(maps.shape[0] * share):
        size = part.stop - part.start
        some = maps[part.start // share : part.stop // share].reshape(size, -1)
        each = dot(some, every, ((1,), (1,))).reshape(size // rank, rank, -1)
        total += jnp.sum(jnp.where(own_rows(slot, part.start, size, rank), each, 0.0), axis=0)
    total = jnp.where(of_source(sources, width), total[None], 0.0).reshape(height, width)
    high = total.astype(jnp.bfloat16)
    low = (total - high.astype(jnp.float32)).astype(jnp.bfloat16)
    place = placing(spots[...], places)
    for k, part in enumerate((high, low)):
        out[k] = dot(part, place, ((1,), (1,))).astype(out.dtype)


def down_kernel(act, grad, rows, spots, starts, out, total):
    sources, width = act.shape[0], rows.shape[1]
    rank, places = grad.shape[0] // sources, grad.shape[1]
    step = pl.program_id(0)

    @pl.when(step == 0)
    def _():
        total[...] = jnp.zeros_like(total)

    slot = slot_of(rows[...], starts[...])
    every = all_rows(act, width // sources)
    wide = dot(grad[...], placing(spots[...], places), ((1,), (0,)))
    wide = wide.reshape(sources, rank, width)
    wide = jnp.sum(jnp.where(of_source(sources, width), wide, 0.0), axis=0, keepdims=True)
    for part in slot_chunks(total.shape[0]):
        size = part.stop - part.start
        placed = jnp.where(own_rows(slot, part.start, size, rank), wide, 0.0)
        placed = placed.reshape(size, -1).astype(jnp.bfloat16)
        total[part, :] += dot(placed, every, ((1,), (0,)))

    @pl.when(step == pl.num_programs(0) - 1)
    def _():
        out[...] = (adapter_scale * total[...]).astype(out.dtype)


def feature_calls(received, tokens, share, rank, places, starts):
    devices, packed, features = received.shape
    width = devices * share
    sources = 4
    grid = (devices // sources,)
    act = pl.BlockSpec((sources, packed, features), lambda j: (j, 0, 0))
    maps = pl.BlockSpec((devices, share, features), lambda j: (0, tokens // share, 0))
    rows = pl.BlockSpec((1, sources * tokens), lambda j: (0, j))
    begin = pl.BlockSpec((starts, 1), lambda j: (0, 0))
    placed = pl.BlockSpec((sources * rank, places), lambda j: (j, 0))
    cost = pl.CostEstimate(
        flops=2 * devices * tokens * width * features,
        bytes_accessed=2 * devices * tokens * features,
        transcendentals=0,
    )
    params = pltpu.CompilerParams(vmem_limit_bytes=VMEM)
    hidden = pl.pallas_call(
        hidden_kernel,
        grid=grid,
        in_specs=[act, maps, rows, rows, begin],
        out_specs=pl.BlockSpec((2, sources * rank, places), lambda j: (0, j, 0)),
        out_shape=jax.ShapeDtypeStruct((2, devices * rank, places), received.dtype),
        cost_estimate=cost,
        compiler_params=params,
    )
    down = pl.pallas_call(
        down_kernel,
        grid=grid,
        in_specs=[act, placed, rows, rows, begin],
        out_specs=pl.BlockSpec((width, features), lambda j: (0, 0)),
        out_shape=jax.ShapeDtypeStruct((width, features), jnp.bfloat16),
        scratch_shapes=[pltpu.VMEM((width, features), jnp.float32)],
        cost_estimate=cost,
        compiler_params=params,
    )
    return hidden, down


def local(
    activations,
    cotangent,
    token_layout_row,
    tenant_first_row,
    frozen_value_weight,
    adapter_down_maps,
    adapter_up_maps,
):
    devices = lax.axis_size("blk")
    device = lax.axis_index("blk")
    tokens = activations.shape[0]
    resident, rank, width = adapter_down_maps.shape
    out_width = cotangent.shape[1]
    features = width // devices
    share = resident * rank
    resident_rows = resident * BLOCK
    cap = resident_rows // devices
    start_ids = tenant_first_row // BLOCK

    column = weight_column(frozen_value_weight)

    first_block = device * resident
    block_numbers = first_block + jnp.arange(resident, dtype=jnp.int32)
    begin = starts_of(block_numbers, start_ids)
    is_local = (begin >= first_block) & (begin <= block_numbers)
    home_slot = jnp.clip(begin - first_block, 0, resident - 1)
    last_map = jnp.concatenate(
        [
            lax.dynamic_index_in_dim(maps, home_slot[resident - 1], 0, keepdims=False)
            for maps in (adapter_down_maps, adapter_up_maps)
        ],
        axis=1,
    )
    carried = jnp.zeros_like(last_map)
    for step in range(1, HOPS + 1):
        home = (device - step) % devices
        carried = jnp.where(begin[0] // resident == home, moved(last_map, step), carried)

    def of_blocks(maps, own):
        blocks = []
        for b in range(resident):
            chosen = own
            for k in range(b + 1):
                chosen = jnp.where(is_local[b] & (home_slot[b] == k), maps[k], chosen)
            blocks.append(chosen)
        return jnp.concatenate(blocks, axis=0)

    down_blocks = of_blocks(adapter_down_maps, carried[:, :width])
    up_blocks = of_blocks(adapter_up_maps, carried[:, width:])

    sent_cot, digits = pack_rows(token_layout_row, cotangent, devices, cap, features)
    flat_maps = adapter_down_maps.reshape(share, width)
    received = pack_features(activations, flat_maps, sent_cot, digits, devices)
    received = after(received, column, carried)
    received = lax.all_to_all(received, "blk", split_axis=0, concat_axis=0)
    recv_cot = [
        received[:, tokens + share + k * cap : tokens + share + (k + 1) * cap].reshape(
            resident_rows, features
        )
        for k in range(out_width // features)
    ]
    per_digit = -(-tokens // features)
    digits = received[:, tokens + 2 * share : tokens + 2 * share + 5 * per_digit]
    digits = digits.reshape(devices, 5, per_digit * features)[:, :, :tokens]
    rows_all, place_all = from_digits(digits)

    spots = device * cap + jnp.arange(cap, dtype=jnp.int32)
    hit = place_all[:, None, :] == spots[None, :, None]
    row_in = rows_all - device * resident_rows + 1
    row_in = jnp.sum(jnp.where(hit, row_in[:, None, :], 0), axis=2).reshape(-1) - 1
    arrange = row_in[:, None] == jnp.arange(resident_rows, dtype=jnp.int32)[None, :]
    arrange = arrange.astype(jnp.bfloat16)
    in_block = row_in[:, None] // BLOCK == jnp.arange(share, dtype=jnp.int32)[None, :] // rank

    grad_in = sum(
        dot(part, up_blocks[:, k * features : (k + 1) * features], ((1,), (1,)))
        for k, part in enumerate(recv_cot)
    )
    grad_in = jnp.where(in_block, grad_in, 0.0).astype(jnp.bfloat16)
    grad_in = sum(grad_in[:, b * rank : (b + 1) * rank] for b in range(resident))
    grad_sent = grad_in.reshape(devices, cap, rank).transpose(1, 0, 2).reshape(cap, -1)

    rows_all, place_all = rows_all.reshape(1, -1), place_all.reshape(1, -1)

    cot_rows = jnp.concatenate(
        [dot(arrange, part, ((0,), (0,))).astype(jnp.bfloat16) for part in recv_cot], axis=1
    )
    grad_rows = dot(arrange, grad_in, ((0,), (0,))).astype(jnp.bfloat16)

    starts = start_ids[:, None]
    hidden_call, down_call = feature_calls(
        received, tokens, share, rank, resident_rows, starts.shape[0]
    )
    shares = hidden_call(received, received, rows_all, place_all, starts)

    shares = shares.reshape(-1, resident_rows).T.reshape(devices, cap, -1)
    copies = jnp.broadcast_to(grad_sent[None], (devices,) + grad_sent.shape)
    small = jnp.concatenate([copies, shares], axis=2)
    small = lax.all_to_all(small, "blk", split_axis=0, concat_axis=0)
    each = devices * rank
    grad_all = small[:, :, :each].reshape(resident_rows, each).T
    hidden = jnp.sum(small[:, :, each:].astype(jnp.float32), axis=0)
    hidden = (hidden[:, :each] + hidden[:, each:]).astype(jnp.bfloat16)
    hidden = hidden.reshape(cap, devices, rank).transpose(1, 0, 2).reshape(-1, rank)

    down_f = down_call(received, grad_all, rows_all, place_all, starts)
    down_home = lax.all_to_all(down_f, "blk", split_axis=0, concat_axis=1, tiled=True)
    down_map_gradient = down_home.astype(jnp.float32).reshape(resident, rank, width)

    wide = jnp.where(in_block, jnp.concatenate([hidden] * resident, axis=1), 0)
    up_all = [dot(wide, part, ((0,), (0,))) for part in recv_cot]
    up_all = jnp.concatenate(up_all, axis=1).reshape(resident, rank, out_width)
    up_parts = [up_all[b] for b in range(resident)]

    tail = sum(jnp.where(is_local[b], 0.0, up_parts[b]) for b in range(resident))
    far = jnp.zeros_like(tail)
    for step in range(1, HOPS + 1):
        other = (device + step) % devices * resident
        theirs = starts_of(other[None], start_ids)[0]
        far = far + jnp.where(theirs // resident == device, moved(tail, -step), 0.0)
    up_grads = []
    for k in range(resident):
        total = jnp.where(begin[resident - 1] == first_block + k, far, 0.0)
        for b in range(resident):
            total = total + jnp.where(is_local[b] & (home_slot[b] == k), up_parts[b], 0.0)
        up_grads.append(adapter_scale * total)
    up_map_gradient = jnp.stack(up_grads)

    pieces = weight_quarters(column, shares)
    group = lax.axis_index("groups")
    quarter = device % 4
    firsts = [quarter, quarter ^ 1, quarter ^ 2, quarter ^ 3]
    if column.shape[1] % LANES == 0:
        out = None
        for number, (piece, first) in enumerate(zip(pieces, firsts)):
            if number == 2:
                grad_rows = after(grad_rows, down_f)
            out = write_quarter(piece, first, group, cot_rows, grad_rows, down_blocks, out)
    else:
        weight = together(pieces, firsts, group)
        lora = [
            dot(
                grad_rows[b * BLOCK : (b + 1) * BLOCK],
                down_blocks[b * rank : (b + 1) * rank],
                ((1,), (0,)),
            )
            for b in range(resident)
        ]
        lora = (adapter_scale * jnp.concatenate(lora, axis=0)).astype(jnp.bfloat16)
        out = dot(cot_rows, weight, ((1,), (1,))) + lora.astype(jnp.float32)
        out = out.astype(jnp.bfloat16)

    return (out, down_map_gradient, up_map_gradient)


def solution(mesh):
    return jax.shard_map(
        local,
        mesh=mesh,
        in_specs=(
            P(("groups", "blk"), None),
            P(("groups", "blk"), None),
            P(("groups", "blk")),
            P("groups"),
            P("blk", None),
            P(("groups", "blk"), None, None),
            P(("groups", "blk"), None, None),
        ),
        out_specs=(
            P(("groups", "blk"), None),
            P(("groups", "blk"), None, None),
            P(("groups", "blk"), None, None),
        ),
        check_vma=False,
    )
```

```python
import functools

import jax
import jax.numpy as jnp
from jax import lax
from jax.experimental import pallas as pl
from jax.experimental.pallas import tpu as pltpu
from jax.sharding import PartitionSpec as P

BLOCK = 128
HOPS = 4
LANES = 128
DIGIT = 64
VMEM = 56 << 20

adapter_scale = 2.0


def moved(value, steps):
    count = lax.axis_size("blk")
    return lax.ppermute(value, "blk", [(i, (i + steps) % count) for i in range(count)])


def to_all(value):
    count = lax.axis_size("blk")
    copies = jnp.broadcast_to(value[None], (count,) + value.shape)
    return lax.all_to_all(copies, "blk", split_axis=0, concat_axis=0)


def after(value, *others):
    anywhere = pl.BlockSpec(memory_space=pl.ANY)
    return pl.pallas_call(
        lambda *refs: None,
        in_specs=[anywhere] * (1 + len(others)),
        out_specs=anywhere,
        out_shape=jax.ShapeDtypeStruct(value.shape, value.dtype),
        input_output_aliases={0: 0},
        cost_estimate=pl.CostEstimate(flops=0, bytes_accessed=0, transcendentals=0),
        compiler_params=pltpu.CompilerParams(vmem_limit_bytes=VMEM),
    )(value, *others)


def dot(a, b, dims):
    return lax.dot_general(a, b, (dims, ((), ())), preferred_element_type=jnp.float32)


def starts_of(blocks, start_ids):
    latest = jnp.max(
        jnp.where(start_ids[None, :] <= blocks[:, None], start_ids[None, :], -1), axis=1
    )
    return jnp.where(latest >= 0, latest, jnp.max(start_ids))


def as_digits(rows, places):
    return (
        rows % DIGIT,
        rows // DIGIT % DIGIT,
        rows // (DIGIT * DIGIT),
        places % DIGIT,
        places // DIGIT,
    )


def from_digits(digits):
    low, middle, high, place, place_high = [digits[:, k].astype(jnp.int32) for k in range(5)]
    return (high * DIGIT + middle) * DIGIT + low, place_high * DIGIT + place


def weight_column(weight):
    count = lax.axis_size("blk")
    half = weight.shape[0] // 2
    lines = [list(range(k, count, 4)) for k in range(4)]
    mine = lax.dynamic_slice_in_dim(weight, lax.axis_index("groups") * half, half, 0)
    return lax.all_gather(mine, "blk", axis_index_groups=lines)


def weight_quarters(column):
    count = lax.axis_size("blk")

    def over(piece, bit):
        return lax.ppermute(piece, "blk", [(i, i ^ bit) for i in range(count)])

    def groups(piece):
        return lax.ppermute(piece, "groups", [(0, 1), (1, 0)])

    own = [column, groups(column)]
    across = over(column, 2)
    across = [across, groups(across)]

    def quarter(number, late=None):
        mine, theirs = across if number >= 2 else own
        if number % 2 == 0:
            return [mine, theirs]
        if late is not None:
            theirs = after(theirs, late)
        return [over(mine, 1), over(theirs, 1)]

    return quarter


def quarter_kernel(where, cot, grad, down, mine, theirs, *rest):
    out, token = rest[-2:]
    token[...] = jnp.zeros_like(token)
    half = mine.shape[1]
    lora = adapter_scale * dot(grad[...], down[...], ((1,), (0,)))
    lora = lora.astype(jnp.bfloat16).astype(jnp.float32)

    def product(group):
        for k, piece in enumerate((mine, theirs) if group == 0 else (theirs, mine)):
            part = slice(k * half, (k + 1) * half)
            frozen = dot(cot[...], piece[0], ((1,), (1,)))
            out[:, part] = (frozen + lora[:, part]).astype(jnp.bfloat16)

    for group in range(2):
        pl.when(where[1] == group)(functools.partial(product, group))


def write_quarter(quarter, first, group, cot, grad, down, out=None):
    rows, depth = cot.shape
    width = down.shape[1]
    shards, part, _ = quarter[0].shape
    stripe = part * len(quarter)
    where = jnp.stack([first, group]).astype(jnp.int32)
    specs = [
        pl.BlockSpec((rows, depth), lambda j, where: (0, 0)),
        pl.BlockSpec(grad.shape, lambda j, where: (0, 0)),
        pl.BlockSpec((down.shape[0], stripe), lambda j, where: (0, 4 * j + where[0])),
    ] + [pl.BlockSpec((1, part, depth), lambda j, where: (j, 0, 0)) for _ in quarter]
    args = [where, cot, grad, down] + quarter
    alias = {}
    if out is not None:
        specs.append(pl.BlockSpec(memory_space=pl.ANY))
        args.append(out)
        alias = {len(args) - 1: 0}
    return pl.pallas_call(
        quarter_kernel,
        grid_spec=pltpu.PrefetchScalarGridSpec(
            num_scalar_prefetch=1,
            grid=(shards,),
            in_specs=specs,
            out_specs=[
                pl.BlockSpec((rows, stripe), lambda j, where: (0, 4 * j + where[0])),
                pl.BlockSpec((8, LANES), lambda j, where: (0, 0)),
            ],
        ),
        out_shape=[
            jax.ShapeDtypeStruct((rows, width), jnp.bfloat16),
            jax.ShapeDtypeStruct((8, LANES), jnp.float32),
        ],
        input_output_aliases=alias,
        cost_estimate=pl.CostEstimate(
            flops=2 * rows * depth * stripe * shards,
            bytes_accessed=2 * (depth + rows) * stripe * shards,
            transcendentals=0,
        ),
        compiler_params=pltpu.CompilerParams(vmem_limit_bytes=VMEM),
    )(*args)


def together(pieces, firsts, group):
    shards, part, depth = pieces[0][0].shape
    weight = jnp.zeros((shards, 4, 2, part, depth), jnp.bfloat16)
    for quarter, first in zip(pieces, firsts):
        for k, piece in enumerate(quarter):
            place = (0, first, group if k == 0 else 1 - group, 0, 0)
            weight = lax.dynamic_update_slice(weight, piece[:, None, None], place)
    return weight.reshape(-1, depth)


def rows_kernel(rows, cot, out, place):
    devices, packed, features = out.shape
    shared = packed - 16
    folds = cot.shape[1] // features
    cap = shared // folds
    target = rows[...] // (cap * devices)
    to = lax.broadcasted_iota(jnp.int32, (16, features), 0) == target
    first = lax.broadcasted_iota(jnp.int32, (features, features), 0)
    later = lax.broadcasted_iota(jnp.int32, (features, features), 1)
    earlier = jnp.where(first < later, 1.0, 0.0).astype(jnp.bfloat16)
    ahead = dot(jnp.where(to, 1.0, 0.0).astype(jnp.bfloat16), earlier, ((1,), (0,)))
    ahead = jnp.sum(jnp.where(to, ahead, 0.0), axis=0, keepdims=True)
    place[...] = target * cap + ahead.astype(jnp.int32)
    which = lax.broadcasted_iota(jnp.int32, (16, features), 0)
    digits = jnp.zeros((16, features), jnp.int32)
    for k, digit in enumerate(as_digits(rows[...], place[...])):
        digits = jnp.where(which == k, digit, digits)
    digits = digits.astype(jnp.float32).astype(out.dtype)
    send = placing(place[:, : cot.shape[0]], cap * devices)
    for f in range(folds):
        sent = dot(send, cot[:, f * features : (f + 1) * features], ((1,), (0,)))
        for k in range(devices):
            some = sent[k * cap : (k + 1) * cap].astype(out.dtype)
            out[k, f * cap : (f + 1) * cap, :] = some
    for k in range(devices):
        out[k, shared:, :] = digits


def pack_rows(rows, cot, devices, cap, features):
    tokens = rows.shape[0]
    folds = cot.shape[1] // features
    if features % LANES == 0 and cap % 8 == 0 and features >= tokens and devices <= 16:
        padding = jnp.full((features - tokens,), 16 * cap * devices, jnp.int32)
        return pl.pallas_call(
            rows_kernel,
            out_shape=jax.ShapeDtypeStruct((devices, folds * cap + 16, features), cot.dtype),
            scratch_shapes=[pltpu.VMEM((1, features), jnp.int32)],
            cost_estimate=pl.CostEstimate(
                flops=2 * devices * cap * tokens * cot.shape[1],
                bytes_accessed=6 * cot.size,
                transcendentals=0,
            ),
            compiler_params=pltpu.CompilerParams(vmem_limit_bytes=VMEM),
        )(jnp.concatenate([rows, padding])[None], cot)
    target = rows // (cap * devices)
    order = jnp.arange(tokens, dtype=jnp.int32)
    before = (target[:, None] == target[None, :]) & (order[None, :] < order[:, None])
    place = target * cap + jnp.sum(before.astype(jnp.int32), axis=1)
    send = jnp.arange(cap * devices, dtype=jnp.int32)[:, None] == place[None, :]
    sent = dot(send.astype(jnp.bfloat16), cot, ((1,), (0,))).astype(jnp.bfloat16)
    sent = sent.reshape(devices, cap, cot.shape[1])
    digits = jnp.stack(as_digits(rows, place)).astype(jnp.bfloat16)
    digits = jnp.pad(digits, ((0, 0), (0, -tokens % features))).reshape(-1, features)
    digits = jnp.pad(digits, ((0, -digits.shape[0] % 16), (0, 0)))
    parts = [sent[:, :, k : k + features] for k in range(0, cot.shape[1], features)]
    parts += [jnp.broadcast_to(digits[None], (devices,) + digits.shape)]
    return jnp.concatenate(parts, axis=1)


def features_kernel(act, maps, out):
    targets, _, features = out.shape
    tokens = act.shape[0]
    for k in range(targets):
        part = slice(k * features, (k + 1) * features)
        out[k, :tokens, :] = act[:, part]
        out[k, tokens:, :] = maps[:, part]


def pack_features(act, maps, devices):
    tokens, width = act.shape
    features = width // devices
    shared = maps.shape[0]
    targets = 4
    if features % LANES == 0:
        return pl.pallas_call(
            features_kernel,
            grid=(devices // targets,),
            in_specs=[
                pl.BlockSpec((tokens, targets * features), lambda j: (0, j)),
                pl.BlockSpec((shared, targets * features), lambda j: (0, j)),
            ],
            out_specs=pl.BlockSpec((targets, tokens + shared, features), lambda j: (j, 0, 0)),
            out_shape=jax.ShapeDtypeStruct((devices, tokens + shared, features), act.dtype),
            cost_estimate=pl.CostEstimate(
                flops=0, bytes_accessed=4 * (tokens + shared) * width, transcendentals=0
            ),
            compiler_params=pltpu.CompilerParams(vmem_limit_bytes=VMEM),
        )(act, maps)
    both = jnp.concatenate([act, maps], axis=0)
    return both.reshape(tokens + shared, devices, features).transpose(1, 0, 2)


def slot_chunks(width):
    size = min(width, 768)
    while width % size:
        size //= 2
    return [slice(k, k + size) for k in range(0, width, size)]


def slot_of(rows, starts):
    blocks = rows // BLOCK
    latest = jnp.max(jnp.where(starts <= blocks, starts, -1), axis=0, keepdims=True)
    return jnp.where(latest >= 0, latest, jnp.max(starts))


def own_rows(slot, first, size, rank):
    index = first // rank + lax.broadcasted_iota(jnp.int32, (size // rank, rank, 1), 0)
    return index == slot[None]


def placing(place, places):
    hit = lax.broadcasted_iota(jnp.int32, (places, place.shape[1]), 0) == place
    return jnp.where(hit, 1.0, 0.0).astype(jnp.bfloat16)


def all_rows(act, tokens):
    return jnp.concatenate([act[k, :tokens, :] for k in range(act.shape[0])], axis=0)


def of_source(sources, width):
    lane = lax.broadcasted_iota(jnp.int32, (sources, 1, width), 2)
    return lane // (width // sources) == lax.broadcasted_iota(
        jnp.int32, (sources, 1, width), 0
    )


def hidden_kernel(act, maps, rows, spots, starts, out):
    sources, share, width = act.shape[0], maps.shape[1], rows.shape[1]
    _, height, places = out.shape
    rank = height // sources
    slot = slot_of(rows[...], starts[...])
    every = all_rows(act, width // sources)
    total = jnp.zeros((rank, width), jnp.float32)
    for part in slot_chunks(maps.shape[0] * share):
        size = part.stop - part.start
        some = maps[part.start // share : part.stop // share].reshape(size, -1)
        each = dot(some, every, ((1,), (1,))).reshape(size // rank, rank, -1)
        total += jnp.sum(jnp.where(own_rows(slot, part.start, size, rank), each, 0.0), axis=0)
    total = jnp.where(of_source(sources, width), total[None], 0.0).reshape(height, width)
    high = total.astype(jnp.bfloat16)
    low = (total - high.astype(jnp.float32)).astype(jnp.bfloat16)
    place = placing(spots[...], places)
    for k, part in enumerate((high, low)):
        out[k] = dot(part, place, ((1,), (1,))).astype(out.dtype)


def down_kernel(act, grad, rows, spots, starts, out, total):
    sources, width = act.shape[0], rows.shape[1]
    rank, places = grad.shape[0] // sources, grad.shape[1]
    step = pl.program_id(0)

    @pl.when(step == 0)
    def _():
        total[...] = jnp.zeros_like(total)

    slot = slot_of(rows[...], starts[...])
    every = all_rows(act, width // sources)
    wide = dot(grad[...], placing(spots[...], places), ((1,), (0,)))
    wide = wide.reshape(sources, rank, width)
    wide = jnp.sum(jnp.where(of_source(sources, width), wide, 0.0), axis=0, keepdims=True)
    for part in slot_chunks(total.shape[0]):
        size = part.stop - part.start
        placed = jnp.where(own_rows(slot, part.start, size, rank), wide, 0.0)
        placed = placed.reshape(size, -1).astype(jnp.bfloat16)
        total[part, :] += dot(placed, every, ((1,), (0,)))

    @pl.when(step == pl.num_programs(0) - 1)
    def _():
        out[...] = (adapter_scale * total[...]).astype(out.dtype)


def feature_calls(received, tokens, share, rank, places, starts):
    devices, packed, features = received.shape
    width = devices * share
    sources = 4
    grid = (devices // sources,)
    act = pl.BlockSpec((sources, packed, features), lambda j: (j, 0, 0))
    maps = pl.BlockSpec((devices, share, features), lambda j: (0, tokens // share, 0))
    rows = pl.BlockSpec((1, sources * tokens), lambda j: (0, j))
    begin = pl.BlockSpec((starts, 1), lambda j: (0, 0))
    placed = pl.BlockSpec((sources * rank, places), lambda j: (j, 0))
    cost = pl.CostEstimate(
        flops=2 * devices * tokens * width * features,
        bytes_accessed=2 * devices * tokens * features,
        transcendentals=0,
    )
    params = pltpu.CompilerParams(vmem_limit_bytes=VMEM)
    hidden = pl.pallas_call(
        hidden_kernel,
        grid=grid,
        in_specs=[act, maps, rows, rows, begin],
        out_specs=pl.BlockSpec((2, sources * rank, places), lambda j: (0, j, 0)),
        out_shape=jax.ShapeDtypeStruct((2, devices * rank, places), received.dtype),
        cost_estimate=cost,
        compiler_params=params,
    )
    down = pl.pallas_call(
        down_kernel,
        grid=grid,
        in_specs=[act, placed, rows, rows, begin],
        out_specs=pl.BlockSpec((width, features), lambda j: (0, 0)),
        out_shape=jax.ShapeDtypeStruct((width, features), jnp.bfloat16),
        scratch_shapes=[pltpu.VMEM((width, features), jnp.float32)],
        cost_estimate=cost,
        compiler_params=params,
    )
    return hidden, down


def local(
    activations,
    cotangent,
    token_layout_row,
    tenant_first_row,
    frozen_value_weight,
    adapter_down_maps,
    adapter_up_maps,
):
    devices = lax.axis_size("blk")
    device = lax.axis_index("blk")
    tokens = activations.shape[0]
    resident, rank, width = adapter_down_maps.shape
    out_width = cotangent.shape[1]
    features = width // devices
    share = resident * rank
    resident_rows = resident * BLOCK
    cap = resident_rows // devices
    start_ids = tenant_first_row // BLOCK

    column = weight_column(frozen_value_weight)

    first_block = device * resident
    block_numbers = first_block + jnp.arange(resident, dtype=jnp.int32)
    begin = starts_of(block_numbers, start_ids)
    is_local = (begin >= first_block) & (begin <= block_numbers)
    home_slot = jnp.clip(begin - first_block, 0, resident - 1)
    last_map = jnp.concatenate(
        [
            lax.dynamic_index_in_dim(maps, home_slot[resident - 1], 0, keepdims=False)
            for maps in (adapter_down_maps, adapter_up_maps)
        ],
        axis=1,
    )
    carried = jnp.zeros_like(last_map)
    for step in range(1, HOPS + 1):
        home = (device - step) % devices
        carried = jnp.where(begin[0] // resident == home, moved(last_map, step), carried)

    def of_blocks(maps, own):
        blocks = []
        for b in range(resident):
            chosen = own
            for k in range(b + 1):
                chosen = jnp.where(is_local[b] & (home_slot[b] == k), maps[k], chosen)
            blocks.append(chosen)
        return jnp.concatenate(blocks, axis=0)

    down_blocks = of_blocks(adapter_down_maps, carried[:, :width])
    up_blocks = of_blocks(adapter_up_maps, carried[:, width:])

    sent_rows = pack_rows(token_layout_row, cotangent, devices, cap, features)
    got_rows = lax.all_to_all(sent_rows, "blk", split_axis=0, concat_axis=0)
    recv_cot = [
        got_rows[:, k * cap : (k + 1) * cap].reshape(resident_rows, features)
        for k in range(out_width // features)
    ]
    per_digit = -(-tokens // features)
    digits = got_rows[:, share : share + 5 * per_digit]
    digits = digits.reshape(devices, 5, per_digit * features)[:, :, :tokens]
    rows_all, place_all = from_digits(digits)

    flat_maps = adapter_down_maps.reshape(share, width)
    received = after(pack_features(activations, flat_maps, devices), got_rows)
    received = lax.all_to_all(received, "blk", split_axis=0, concat_axis=0)

    spots = device * cap + jnp.arange(cap, dtype=jnp.int32)
    hit = place_all[:, None, :] == spots[None, :, None]
    row_in = rows_all - device * resident_rows + 1
    row_in = jnp.sum(jnp.where(hit, row_in[:, None, :], 0), axis=2).reshape(-1) - 1
    arrange = row_in[:, None] == jnp.arange(resident_rows, dtype=jnp.int32)[None, :]
    arrange = arrange.astype(jnp.bfloat16)
    in_block = row_in[:, None] // BLOCK == jnp.arange(share, dtype=jnp.int32)[None, :] // rank

    grad_in = sum(
        dot(part, up_blocks[:, k * features : (k + 1) * features], ((1,), (1,)))
        for k, part in enumerate(recv_cot)
    )
    grad_in = jnp.where(in_block, grad_in, 0.0).astype(jnp.bfloat16)
    grad_in = sum(grad_in[:, b * rank : (b + 1) * rank] for b in range(resident))
    grad_sent = grad_in.reshape(devices, cap, rank).transpose(1, 0, 2).reshape(cap, -1)

    rows_all, place_all = rows_all.reshape(1, -1), place_all.reshape(1, -1)

    cot_rows = jnp.concatenate(
        [dot(arrange, part, ((0,), (0,))).astype(jnp.bfloat16) for part in recv_cot], axis=1
    )
    grad_rows = dot(arrange, grad_in, ((0,), (0,))).astype(jnp.bfloat16)

    in_rows = jnp.arange(resident_rows, dtype=jnp.int32)[:, None] // BLOCK
    in_rows = in_rows == jnp.arange(share, dtype=jnp.int32)[None, :] // rank
    grad_wide = jnp.where(in_rows, jnp.concatenate([grad_rows] * resident, axis=1), 0)
    group = lax.axis_index("groups")
    firsts = [(device % 4) ^ k for k in range(4)]
    pieces = weight_quarters(column)
    tiled = column.shape[1] % LANES == 0
    if tiled:
        out = None
        for quarter in (0, 1):
            out, token = write_quarter(
                pieces(quarter), firsts[quarter], group, cot_rows, grad_wide, down_blocks, out
            )
        place_all = after(place_all, token)

    starts = start_ids[:, None]
    hidden_call, down_call = feature_calls(
        received, tokens, share, rank, resident_rows, starts.shape[0]
    )
    shares = hidden_call(received, received, rows_all, place_all, starts)

    shares = shares.reshape(-1, resident_rows).T.reshape(devices, cap, -1)
    copies = jnp.broadcast_to(grad_sent[None], (devices,) + grad_sent.shape)
    small = jnp.concatenate([copies, shares], axis=2)
    small = lax.all_to_all(small, "blk", split_axis=0, concat_axis=0)
    each = devices * rank
    grad_all = small[:, :, :each].reshape(resident_rows, each).T
    hidden = jnp.sum(small[:, :, each:].astype(jnp.float32), axis=0)
    hidden = (hidden[:, :each] + hidden[:, each:]).astype(jnp.bfloat16)
    hidden = hidden.reshape(cap, devices, rank).transpose(1, 0, 2).reshape(-1, rank)

    down_f = down_call(received, grad_all, rows_all, place_all, starts)
    down_home = lax.all_to_all(down_f, "blk", split_axis=0, concat_axis=1, tiled=True)
    down_map_gradient = down_home.astype(jnp.float32).reshape(resident, rank, width)

    wide = jnp.where(in_block, jnp.concatenate([hidden] * resident, axis=1), 0)
    up_all = [dot(wide, part, ((0,), (0,))) for part in recv_cot]
    up_all = jnp.concatenate(up_all, axis=1).reshape(resident, rank, out_width)
    up_parts = [up_all[b] for b in range(resident)]

    tail = sum(jnp.where(is_local[b], 0.0, up_parts[b]) for b in range(resident))
    far = jnp.zeros_like(tail)
    for step in range(1, HOPS + 1):
        other = (device + step) % devices * resident
        theirs = starts_of(other[None], start_ids)[0]
        far = far + jnp.where(theirs // resident == device, moved(tail, -step), 0.0)
    up_grads = []
    for k in range(resident):
        total = jnp.where(begin[resident - 1] == first_block + k, far, 0.0)
        for b in range(resident):
            total = total + jnp.where(is_local[b] & (home_slot[b] == k), up_parts[b], 0.0)
        up_grads.append(adapter_scale * total)
    up_map_gradient = jnp.stack(up_grads)

    if tiled:
        late = after(grad_wide, down_f)
        for quarter in (2, 3):
            out, _ = write_quarter(
                pieces(quarter, shares), firsts[quarter], group, cot_rows, late, down_blocks, out
            )
    else:
        weight = together([pieces(k, shares) for k in range(4)], firsts, group)
        lora = adapter_scale * dot(grad_wide, down_blocks, ((1,), (0,)))
        out = dot(cot_rows, weight, ((1,), (1,)))
        out = (out + lora.astype(jnp.bfloat16).astype(jnp.float32)).astype(jnp.bfloat16)
    return (out, down_map_gradient, up_map_gradient)


def solution(mesh):
    return jax.shard_map(
        local,
        mesh=mesh,
        in_specs=(
            P(("groups", "blk"), None),
            P(("groups", "blk"), None),
            P(("groups", "blk")),
            P("groups"),
            P("blk", None),
            P(("groups", "blk"), None, None),
            P(("groups", "blk"), None, None),
        ),
        out_specs=(
            P(("groups", "blk"), None),
            P(("groups", "blk"), None, None),
            P(("groups", "blk"), None, None),
        ),
        check_vma=False,
    )
```

```python
import functools

import jax
import jax.numpy as jnp
from jax import lax
from jax.experimental import pallas as pl
from jax.experimental.pallas import tpu as pltpu
from jax.sharding import PartitionSpec as P

BLOCK = 128
HOPS = 4
LANES = 128
DIGIT = 64
VMEM = 56 << 20

adapter_scale = 2.0


def moved(value, steps):
    count = lax.axis_size("blk")
    return lax.ppermute(value, "blk", [(i, (i + steps) % count) for i in range(count)])


def to_all(value):
    count = lax.axis_size("blk")
    copies = jnp.broadcast_to(value[None], (count,) + value.shape)
    return lax.all_to_all(copies, "blk", split_axis=0, concat_axis=0)


def after(value, *others):
    anywhere = pl.BlockSpec(memory_space=pl.ANY)
    return pl.pallas_call(
        lambda *refs: None,
        in_specs=[anywhere] * (1 + len(others)),
        out_specs=anywhere,
        out_shape=jax.ShapeDtypeStruct(value.shape, value.dtype),
        input_output_aliases={0: 0},
        cost_estimate=pl.CostEstimate(flops=0, bytes_accessed=0, transcendentals=0),
        compiler_params=pltpu.CompilerParams(vmem_limit_bytes=VMEM),
    )(value, *others)


def dot(a, b, dims):
    return lax.dot_general(a, b, (dims, ((), ())), preferred_element_type=jnp.float32)


def starts_of(blocks, start_ids):
    latest = jnp.max(
        jnp.where(start_ids[None, :] <= blocks[:, None], start_ids[None, :], -1), axis=1
    )
    return jnp.where(latest >= 0, latest, jnp.max(start_ids))


def as_digits(rows, places):
    return (
        rows % DIGIT,
        rows // DIGIT % DIGIT,
        rows // (DIGIT * DIGIT),
        places % DIGIT,
        places // DIGIT,
    )


def from_digits(digits):
    low, middle, high, place, place_high = [digits[:, k].astype(jnp.int32) for k in range(5)]
    return (high * DIGIT + middle) * DIGIT + low, place_high * DIGIT + place


def weight_column(weight):
    count = lax.axis_size("blk")
    half = weight.shape[0] // 2
    lines = [list(range(k, count, 4)) for k in range(4)]
    mine = lax.dynamic_slice_in_dim(weight, lax.axis_index("groups") * half, half, 0)
    return lax.all_gather(mine, "blk", axis_index_groups=lines)


CHUNKS = 2


def weight_quarters(column):
    count = lax.axis_size("blk")
    size = column.shape[1] // CHUNKS

    def over(piece, bit):
        return lax.ppermute(piece, "blk", [(i, i ^ bit) for i in range(count)])

    def groups(piece):
        return lax.ppermute(piece, "groups", [(0, 1), (1, 0)])

    mine = [column[:, k * size : (k + 1) * size] for k in range(CHUNKS)]
    quarters = []
    for side in (mine, [over(piece, 2) for piece in mine]):
        both = side + [groups(piece) for piece in side]
        quarters += [both, [over(piece, 1) for piece in both]]
    return quarters


def quarter_kernel(where, cot, grad, down, *rest):
    pieces = rest[: 2 * CHUNKS]
    out, token = rest[-2:]
    token[...] = jnp.zeros_like(token)
    lora = adapter_scale * dot(grad[...], down[...], ((1,), (0,)))
    lora = lora.astype(jnp.bfloat16).astype(jnp.float32)

    def product(group):
        order = pieces[group * CHUNKS :] + pieces[: group * CHUNKS]
        weight = jnp.concatenate([piece[0] for piece in order], axis=0)
        frozen = dot(cot[...], weight, ((1,), (1,)))
        out[...] = (frozen + lora).astype(jnp.bfloat16)

    for group in range(2):
        pl.when(where[1] == group)(functools.partial(product, group))


def write_quarter(quarter, first, group, cot, grad, down, out=None):
    rows, depth = cot.shape
    width = down.shape[1]
    shards, part, _ = quarter[0].shape
    stripe = part * len(quarter)
    where = jnp.stack([first, group]).astype(jnp.int32)
    specs = [
        pl.BlockSpec((rows, depth), lambda j, where: (0, 0)),
        pl.BlockSpec(grad.shape, lambda j, where: (0, 0)),
        pl.BlockSpec((down.shape[0], stripe), lambda j, where: (0, 4 * j + where[0])),
    ] + [pl.BlockSpec((1, part, depth), lambda j, where: (j, 0, 0)) for _ in quarter]
    args = [where, cot, grad, down] + quarter
    alias = {}
    if out is not None:
        specs.append(pl.BlockSpec(memory_space=pl.ANY))
        args.append(out)
        alias = {len(args) - 1: 0}
    return pl.pallas_call(
        quarter_kernel,
        grid_spec=pltpu.PrefetchScalarGridSpec(
            num_scalar_prefetch=1,
            grid=(shards,),
            in_specs=specs,
            out_specs=[
                pl.BlockSpec((rows, stripe), lambda j, where: (0, 4 * j + where[0])),
                pl.BlockSpec((8, LANES), lambda j, where: (0, 0)),
            ],
        ),
        out_shape=[
            jax.ShapeDtypeStruct((rows, width), jnp.bfloat16),
            jax.ShapeDtypeStruct((8, LANES), jnp.float32),
        ],
        input_output_aliases=alias,
        cost_estimate=pl.CostEstimate(
            flops=2 * rows * depth * stripe * shards,
            bytes_accessed=2 * (depth + rows) * stripe * shards,
            transcendentals=0,
        ),
        compiler_params=pltpu.CompilerParams(vmem_limit_bytes=VMEM),
    )(*args)


def together(pieces, firsts, group):
    shards, part, depth = pieces[0][0].shape
    weight = jnp.zeros((shards, 4, 2, CHUNKS, part, depth), jnp.bfloat16)
    for quarter, first in zip(pieces, firsts):
        for k, piece in enumerate(quarter):
            half = group if k < CHUNKS else 1 - group
            place = (0, first, half, k % CHUNKS, 0, 0)
            weight = lax.dynamic_update_slice(weight, piece[:, None, None, None], place)
    return weight.reshape(-1, depth)


def rows_kernel(rows, cot, out, place):
    devices, packed, features = out.shape
    shared = packed - 16
    folds = cot.shape[1] // features
    cap = shared // folds
    target = rows[...] // (cap * devices)
    to = lax.broadcasted_iota(jnp.int32, (16, features), 0) == target
    first = lax.broadcasted_iota(jnp.int32, (features, features), 0)
    later = lax.broadcasted_iota(jnp.int32, (features, features), 1)
    earlier = jnp.where(first < later, 1.0, 0.0).astype(jnp.bfloat16)
    ahead = dot(jnp.where(to, 1.0, 0.0).astype(jnp.bfloat16), earlier, ((1,), (0,)))
    ahead = jnp.sum(jnp.where(to, ahead, 0.0), axis=0, keepdims=True)
    place[...] = target * cap + ahead.astype(jnp.int32)
    which = lax.broadcasted_iota(jnp.int32, (16, features), 0)
    digits = jnp.zeros((16, features), jnp.int32)
    for k, digit in enumerate(as_digits(rows[...], place[...])):
        digits = jnp.where(which == k, digit, digits)
    digits = digits.astype(jnp.float32).astype(out.dtype)
    send = placing(place[:, : cot.shape[0]], cap * devices)
    for f in range(folds):
        sent = dot(send, cot[:, f * features : (f + 1) * features], ((1,), (0,)))
        for k in range(devices):
            some = sent[k * cap : (k + 1) * cap].astype(out.dtype)
            out[k, f * cap : (f + 1) * cap, :] = some
    for k in range(devices):
        out[k, shared:, :] = digits


def pack_rows(rows, cot, devices, cap, features):
    tokens = rows.shape[0]
    folds = cot.shape[1] // features
    if features % LANES == 0 and cap % 8 == 0 and features >= tokens and devices <= 16:
        padding = jnp.full((features - tokens,), 16 * cap * devices, jnp.int32)
        return pl.pallas_call(
            rows_kernel,
            out_shape=jax.ShapeDtypeStruct((devices, folds * cap + 16, features), cot.dtype),
            scratch_shapes=[pltpu.VMEM((1, features), jnp.int32)],
            cost_estimate=pl.CostEstimate(
                flops=2 * devices * cap * tokens * cot.shape[1],
                bytes_accessed=6 * cot.size,
                transcendentals=0,
            ),
            compiler_params=pltpu.CompilerParams(vmem_limit_bytes=VMEM),
        )(jnp.concatenate([rows, padding])[None], cot)
    target = rows // (cap * devices)
    order = jnp.arange(tokens, dtype=jnp.int32)
    before = (target[:, None] == target[None, :]) & (order[None, :] < order[:, None])
    place = target * cap + jnp.sum(before.astype(jnp.int32), axis=1)
    send = jnp.arange(cap * devices, dtype=jnp.int32)[:, None] == place[None, :]
    sent = dot(send.astype(jnp.bfloat16), cot, ((1,), (0,))).astype(jnp.bfloat16)
    sent = sent.reshape(devices, cap, cot.shape[1])
    digits = jnp.stack(as_digits(rows, place)).astype(jnp.bfloat16)
    digits = jnp.pad(digits, ((0, 0), (0, -tokens % features))).reshape(-1, features)
    digits = jnp.pad(digits, ((0, -digits.shape[0] % 16), (0, 0)))
    parts = [sent[:, :, k : k + features] for k in range(0, cot.shape[1], features)]
    parts += [jnp.broadcast_to(digits[None], (devices,) + digits.shape)]
    return jnp.concatenate(parts, axis=1)


def features_kernel(act, maps, out):
    targets, _, features = out.shape
    tokens = act.shape[0]
    for k in range(targets):
        part = slice(k * features, (k + 1) * features)
        out[k, :tokens, :] = act[:, part]
        out[k, tokens:, :] = maps[:, part]


def pack_features(act, maps, devices):
    tokens, width = act.shape
    features = width // devices
    shared = maps.shape[0]
    targets = 4
    if features % LANES == 0:
        return pl.pallas_call(
            features_kernel,
            grid=(devices // targets,),
            in_specs=[
                pl.BlockSpec((tokens, targets * features), lambda j: (0, j)),
                pl.BlockSpec((shared, targets * features), lambda j: (0, j)),
            ],
            out_specs=pl.BlockSpec((targets, tokens + shared, features), lambda j: (j, 0, 0)),
            out_shape=jax.ShapeDtypeStruct((devices, tokens + shared, features), act.dtype),
            cost_estimate=pl.CostEstimate(
                flops=0, bytes_accessed=4 * (tokens + shared) * width, transcendentals=0
            ),
            compiler_params=pltpu.CompilerParams(vmem_limit_bytes=VMEM),
        )(act, maps)
    both = jnp.concatenate([act, maps], axis=0)
    return both.reshape(tokens + shared, devices, features).transpose(1, 0, 2)


def slot_chunks(width):
    size = min(width, 768)
    while width % size:
        size //= 2
    return [slice(k, k + size) for k in range(0, width, size)]


def slot_of(rows, starts):
    blocks = rows // BLOCK
    latest = jnp.max(jnp.where(starts <= blocks, starts, -1), axis=0, keepdims=True)
    return jnp.where(latest >= 0, latest, jnp.max(starts))


def own_rows(slot, first, size, rank):
    index = first // rank + lax.broadcasted_iota(jnp.int32, (size // rank, rank, 1), 0)
    return index == slot[None]


def placing(place, places):
    hit = lax.broadcasted_iota(jnp.int32, (places, place.shape[1]), 0) == place
    return jnp.where(hit, 1.0, 0.0).astype(jnp.bfloat16)


def all_rows(act, tokens):
    return jnp.concatenate([act[k, :tokens, :] for k in range(act.shape[0])], axis=0)


def of_source(sources, width):
    lane = lax.broadcasted_iota(jnp.int32, (sources, 1, width), 2)
    return lane // (width // sources) == lax.broadcasted_iota(
        jnp.int32, (sources, 1, width), 0
    )


def hidden_kernel(act, maps, rows, spots, starts, out):
    sources, share, width = act.shape[0], maps.shape[1], rows.shape[1]
    _, height, places = out.shape
    rank = height // sources
    slot = slot_of(rows[...], starts[...])
    every = all_rows(act, width // sources)
    total = jnp.zeros((rank, width), jnp.float32)
    for part in slot_chunks(maps.shape[0] * share):
        size = part.stop - part.start
        some = maps[part.start // share : part.stop // share].reshape(size, -1)
        each = dot(some, every, ((1,), (1,))).reshape(size // rank, rank, -1)
        total += jnp.sum(jnp.where(own_rows(slot, part.start, size, rank), each, 0.0), axis=0)
    total = jnp.where(of_source(sources, width), total[None], 0.0).reshape(height, width)
    high = total.astype(jnp.bfloat16)
    low = (total - high.astype(jnp.float32)).astype(jnp.bfloat16)
    place = placing(spots[...], places)
    for k, part in enumerate((high, low)):
        out[k] = dot(part, place, ((1,), (1,))).astype(out.dtype)


def down_kernel(act, grad, rows, spots, starts, out, total):
    sources, width = act.shape[0], rows.shape[1]
    rank, places = grad.shape[0] // sources, grad.shape[1]
    step = pl.program_id(0)

    @pl.when(step == 0)
    def _():
        total[...] = jnp.zeros_like(total)

    slot = slot_of(rows[...], starts[...])
    every = all_rows(act, width // sources)
    wide = dot(grad[...], placing(spots[...], places), ((1,), (0,)))
    wide = wide.reshape(sources, rank, width)
    wide = jnp.sum(jnp.where(of_source(sources, width), wide, 0.0), axis=0, keepdims=True)
    for part in slot_chunks(total.shape[0]):
        size = part.stop - part.start
        placed = jnp.where(own_rows(slot, part.start, size, rank), wide, 0.0)
        placed = placed.reshape(size, -1).astype(jnp.bfloat16)
        total[part, :] += dot(placed, every, ((1,), (0,)))

    @pl.when(step == pl.num_programs(0) - 1)
    def _():
        out[...] = (adapter_scale * total[...]).astype(out.dtype)


def feature_calls(received, tokens, share, rank, places, starts):
    devices, packed, features = received.shape
    width = devices * share
    sources = 4
    grid = (devices // sources,)
    act = pl.BlockSpec((sources, packed, features), lambda j: (j, 0, 0))
    maps = pl.BlockSpec((devices, share, features), lambda j: (0, tokens // share, 0))
    rows = pl.BlockSpec((1, sources * tokens), lambda j: (0, j))
    begin = pl.BlockSpec((starts, 1), lambda j: (0, 0))
    placed = pl.BlockSpec((sources * rank, places), lambda j: (j, 0))
    cost = pl.CostEstimate(
        flops=2 * devices * tokens * width * features,
        bytes_accessed=2 * devices * tokens * features,
        transcendentals=0,
    )
    params = pltpu.CompilerParams(vmem_limit_bytes=VMEM)
    hidden = pl.pallas_call(
        hidden_kernel,
        grid=grid,
        in_specs=[act, maps, rows, rows, begin],
        out_specs=pl.BlockSpec((2, sources * rank, places), lambda j: (0, j, 0)),
        out_shape=jax.ShapeDtypeStruct((2, devices * rank, places), received.dtype),
        cost_estimate=cost,
        compiler_params=params,
    )
    down = pl.pallas_call(
        down_kernel,
        grid=grid,
        in_specs=[act, placed, rows, rows, begin],
        out_specs=pl.BlockSpec((width, features), lambda j: (0, 0)),
        out_shape=jax.ShapeDtypeStruct((width, features), jnp.bfloat16),
        scratch_shapes=[pltpu.VMEM((width, features), jnp.float32)],
        cost_estimate=cost,
        compiler_params=params,
    )
    return hidden, down


def local(
    activations,
    cotangent,
    token_layout_row,
    tenant_first_row,
    frozen_value_weight,
    adapter_down_maps,
    adapter_up_maps,
):
    devices = lax.axis_size("blk")
    device = lax.axis_index("blk")
    tokens = activations.shape[0]
    resident, rank, width = adapter_down_maps.shape
    out_width = cotangent.shape[1]
    features = width // devices
    share = resident * rank
    resident_rows = resident * BLOCK
    cap = resident_rows // devices
    start_ids = tenant_first_row // BLOCK

    quarters = weight_quarters(weight_column(frozen_value_weight))

    first_block = device * resident
    block_numbers = first_block + jnp.arange(resident, dtype=jnp.int32)
    begin = starts_of(block_numbers, start_ids)
    is_local = (begin >= first_block) & (begin <= block_numbers)
    home_slot = jnp.clip(begin - first_block, 0, resident - 1)
    last_map = jnp.concatenate(
        [
            lax.dynamic_index_in_dim(maps, home_slot[resident - 1], 0, keepdims=False)
            for maps in (adapter_down_maps, adapter_up_maps)
        ],
        axis=1,
    )
    carried = jnp.zeros_like(last_map)
    for step in range(1, HOPS + 1):
        home = (device - step) % devices
        carried = jnp.where(begin[0] // resident == home, moved(last_map, step), carried)

    def of_blocks(maps, own):
        blocks = []
        for b in range(resident):
            chosen = own
            for k in range(b + 1):
                chosen = jnp.where(is_local[b] & (home_slot[b] == k), maps[k], chosen)
            blocks.append(chosen)
        return jnp.concatenate(blocks, axis=0)

    down_blocks = of_blocks(adapter_down_maps, carried[:, :width])
    up_blocks = of_blocks(adapter_up_maps, carried[:, width:])

    sent_rows = pack_rows(token_layout_row, cotangent, devices, cap, features)
    own, _, across, _ = quarters
    sent_rows = after(sent_rows, carried, own[CHUNKS], across[0])
    got_rows = lax.all_to_all(sent_rows, "blk", split_axis=0, concat_axis=0)
    recv_cot = [
        got_rows[:, k * cap : (k + 1) * cap].reshape(resident_rows, features)
        for k in range(out_width // features)
    ]
    per_digit = -(-tokens // features)
    digits = got_rows[:, share : share + 5 * per_digit]
    digits = digits.reshape(devices, 5, per_digit * features)[:, :, :tokens]
    rows_all, place_all = from_digits(digits)

    flat_maps = adapter_down_maps.reshape(share, width)
    received = pack_features(activations, flat_maps, devices)
    received = after(received, got_rows, own[-1], across[CHUNKS - 1])
    received = lax.all_to_all(received, "blk", split_axis=0, concat_axis=0)

    spots = device * cap + jnp.arange(cap, dtype=jnp.int32)
    hit = place_all[:, None, :] == spots[None, :, None]
    row_in = rows_all - device * resident_rows + 1
    row_in = jnp.sum(jnp.where(hit, row_in[:, None, :], 0), axis=2).reshape(-1) - 1
    arrange = row_in[:, None] == jnp.arange(resident_rows, dtype=jnp.int32)[None, :]
    arrange = arrange.astype(jnp.bfloat16)
    in_block = row_in[:, None] // BLOCK == jnp.arange(share, dtype=jnp.int32)[None, :] // rank

    grad_in = sum(
        dot(part, up_blocks[:, k * features : (k + 1) * features], ((1,), (1,)))
        for k, part in enumerate(recv_cot)
    )
    grad_in = jnp.where(in_block, grad_in, 0.0).astype(jnp.bfloat16)
    grad_in = sum(grad_in[:, b * rank : (b + 1) * rank] for b in range(resident))
    grad_sent = grad_in.reshape(devices, cap, rank).transpose(1, 0, 2).reshape(cap, -1)

    rows_all, place_all = rows_all.reshape(1, -1), place_all.reshape(1, -1)

    cot_rows = jnp.concatenate(
        [dot(arrange, part, ((0,), (0,))).astype(jnp.bfloat16) for part in recv_cot], axis=1
    )
    grad_rows = dot(arrange, grad_in, ((0,), (0,))).astype(jnp.bfloat16)

    in_rows = jnp.arange(resident_rows, dtype=jnp.int32)[:, None] // BLOCK
    in_rows = in_rows == jnp.arange(share, dtype=jnp.int32)[None, :] // rank
    grad_wide = jnp.where(in_rows, jnp.concatenate([grad_rows] * resident, axis=1), 0)
    group = lax.axis_index("groups")
    firsts = [(device % 4) ^ k for k in range(4)]
    if own[0].shape[1] % LANES == 0:
        out = None
        for quarter, first in zip(quarters, firsts):
            out, token = write_quarter(
                quarter, first, group, cot_rows, grad_wide, down_blocks, out
            )
        place_all = after(place_all, token)
    else:
        weight = together(quarters, firsts, group)
        lora = adapter_scale * dot(grad_wide, down_blocks, ((1,), (0,)))
        out = dot(cot_rows, weight, ((1,), (1,)))
        out = (out + lora.astype(jnp.bfloat16).astype(jnp.float32)).astype(jnp.bfloat16)

    starts = start_ids[:, None]
    hidden_call, down_call = feature_calls(
        received, tokens, share, rank, resident_rows, starts.shape[0]
    )
    shares = hidden_call(received, received, rows_all, place_all, starts)

    shares = shares.reshape(-1, resident_rows).T.reshape(devices, cap, -1)
    copies = jnp.broadcast_to(grad_sent[None], (devices,) + grad_sent.shape)
    small = jnp.concatenate([copies, shares], axis=2)
    small = lax.all_to_all(small, "blk", split_axis=0, concat_axis=0)
    each = devices * rank
    grad_all = small[:, :, :each].reshape(resident_rows, each).T
    hidden = jnp.sum(small[:, :, each:].astype(jnp.float32), axis=0)
    hidden = (hidden[:, :each] + hidden[:, each:]).astype(jnp.bfloat16)
    hidden = hidden.reshape(cap, devices, rank).transpose(1, 0, 2).reshape(-1, rank)

    down_f = down_call(received, grad_all, rows_all, place_all, starts)
    down_home = lax.all_to_all(down_f, "blk", split_axis=0, concat_axis=1, tiled=True)
    down_map_gradient = down_home.astype(jnp.float32).reshape(resident, rank, width)

    wide = jnp.where(in_block, jnp.concatenate([hidden] * resident, axis=1), 0)
    up_all = [dot(wide, part, ((0,), (0,))) for part in recv_cot]
    up_all = jnp.concatenate(up_all, axis=1).reshape(resident, rank, out_width)
    up_parts = [up_all[b] for b in range(resident)]

    tail = sum(jnp.where(is_local[b], 0.0, up_parts[b]) for b in range(resident))
    far = jnp.zeros_like(tail)
    for step in range(1, HOPS + 1):
        other = (device + step) % devices * resident
        theirs = starts_of(other[None], start_ids)[0]
        far = far + jnp.where(theirs // resident == device, moved(tail, -step), 0.0)
    up_grads = []
    for k in range(resident):
        total = jnp.where(begin[resident - 1] == first_block + k, far, 0.0)
        for b in range(resident):
            total = total + jnp.where(is_local[b] & (home_slot[b] == k), up_parts[b], 0.0)
        up_grads.append(adapter_scale * total)
    up_map_gradient = jnp.stack(up_grads)

    return (out, down_map_gradient, up_map_gradient)


def solution(mesh):
    return jax.shard_map(
        local,
        mesh=mesh,
        in_specs=(
            P(("groups", "blk"), None),
            P(("groups", "blk"), None),
            P(("groups", "blk")),
            P("groups"),
            P("blk", None),
            P(("groups", "blk"), None, None),
            P(("groups", "blk"), None, None),
        ),
        out_specs=(
            P(("groups", "blk"), None),
            P(("groups", "blk"), None, None),
            P(("groups", "blk"), None, None),
        ),
        check_vma=False,
    )
```

```python
import functools

import jax
import jax.numpy as jnp
from jax import lax
from jax.experimental import pallas as pl
from jax.experimental.pallas import tpu as pltpu
from jax.sharding import PartitionSpec as P

BLOCK = 128
HOPS = 4
LANES = 128
DIGIT = 64
VMEM = 56 << 20

adapter_scale = 2.0


def moved(value, steps):
    count = lax.axis_size("blk")
    return lax.ppermute(value, "blk", [(i, (i + steps) % count) for i in range(count)])


def to_all(value):
    count = lax.axis_size("blk")
    copies = jnp.broadcast_to(value[None], (count,) + value.shape)
    return lax.all_to_all(copies, "blk", split_axis=0, concat_axis=0)


def after(value, *others):
    anywhere = pl.BlockSpec(memory_space=pl.ANY)
    return pl.pallas_call(
        lambda *refs: None,
        in_specs=[anywhere] * (1 + len(others)),
        out_specs=anywhere,
        out_shape=jax.ShapeDtypeStruct(value.shape, value.dtype),
        input_output_aliases={0: 0},
        cost_estimate=pl.CostEstimate(flops=0, bytes_accessed=0, transcendentals=0),
        compiler_params=pltpu.CompilerParams(vmem_limit_bytes=VMEM),
    )(value, *others)


def dot(a, b, dims):
    return lax.dot_general(a, b, (dims, ((), ())), preferred_element_type=jnp.float32)


def starts_of(blocks, start_ids):
    latest = jnp.max(
        jnp.where(start_ids[None, :] <= blocks[:, None], start_ids[None, :], -1), axis=1
    )
    return jnp.where(latest >= 0, latest, jnp.max(start_ids))


def as_digits(rows, places):
    return (
        rows % DIGIT,
        rows // DIGIT % DIGIT,
        rows // (DIGIT * DIGIT),
        places % DIGIT,
        places // DIGIT,
    )


def from_digits(digits):
    low, middle, high, place, place_high = [digits[:, k].astype(jnp.int32) for k in range(5)]
    return (high * DIGIT + middle) * DIGIT + low, place_high * DIGIT + place


CHUNKS = 2


def near_lines(count):
    return count // 4 <= 4


def line_order():
    count = lax.axis_size("blk")
    shards = jnp.arange(count // 4, dtype=jnp.int32)
    if near_lines(count):
        return (lax.axis_index("blk") // 4 - shards) % (count // 4)
    return shards


def weight_pieces(weight):
    count = lax.axis_size("blk")
    half = weight.shape[0] // 2
    size = half // CHUNKS
    first = lax.axis_index("groups") * half

    def over(piece, bit):
        return lax.ppermute(piece, "blk", [(i, i ^ bit) for i in range(count)])

    def groups(piece):
        return lax.ppermute(piece, "groups", [(0, 1), (1, 0)])

    def column(chunk):
        mine = lax.dynamic_slice_in_dim(weight, first + chunk * size, size, 0)
        if near_lines(count):
            return jnp.stack([mine] + [moved(mine, 4 * k) for k in range(1, count // 4)])
        lines = [list(range(k, count, 4)) for k in range(4)]
        return lax.all_gather(mine, "blk", axis_index_groups=lines)

    columns = [column(k) for k in range(CHUNKS)]
    pieces = []
    for mine in (columns, [over(column, 2) for column in columns]):
        both = mine + [groups(piece) for piece in mine]
        pieces += [both, [over(piece, 1) for piece in both]]
    return pieces


def quarter_kernel(where, cot, grad, down, *rest):
    pieces = rest[: 2 * CHUNKS]
    out, token = rest[-2:]
    token[...] = jnp.zeros_like(token)
    rank = grad.shape[1]
    lora = [
        adapter_scale
        * dot(
            grad[b * BLOCK : (b + 1) * BLOCK, :],
            down[b * rank : (b + 1) * rank, :],
            ((1,), (0,)),
        )
        for b in range(cot.shape[0] // BLOCK)
    ]
    lora = jnp.concatenate(lora, axis=0).astype(jnp.bfloat16).astype(jnp.float32)

    def product(group):
        order = pieces[group * CHUNKS :] + pieces[: group * CHUNKS]
        weight = jnp.concatenate([piece[0] for piece in order], axis=0)
        frozen = dot(cot[...], weight, ((1,), (1,)))
        out[...] = (frozen + lora).astype(jnp.bfloat16)

    for group in range(2):
        pl.when(where[where.shape[0] - 1] == group)(functools.partial(product, group))


def write_quarter(quarter, first, group, cot, grad, down, out=None):
    rows, depth = cot.shape
    width = down.shape[1]
    shards, part, _ = quarter[0].shape
    stripe = part * len(quarter)
    where = jnp.concatenate([4 * line_order() + first, group[None]]).astype(jnp.int32)
    specs = [
        pl.BlockSpec((rows, depth), lambda j, where: (0, 0)),
        pl.BlockSpec(grad.shape, lambda j, where: (0, 0)),
        pl.BlockSpec((down.shape[0], stripe), lambda j, where: (0, where[j])),
    ] + [pl.BlockSpec((1, part, depth), lambda j, where: (j, 0, 0)) for _ in quarter]
    args = [where, cot, grad, down] + quarter
    alias = {}
    if out is not None:
        specs.append(pl.BlockSpec(memory_space=pl.ANY))
        args.append(out)
        alias = {len(args) - 1: 0}
    return pl.pallas_call(
        quarter_kernel,
        grid_spec=pltpu.PrefetchScalarGridSpec(
            num_scalar_prefetch=1,
            grid=(shards,),
            in_specs=specs,
            out_specs=[
                pl.BlockSpec((rows, stripe), lambda j, where: (0, where[j])),
                pl.BlockSpec((8, LANES), lambda j, where: (0, 0)),
            ],
        ),
        out_shape=[
            jax.ShapeDtypeStruct((rows, width), jnp.bfloat16),
            jax.ShapeDtypeStruct((8, LANES), jnp.float32),
        ],
        input_output_aliases=alias,
        cost_estimate=pl.CostEstimate(
            flops=2 * rows * depth * stripe * shards,
            bytes_accessed=2 * (depth + rows) * stripe * shards,
            transcendentals=0,
        ),
        compiler_params=pltpu.CompilerParams(vmem_limit_bytes=VMEM),
    )(*args)


def together(pieces, firsts, group):
    shards, part, depth = pieces[0][0].shape
    weight = jnp.zeros((shards, 4, 2, CHUNKS, part, depth), jnp.bfloat16)
    order = line_order()
    for quarter, first in zip(pieces, firsts):
        for k, piece in enumerate(quarter):
            half = group if k < CHUNKS else 1 - group
            if not near_lines(4 * shards):
                place = (0, first, half, k % CHUNKS, 0, 0)
                weight = lax.dynamic_update_slice(weight, piece[:, None, None, None], place)
                continue
            for j in range(shards):
                place = (order[j], first, half, k % CHUNKS, 0, 0)
                shard = piece[j][None, None, None, None]
                weight = lax.dynamic_update_slice(weight, shard, place)
    return weight.reshape(-1, depth)


def rows_kernel(rows, cot, out, place):
    devices, packed, features = out.shape
    shared = packed - 16
    folds = cot.shape[1] // features
    cap = shared // folds
    target = rows[...] // (cap * devices)
    to = lax.broadcasted_iota(jnp.int32, (16, features), 0) == target
    first = lax.broadcasted_iota(jnp.int32, (features, features), 0)
    later = lax.broadcasted_iota(jnp.int32, (features, features), 1)
    earlier = jnp.where(first < later, 1.0, 0.0).astype(jnp.bfloat16)
    ahead = dot(jnp.where(to, 1.0, 0.0).astype(jnp.bfloat16), earlier, ((1,), (0,)))
    ahead = jnp.sum(jnp.where(to, ahead, 0.0), axis=0, keepdims=True)
    place[...] = target * cap + ahead.astype(jnp.int32)
    which = lax.broadcasted_iota(jnp.int32, (16, features), 0)
    digits = jnp.zeros((16, features), jnp.int32)
    for k, digit in enumerate(as_digits(rows[...], place[...])):
        digits = jnp.where(which == k, digit, digits)
    digits = digits.astype(jnp.float32).astype(out.dtype)
    send = placing(place[:, : cot.shape[0]], cap * devices)
    for f in range(folds):
        sent = dot(send, cot[:, f * features : (f + 1) * features], ((1,), (0,)))
        for k in range(devices):
            some = sent[k * cap : (k + 1) * cap].astype(out.dtype)
            out[k, f * cap : (f + 1) * cap, :] = some
    for k in range(devices):
        out[k, shared:, :] = digits


def pack_rows(rows, cot, devices, cap, features):
    tokens = rows.shape[0]
    folds = cot.shape[1] // features
    if features % LANES == 0 and cap % 8 == 0 and features >= tokens and devices <= 16:
        padding = jnp.full((features - tokens,), 16 * cap * devices, jnp.int32)
        return pl.pallas_call(
            rows_kernel,
            out_shape=jax.ShapeDtypeStruct((devices, folds * cap + 16, features), cot.dtype),
            scratch_shapes=[pltpu.VMEM((1, features), jnp.int32)],
            cost_estimate=pl.CostEstimate(
                flops=2 * devices * cap * tokens * cot.shape[1],
                bytes_accessed=6 * cot.size,
                transcendentals=0,
            ),
            compiler_params=pltpu.CompilerParams(vmem_limit_bytes=VMEM),
        )(jnp.concatenate([rows, padding])[None], cot)
    target = rows // (cap * devices)
    order = jnp.arange(tokens, dtype=jnp.int32)
    before = (target[:, None] == target[None, :]) & (order[None, :] < order[:, None])
    place = target * cap + jnp.sum(before.astype(jnp.int32), axis=1)
    send = jnp.arange(cap * devices, dtype=jnp.int32)[:, None] == place[None, :]
    sent = dot(send.astype(jnp.bfloat16), cot, ((1,), (0,))).astype(jnp.bfloat16)
    sent = sent.reshape(devices, cap, cot.shape[1])
    digits = jnp.stack(as_digits(rows, place)).astype(jnp.bfloat16)
    digits = jnp.pad(digits, ((0, 0), (0, -tokens % features))).reshape(-1, features)
    digits = jnp.pad(digits, ((0, -digits.shape[0] % 16), (0, 0)))
    parts = [sent[:, :, k : k + features] for k in range(0, cot.shape[1], features)]
    parts += [jnp.broadcast_to(digits[None], (devices,) + digits.shape)]
    return jnp.concatenate(parts, axis=1)


def features_kernel(act, maps, out):
    targets, _, features = out.shape
    tokens = act.shape[0]
    for k in range(targets):
        part = slice(k * features, (k + 1) * features)
        out[k, :tokens, :] = act[:, part]
        out[k, tokens:, :] = maps[:, part]


def pack_features(act, maps, devices):
    tokens, width = act.shape
    features = width // devices
    shared = maps.shape[0]
    targets = 4
    if features % LANES == 0:
        return pl.pallas_call(
            features_kernel,
            grid=(devices // targets,),
            in_specs=[
                pl.BlockSpec((tokens, targets * features), lambda j: (0, j)),
                pl.BlockSpec((shared, targets * features), lambda j: (0, j)),
            ],
            out_specs=pl.BlockSpec((targets, tokens + shared, features), lambda j: (j, 0, 0)),
            out_shape=jax.ShapeDtypeStruct((devices, tokens + shared, features), act.dtype),
            cost_estimate=pl.CostEstimate(
                flops=0, bytes_accessed=4 * (tokens + shared) * width, transcendentals=0
            ),
            compiler_params=pltpu.CompilerParams(vmem_limit_bytes=VMEM),
        )(act, maps)
    both = jnp.concatenate([act, maps], axis=0)
    return both.reshape(tokens + shared, devices, features).transpose(1, 0, 2)


def slot_chunks(width):
    size = min(width, 768)
    while width % size:
        size //= 2
    return [slice(k, k + size) for k in range(0, width, size)]


def slot_of(rows, starts):
    blocks = rows // BLOCK
    latest = jnp.max(jnp.where(starts <= blocks, starts, -1), axis=0, keepdims=True)
    return jnp.where(latest >= 0, latest, jnp.max(starts))


def own_rows(slot, first, size, rank):
    index = first // rank + lax.broadcasted_iota(jnp.int32, (size // rank, rank, 1), 0)
    return index == slot[None]


def placing(place, places):
    hit = lax.broadcasted_iota(jnp.int32, (places, place.shape[1]), 0) == place
    return jnp.where(hit, 1.0, 0.0).astype(jnp.bfloat16)


def all_rows(act, tokens):
    return jnp.concatenate([act[k, :tokens, :] for k in range(act.shape[0])], axis=0)


def of_source(sources, width):
    lane = lax.broadcasted_iota(jnp.int32, (sources, 1, width), 2)
    return lane // (width // sources) == lax.broadcasted_iota(
        jnp.int32, (sources, 1, width), 0
    )


def hidden_kernel(act, maps, rows, spots, starts, out):
    sources, share, width = act.shape[0], maps.shape[1], rows.shape[1]
    rank, places = out.shape[0] // sources, out.shape[1]
    slot = slot_of(rows[...], starts[...])
    every = all_rows(act, width // sources)
    total = jnp.zeros((rank, width), jnp.float32)
    for part in slot_chunks(maps.shape[0] * share):
        size = part.stop - part.start
        some = maps[part.start // share : part.stop // share].reshape(size, -1)
        each = dot(some, every, ((1,), (1,))).reshape(size // rank, rank, -1)
        total += jnp.sum(jnp.where(own_rows(slot, part.start, size, rank), each, 0.0), axis=0)
    total = jnp.where(of_source(sources, width), total[None], 0.0).reshape(out.shape[0], width)
    high = total.astype(jnp.bfloat16)
    low = (total - high.astype(jnp.float32)).astype(jnp.bfloat16)
    place = placing(spots[...], places)
    out[...] = dot(high, place, ((1,), (1,))) + dot(low, place, ((1,), (1,)))


def down_kernel(act, grad, rows, spots, starts, out, total):
    sources, width = act.shape[0], rows.shape[1]
    rank, places = grad.shape[0] // sources, grad.shape[1]
    step = pl.program_id(0)

    @pl.when(step == 0)
    def _():
        total[...] = jnp.zeros_like(total)

    slot = slot_of(rows[...], starts[...])
    every = all_rows(act, width // sources)
    wide = dot(grad[...], placing(spots[...], places), ((1,), (0,)))
    wide = wide.reshape(sources, rank, width)
    wide = jnp.sum(jnp.where(of_source(sources, width), wide, 0.0), axis=0, keepdims=True)
    for part in slot_chunks(total.shape[0]):
        size = part.stop - part.start
        placed = jnp.where(own_rows(slot, part.start, size, rank), wide, 0.0)
        placed = placed.reshape(size, -1).astype(jnp.bfloat16)
        total[part, :] += dot(placed, every, ((1,), (0,)))

    @pl.when(step == pl.num_programs(0) - 1)
    def _():
        out[...] = (adapter_scale * total[...]).astype(out.dtype)


def feature_calls(received, tokens, share, rank, places, starts):
    devices, packed, features = received.shape
    width = devices * share
    sources = 4
    grid = (devices // sources,)
    act = pl.BlockSpec((sources, packed, features), lambda j: (j, 0, 0))
    maps = pl.BlockSpec((devices, share, features), lambda j: (0, tokens // share, 0))
    rows = pl.BlockSpec((1, sources * tokens), lambda j: (0, j))
    begin = pl.BlockSpec((starts, 1), lambda j: (0, 0))
    placed = pl.BlockSpec((sources * rank, places), lambda j: (j, 0))
    cost = pl.CostEstimate(
        flops=2 * devices * tokens * width * features,
        bytes_accessed=2 * devices * tokens * features,
        transcendentals=0,
    )
    params = pltpu.CompilerParams(vmem_limit_bytes=VMEM)
    hidden = pl.pallas_call(
        hidden_kernel,
        grid=grid,
        in_specs=[act, maps, rows, rows, begin],
        out_specs=placed,
        out_shape=jax.ShapeDtypeStruct((devices * rank, places), jnp.float32),
        cost_estimate=cost,
        compiler_params=params,
    )
    down = pl.pallas_call(
        down_kernel,
        grid=grid,
        in_specs=[act, placed, rows, rows, begin],
        out_specs=pl.BlockSpec((width, features), lambda j: (0, 0)),
        out_shape=jax.ShapeDtypeStruct((width, features), jnp.bfloat16),
        scratch_shapes=[pltpu.VMEM((width, features), jnp.float32)],
        cost_estimate=cost,
        compiler_params=params,
    )
    return hidden, down


def local(
    activations,
    cotangent,
    token_layout_row,
    tenant_first_row,
    frozen_value_weight,
    adapter_down_maps,
    adapter_up_maps,
):
    devices = lax.axis_size("blk")
    device = lax.axis_index("blk")
    tokens = activations.shape[0]
    resident, rank, width = adapter_down_maps.shape
    out_width = cotangent.shape[1]
    features = width // devices
    share = resident * rank
    resident_rows = resident * BLOCK
    cap = resident_rows // devices
    start_ids = tenant_first_row // BLOCK

    pieces = weight_pieces(frozen_value_weight)

    first_block = device * resident
    block_numbers = first_block + jnp.arange(resident, dtype=jnp.int32)
    begin = starts_of(block_numbers, start_ids)
    is_local = (begin >= first_block) & (begin <= block_numbers)
    home_slot = jnp.clip(begin - first_block, 0, resident - 1)
    last_map = jnp.concatenate(
        [
            lax.dynamic_index_in_dim(maps, home_slot[resident - 1], 0, keepdims=False)
            for maps in (adapter_down_maps, adapter_up_maps)
        ],
        axis=1,
    )
    carried = jnp.zeros_like(last_map)
    for step in range(1, HOPS + 1):
        home = (device - step) % devices
        carried = jnp.where(begin[0] // resident == home, moved(last_map, step), carried)

    def of_blocks(maps, own):
        blocks = []
        for b in range(resident):
            chosen = own
            for k in range(b + 1):
                chosen = jnp.where(is_local[b] & (home_slot[b] == k), maps[k], chosen)
            blocks.append(chosen)
        return jnp.concatenate(blocks, axis=0)

    down_blocks = of_blocks(adapter_down_maps, carried[:, :width])
    up_blocks = of_blocks(adapter_up_maps, carried[:, width:])

    sent_rows = pack_rows(token_layout_row, cotangent, devices, cap, features)
    own, _, across, _ = pieces
    early = [own[CHUNKS - 1], own[CHUNKS], across[0], carried]
    sent_rows = after(sent_rows, *early)
    got_rows = lax.all_to_all(sent_rows, "blk", split_axis=0, concat_axis=0)
    recv_cot = [
        got_rows[:, k * cap : (k + 1) * cap].reshape(resident_rows, features)
        for k in range(out_width // features)
    ]
    per_digit = -(-tokens // features)
    digits = got_rows[:, share : share + 5 * per_digit]
    digits = digits.reshape(devices, 5, per_digit * features)[:, :, :tokens]
    rows_all, place_all = from_digits(digits)

    spots = device * cap + jnp.arange(cap, dtype=jnp.int32)
    hit = place_all[:, None, :] == spots[None, :, None]
    row_in = rows_all - device * resident_rows + 1
    row_in = jnp.sum(jnp.where(hit, row_in[:, None, :], 0), axis=2).reshape(-1) - 1
    arrange = row_in[:, None] == jnp.arange(resident_rows, dtype=jnp.int32)[None, :]
    arrange = arrange.astype(jnp.bfloat16)
    in_block = row_in[:, None] // BLOCK == jnp.arange(share, dtype=jnp.int32)[None, :] // rank

    grad_in = sum(
        dot(part, up_blocks[:, k * features : (k + 1) * features], ((1,), (1,)))
        for k, part in enumerate(recv_cot)
    )
    grad_in = jnp.where(in_block, grad_in, 0.0).astype(jnp.bfloat16)
    grad_in = sum(grad_in[:, b * rank : (b + 1) * rank] for b in range(resident))
    grad_sent = grad_in.reshape(devices, cap, rank).transpose(1, 0, 2).reshape(cap, -1)

    flat_maps = adapter_down_maps.reshape(share, width)
    received = pack_features(activations, flat_maps, devices)
    received = after(received, got_rows)
    received = lax.all_to_all(received, "blk", split_axis=0, concat_axis=0)
    grad_all = to_all(after(grad_sent, received)).reshape(resident_rows, -1).T

    rows_all, place_all = rows_all.reshape(1, -1), place_all.reshape(1, -1)

    cot_rows = jnp.concatenate(
        [dot(arrange, part, ((0,), (0,))).astype(jnp.bfloat16) for part in recv_cot], axis=1
    )
    grad_rows = dot(arrange, grad_in, ((0,), (0,))).astype(jnp.bfloat16)
    group = lax.axis_index("groups")
    quarter = device % 4
    firsts = [quarter, quarter ^ 1, quarter ^ 2, quarter ^ 3]
    if own[0].shape[1] % LANES == 0:
        out = None
        for number, (piece, first) in enumerate(zip(pieces, firsts)):
            out, token = write_quarter(
                piece, first, group, cot_rows, grad_rows, down_blocks, out
            )
            if number == 2:
                place_all = after(place_all, token)
    else:
        weight = together(pieces, firsts, group)
        lora = [
            dot(
                grad_rows[b * BLOCK : (b + 1) * BLOCK],
                down_blocks[b * rank : (b + 1) * rank],
                ((1,), (0,)),
            )
            for b in range(resident)
        ]
        lora = (adapter_scale * jnp.concatenate(lora, axis=0)).astype(jnp.bfloat16)
        out = dot(cot_rows, weight, ((1,), (1,))) + lora.astype(jnp.float32)
        out = out.astype(jnp.bfloat16)

    starts = start_ids[:, None]
    hidden_call, down_call = feature_calls(
        received, tokens, share, rank, resident_rows, starts.shape[0]
    )
    shares = hidden_call(received, received, rows_all, place_all, starts)
    rows_all = after(rows_all, shares)
    down_f = down_call(received, grad_all, rows_all, place_all, starts)
    hidden = shares.T.reshape(devices, cap, -1)
    hidden = lax.all_to_all(hidden, "blk", split_axis=0, concat_axis=0)
    hidden = jnp.sum(hidden, axis=0).astype(jnp.bfloat16)
    hidden = hidden.reshape(cap, devices, rank).transpose(1, 0, 2).reshape(-1, rank)
    down_home = lax.all_to_all(down_f, "blk", split_axis=0, concat_axis=1, tiled=True)
    down_map_gradient = down_home.astype(jnp.float32).reshape(resident, rank, width)

    wide = jnp.where(in_block, jnp.concatenate([hidden] * resident, axis=1), 0)
    up_all = [dot(wide, part, ((0,), (0,))) for part in recv_cot]
    up_all = jnp.concatenate(up_all, axis=1).reshape(resident, rank, out_width)
    up_parts = [up_all[b] for b in range(resident)]

    tail = sum(jnp.where(is_local[b], 0.0, up_parts[b]) for b in range(resident))
    far = jnp.zeros_like(tail)
    for step in range(1, HOPS + 1):
        other = (device + step) % devices * resident
        theirs = starts_of(other[None], start_ids)[0]
        far = far + jnp.where(theirs // resident == device, moved(tail, -step), 0.0)
    up_grads = []
    for k in range(resident):
        total = jnp.where(begin[resident - 1] == first_block + k, far, 0.0)
        for b in range(resident):
            total = total + jnp.where(is_local[b] & (home_slot[b] == k), up_parts[b], 0.0)
        up_grads.append(adapter_scale * total)
    up_map_gradient = jnp.stack(up_grads)

    return (out, down_map_gradient, up_map_gradient)


def solution(mesh):
    return jax.shard_map(
        local,
        mesh=mesh,
        in_specs=(
            P(("groups", "blk"), None),
            P(("groups", "blk"), None),
            P(("groups", "blk")),
            P("groups"),
            P("blk", None),
            P(("groups", "blk"), None, None),
            P(("groups", "blk"), None, None),
        ),
        out_specs=(
            P(("groups", "blk"), None),
            P(("groups", "blk"), None, None),
            P(("groups", "blk"), None, None),
        ),
        check_vma=False,
    )
```

```python
import functools

import jax
import jax.numpy as jnp
from jax import lax
from jax.experimental import pallas as pl
from jax.experimental.pallas import tpu as pltpu
from jax.sharding import PartitionSpec as P

BLOCK = 128
HOPS = 4
LANES = 128
DIGIT = 64
VMEM = 56 << 20

adapter_scale = 2.0


def moved(value, steps):
    count = lax.axis_size("blk")
    return lax.ppermute(value, "blk", [(i, (i + steps) % count) for i in range(count)])


def to_all(value):
    count = lax.axis_size("blk")
    copies = jnp.broadcast_to(value[None], (count,) + value.shape)
    return lax.all_to_all(copies, "blk", split_axis=0, concat_axis=0)


def after(value, *others):
    anywhere = pl.BlockSpec(memory_space=pl.ANY)
    return pl.pallas_call(
        lambda *refs: None,
        in_specs=[anywhere] * (1 + len(others)),
        out_specs=anywhere,
        out_shape=jax.ShapeDtypeStruct(value.shape, value.dtype),
        input_output_aliases={0: 0},
        cost_estimate=pl.CostEstimate(flops=0, bytes_accessed=0, transcendentals=0),
        compiler_params=pltpu.CompilerParams(vmem_limit_bytes=VMEM),
    )(value, *others)


def dot(a, b, dims):
    return lax.dot_general(a, b, (dims, ((), ())), preferred_element_type=jnp.float32)


def starts_of(blocks, start_ids):
    latest = jnp.max(
        jnp.where(start_ids[None, :] <= blocks[:, None], start_ids[None, :], -1), axis=1
    )
    return jnp.where(latest >= 0, latest, jnp.max(start_ids))


def as_digits(rows, places):
    return (
        rows % DIGIT,
        rows // DIGIT % DIGIT,
        rows // (DIGIT * DIGIT),
        places % DIGIT,
        places // DIGIT,
    )


def from_digits(digits):
    low, middle, high, place, place_high = [digits[:, k].astype(jnp.int32) for k in range(5)]
    return (high * DIGIT + middle) * DIGIT + low, place_high * DIGIT + place


CHUNKS = 2


def near_lines(count):
    return count // 4 <= 4


def line_order():
    count = lax.axis_size("blk")
    shards = jnp.arange(count // 4, dtype=jnp.int32)
    if near_lines(count):
        return (lax.axis_index("blk") // 4 - shards) % (count // 4)
    return shards


def weight_pieces(weight):
    count = lax.axis_size("blk")
    half = weight.shape[0] // 2
    size = half // CHUNKS
    first = lax.axis_index("groups") * half

    def over(piece, bit):
        return lax.ppermute(piece, "blk", [(i, i ^ bit) for i in range(count)])

    def groups(piece):
        return lax.ppermute(piece, "groups", [(0, 1), (1, 0)])

    def column(chunk):
        mine = lax.dynamic_slice_in_dim(weight, first + chunk * size, size, 0)
        if near_lines(count):
            return jnp.stack([mine] + [moved(mine, 4 * k) for k in range(1, count // 4)])
        lines = [list(range(k, count, 4)) for k in range(4)]
        return lax.all_gather(mine, "blk", axis_index_groups=lines)

    columns = [column(k) for k in range(CHUNKS)]
    pieces = []
    for mine in (columns, [over(column, 2) for column in columns]):
        both = mine + [groups(piece) for piece in mine]
        pieces += [both, [over(piece, 1) for piece in both]]
    return pieces


def quarter_kernel(where, cot, grad, down, *rest):
    pieces = rest[: 2 * CHUNKS]
    out, token = rest[-2:]
    token[...] = jnp.zeros_like(token)
    rank = grad.shape[1]
    lora = [
        adapter_scale
        * dot(
            grad[b * BLOCK : (b + 1) * BLOCK, :],
            down[b * rank : (b + 1) * rank, :],
            ((1,), (0,)),
        )
        for b in range(cot.shape[0] // BLOCK)
    ]
    lora = jnp.concatenate(lora, axis=0).astype(jnp.bfloat16).astype(jnp.float32)

    def product(group):
        order = pieces[group * CHUNKS :] + pieces[: group * CHUNKS]
        weight = jnp.concatenate([piece[0] for piece in order], axis=0)
        frozen = dot(cot[...], weight, ((1,), (1,)))
        out[...] = (frozen + lora).astype(jnp.bfloat16)

    for group in range(2):
        pl.when(where[where.shape[0] - 1] == group)(functools.partial(product, group))


def write_quarter(quarter, first, group, cot, grad, down, out=None):
    rows, depth = cot.shape
    width = down.shape[1]
    shards, part, _ = quarter[0].shape
    stripe = part * len(quarter)
    where = jnp.concatenate([4 * line_order() + first, group[None]]).astype(jnp.int32)
    specs = [
        pl.BlockSpec((rows, depth), lambda j, where: (0, 0)),
        pl.BlockSpec(grad.shape, lambda j, where: (0, 0)),
        pl.BlockSpec((down.shape[0], stripe), lambda j, where: (0, where[j])),
    ] + [pl.BlockSpec((1, part, depth), lambda j, where: (j, 0, 0)) for _ in quarter]
    args = [where, cot, grad, down] + quarter
    alias = {}
    if out is not None:
        specs.append(pl.BlockSpec(memory_space=pl.ANY))
        args.append(out)
        alias = {len(args) - 1: 0}
    return pl.pallas_call(
        quarter_kernel,
        grid_spec=pltpu.PrefetchScalarGridSpec(
            num_scalar_prefetch=1,
            grid=(shards,),
            in_specs=specs,
            out_specs=[
                pl.BlockSpec((rows, stripe), lambda j, where: (0, where[j])),
                pl.BlockSpec((8, LANES), lambda j, where: (0, 0)),
            ],
        ),
        out_shape=[
            jax.ShapeDtypeStruct((rows, width), jnp.bfloat16),
            jax.ShapeDtypeStruct((8, LANES), jnp.float32),
        ],
        input_output_aliases=alias,
        cost_estimate=pl.CostEstimate(
            flops=2 * rows * depth * stripe * shards,
            bytes_accessed=2 * (depth + rows) * stripe * shards,
            transcendentals=0,
        ),
        compiler_params=pltpu.CompilerParams(vmem_limit_bytes=VMEM),
    )(*args)


def together(pieces, firsts, group):
    shards, part, depth = pieces[0][0].shape
    weight = jnp.zeros((shards, 4, 2, CHUNKS, part, depth), jnp.bfloat16)
    order = line_order()
    for quarter, first in zip(pieces, firsts):
        for k, piece in enumerate(quarter):
            half = group if k < CHUNKS else 1 - group
            if not near_lines(4 * shards):
                place = (0, first, half, k % CHUNKS, 0, 0)
                weight = lax.dynamic_update_slice(weight, piece[:, None, None, None], place)
                continue
            for j in range(shards):
                place = (order[j], first, half, k % CHUNKS, 0, 0)
                shard = piece[j][None, None, None, None]
                weight = lax.dynamic_update_slice(weight, shard, place)
    return weight.reshape(-1, depth)


def rows_kernel(rows, cot, out, place):
    devices, packed, features = out.shape
    shared = packed - 16
    folds = cot.shape[1] // features
    cap = shared // folds
    target = rows[...] // (cap * devices)
    to = lax.broadcasted_iota(jnp.int32, (16, features), 0) == target
    first = lax.broadcasted_iota(jnp.int32, (features, features), 0)
    later = lax.broadcasted_iota(jnp.int32, (features, features), 1)
    earlier = jnp.where(first < later, 1.0, 0.0).astype(jnp.bfloat16)
    ahead = dot(jnp.where(to, 1.0, 0.0).astype(jnp.bfloat16), earlier, ((1,), (0,)))
    ahead = jnp.sum(jnp.where(to, ahead, 0.0), axis=0, keepdims=True)
    place[...] = target * cap + ahead.astype(jnp.int32)
    which = lax.broadcasted_iota(jnp.int32, (16, features), 0)
    digits = jnp.zeros((16, features), jnp.int32)
    for k, digit in enumerate(as_digits(rows[...], place[...])):
        digits = jnp.where(which == k, digit, digits)
    digits = digits.astype(jnp.float32).astype(out.dtype)
    send = placing(place[:, : cot.shape[0]], cap * devices)
    for f in range(folds):
        sent = dot(send, cot[:, f * features : (f + 1) * features], ((1,), (0,)))
        for k in range(devices):
            some = sent[k * cap : (k + 1) * cap].astype(out.dtype)
            out[k, f * cap : (f + 1) * cap, :] = some
    for k in range(devices):
        out[k, shared:, :] = digits


def pack_rows(rows, cot, devices, cap, features):
    tokens = rows.shape[0]
    folds = cot.shape[1] // features
    if features % LANES == 0 and cap % 8 == 0 and features >= tokens and devices <= 16:
        padding = jnp.full((features - tokens,), 16 * cap * devices, jnp.int32)
        return pl.pallas_call(
            rows_kernel,
            out_shape=jax.ShapeDtypeStruct((devices, folds * cap + 16, features), cot.dtype),
            scratch_shapes=[pltpu.VMEM((1, features), jnp.int32)],
            cost_estimate=pl.CostEstimate(
                flops=2 * devices * cap * tokens * cot.shape[1],
                bytes_accessed=6 * cot.size,
                transcendentals=0,
            ),
            compiler_params=pltpu.CompilerParams(vmem_limit_bytes=VMEM),
        )(jnp.concatenate([rows, padding])[None], cot)
    target = rows // (cap * devices)
    order = jnp.arange(tokens, dtype=jnp.int32)
    before = (target[:, None] == target[None, :]) & (order[None, :] < order[:, None])
    place = target * cap + jnp.sum(before.astype(jnp.int32), axis=1)
    send = jnp.arange(cap * devices, dtype=jnp.int32)[:, None] == place[None, :]
    sent = dot(send.astype(jnp.bfloat16), cot, ((1,), (0,))).astype(jnp.bfloat16)
    sent = sent.reshape(devices, cap, cot.shape[1])
    digits = jnp.stack(as_digits(rows, place)).astype(jnp.bfloat16)
    digits = jnp.pad(digits, ((0, 0), (0, -tokens % features))).reshape(-1, features)
    digits = jnp.pad(digits, ((0, -digits.shape[0] % 16), (0, 0)))
    parts = [sent[:, :, k : k + features] for k in range(0, cot.shape[1], features)]
    parts += [jnp.broadcast_to(digits[None], (devices,) + digits.shape)]
    return jnp.concatenate(parts, axis=1)


def features_kernel(act, maps, out):
    targets, _, features = out.shape
    tokens = act.shape[0]
    for k in range(targets):
        part = slice(k * features, (k + 1) * features)
        out[k, :tokens, :] = act[:, part]
        out[k, tokens:, :] = maps[:, part]


def pack_features(act, maps, devices):
    tokens, width = act.shape
    features = width // devices
    shared = maps.shape[0]
    targets = 4
    if features % LANES == 0:
        return pl.pallas_call(
            features_kernel,
            grid=(devices // targets,),
            in_specs=[
                pl.BlockSpec((tokens, targets * features), lambda j: (0, j)),
                pl.BlockSpec((shared, targets * features), lambda j: (0, j)),
            ],
            out_specs=pl.BlockSpec((targets, tokens + shared, features), lambda j: (j, 0, 0)),
            out_shape=jax.ShapeDtypeStruct((devices, tokens + shared, features), act.dtype),
            cost_estimate=pl.CostEstimate(
                flops=0, bytes_accessed=4 * (tokens + shared) * width, transcendentals=0
            ),
            compiler_params=pltpu.CompilerParams(vmem_limit_bytes=VMEM),
        )(act, maps)
    both = jnp.concatenate([act, maps], axis=0)
    return both.reshape(tokens + shared, devices, features).transpose(1, 0, 2)


def slot_chunks(width):
    size = min(width, 768)
    while width % size:
        size //= 2
    return [slice(k, k + size) for k in range(0, width, size)]


def slot_of(rows, starts):
    blocks = rows // BLOCK
    latest = jnp.max(jnp.where(starts <= blocks, starts, -1), axis=0, keepdims=True)
    return jnp.where(latest >= 0, latest, jnp.max(starts))


def own_rows(slot, first, size, rank):
    index = first // rank + lax.broadcasted_iota(jnp.int32, (size // rank, rank, 1), 0)
    return index == slot[None]


def placing(place, places):
    hit = lax.broadcasted_iota(jnp.int32, (places, place.shape[1]), 0) == place
    return jnp.where(hit, 1.0, 0.0).astype(jnp.bfloat16)


def all_rows(act, tokens):
    return jnp.concatenate([act[k, :tokens, :] for k in range(act.shape[0])], axis=0)


def of_source(sources, width):
    lane = lax.broadcasted_iota(jnp.int32, (sources, 1, width), 2)
    return lane // (width // sources) == lax.broadcasted_iota(
        jnp.int32, (sources, 1, width), 0
    )


def hidden_kernel(act, maps, rows, spots, starts, out):
    sources, share, width = act.shape[0], maps.shape[1], rows.shape[1]
    rank, places = out.shape[0] // sources, out.shape[1]
    slot = slot_of(rows[...], starts[...])
    every = all_rows(act, width // sources)
    total = jnp.zeros((rank, width), jnp.float32)
    for part in slot_chunks(maps.shape[0] * share):
        size = part.stop - part.start
        some = maps[part.start // share : part.stop // share].reshape(size, -1)
        each = dot(some, every, ((1,), (1,))).reshape(size // rank, rank, -1)
        total += jnp.sum(jnp.where(own_rows(slot, part.start, size, rank), each, 0.0), axis=0)
    total = jnp.where(of_source(sources, width), total[None], 0.0).reshape(out.shape[0], width)
    high = total.astype(jnp.bfloat16)
    low = (total - high.astype(jnp.float32)).astype(jnp.bfloat16)
    place = placing(spots[...], places)
    out[...] = dot(high, place, ((1,), (1,))) + dot(low, place, ((1,), (1,)))


def down_kernel(act, grad, rows, spots, starts, out, total):
    sources, width = act.shape[0], rows.shape[1]
    rank, places = grad.shape[0] // sources, grad.shape[1]
    step = pl.program_id(0)

    @pl.when(step == 0)
    def _():
        total[...] = jnp.zeros_like(total)

    slot = slot_of(rows[...], starts[...])
    every = all_rows(act, width // sources)
    wide = dot(grad[...], placing(spots[...], places), ((1,), (0,)))
    wide = wide.reshape(sources, rank, width)
    wide = jnp.sum(jnp.where(of_source(sources, width), wide, 0.0), axis=0, keepdims=True)
    for part in slot_chunks(total.shape[0]):
        size = part.stop - part.start
        placed = jnp.where(own_rows(slot, part.start, size, rank), wide, 0.0)
        placed = placed.reshape(size, -1).astype(jnp.bfloat16)
        total[part, :] += dot(placed, every, ((1,), (0,)))

    @pl.when(step == pl.num_programs(0) - 1)
    def _():
        out[...] = (adapter_scale * total[...]).astype(out.dtype)


def feature_calls(received, tokens, share, rank, places, starts):
    devices, packed, features = received.shape
    width = devices * share
    sources = 4
    grid = (devices // sources,)
    act = pl.BlockSpec((sources, packed, features), lambda j: (j, 0, 0))
    maps = pl.BlockSpec((devices, share, features), lambda j: (0, tokens // share, 0))
    rows = pl.BlockSpec((1, sources * tokens), lambda j: (0, j))
    begin = pl.BlockSpec((starts, 1), lambda j: (0, 0))
    placed = pl.BlockSpec((sources * rank, places), lambda j: (j, 0))
    cost = pl.CostEstimate(
        flops=2 * devices * tokens * width * features,
        bytes_accessed=2 * devices * tokens * features,
        transcendentals=0,
    )
    params = pltpu.CompilerParams(vmem_limit_bytes=VMEM)
    hidden = pl.pallas_call(
        hidden_kernel,
        grid=grid,
        in_specs=[act, maps, rows, rows, begin],
        out_specs=placed,
        out_shape=jax.ShapeDtypeStruct((devices * rank, places), jnp.float32),
        cost_estimate=cost,
        compiler_params=params,
    )
    down = pl.pallas_call(
        down_kernel,
        grid=grid,
        in_specs=[act, placed, rows, rows, begin],
        out_specs=pl.BlockSpec((width, features), lambda j: (0, 0)),
        out_shape=jax.ShapeDtypeStruct((width, features), jnp.bfloat16),
        scratch_shapes=[pltpu.VMEM((width, features), jnp.float32)],
        cost_estimate=cost,
        compiler_params=params,
    )
    return hidden, down


def local(
    activations,
    cotangent,
    token_layout_row,
    tenant_first_row,
    frozen_value_weight,
    adapter_down_maps,
    adapter_up_maps,
):
    devices = lax.axis_size("blk")
    device = lax.axis_index("blk")
    tokens = activations.shape[0]
    resident, rank, width = adapter_down_maps.shape
    out_width = cotangent.shape[1]
    features = width // devices
    share = resident * rank
    resident_rows = resident * BLOCK
    cap = resident_rows // devices
    start_ids = tenant_first_row // BLOCK

    pieces = weight_pieces(frozen_value_weight)

    first_block = device * resident
    block_numbers = first_block + jnp.arange(resident, dtype=jnp.int32)
    begin = starts_of(block_numbers, start_ids)
    is_local = (begin >= first_block) & (begin <= block_numbers)
    home_slot = jnp.clip(begin - first_block, 0, resident - 1)
    last_map = jnp.concatenate(
        [
            lax.dynamic_index_in_dim(maps, home_slot[resident - 1], 0, keepdims=False)
            for maps in (adapter_down_maps, adapter_up_maps)
        ],
        axis=1,
    )
    carried = jnp.zeros_like(last_map)
    for step in range(1, HOPS + 1):
        home = (device - step) % devices
        carried = jnp.where(begin[0] // resident == home, moved(last_map, step), carried)

    def of_blocks(maps, own):
        blocks = []
        for b in range(resident):
            chosen = own
            for k in range(b + 1):
                chosen = jnp.where(is_local[b] & (home_slot[b] == k), maps[k], chosen)
            blocks.append(chosen)
        return jnp.concatenate(blocks, axis=0)

    down_blocks = of_blocks(adapter_down_maps, carried[:, :width])
    up_blocks = of_blocks(adapter_up_maps, carried[:, width:])

    sent_rows = pack_rows(token_layout_row, cotangent, devices, cap, features)
    own, _, across, _ = pieces
    sent_rows = after(sent_rows, *own[:CHUNKS], carried)
    got_rows = lax.all_to_all(sent_rows, "blk", split_axis=0, concat_axis=0)
    recv_cot = [
        got_rows[:, k * cap : (k + 1) * cap].reshape(resident_rows, features)
        for k in range(out_width // features)
    ]
    per_digit = -(-tokens // features)
    digits = got_rows[:, share : share + 5 * per_digit]
    digits = digits.reshape(devices, 5, per_digit * features)[:, :, :tokens]
    rows_all, place_all = from_digits(digits)

    spots = device * cap + jnp.arange(cap, dtype=jnp.int32)
    hit = place_all[:, None, :] == spots[None, :, None]
    row_in = rows_all - device * resident_rows + 1
    row_in = jnp.sum(jnp.where(hit, row_in[:, None, :], 0), axis=2).reshape(-1) - 1
    arrange = row_in[:, None] == jnp.arange(resident_rows, dtype=jnp.int32)[None, :]
    arrange = arrange.astype(jnp.bfloat16)
    in_block = row_in[:, None] // BLOCK == jnp.arange(share, dtype=jnp.int32)[None, :] // rank

    grad_in = sum(
        dot(part, up_blocks[:, k * features : (k + 1) * features], ((1,), (1,)))
        for k, part in enumerate(recv_cot)
    )
    grad_in = jnp.where(in_block, grad_in, 0.0).astype(jnp.bfloat16)
    grad_in = sum(grad_in[:, b * rank : (b + 1) * rank] for b in range(resident))
    grad_sent = grad_in.reshape(devices, cap, rank).transpose(1, 0, 2).reshape(cap, -1)

    flat_maps = adapter_down_maps.reshape(share, width)
    received = pack_features(activations, flat_maps, devices)
    received = after(received, got_rows, own[CHUNKS], across[0])
    received = lax.all_to_all(received, "blk", split_axis=0, concat_axis=0)
    grad_all = to_all(after(grad_sent, received)).reshape(resident_rows, -1).T

    rows_all, place_all = rows_all.reshape(1, -1), place_all.reshape(1, -1)

    cot_rows = jnp.concatenate(
        [dot(arrange, part, ((0,), (0,))).astype(jnp.bfloat16) for part in recv_cot], axis=1
    )
    grad_rows = dot(arrange, grad_in, ((0,), (0,))).astype(jnp.bfloat16)
    group = lax.axis_index("groups")
    quarter = device % 4
    firsts = [quarter, quarter ^ 1, quarter ^ 2, quarter ^ 3]
    if own[0].shape[1] % LANES == 0:
        out = None
        for piece, first in zip(pieces[:2], firsts):
            out, token = write_quarter(
                piece, first, group, cot_rows, grad_rows, down_blocks, out
            )
        place_all = after(place_all, token)
    else:
        weight = together(pieces, firsts, group)
        lora = [
            dot(
                grad_rows[b * BLOCK : (b + 1) * BLOCK],
                down_blocks[b * rank : (b + 1) * rank],
                ((1,), (0,)),
            )
            for b in range(resident)
        ]
        lora = (adapter_scale * jnp.concatenate(lora, axis=0)).astype(jnp.bfloat16)
        out = dot(cot_rows, weight, ((1,), (1,))) + lora.astype(jnp.float32)
        out = out.astype(jnp.bfloat16)

    starts = start_ids[:, None]
    hidden_call, down_call = feature_calls(
        received, tokens, share, rank, resident_rows, starts.shape[0]
    )
    shares = hidden_call(received, received, rows_all, place_all, starts)
    rows_all = after(rows_all, shares)
    down_f = down_call(received, grad_all, rows_all, place_all, starts)
    hidden = shares.T.reshape(devices, cap, -1)
    hidden = lax.all_to_all(hidden, "blk", split_axis=0, concat_axis=0)
    hidden = jnp.sum(hidden, axis=0).astype(jnp.bfloat16)
    hidden = hidden.reshape(cap, devices, rank).transpose(1, 0, 2).reshape(-1, rank)
    down_home = lax.all_to_all(down_f, "blk", split_axis=0, concat_axis=1, tiled=True)
    down_map_gradient = down_home.astype(jnp.float32).reshape(resident, rank, width)

    wide = jnp.where(in_block, jnp.concatenate([hidden] * resident, axis=1), 0)
    up_all = [dot(wide, part, ((0,), (0,))) for part in recv_cot]
    up_all = jnp.concatenate(up_all, axis=1).reshape(resident, rank, out_width)
    up_parts = [up_all[b] for b in range(resident)]

    tail = sum(jnp.where(is_local[b], 0.0, up_parts[b]) for b in range(resident))
    far = jnp.zeros_like(tail)
    for step in range(1, HOPS + 1):
        other = (device + step) % devices * resident
        theirs = starts_of(other[None], start_ids)[0]
        far = far + jnp.where(theirs // resident == device, moved(tail, -step), 0.0)
    up_grads = []
    for k in range(resident):
        total = jnp.where(begin[resident - 1] == first_block + k, far, 0.0)
        for b in range(resident):
            total = total + jnp.where(is_local[b] & (home_slot[b] == k), up_parts[b], 0.0)
        up_grads.append(adapter_scale * total)
    up_map_gradient = jnp.stack(up_grads)

    if own[0].shape[1] % LANES == 0:
        late = after(grad_rows, down_f)
        for piece, first in zip(pieces[2:], firsts[2:]):
            out, _ = write_quarter(piece, first, group, cot_rows, late, down_blocks, out)
    return (out, down_map_gradient, up_map_gradient)


def solution(mesh):
    return jax.shard_map(
        local,
        mesh=mesh,
        in_specs=(
            P(("groups", "blk"), None),
            P(("groups", "blk"), None),
            P(("groups", "blk")),
            P("groups"),
            P("blk", None),
            P(("groups", "blk"), None, None),
            P(("groups", "blk"), None, None),
        ),
        out_specs=(
            P(("groups", "blk"), None),
            P(("groups", "blk"), None, None),
            P(("groups", "blk"), None, None),
        ),
        check_vma=False,
    )
```

```python
import functools

import jax
import jax.numpy as jnp
from jax import lax
from jax.experimental import pallas as pl
from jax.experimental.pallas import tpu as pltpu
from jax.sharding import PartitionSpec as P

BLOCK = 128
HOPS = 4
LANES = 128
DIGIT = 64
VMEM = 56 << 20

adapter_scale = 2.0


def moved(value, steps):
    count = lax.axis_size("blk")
    return lax.ppermute(value, "blk", [(i, (i + steps) % count) for i in range(count)])


def to_all(value):
    count = lax.axis_size("blk")
    copies = jnp.broadcast_to(value[None], (count,) + value.shape)
    return lax.all_to_all(copies, "blk", split_axis=0, concat_axis=0)


def after(value, *others):
    anywhere = pl.BlockSpec(memory_space=pl.ANY)
    return pl.pallas_call(
        lambda *refs: None,
        in_specs=[anywhere] * (1 + len(others)),
        out_specs=anywhere,
        out_shape=jax.ShapeDtypeStruct(value.shape, value.dtype),
        input_output_aliases={0: 0},
        cost_estimate=pl.CostEstimate(flops=0, bytes_accessed=0, transcendentals=0),
        compiler_params=pltpu.CompilerParams(vmem_limit_bytes=VMEM),
    )(value, *others)


def dot(a, b, dims):
    return lax.dot_general(a, b, (dims, ((), ())), preferred_element_type=jnp.float32)


def starts_of(blocks, start_ids):
    latest = jnp.max(
        jnp.where(start_ids[None, :] <= blocks[:, None], start_ids[None, :], -1), axis=1
    )
    return jnp.where(latest >= 0, latest, jnp.max(start_ids))


def as_digits(rows, places):
    return (
        rows % DIGIT,
        rows // DIGIT % DIGIT,
        rows // (DIGIT * DIGIT),
        places % DIGIT,
        places // DIGIT,
    )


def from_digits(digits):
    low, middle, high, place, place_high = [digits[:, k].astype(jnp.int32) for k in range(5)]
    return (high * DIGIT + middle) * DIGIT + low, place_high * DIGIT + place


CHUNKS = 2


def near_lines(count):
    return count // 4 <= 4


def line_order():
    count = lax.axis_size("blk")
    shards = jnp.arange(count // 4, dtype=jnp.int32)
    if near_lines(count):
        return lax.rem(lax.div(lax.axis_index("blk"), 4) + count // 4 - shards, count // 4)
    return shards


def weight_pieces(weight):
    count = lax.axis_size("blk")
    half = weight.shape[0] // 2
    size = half // CHUNKS
    first = lax.axis_index("groups") * half

    def over(piece, bit):
        return lax.ppermute(piece, "blk", [(i, i ^ bit) for i in range(count)])

    def groups(piece):
        return lax.ppermute(piece, "groups", [(0, 1), (1, 0)])

    def column(chunk):
        mine = lax.dynamic_slice_in_dim(weight, first + chunk * size, size, 0)
        if near_lines(count):
            return jnp.stack([mine] + [moved(mine, 4 * k) for k in range(1, count // 4)])
        lines = [list(range(k, count, 4)) for k in range(4)]
        return lax.all_gather(mine, "blk", axis_index_groups=lines)

    columns = [column(k) for k in range(CHUNKS)]
    pieces = []
    for mine in (columns, [over(column, 2) for column in columns]):
        both = mine + [groups(piece) for piece in mine]
        pieces += [both, [over(piece, 1) for piece in both]]
    return pieces


def quarter_kernel(where, cot, grad, down, *rest):
    pieces = rest[: 2 * CHUNKS]
    out, token = rest[-2:]
    token[...] = jnp.zeros_like(token)
    rank = grad.shape[1]
    lora = [
        adapter_scale
        * dot(
            grad[b * BLOCK : (b + 1) * BLOCK, :],
            down[b * rank : (b + 1) * rank, :],
            ((1,), (0,)),
        )
        for b in range(cot.shape[0] // BLOCK)
    ]
    lora = jnp.concatenate(lora, axis=0).astype(jnp.bfloat16).astype(jnp.float32)

    def product(group):
        order = pieces[group * CHUNKS :] + pieces[: group * CHUNKS]
        weight = jnp.concatenate([piece[0] for piece in order], axis=0)
        frozen = dot(cot[...], weight, ((1,), (1,)))
        out[...] = (frozen + lora).astype(jnp.bfloat16)

    for group in range(2):
        pl.when(where[where.shape[0] - 1] == group)(functools.partial(product, group))


def write_quarter(quarter, first, group, cot, grad, down, out=None):
    rows, depth = cot.shape
    width = down.shape[1]
    shards, part, _ = quarter[0].shape
    stripe = part * len(quarter)
    where = jnp.concatenate([4 * line_order() + first, group[None]]).astype(jnp.int32)
    specs = [
        pl.BlockSpec((rows, depth), lambda j, where: (0, 0)),
        pl.BlockSpec(grad.shape, lambda j, where: (0, 0)),
        pl.BlockSpec((down.shape[0], stripe), lambda j, where: (0, where[j])),
    ] + [pl.BlockSpec((1, part, depth), lambda j, where: (j, 0, 0)) for _ in quarter]
    args = [where, cot, grad, down] + quarter
    alias = {}
    if out is not None:
        specs.append(pl.BlockSpec(memory_space=pl.ANY))
        args.append(out)
        alias = {len(args) - 1: 0}
    return pl.pallas_call(
        quarter_kernel,
        grid_spec=pltpu.PrefetchScalarGridSpec(
            num_scalar_prefetch=1,
            grid=(shards,),
            in_specs=specs,
            out_specs=[
                pl.BlockSpec((rows, stripe), lambda j, where: (0, where[j])),
                pl.BlockSpec((8, LANES), lambda j, where: (0, 0)),
            ],
        ),
        out_shape=[
            jax.ShapeDtypeStruct((rows, width), jnp.bfloat16),
            jax.ShapeDtypeStruct((8, LANES), jnp.float32),
        ],
        input_output_aliases=alias,
        cost_estimate=pl.CostEstimate(
            flops=2 * rows * depth * stripe * shards,
            bytes_accessed=2 * (depth + rows) * stripe * shards,
            transcendentals=0,
        ),
        compiler_params=pltpu.CompilerParams(vmem_limit_bytes=VMEM),
    )(*args)


def together(pieces, firsts, group):
    shards, part, depth = pieces[0][0].shape
    weight = jnp.zeros((shards, 4, 2, CHUNKS, part, depth), jnp.bfloat16)
    order = line_order()
    for quarter, first in zip(pieces, firsts):
        for k, piece in enumerate(quarter):
            half = group if k < CHUNKS else 1 - group
            if not near_lines(4 * shards):
                place = (0, first, half, k % CHUNKS, 0, 0)
                weight = lax.dynamic_update_slice(weight, piece[:, None, None, None], place)
                continue
            for j in range(shards):
                place = (order[j], first, half, k % CHUNKS, 0, 0)
                shard = piece[j][None, None, None, None]
                weight = lax.dynamic_update_slice(weight, shard, place)
    return weight.reshape(-1, depth)


def rows_kernel(rows, cot, out, place):
    devices, packed, features = out.shape
    shared = packed - 16
    folds = cot.shape[1] // features
    cap = shared // folds
    target = rows[...] // (cap * devices)
    to = lax.broadcasted_iota(jnp.int32, (16, features), 0) == target
    first = lax.broadcasted_iota(jnp.int32, (features, features), 0)
    later = lax.broadcasted_iota(jnp.int32, (features, features), 1)
    earlier = jnp.where(first < later, 1.0, 0.0).astype(jnp.bfloat16)
    ahead = dot(jnp.where(to, 1.0, 0.0).astype(jnp.bfloat16), earlier, ((1,), (0,)))
    ahead = jnp.sum(jnp.where(to, ahead, 0.0), axis=0, keepdims=True)
    place[...] = target * cap + ahead.astype(jnp.int32)
    which = lax.broadcasted_iota(jnp.int32, (16, features), 0)
    digits = jnp.zeros((16, features), jnp.int32)
    for k, digit in enumerate(as_digits(rows[...], place[...])):
        digits = jnp.where(which == k, digit, digits)
    digits = digits.astype(jnp.float32).astype(out.dtype)
    send = placing(place[:, : cot.shape[0]], cap * devices)
    for f in range(folds):
        sent = dot(send, cot[:, f * features : (f + 1) * features], ((1,), (0,)))
        for k in range(devices):
            some = sent[k * cap : (k + 1) * cap].astype(out.dtype)
            out[k, f * cap : (f + 1) * cap, :] = some
    for k in range(devices):
        out[k, shared:, :] = digits


def pack_rows(rows, cot, devices, cap, features):
    tokens = rows.shape[0]
    folds = cot.shape[1] // features
    if features % LANES == 0 and cap % 8 == 0 and features >= tokens and devices <= 16:
        padding = jnp.full((features - tokens,), 16 * cap * devices, jnp.int32)
        return pl.pallas_call(
            rows_kernel,
            out_shape=jax.ShapeDtypeStruct((devices, folds * cap + 16, features), cot.dtype),
            scratch_shapes=[pltpu.VMEM((1, features), jnp.int32)],
            cost_estimate=pl.CostEstimate(
                flops=2 * devices * cap * tokens * cot.shape[1],
                bytes_accessed=6 * cot.size,
                transcendentals=0,
            ),
            compiler_params=pltpu.CompilerParams(vmem_limit_bytes=VMEM),
        )(jnp.concatenate([rows, padding])[None], cot)
    target = rows // (cap * devices)
    order = jnp.arange(tokens, dtype=jnp.int32)
    before = (target[:, None] == target[None, :]) & (order[None, :] < order[:, None])
    place = target * cap + jnp.sum(before.astype(jnp.int32), axis=1)
    send = jnp.arange(cap * devices, dtype=jnp.int32)[:, None] == place[None, :]
    sent = dot(send.astype(jnp.bfloat16), cot, ((1,), (0,))).astype(jnp.bfloat16)
    sent = sent.reshape(devices, cap, cot.shape[1])
    digits = jnp.stack(as_digits(rows, place)).astype(jnp.bfloat16)
    digits = jnp.pad(digits, ((0, 0), (0, -tokens % features))).reshape(-1, features)
    digits = jnp.pad(digits, ((0, -digits.shape[0] % 16), (0, 0)))
    parts = [sent[:, :, k : k + features] for k in range(0, cot.shape[1], features)]
    parts += [jnp.broadcast_to(digits[None], (devices,) + digits.shape)]
    return jnp.concatenate(parts, axis=1)


def features_kernel(act, maps, out):
    targets, _, features = out.shape
    tokens = act.shape[0]
    for k in range(targets):
        part = slice(k * features, (k + 1) * features)
        out[k, :tokens, :] = act[:, part]
        out[k, tokens:, :] = maps[:, part]


def pack_features(act, maps, devices):
    tokens, width = act.shape
    features = width // devices
    shared = maps.shape[0]
    targets = 4
    if features % LANES == 0:
        return pl.pallas_call(
            features_kernel,
            grid=(devices // targets,),
            in_specs=[
                pl.BlockSpec((tokens, targets * features), lambda j: (0, j)),
                pl.BlockSpec((shared, targets * features), lambda j: (0, j)),
            ],
            out_specs=pl.BlockSpec((targets, tokens + shared, features), lambda j: (j, 0, 0)),
            out_shape=jax.ShapeDtypeStruct((devices, tokens + shared, features), act.dtype),
            cost_estimate=pl.CostEstimate(
                flops=0, bytes_accessed=4 * (tokens + shared) * width, transcendentals=0
            ),
            compiler_params=pltpu.CompilerParams(vmem_limit_bytes=VMEM),
        )(act, maps)
    both = jnp.concatenate([act, maps], axis=0)
    return both.reshape(tokens + shared, devices, features).transpose(1, 0, 2)


def slot_chunks(width):
    size = min(width, 768)
    while width % size:
        size //= 2
    return [slice(k, k + size) for k in range(0, width, size)]


def slot_of(rows, starts):
    blocks = rows // BLOCK
    latest = jnp.max(jnp.where(starts <= blocks, starts, -1), axis=0, keepdims=True)
    return jnp.where(latest >= 0, latest, jnp.max(starts))


def own_rows(slot, first, size, rank):
    index = first // rank + lax.broadcasted_iota(jnp.int32, (size // rank, rank, 1), 0)
    return index == slot[None]


def placing(place, places):
    hit = lax.broadcasted_iota(jnp.int32, (places, place.shape[1]), 0) == place
    return jnp.where(hit, 1.0, 0.0).astype(jnp.bfloat16)


def all_rows(act, tokens):
    return jnp.concatenate([act[k, :tokens, :] for k in range(act.shape[0])], axis=0)


def of_source(sources, width):
    lane = lax.broadcasted_iota(jnp.int32, (sources, 1, width), 2)
    return lane // (width // sources) == lax.broadcasted_iota(
        jnp.int32, (sources, 1, width), 0
    )


def hidden_kernel(act, maps, rows, spots, starts, out):
    sources, share, width = act.shape[0], maps.shape[1], rows.shape[1]
    rank, places = out.shape[0] // sources, out.shape[1]
    slot = slot_of(rows[...], starts[...])
    every = all_rows(act, width // sources)
    total = jnp.zeros((rank, width), jnp.float32)
    for part in slot_chunks(maps.shape[0] * share):
        size = part.stop - part.start
        some = maps[part.start // share : part.stop // share].reshape(size, -1)
        each = dot(some, every, ((1,), (1,))).reshape(size // rank, rank, -1)
        total += jnp.sum(jnp.where(own_rows(slot, part.start, size, rank), each, 0.0), axis=0)
    total = jnp.where(of_source(sources, width), total[None], 0.0).reshape(out.shape[0], width)
    high = total.astype(jnp.bfloat16)
    low = (total - high.astype(jnp.float32)).astype(jnp.bfloat16)
    place = placing(spots[...], places)
    out[...] = dot(high, place, ((1,), (1,))) + dot(low, place, ((1,), (1,)))


def down_kernel(act, grad, rows, spots, starts, out, total):
    sources, width = act.shape[0], rows.shape[1]
    rank, places = grad.shape[0] // sources, grad.shape[1]
    step = pl.program_id(0)

    @pl.when(step == 0)
    def _():
        total[...] = jnp.zeros_like(total)

    slot = slot_of(rows[...], starts[...])
    every = all_rows(act, width // sources)
    wide = dot(grad[...], placing(spots[...], places), ((1,), (0,)))
    wide = wide.reshape(sources, rank, width)
    wide = jnp.sum(jnp.where(of_source(sources, width), wide, 0.0), axis=0, keepdims=True)
    for part in slot_chunks(total.shape[0]):
        size = part.stop - part.start
        placed = jnp.where(own_rows(slot, part.start, size, rank), wide, 0.0)
        placed = placed.reshape(size, -1).astype(jnp.bfloat16)
        total[part, :] += dot(placed, every, ((1,), (0,)))

    @pl.when(step == pl.num_programs(0) - 1)
    def _():
        out[...] = (adapter_scale * total[...]).astype(out.dtype)


def feature_calls(received, tokens, share, rank, places, starts):
    devices, packed, features = received.shape
    width = devices * share
    sources = 4
    grid = (devices // sources,)
    act = pl.BlockSpec((sources, packed, features), lambda j: (j, 0, 0))
    maps = pl.BlockSpec((devices, share, features), lambda j: (0, tokens // share, 0))
    rows = pl.BlockSpec((1, sources * tokens), lambda j: (0, j))
    begin = pl.BlockSpec((starts, 1), lambda j: (0, 0))
    placed = pl.BlockSpec((sources * rank, places), lambda j: (j, 0))
    cost = pl.CostEstimate(
        flops=2 * devices * tokens * width * features,
        bytes_accessed=2 * devices * tokens * features,
        transcendentals=0,
    )
    params = pltpu.CompilerParams(vmem_limit_bytes=VMEM)
    hidden = pl.pallas_call(
        hidden_kernel,
        grid=grid,
        in_specs=[act, maps, rows, rows, begin],
        out_specs=placed,
        out_shape=jax.ShapeDtypeStruct((devices * rank, places), jnp.float32),
        cost_estimate=cost,
        compiler_params=params,
    )
    down = pl.pallas_call(
        down_kernel,
        grid=grid,
        in_specs=[act, placed, rows, rows, begin],
        out_specs=pl.BlockSpec((width, features), lambda j: (0, 0)),
        out_shape=jax.ShapeDtypeStruct((width, features), jnp.bfloat16),
        scratch_shapes=[pltpu.VMEM((width, features), jnp.float32)],
        cost_estimate=cost,
        compiler_params=params,
    )
    return hidden, down


def local(
    activations,
    cotangent,
    token_layout_row,
    tenant_first_row,
    frozen_value_weight,
    adapter_down_maps,
    adapter_up_maps,
):
    devices = lax.axis_size("blk")
    device = lax.axis_index("blk")
    tokens = activations.shape[0]
    resident, rank, width = adapter_down_maps.shape
    out_width = cotangent.shape[1]
    features = width // devices
    share = resident * rank
    resident_rows = resident * BLOCK
    cap = resident_rows // devices
    start_ids = tenant_first_row // BLOCK

    pieces = weight_pieces(frozen_value_weight)

    first_block = device * resident
    block_numbers = first_block + jnp.arange(resident, dtype=jnp.int32)
    begin = starts_of(block_numbers, start_ids)
    hops = jnp.arange(1, HOPS + 1, dtype=jnp.int32)
    is_local = (begin >= first_block) & (begin <= block_numbers)
    home_slot = jnp.clip(begin - first_block, 0, resident - 1)
    own_slots = jnp.arange(resident, dtype=jnp.int32)
    chosen_slot = is_local[:, None] & (home_slot[:, None] == own_slots[None, :])
    others = lax.rem(device + hops, devices) * resident
    to_me = lax.div(starts_of(others, start_ids), resident) == device
    continues = begin[resident - 1] == first_block + own_slots
    last_map = jnp.concatenate(
        [
            lax.dynamic_index_in_dim(maps, home_slot[resident - 1], 0, keepdims=False)
            for maps in (adapter_down_maps, adapter_up_maps)
        ],
        axis=1,
    )
    homes = lax.rem(device + devices - hops, devices)
    from_home = lax.div(begin[:1], resident) == homes
    carried = jnp.zeros_like(last_map)
    for step in range(1, HOPS + 1):
        carried = jnp.where(from_home[step - 1], moved(last_map, step), carried)

    def of_blocks(maps, own):
        blocks = []
        for b in range(resident):
            chosen = own
            for k in range(b + 1):
                chosen = jnp.where(chosen_slot[b, k], maps[k], chosen)
            blocks.append(chosen)
        return jnp.concatenate(blocks, axis=0)

    down_blocks = of_blocks(adapter_down_maps, carried[:, :width])
    up_blocks = of_blocks(adapter_up_maps, carried[:, width:])

    sent_rows = pack_rows(token_layout_row, cotangent, devices, cap, features)
    own, _, across, _ = pieces
    sent_rows = after(sent_rows, *own[:CHUNKS], carried)
    got_rows = lax.all_to_all(sent_rows, "blk", split_axis=0, concat_axis=0)
    recv_cot = [
        got_rows[:, k * cap : (k + 1) * cap].reshape(resident_rows, features)
        for k in range(out_width // features)
    ]
    per_digit = -(-tokens // features)
    digits = got_rows[:, share : share + 5 * per_digit]
    digits = digits.reshape(devices, 5, per_digit * features)[:, :, :tokens]
    rows_all, place_all = from_digits(digits)

    spots = device * cap + jnp.arange(cap, dtype=jnp.int32)
    hit = place_all[:, None, :] == spots[None, :, None]
    row_in = rows_all - device * resident_rows + 1
    row_in = jnp.sum(jnp.where(hit, row_in[:, None, :], 0), axis=2).reshape(-1) - 1
    arrange = row_in[:, None] == jnp.arange(resident_rows, dtype=jnp.int32)[None, :]
    arrange = arrange.astype(jnp.bfloat16)
    in_block = row_in[:, None] // BLOCK == jnp.arange(share, dtype=jnp.int32)[None, :] // rank

    grad_in = sum(
        dot(part, up_blocks[:, k * features : (k + 1) * features], ((1,), (1,)))
        for k, part in enumerate(recv_cot)
    )
    grad_in = jnp.where(in_block, grad_in, 0.0).astype(jnp.bfloat16)
    grad_in = sum(grad_in[:, b * rank : (b + 1) * rank] for b in range(resident))
    grad_sent = grad_in.reshape(devices, cap, rank).transpose(1, 0, 2).reshape(cap, -1)

    flat_maps = adapter_down_maps.reshape(share, width)
    received = pack_features(activations, flat_maps, devices)
    received = after(received, got_rows)
    received = lax.all_to_all(received, "blk", split_axis=0, concat_axis=0)
    grad_all = to_all(after(grad_sent, received)).reshape(resident_rows, -1).T

    rows_all, place_all = rows_all.reshape(1, -1), place_all.reshape(1, -1)

    cot_rows = jnp.concatenate(
        [dot(arrange, part, ((0,), (0,))).astype(jnp.bfloat16) for part in recv_cot], axis=1
    )
    grad_rows = dot(arrange, grad_in, ((0,), (0,))).astype(jnp.bfloat16)
    group = lax.axis_index("groups")
    quarter = lax.rem(device, 4)
    firsts = [quarter, quarter ^ 1, quarter ^ 2, quarter ^ 3]
    if own[0].shape[1] % LANES == 0:
        out = None
        for piece, first in zip(pieces[:2], firsts):
            out, token = write_quarter(
                piece, first, group, cot_rows, grad_rows, down_blocks, out
            )
        place_all = after(place_all, token)
    else:
        weight = together(pieces, firsts, group)
        lora = [
            dot(
                grad_rows[b * BLOCK : (b + 1) * BLOCK],
                down_blocks[b * rank : (b + 1) * rank],
                ((1,), (0,)),
            )
            for b in range(resident)
        ]
        lora = (adapter_scale * jnp.concatenate(lora, axis=0)).astype(jnp.bfloat16)
        out = dot(cot_rows, weight, ((1,), (1,))) + lora.astype(jnp.float32)
        out = out.astype(jnp.bfloat16)

    starts = start_ids[:, None]
    hidden_call, down_call = feature_calls(
        received, tokens, share, rank, resident_rows, starts.shape[0]
    )
    shares = hidden_call(received, received, rows_all, place_all, starts)
    rows_all = after(rows_all, shares)
    down_f = down_call(received, grad_all, rows_all, place_all, starts)
    hidden = shares.T.reshape(devices, cap, -1)
    hidden = lax.all_to_all(hidden, "blk", split_axis=0, concat_axis=0)
    hidden = jnp.sum(hidden, axis=0).astype(jnp.bfloat16)
    hidden = hidden.reshape(cap, devices, rank).transpose(1, 0, 2).reshape(-1, rank)
    down_home = lax.all_to_all(down_f, "blk", split_axis=0, concat_axis=1, tiled=True)
    down_map_gradient = down_home.astype(jnp.float32).reshape(resident, rank, width)

    wide = jnp.where(in_block, jnp.concatenate([hidden] * resident, axis=1), 0)
    up_all = [dot(wide, part, ((0,), (0,))) for part in recv_cot]
    up_all = jnp.concatenate(up_all, axis=1).reshape(resident, rank, out_width)
    up_parts = [up_all[b] for b in range(resident)]

    tail = sum(jnp.where(is_local[b], 0.0, up_parts[b]) for b in range(resident))
    far = jnp.zeros_like(tail)
    for step in range(1, HOPS + 1):
        far = far + jnp.where(to_me[step - 1], moved(tail, -step), 0.0)
    up_grads = []
    for k in range(resident):
        total = jnp.where(continues[k], far, 0.0)
        for b in range(resident):
            total = total + jnp.where(chosen_slot[b, k], up_parts[b], 0.0)
        up_grads.append(adapter_scale * total)
    up_map_gradient = jnp.stack(up_grads)

    if own[0].shape[1] % LANES == 0:
        late = after(grad_rows, down_f)
        for piece, first in zip(pieces[2:], firsts[2:]):
            out, _ = write_quarter(piece, first, group, cot_rows, late, down_blocks, out)
    return (out, down_map_gradient, up_map_gradient)


def solution(mesh):
    return jax.shard_map(
        local,
        mesh=mesh,
        in_specs=(
            P(("groups", "blk"), None),
            P(("groups", "blk"), None),
            P(("groups", "blk")),
            P("groups"),
            P("blk", None),
            P(("groups", "blk"), None, None),
            P(("groups", "blk"), None, None),
        ),
        out_specs=(
            P(("groups", "blk"), None),
            P(("groups", "blk"), None, None),
            P(("groups", "blk"), None, None),
        ),
        check_vma=False,
    )
```

```python
import functools

import jax
import jax.numpy as jnp
from jax import lax
from jax.experimental import pallas as pl
from jax.experimental.pallas import tpu as pltpu
from jax.sharding import PartitionSpec as P

BLOCK = 128
HOPS = 4
LANES = 128
DIGIT = 64
VMEM = 56 << 20

adapter_scale = 2.0


def moved(value, steps):
    count = lax.axis_size("blk")
    return lax.ppermute(value, "blk", [(i, (i + steps) % count) for i in range(count)])


def to_all(value):
    count = lax.axis_size("blk")
    copies = jnp.broadcast_to(value[None], (count,) + value.shape)
    return lax.all_to_all(copies, "blk", split_axis=0, concat_axis=0)


def after(value, *others):
    anywhere = pl.BlockSpec(memory_space=pl.ANY)
    return pl.pallas_call(
        lambda *refs: None,
        in_specs=[anywhere] * (1 + len(others)),
        out_specs=anywhere,
        out_shape=jax.ShapeDtypeStruct(value.shape, value.dtype),
        input_output_aliases={0: 0},
        cost_estimate=pl.CostEstimate(flops=0, bytes_accessed=0, transcendentals=0),
        compiler_params=pltpu.CompilerParams(vmem_limit_bytes=VMEM),
    )(value, *others)


def dot(a, b, dims):
    return lax.dot_general(a, b, (dims, ((), ())), preferred_element_type=jnp.float32)


def starts_of(blocks, start_ids):
    latest = jnp.max(
        jnp.where(start_ids[None, :] <= blocks[:, None], start_ids[None, :], -1), axis=1
    )
    return jnp.where(latest >= 0, latest, jnp.max(start_ids))


def as_digits(rows, places):
    return (
        rows % DIGIT,
        rows // DIGIT % DIGIT,
        rows // (DIGIT * DIGIT),
        places % DIGIT,
        places // DIGIT,
    )


def from_digits(digits):
    low, middle, high, place, place_high = [digits[:, k].astype(jnp.int32) for k in range(5)]
    return (high * DIGIT + middle) * DIGIT + low, place_high * DIGIT + place


CHUNKS = 2


def near_lines(count):
    return count // 4 <= 4


def line_order():
    count = lax.axis_size("blk")
    shards = jnp.arange(count // 4, dtype=jnp.int32)
    if near_lines(count):
        return lax.rem(lax.div(lax.axis_index("blk"), 4) + count // 4 - shards, count // 4)
    return shards


def weight_pieces(weight):
    count = lax.axis_size("blk")
    half = weight.shape[0] // 2
    size = half // CHUNKS
    first = lax.axis_index("groups") * half

    def over(piece, bit):
        return lax.ppermute(piece, "blk", [(i, i ^ bit) for i in range(count)])

    def groups(piece):
        return lax.ppermute(piece, "groups", [(0, 1), (1, 0)])

    def column(chunk):
        mine = lax.dynamic_slice_in_dim(weight, first + chunk * size, size, 0)
        if near_lines(count):
            return jnp.stack([mine] + [moved(mine, 4 * k) for k in range(1, count // 4)])
        lines = [list(range(k, count, 4)) for k in range(4)]
        return lax.all_gather(mine, "blk", axis_index_groups=lines)

    columns = [column(k) for k in range(CHUNKS)]
    own = columns + [groups(piece) for piece in columns]
    across = [over(piece, 2) for piece in columns]

    def rest(late):
        mine = [after(piece, late) for piece in across]
        both = mine + [groups(piece) for piece in mine]
        return [both, [over(piece, 1) for piece in both]]

    return [own, [over(piece, 1) for piece in own]], rest


def quarter_kernel(where, cot, grad, down, *rest):
    pieces = rest[: 2 * CHUNKS]
    out, token = rest[-2:]
    token[...] = jnp.zeros_like(token)
    rank = grad.shape[1]
    lora = [
        adapter_scale
        * dot(
            grad[b * BLOCK : (b + 1) * BLOCK, :],
            down[b * rank : (b + 1) * rank, :],
            ((1,), (0,)),
        )
        for b in range(cot.shape[0] // BLOCK)
    ]
    lora = jnp.concatenate(lora, axis=0).astype(jnp.bfloat16).astype(jnp.float32)

    def product(group):
        order = pieces[group * CHUNKS :] + pieces[: group * CHUNKS]
        weight = jnp.concatenate([piece[0] for piece in order], axis=0)
        frozen = dot(cot[...], weight, ((1,), (1,)))
        out[...] = (frozen + lora).astype(jnp.bfloat16)

    for group in range(2):
        pl.when(where[where.shape[0] - 1] == group)(functools.partial(product, group))


def write_quarter(quarter, first, group, cot, grad, down, out=None):
    rows, depth = cot.shape
    width = down.shape[1]
    shards, part, _ = quarter[0].shape
    stripe = part * len(quarter)
    where = jnp.concatenate([4 * line_order() + first, group[None]]).astype(jnp.int32)
    specs = [
        pl.BlockSpec((rows, depth), lambda j, where: (0, 0)),
        pl.BlockSpec(grad.shape, lambda j, where: (0, 0)),
        pl.BlockSpec((down.shape[0], stripe), lambda j, where: (0, where[j])),
    ] + [pl.BlockSpec((1, part, depth), lambda j, where: (j, 0, 0)) for _ in quarter]
    args = [where, cot, grad, down] + quarter
    alias = {}
    if out is not None:
        specs.append(pl.BlockSpec(memory_space=pl.ANY))
        args.append(out)
        alias = {len(args) - 1: 0}
    return pl.pallas_call(
        quarter_kernel,
        grid_spec=pltpu.PrefetchScalarGridSpec(
            num_scalar_prefetch=1,
            grid=(shards,),
            in_specs=specs,
            out_specs=[
                pl.BlockSpec((rows, stripe), lambda j, where: (0, where[j])),
                pl.BlockSpec((8, LANES), lambda j, where: (0, 0)),
            ],
        ),
        out_shape=[
            jax.ShapeDtypeStruct((rows, width), jnp.bfloat16),
            jax.ShapeDtypeStruct((8, LANES), jnp.float32),
        ],
        input_output_aliases=alias,
        cost_estimate=pl.CostEstimate(
            flops=2 * rows * depth * stripe * shards,
            bytes_accessed=2 * (depth + rows) * stripe * shards,
            transcendentals=0,
        ),
        compiler_params=pltpu.CompilerParams(vmem_limit_bytes=VMEM),
    )(*args)


def together(pieces, firsts, group):
    shards, part, depth = pieces[0][0].shape
    weight = jnp.zeros((shards, 4, 2, CHUNKS, part, depth), jnp.bfloat16)
    order = line_order()
    for quarter, first in zip(pieces, firsts):
        for k, piece in enumerate(quarter):
            half = group if k < CHUNKS else 1 - group
            if not near_lines(4 * shards):
                place = (0, first, half, k % CHUNKS, 0, 0)
                weight = lax.dynamic_update_slice(weight, piece[:, None, None, None], place)
                continue
            for j in range(shards):
                place = (order[j], first, half, k % CHUNKS, 0, 0)
                shard = piece[j][None, None, None, None]
                weight = lax.dynamic_update_slice(weight, shard, place)
    return weight.reshape(-1, depth)


def rows_kernel(rows, cot, out, place):
    devices, packed, features = out.shape
    shared = packed - 16
    folds = cot.shape[1] // features
    cap = shared // folds
    target = rows[...] // (cap * devices)
    to = lax.broadcasted_iota(jnp.int32, (16, features), 0) == target
    first = lax.broadcasted_iota(jnp.int32, (features, features), 0)
    later = lax.broadcasted_iota(jnp.int32, (features, features), 1)
    earlier = jnp.where(first < later, 1.0, 0.0).astype(jnp.bfloat16)
    ahead = dot(jnp.where(to, 1.0, 0.0).astype(jnp.bfloat16), earlier, ((1,), (0,)))
    ahead = jnp.sum(jnp.where(to, ahead, 0.0), axis=0, keepdims=True)
    place[...] = target * cap + ahead.astype(jnp.int32)
    which = lax.broadcasted_iota(jnp.int32, (16, features), 0)
    digits = jnp.zeros((16, features), jnp.int32)
    for k, digit in enumerate(as_digits(rows[...], place[...])):
        digits = jnp.where(which == k, digit, digits)
    digits = digits.astype(jnp.float32).astype(out.dtype)
    send = placing(place[:, : cot.shape[0]], cap * devices)
    for f in range(folds):
        sent = dot(send, cot[:, f * features : (f + 1) * features], ((1,), (0,)))
        for k in range(devices):
            some = sent[k * cap : (k + 1) * cap].astype(out.dtype)
            out[k, f * cap : (f + 1) * cap, :] = some
    for k in range(devices):
        out[k, shared:, :] = digits


def pack_rows(rows, cot, devices, cap, features):
    tokens = rows.shape[0]
    folds = cot.shape[1] // features
    if features % LANES == 0 and cap % 8 == 0 and features >= tokens and devices <= 16:
        padding = jnp.full((features - tokens,), 16 * cap * devices, jnp.int32)
        return pl.pallas_call(
            rows_kernel,
            out_shape=jax.ShapeDtypeStruct((devices, folds * cap + 16, features), cot.dtype),
            scratch_shapes=[pltpu.VMEM((1, features), jnp.int32)],
            cost_estimate=pl.CostEstimate(
                flops=2 * devices * cap * tokens * cot.shape[1],
                bytes_accessed=6 * cot.size,
                transcendentals=0,
            ),
            compiler_params=pltpu.CompilerParams(vmem_limit_bytes=VMEM),
        )(jnp.concatenate([rows, padding])[None], cot)
    target = rows // (cap * devices)
    order = jnp.arange(tokens, dtype=jnp.int32)
    before = (target[:, None] == target[None, :]) & (order[None, :] < order[:, None])
    place = target * cap + jnp.sum(before.astype(jnp.int32), axis=1)
    send = jnp.arange(cap * devices, dtype=jnp.int32)[:, None] == place[None, :]
    sent = dot(send.astype(jnp.bfloat16), cot, ((1,), (0,))).astype(jnp.bfloat16)
    sent = sent.reshape(devices, cap, cot.shape[1])
    digits = jnp.stack(as_digits(rows, place)).astype(jnp.bfloat16)
    digits = jnp.pad(digits, ((0, 0), (0, -tokens % features))).reshape(-1, features)
    digits = jnp.pad(digits, ((0, -digits.shape[0] % 16), (0, 0)))
    parts = [sent[:, :, k : k + features] for k in range(0, cot.shape[1], features)]
    parts += [jnp.broadcast_to(digits[None], (devices,) + digits.shape)]
    return jnp.concatenate(parts, axis=1)


def features_kernel(act, maps, out):
    targets, _, features = out.shape
    tokens = act.shape[0]
    for k in range(targets):
        part = slice(k * features, (k + 1) * features)
        out[k, :tokens, :] = act[:, part]
        out[k, tokens:, :] = maps[:, part]


def pack_features(act, maps, devices):
    tokens, width = act.shape
    features = width // devices
    shared = maps.shape[0]
    targets = 4
    if features % LANES == 0:
        return pl.pallas_call(
            features_kernel,
            grid=(devices // targets,),
            in_specs=[
                pl.BlockSpec((tokens, targets * features), lambda j: (0, j)),
                pl.BlockSpec((shared, targets * features), lambda j: (0, j)),
            ],
            out_specs=pl.BlockSpec((targets, tokens + shared, features), lambda j: (j, 0, 0)),
            out_shape=jax.ShapeDtypeStruct((devices, tokens + shared, features), act.dtype),
            cost_estimate=pl.CostEstimate(
                flops=0, bytes_accessed=4 * (tokens + shared) * width, transcendentals=0
            ),
            compiler_params=pltpu.CompilerParams(vmem_limit_bytes=VMEM),
        )(act, maps)
    both = jnp.concatenate([act, maps], axis=0)
    return both.reshape(tokens + shared, devices, features).transpose(1, 0, 2)


def slot_chunks(width):
    size = min(width, 768)
    while width % size:
        size //= 2
    return [slice(k, k + size) for k in range(0, width, size)]


def slot_of(rows, starts):
    blocks = rows // BLOCK
    latest = jnp.max(jnp.where(starts <= blocks, starts, -1), axis=0, keepdims=True)
    return jnp.where(latest >= 0, latest, jnp.max(starts))


def own_rows(slot, first, size, rank):
    index = first // rank + lax.broadcasted_iota(jnp.int32, (size // rank, rank, 1), 0)
    return index == slot[None]


def placing(place, places):
    hit = lax.broadcasted_iota(jnp.int32, (places, place.shape[1]), 0) == place
    return jnp.where(hit, 1.0, 0.0).astype(jnp.bfloat16)


def all_rows(act, tokens):
    return jnp.concatenate([act[k, :tokens, :] for k in range(act.shape[0])], axis=0)


def of_source(sources, width):
    lane = lax.broadcasted_iota(jnp.int32, (sources, 1, width), 2)
    return lane // (width // sources) == lax.broadcasted_iota(
        jnp.int32, (sources, 1, width), 0
    )


def hidden_kernel(act, maps, rows, spots, starts, out):
    sources, share, width = act.shape[0], maps.shape[1], rows.shape[1]
    rank, places = out.shape[0] // sources, out.shape[1]
    slot = slot_of(rows[...], starts[...])
    every = all_rows(act, width // sources)
    total = jnp.zeros((rank, width), jnp.float32)
    for part in slot_chunks(maps.shape[0] * share):
        size = part.stop - part.start
        some = maps[part.start // share : part.stop // share].reshape(size, -1)
        each = dot(some, every, ((1,), (1,))).reshape(size // rank, rank, -1)
        total += jnp.sum(jnp.where(own_rows(slot, part.start, size, rank), each, 0.0), axis=0)
    total = jnp.where(of_source(sources, width), total[None], 0.0).reshape(out.shape[0], width)
    high = total.astype(jnp.bfloat16)
    low = (total - high.astype(jnp.float32)).astype(jnp.bfloat16)
    place = placing(spots[...], places)
    out[...] = dot(high, place, ((1,), (1,))) + dot(low, place, ((1,), (1,)))


def down_kernel(act, grad, rows, spots, starts, out, total):
    sources, width = act.shape[0], rows.shape[1]
    rank, places = grad.shape[0] // sources, grad.shape[1]
    step = pl.program_id(0)

    @pl.when(step == 0)
    def _():
        total[...] = jnp.zeros_like(total)

    slot = slot_of(rows[...], starts[...])
    every = all_rows(act, width // sources)
    wide = dot(grad[...], placing(spots[...], places), ((1,), (0,)))
    wide = wide.reshape(sources, rank, width)
    wide = jnp.sum(jnp.where(of_source(sources, width), wide, 0.0), axis=0, keepdims=True)
    for part in slot_chunks(total.shape[0]):
        size = part.stop - part.start
        placed = jnp.where(own_rows(slot, part.start, size, rank), wide, 0.0)
        placed = placed.reshape(size, -1).astype(jnp.bfloat16)
        total[part, :] += dot(placed, every, ((1,), (0,)))

    @pl.when(step == pl.num_programs(0) - 1)
    def _():
        out[...] = (adapter_scale * total[...]).astype(out.dtype)


def feature_calls(received, tokens, share, rank, places, starts):
    devices, packed, features = received.shape
    width = devices * share
    sources = 4
    grid = (devices // sources,)
    act = pl.BlockSpec((sources, packed, features), lambda j: (j, 0, 0))
    maps = pl.BlockSpec((devices, share, features), lambda j: (0, tokens // share, 0))
    rows = pl.BlockSpec((1, sources * tokens), lambda j: (0, j))
    begin = pl.BlockSpec((starts, 1), lambda j: (0, 0))
    placed = pl.BlockSpec((sources * rank, places), lambda j: (j, 0))
    cost = pl.CostEstimate(
        flops=2 * devices * tokens * width * features,
        bytes_accessed=2 * devices * tokens * features,
        transcendentals=0,
    )
    params = pltpu.CompilerParams(vmem_limit_bytes=VMEM)
    hidden = pl.pallas_call(
        hidden_kernel,
        grid=grid,
        in_specs=[act, maps, rows, rows, begin],
        out_specs=placed,
        out_shape=jax.ShapeDtypeStruct((devices * rank, places), jnp.float32),
        cost_estimate=cost,
        compiler_params=params,
    )
    down = pl.pallas_call(
        down_kernel,
        grid=grid,
        in_specs=[act, placed, rows, rows, begin],
        out_specs=pl.BlockSpec((width, features), lambda j: (0, 0)),
        out_shape=jax.ShapeDtypeStruct((width, features), jnp.bfloat16),
        scratch_shapes=[pltpu.VMEM((width, features), jnp.float32)],
        cost_estimate=cost,
        compiler_params=params,
    )
    return hidden, down


def local(
    activations,
    cotangent,
    token_layout_row,
    tenant_first_row,
    frozen_value_weight,
    adapter_down_maps,
    adapter_up_maps,
):
    devices = lax.axis_size("blk")
    device = lax.axis_index("blk")
    tokens = activations.shape[0]
    resident, rank, width = adapter_down_maps.shape
    out_width = cotangent.shape[1]
    features = width // devices
    share = resident * rank
    resident_rows = resident * BLOCK
    cap = resident_rows // devices
    start_ids = tenant_first_row // BLOCK

    pieces, rest_of_pieces = weight_pieces(frozen_value_weight)

    first_block = device * resident
    block_numbers = first_block + jnp.arange(resident, dtype=jnp.int32)
    begin = starts_of(block_numbers, start_ids)
    hops = jnp.arange(1, HOPS + 1, dtype=jnp.int32)
    is_local = (begin >= first_block) & (begin <= block_numbers)
    home_slot = jnp.clip(begin - first_block, 0, resident - 1)
    row, place_in = jnp.arange(share, dtype=jnp.int32), jnp.arange(HOPS * rank, dtype=jnp.int32)
    same = row[:, None] % rank == row[None, :] % rank
    same_far = row[:, None] % rank == place_in[None, :] % rank
    others = lax.rem(device + hops, devices) * resident
    to_me = lax.div(starts_of(others, start_ids), resident) == device
    home_of = jnp.where(is_local, home_slot, -1)
    home_of = jnp.broadcast_to(home_of[:, None], (resident, rank)).reshape(-1)
    from_own = same & (home_of[:, None] == row[None, :] // rank)
    to_own = same & (home_of[None, :] == row[:, None] // rank)
    remote = same[:rank] & (home_of < 0)[None, :]
    continues = (begin[resident - 1] - first_block) == row // rank
    to_me = jnp.broadcast_to(to_me[:, None], (HOPS, rank)).reshape(-1)
    from_tails = same_far & continues[:, None] & to_me[None, :]
    last_map = jnp.concatenate(
        [
            lax.dynamic_index_in_dim(maps, home_slot[resident - 1], 0, keepdims=False)
            for maps in (adapter_down_maps, adapter_up_maps)
        ],
        axis=1,
    )
    homes = lax.rem(device + devices - hops, devices)
    from_home = lax.div(begin[:1], resident) == homes
    from_home = jnp.broadcast_to(from_home[:, None], (HOPS, rank)).reshape(-1)
    from_far = same_far & (home_of < 0)[:, None] & from_home[None, :]
    carried = [moved(last_map, step) for step in range(1, HOPS + 1)]
    every_carried = jnp.concatenate(carried, axis=0)

    def of_blocks(maps, far):
        own = dot(from_own.astype(jnp.bfloat16), maps.reshape(share, -1), ((1,), (0,)))
        return (own + dot(from_far.astype(jnp.bfloat16), far, ((1,), (0,)))).astype(jnp.bfloat16)

    down_blocks = of_blocks(adapter_down_maps, every_carried[:, :width])
    up_blocks = of_blocks(adapter_up_maps, every_carried[:, width:])

    sent_rows = pack_rows(token_layout_row, cotangent, devices, cap, features)
    own = pieces[0]
    sent_rows = after(sent_rows, *own[:CHUNKS], *carried)
    got_rows = lax.all_to_all(sent_rows, "blk", split_axis=0, concat_axis=0)
    recv_cot = [
        got_rows[:, k * cap : (k + 1) * cap].reshape(resident_rows, features)
        for k in range(out_width // features)
    ]
    per_digit = -(-tokens // features)
    digits = got_rows[:, share : share + 5 * per_digit]
    digits = digits.reshape(devices, 5, per_digit * features)[:, :, :tokens]
    rows_all, place_all = from_digits(digits)

    spots = device * cap + jnp.arange(cap, dtype=jnp.int32)
    hit = place_all[:, None, :] == spots[None, :, None]
    row_in = rows_all - device * resident_rows + 1
    row_in = jnp.sum(jnp.where(hit, row_in[:, None, :], 0), axis=2).reshape(-1) - 1
    arrange = row_in[:, None] == jnp.arange(resident_rows, dtype=jnp.int32)[None, :]
    arrange = arrange.astype(jnp.bfloat16)
    in_block = row_in[:, None] // BLOCK == jnp.arange(share, dtype=jnp.int32)[None, :] // rank

    grad_in = sum(
        dot(part, up_blocks[:, k * features : (k + 1) * features], ((1,), (1,)))
        for k, part in enumerate(recv_cot)
    )
    grad_in = jnp.where(in_block, grad_in, 0.0).astype(jnp.bfloat16)
    grad_in = sum(grad_in[:, b * rank : (b + 1) * rank] for b in range(resident))
    grad_sent = grad_in.reshape(devices, cap, rank).transpose(1, 0, 2).reshape(cap, -1)

    flat_maps = adapter_down_maps.reshape(share, width)
    received = pack_features(activations, flat_maps, devices)
    received = after(received, got_rows)
    received = lax.all_to_all(received, "blk", split_axis=0, concat_axis=0)
    grad_all = to_all(after(grad_sent, received)).reshape(resident_rows, -1).T

    rows_all, place_all = rows_all.reshape(1, -1), place_all.reshape(1, -1)

    cot_rows = jnp.concatenate(
        [dot(arrange, part, ((0,), (0,))).astype(jnp.bfloat16) for part in recv_cot], axis=1
    )
    grad_rows = dot(arrange, grad_in, ((0,), (0,))).astype(jnp.bfloat16)
    group = lax.axis_index("groups")
    quarter = lax.rem(device, 4)
    firsts = [quarter, quarter ^ 1, quarter ^ 2, quarter ^ 3]
    tiled = own[0].shape[1] % LANES == 0
    if tiled:
        out = None
        for piece, first in zip(pieces, firsts):
            out, token = write_quarter(
                piece, first, group, cot_rows, grad_rows, down_blocks, out
            )
        place_all = after(place_all, token)

    starts = start_ids[:, None]
    hidden_call, down_call = feature_calls(
        received, tokens, share, rank, resident_rows, starts.shape[0]
    )
    shares = hidden_call(received, received, rows_all, place_all, starts)
    rows_all = after(rows_all, shares)
    down_f = down_call(received, grad_all, rows_all, place_all, starts)
    hidden = shares.T.reshape(devices, cap, -1)
    hidden = lax.all_to_all(hidden, "blk", split_axis=0, concat_axis=0)
    hidden = jnp.sum(hidden, axis=0).astype(jnp.bfloat16)
    hidden = hidden.reshape(cap, devices, rank).transpose(1, 0, 2).reshape(-1, rank)
    down_home = lax.all_to_all(down_f, "blk", split_axis=0, concat_axis=1, tiled=True)
    down_map_gradient = down_home.astype(jnp.float32).reshape(resident, rank, width)

    wide = jnp.where(in_block, jnp.concatenate([hidden] * resident, axis=1), 0)
    up_all = [dot(wide, part, ((0,), (0,))) for part in recv_cot]
    up_all = jnp.concatenate(up_all, axis=1)

    exact = lax.Precision.HIGHEST
    tail = jnp.dot(remote.astype(jnp.float32), up_all, precision=exact)
    tails = jnp.concatenate([moved(tail, -step) for step in range(1, HOPS + 1)], axis=0)
    up_grads = jnp.dot(to_own.astype(jnp.float32), up_all, precision=exact)
    up_grads = up_grads + jnp.dot(from_tails.astype(jnp.float32), tails, precision=exact)
    up_map_gradient = (adapter_scale * up_grads).reshape(resident, rank, out_width)

    others = rest_of_pieces(shares)
    if tiled:
        late = after(grad_rows, down_f)
        for piece, first in zip(others, firsts[2:]):
            out, _ = write_quarter(piece, first, group, cot_rows, late, down_blocks, out)
    else:
        weight = together(pieces + others, firsts, group)
        lora = [
            dot(
                grad_rows[b * BLOCK : (b + 1) * BLOCK],
                down_blocks[b * rank : (b + 1) * rank],
                ((1,), (0,)),
            )
            for b in range(resident)
        ]
        lora = (adapter_scale * jnp.concatenate(lora, axis=0)).astype(jnp.bfloat16)
        out = dot(cot_rows, weight, ((1,), (1,))) + lora.astype(jnp.float32)
        out = out.astype(jnp.bfloat16)
    return (out, down_map_gradient, up_map_gradient)


def solution(mesh):
    return jax.shard_map(
        local,
        mesh=mesh,
        in_specs=(
            P(("groups", "blk"), None),
            P(("groups", "blk"), None),
            P(("groups", "blk")),
            P("groups"),
            P("blk", None),
            P(("groups", "blk"), None, None),
            P(("groups", "blk"), None, None),
        ),
        out_specs=(
            P(("groups", "blk"), None),
            P(("groups", "blk"), None, None),
            P(("groups", "blk"), None, None),
        ),
        check_vma=False,
    )
```

```python
import functools

import jax
import jax.numpy as jnp
from jax import lax
from jax.experimental import pallas as pl
from jax.experimental.pallas import tpu as pltpu
from jax.sharding import PartitionSpec as P

BLOCK = 128
HOPS = 4
LANES = 128
DIGIT = 64
VMEM = 56 << 20

adapter_scale = 2.0


def moved(value, steps):
    count = lax.axis_size("blk")
    return lax.ppermute(value, "blk", [(i, (i + steps) % count) for i in range(count)])


def to_all(value):
    count = lax.axis_size("blk")
    copies = jnp.broadcast_to(value[None], (count,) + value.shape)
    return lax.all_to_all(copies, "blk", split_axis=0, concat_axis=0)


def after(value, *others):
    anywhere = pl.BlockSpec(memory_space=pl.ANY)
    return pl.pallas_call(
        lambda *refs: None,
        in_specs=[anywhere] * (1 + len(others)),
        out_specs=anywhere,
        out_shape=jax.ShapeDtypeStruct(value.shape, value.dtype),
        input_output_aliases={0: 0},
        cost_estimate=pl.CostEstimate(flops=0, bytes_accessed=0, transcendentals=0),
        compiler_params=pltpu.CompilerParams(vmem_limit_bytes=VMEM),
    )(value, *others)


def dot(a, b, dims):
    return lax.dot_general(a, b, (dims, ((), ())), preferred_element_type=jnp.float32)


def starts_of(blocks, start_ids):
    latest = jnp.max(
        jnp.where(start_ids[None, :] <= blocks[:, None], start_ids[None, :], -1), axis=1
    )
    return jnp.where(latest >= 0, latest, jnp.max(start_ids))


def as_digits(rows, places):
    return (
        rows % DIGIT,
        rows // DIGIT % DIGIT,
        rows // (DIGIT * DIGIT),
        places % DIGIT,
        places // DIGIT,
    )


def from_digits(digits):
    low, middle, high, place, place_high = [digits[:, k].astype(jnp.int32) for k in range(5)]
    return (high * DIGIT + middle) * DIGIT + low, place_high * DIGIT + place


CHUNKS = 2


def near_lines(count):
    return count // 4 <= 4


def line_order():
    count = lax.axis_size("blk")
    shards = jnp.arange(count // 4, dtype=jnp.int32)
    if near_lines(count):
        return lax.rem(lax.div(lax.axis_index("blk"), 4) + count // 4 - shards, count // 4)
    return shards


def weight_pieces(weight):
    count = lax.axis_size("blk")
    half = weight.shape[0] // 2
    size = half // CHUNKS
    first = lax.axis_index("groups") * half

    def over(piece, bit):
        return lax.ppermute(piece, "blk", [(i, i ^ bit) for i in range(count)])

    def groups(piece):
        return lax.ppermute(piece, "groups", [(0, 1), (1, 0)])

    def column(chunk):
        mine = lax.dynamic_slice_in_dim(weight, first + chunk * size, size, 0)
        if near_lines(count):
            return jnp.stack([mine] + [moved(mine, 4 * k) for k in range(1, count // 4)])
        lines = [list(range(k, count, 4)) for k in range(4)]
        return lax.all_gather(mine, "blk", axis_index_groups=lines)

    columns = [column(k) for k in range(CHUNKS)]
    own = columns + [groups(piece) for piece in columns]
    across = [over(piece, 2) for piece in columns]

    def rest(late):
        mine = [after(piece, late) for piece in across]
        both = mine + [groups(piece) for piece in mine]
        return [both, [over(piece, 1) for piece in both]]

    return [own, [over(piece, 1) for piece in own]], rest


def quarter_kernel(where, cot, grad, down, *rest):
    pieces = rest[: 2 * CHUNKS]
    out, token = rest[-2:]
    token[...] = jnp.zeros_like(token)
    rank = grad.shape[1]
    lora = [
        adapter_scale
        * dot(
            grad[b * BLOCK : (b + 1) * BLOCK, :],
            down[b * rank : (b + 1) * rank, :],
            ((1,), (0,)),
        )
        for b in range(cot.shape[0] // BLOCK)
    ]
    lora = jnp.concatenate(lora, axis=0).astype(jnp.bfloat16).astype(jnp.float32)

    def product(group):
        order = pieces[group * CHUNKS :] + pieces[: group * CHUNKS]
        weight = jnp.concatenate([piece[0] for piece in order], axis=0)
        frozen = dot(cot[...], weight, ((1,), (1,)))
        out[...] = (frozen + lora).astype(jnp.bfloat16)

    for group in range(2):
        pl.when(where[where.shape[0] - 1] == group)(functools.partial(product, group))


def write_quarter(quarter, first, group, cot, grad, down, out=None):
    rows, depth = cot.shape
    width = down.shape[1]
    shards, part, _ = quarter[0].shape
    stripe = part * len(quarter)
    where = jnp.concatenate([4 * line_order() + first, group[None]]).astype(jnp.int32)
    specs = [
        pl.BlockSpec((rows, depth), lambda j, where: (0, 0)),
        pl.BlockSpec(grad.shape, lambda j, where: (0, 0)),
        pl.BlockSpec((down.shape[0], stripe), lambda j, where: (0, where[j])),
    ] + [pl.BlockSpec((1, part, depth), lambda j, where: (j, 0, 0)) for _ in quarter]
    args = [where, cot, grad, down] + quarter
    alias = {}
    if out is not None:
        specs.append(pl.BlockSpec(memory_space=pl.ANY))
        args.append(out)
        alias = {len(args) - 1: 0}
    return pl.pallas_call(
        quarter_kernel,
        grid_spec=pltpu.PrefetchScalarGridSpec(
            num_scalar_prefetch=1,
            grid=(shards,),
            in_specs=specs,
            out_specs=[
                pl.BlockSpec((rows, stripe), lambda j, where: (0, where[j])),
                pl.BlockSpec((8, LANES), lambda j, where: (0, 0)),
            ],
        ),
        out_shape=[
            jax.ShapeDtypeStruct((rows, width), jnp.bfloat16),
            jax.ShapeDtypeStruct((8, LANES), jnp.float32),
        ],
        input_output_aliases=alias,
        cost_estimate=pl.CostEstimate(
            flops=2 * rows * depth * stripe * shards,
            bytes_accessed=2 * (depth + rows) * stripe * shards,
            transcendentals=0,
        ),
        compiler_params=pltpu.CompilerParams(vmem_limit_bytes=VMEM),
    )(*args)


def together(pieces, firsts, group):
    shards, part, depth = pieces[0][0].shape
    weight = jnp.zeros((shards, 4, 2, CHUNKS, part, depth), jnp.bfloat16)
    order = line_order()
    for quarter, first in zip(pieces, firsts):
        for k, piece in enumerate(quarter):
            half = group if k < CHUNKS else 1 - group
            if not near_lines(4 * shards):
                place = (0, first, half, k % CHUNKS, 0, 0)
                weight = lax.dynamic_update_slice(weight, piece[:, None, None, None], place)
                continue
            for j in range(shards):
                place = (order[j], first, half, k % CHUNKS, 0, 0)
                shard = piece[j][None, None, None, None]
                weight = lax.dynamic_update_slice(weight, shard, place)
    return weight.reshape(-1, depth)


def rows_kernel(rows, cot, out, place):
    devices, packed, features = out.shape
    shared = packed - 16
    folds = cot.shape[1] // features
    cap = shared // folds
    target = rows[...] // (cap * devices)
    to = lax.broadcasted_iota(jnp.int32, (16, features), 0) == target
    first = lax.broadcasted_iota(jnp.int32, (features, features), 0)
    later = lax.broadcasted_iota(jnp.int32, (features, features), 1)
    earlier = jnp.where(first < later, 1.0, 0.0).astype(jnp.bfloat16)
    ahead = dot(jnp.where(to, 1.0, 0.0).astype(jnp.bfloat16), earlier, ((1,), (0,)))
    ahead = jnp.sum(jnp.where(to, ahead, 0.0), axis=0, keepdims=True)
    place[...] = target * cap + ahead.astype(jnp.int32)
    which = lax.broadcasted_iota(jnp.int32, (16, features), 0)
    digits = jnp.zeros((16, features), jnp.int32)
    for k, digit in enumerate(as_digits(rows[...], place[...])):
        digits = jnp.where(which == k, digit, digits)
    digits = digits.astype(jnp.float32).astype(out.dtype)
    send = placing(place[:, : cot.shape[0]], cap * devices)
    for f in range(folds):
        sent = dot(send, cot[:, f * features : (f + 1) * features], ((1,), (0,)))
        for k in range(devices):
            some = sent[k * cap : (k + 1) * cap].astype(out.dtype)
            out[k, f * cap : (f + 1) * cap, :] = some
    for k in range(devices):
        out[k, shared:, :] = digits


def pack_rows(rows, cot, devices, cap, features):
    tokens = rows.shape[0]
    folds = cot.shape[1] // features
    if features % LANES == 0 and cap % 8 == 0 and features >= tokens and devices <= 16:
        padding = jnp.full((features - tokens,), 16 * cap * devices, jnp.int32)
        return pl.pallas_call(
            rows_kernel,
            out_shape=jax.ShapeDtypeStruct((devices, folds * cap + 16, features), cot.dtype),
            scratch_shapes=[pltpu.VMEM((1, features), jnp.int32)],
            cost_estimate=pl.CostEstimate(
                flops=2 * devices * cap * tokens * cot.shape[1],
                bytes_accessed=6 * cot.size,
                transcendentals=0,
            ),
            compiler_params=pltpu.CompilerParams(vmem_limit_bytes=VMEM),
        )(jnp.concatenate([rows, padding])[None], cot)
    target = rows // (cap * devices)
    order = jnp.arange(tokens, dtype=jnp.int32)
    before = (target[:, None] == target[None, :]) & (order[None, :] < order[:, None])
    place = target * cap + jnp.sum(before.astype(jnp.int32), axis=1)
    send = jnp.arange(cap * devices, dtype=jnp.int32)[:, None] == place[None, :]
    sent = dot(send.astype(jnp.bfloat16), cot, ((1,), (0,))).astype(jnp.bfloat16)
    sent = sent.reshape(devices, cap, cot.shape[1])
    digits = jnp.stack(as_digits(rows, place)).astype(jnp.bfloat16)
    digits = jnp.pad(digits, ((0, 0), (0, -tokens % features))).reshape(-1, features)
    digits = jnp.pad(digits, ((0, -digits.shape[0] % 16), (0, 0)))
    parts = [sent[:, :, k : k + features] for k in range(0, cot.shape[1], features)]
    parts += [jnp.broadcast_to(digits[None], (devices,) + digits.shape)]
    return jnp.concatenate(parts, axis=1)


def features_kernel(act, maps, out):
    targets, _, features = out.shape
    tokens = act.shape[0]
    for k in range(targets):
        part = slice(k * features, (k + 1) * features)
        out[k, :tokens, :] = act[:, part]
        out[k, tokens:, :] = maps[:, part]


def pack_features(act, maps, devices):
    tokens, width = act.shape
    features = width // devices
    shared = maps.shape[0]
    targets = 4
    if features % LANES == 0:
        return pl.pallas_call(
            features_kernel,
            grid=(devices // targets,),
            in_specs=[
                pl.BlockSpec((tokens, targets * features), lambda j: (0, j)),
                pl.BlockSpec((shared, targets * features), lambda j: (0, j)),
            ],
            out_specs=pl.BlockSpec((targets, tokens + shared, features), lambda j: (j, 0, 0)),
            out_shape=jax.ShapeDtypeStruct((devices, tokens + shared, features), act.dtype),
            cost_estimate=pl.CostEstimate(
                flops=0, bytes_accessed=4 * (tokens + shared) * width, transcendentals=0
            ),
            compiler_params=pltpu.CompilerParams(vmem_limit_bytes=VMEM),
        )(act, maps)
    both = jnp.concatenate([act, maps], axis=0)
    return both.reshape(tokens + shared, devices, features).transpose(1, 0, 2)


def slot_chunks(width):
    size = min(width, 768)
    while width % size:
        size //= 2
    return [slice(k, k + size) for k in range(0, width, size)]


def slot_of(rows, starts):
    blocks = rows // BLOCK
    latest = jnp.max(jnp.where(starts <= blocks, starts, -1), axis=0, keepdims=True)
    return jnp.where(latest >= 0, latest, jnp.max(starts))


def own_rows(slot, first, size, rank):
    index = first // rank + lax.broadcasted_iota(jnp.int32, (size // rank, rank, 1), 0)
    return index == slot[None]


def placing(place, places):
    hit = lax.broadcasted_iota(jnp.int32, (places, place.shape[1]), 0) == place
    return jnp.where(hit, 1.0, 0.0).astype(jnp.bfloat16)


def all_rows(act, tokens):
    return jnp.concatenate([act[k, :tokens, :] for k in range(act.shape[0])], axis=0)


def of_source(sources, width):
    lane = lax.broadcasted_iota(jnp.int32, (sources, 1, width), 2)
    return lane // (width // sources) == lax.broadcasted_iota(
        jnp.int32, (sources, 1, width), 0
    )


def hidden_kernel(act, maps, rows, spots, starts, out):
    sources, share, width = act.shape[0], maps.shape[1], rows.shape[1]
    rank, places = out.shape[0] // sources, out.shape[1]
    slot = slot_of(rows[...], starts[...])
    every = all_rows(act, width // sources)
    total = jnp.zeros((rank, width), jnp.float32)
    for part in slot_chunks(maps.shape[0] * share):
        size = part.stop - part.start
        some = maps[part.start // share : part.stop // share].reshape(size, -1)
        each = dot(some, every, ((1,), (1,))).reshape(size // rank, rank, -1)
        total += jnp.sum(jnp.where(own_rows(slot, part.start, size, rank), each, 0.0), axis=0)
    total = jnp.where(of_source(sources, width), total[None], 0.0).reshape(out.shape[0], width)
    high = total.astype(jnp.bfloat16)
    low = (total - high.astype(jnp.float32)).astype(jnp.bfloat16)
    place = placing(spots[...], places)
    out[...] = dot(high, place, ((1,), (1,))) + dot(low, place, ((1,), (1,)))


def down_kernel(act, grad, rows, spots, starts, out, total):
    sources, width = act.shape[0], rows.shape[1]
    rank, places = grad.shape[0] // sources, grad.shape[1]
    step = pl.program_id(0)

    @pl.when(step == 0)
    def _():
        total[...] = jnp.zeros_like(total)

    slot = slot_of(rows[...], starts[...])
    every = all_rows(act, width // sources)
    wide = dot(grad[...], placing(spots[...], places), ((1,), (0,)))
    wide = wide.reshape(sources, rank, width)
    wide = jnp.sum(jnp.where(of_source(sources, width), wide, 0.0), axis=0, keepdims=True)
    for part in slot_chunks(total.shape[0]):
        size = part.stop - part.start
        placed = jnp.where(own_rows(slot, part.start, size, rank), wide, 0.0)
        placed = placed.reshape(size, -1).astype(jnp.bfloat16)
        total[part, :] += dot(placed, every, ((1,), (0,)))

    @pl.when(step == pl.num_programs(0) - 1)
    def _():
        out[...] = (adapter_scale * total[...]).astype(out.dtype)


def feature_calls(received, tokens, share, rank, places, starts):
    devices, packed, features = received.shape
    width = devices * share
    sources = 4
    grid = (devices // sources,)
    act = pl.BlockSpec((sources, packed, features), lambda j: (j, 0, 0))
    maps = pl.BlockSpec((devices, share, features), lambda j: (0, tokens // share, 0))
    rows = pl.BlockSpec((1, sources * tokens), lambda j: (0, j))
    begin = pl.BlockSpec((starts, 1), lambda j: (0, 0))
    placed = pl.BlockSpec((sources * rank, places), lambda j: (j, 0))
    cost = pl.CostEstimate(
        flops=2 * devices * tokens * width * features,
        bytes_accessed=2 * devices * tokens * features,
        transcendentals=0,
    )
    params = pltpu.CompilerParams(vmem_limit_bytes=VMEM)
    hidden = pl.pallas_call(
        hidden_kernel,
        grid=grid,
        in_specs=[act, maps, rows, rows, begin],
        out_specs=placed,
        out_shape=jax.ShapeDtypeStruct((devices * rank, places), jnp.float32),
        cost_estimate=cost,
        compiler_params=params,
    )
    down = pl.pallas_call(
        down_kernel,
        grid=grid,
        in_specs=[act, placed, rows, rows, begin],
        out_specs=pl.BlockSpec((width, features), lambda j: (0, 0)),
        out_shape=jax.ShapeDtypeStruct((width, features), jnp.bfloat16),
        scratch_shapes=[pltpu.VMEM((width, features), jnp.float32)],
        cost_estimate=cost,
        compiler_params=params,
    )
    return hidden, down


def local(
    activations,
    cotangent,
    token_layout_row,
    tenant_first_row,
    frozen_value_weight,
    adapter_down_maps,
    adapter_up_maps,
):
    devices = lax.axis_size("blk")
    device = lax.axis_index("blk")
    tokens = activations.shape[0]
    resident, rank, width = adapter_down_maps.shape
    out_width = cotangent.shape[1]
    features = width // devices
    share = resident * rank
    resident_rows = resident * BLOCK
    cap = resident_rows // devices
    start_ids = tenant_first_row // BLOCK

    pieces, rest_of_pieces = weight_pieces(frozen_value_weight)

    first_block = device * resident
    block_numbers = first_block + jnp.arange(resident, dtype=jnp.int32)
    begin = starts_of(block_numbers, start_ids)
    hops = jnp.arange(1, HOPS + 1, dtype=jnp.int32)
    is_local = (begin >= first_block) & (begin <= block_numbers)
    home_slot = jnp.clip(begin - first_block, 0, resident - 1)
    row, place_in = jnp.arange(share, dtype=jnp.int32), jnp.arange(HOPS * rank, dtype=jnp.int32)
    same = row[:, None] % rank == row[None, :] % rank
    same_far = row[:, None] % rank == place_in[None, :] % rank
    next_ones = lax.rem(device + hops, devices) * resident
    to_me = lax.div(starts_of(next_ones, start_ids), resident) == device
    home_of = jnp.where(is_local, home_slot, -1)
    home_of = jnp.broadcast_to(home_of[:, None], (resident, rank)).reshape(-1)
    from_own = same & (home_of[:, None] == row[None, :] // rank)
    to_own = same & (home_of[None, :] == row[:, None] // rank)
    remote = same[:rank] & (home_of < 0)[None, :]
    continues = (begin[resident - 1] - first_block) == row // rank
    to_me = jnp.broadcast_to(to_me[:, None], (HOPS, rank)).reshape(-1)
    from_tails = same_far & continues[:, None] & to_me[None, :]
    last_map = jnp.concatenate(
        [
            lax.dynamic_index_in_dim(maps, home_slot[resident - 1], 0, keepdims=False)
            for maps in (adapter_down_maps, adapter_up_maps)
        ],
        axis=1,
    )
    homes = lax.rem(device + devices - hops, devices)
    from_home = lax.div(begin[:1], resident) == homes
    from_home = jnp.broadcast_to(from_home[:, None], (HOPS, rank)).reshape(-1)
    from_far = same_far & (home_of < 0)[:, None] & from_home[None, :]
    carried = [moved(last_map, step) for step in range(1, HOPS + 1)]
    every_carried = jnp.concatenate(carried, axis=0)

    def of_blocks(maps, far):
        own = dot(from_own.astype(jnp.bfloat16), maps.reshape(share, -1), ((1,), (0,)))
        return (own + dot(from_far.astype(jnp.bfloat16), far, ((1,), (0,)))).astype(jnp.bfloat16)

    down_blocks = of_blocks(adapter_down_maps, every_carried[:, :width])
    up_blocks = of_blocks(adapter_up_maps, every_carried[:, width:])

    sent_rows = pack_rows(token_layout_row, cotangent, devices, cap, features)
    own = pieces[0]
    sent_rows = after(sent_rows, *own[:CHUNKS], *carried)
    got_rows = lax.all_to_all(sent_rows, "blk", split_axis=0, concat_axis=0)
    recv_cot = [
        got_rows[:, k * cap : (k + 1) * cap].reshape(resident_rows, features)
        for k in range(out_width // features)
    ]
    per_digit = -(-tokens // features)
    digits = got_rows[:, share : share + 5 * per_digit]
    digits = digits.reshape(devices, 5, per_digit * features)[:, :, :tokens]
    rows_all, place_all = from_digits(digits)

    spots = device * cap + jnp.arange(cap, dtype=jnp.int32)
    hit = place_all[:, None, :] == spots[None, :, None]
    row_in = rows_all - device * resident_rows + 1
    row_in = jnp.sum(jnp.where(hit, row_in[:, None, :], 0), axis=2).reshape(-1) - 1
    arrange = row_in[:, None] == jnp.arange(resident_rows, dtype=jnp.int32)[None, :]
    arrange = arrange.astype(jnp.bfloat16)
    in_block = row_in[:, None] // BLOCK == jnp.arange(share, dtype=jnp.int32)[None, :] // rank

    grad_in = sum(
        dot(part, up_blocks[:, k * features : (k + 1) * features], ((1,), (1,)))
        for k, part in enumerate(recv_cot)
    )
    grad_in = jnp.where(in_block, grad_in, 0.0).astype(jnp.bfloat16)
    grad_in = sum(grad_in[:, b * rank : (b + 1) * rank] for b in range(resident))
    grad_sent = grad_in.reshape(devices, cap, rank).transpose(1, 0, 2).reshape(cap, -1)

    flat_maps = adapter_down_maps.reshape(share, width)
    received = pack_features(activations, flat_maps, devices)
    received = after(received, got_rows)
    received = lax.all_to_all(received, "blk", split_axis=0, concat_axis=0)
    grad_all = to_all(after(grad_sent, received)).reshape(resident_rows, -1).T

    rows_all, place_all = rows_all.reshape(1, -1), place_all.reshape(1, -1)

    cot_rows = jnp.concatenate(
        [dot(arrange, part, ((0,), (0,))).astype(jnp.bfloat16) for part in recv_cot], axis=1
    )
    grad_rows = dot(arrange, grad_in, ((0,), (0,))).astype(jnp.bfloat16)
    group = lax.axis_index("groups")
    quarter = lax.rem(device, 4)
    firsts = [quarter, quarter ^ 1, quarter ^ 2, quarter ^ 3]
    tiled = own[0].shape[1] % LANES == 0
    if tiled:
        out, first_done = write_quarter(
            pieces[0], firsts[0], group, cot_rows, grad_rows, down_blocks
        )
        others = rest_of_pieces(first_done)
        out, token = write_quarter(
            pieces[1], firsts[1], group, cot_rows, grad_rows, down_blocks, out
        )
        place_all = after(place_all, token)
    else:
        others = rest_of_pieces(place_all)

    starts = start_ids[:, None]
    hidden_call, down_call = feature_calls(
        received, tokens, share, rank, resident_rows, starts.shape[0]
    )
    shares = hidden_call(received, received, rows_all, place_all, starts)
    rows_all = after(rows_all, shares)
    down_f = down_call(received, grad_all, rows_all, place_all, starts)
    hidden = shares.T.reshape(devices, cap, -1)
    hidden = lax.all_to_all(hidden, "blk", split_axis=0, concat_axis=0)
    hidden = jnp.sum(hidden, axis=0).astype(jnp.bfloat16)
    hidden = hidden.reshape(cap, devices, rank).transpose(1, 0, 2).reshape(-1, rank)
    down_home = lax.all_to_all(down_f, "blk", split_axis=0, concat_axis=1, tiled=True)
    down_map_gradient = down_home.astype(jnp.float32).reshape(resident, rank, width)

    wide = jnp.where(in_block, jnp.concatenate([hidden] * resident, axis=1), 0)
    up_all = [dot(wide, part, ((0,), (0,))) for part in recv_cot]
    up_all = jnp.concatenate(up_all, axis=1)

    exact = lax.Precision.HIGHEST
    tail = jnp.dot(remote.astype(jnp.float32), up_all, precision=exact)
    if tiled:
        tail = after(tail, *others[1])
    tails = jnp.concatenate([moved(tail, -step) for step in range(1, HOPS + 1)], axis=0)
    up_grads = jnp.dot(to_own.astype(jnp.float32), up_all, precision=exact)
    up_grads = up_grads + jnp.dot(from_tails.astype(jnp.float32), tails, precision=exact)
    up_map_gradient = (adapter_scale * up_grads).reshape(resident, rank, out_width)

    if tiled:
        late = after(grad_rows, down_f)
        for piece, first in zip(others, firsts[2:]):
            out, _ = write_quarter(piece, first, group, cot_rows, late, down_blocks, out)
    else:
        weight = together(pieces + others, firsts, group)
        lora = [
            dot(
                grad_rows[b * BLOCK : (b + 1) * BLOCK],
                down_blocks[b * rank : (b + 1) * rank],
                ((1,), (0,)),
            )
            for b in range(resident)
        ]
        lora = (adapter_scale * jnp.concatenate(lora, axis=0)).astype(jnp.bfloat16)
        out = dot(cot_rows, weight, ((1,), (1,))) + lora.astype(jnp.float32)
        out = out.astype(jnp.bfloat16)
    return (out, down_map_gradient, up_map_gradient)


def solution(mesh):
    return jax.shard_map(
        local,
        mesh=mesh,
        in_specs=(
            P(("groups", "blk"), None),
            P(("groups", "blk"), None),
            P(("groups", "blk")),
            P("groups"),
            P("blk", None),
            P(("groups", "blk"), None, None),
            P(("groups", "blk"), None, None),
        ),
        out_specs=(
            P(("groups", "blk"), None),
            P(("groups", "blk"), None, None),
            P(("groups", "blk"), None, None),
        ),
        check_vma=False,
    )
```

```python
import functools

import jax
import jax.numpy as jnp
from jax import lax
from jax.experimental import pallas as pl
from jax.experimental.pallas import tpu as pltpu
from jax.sharding import PartitionSpec as P

BLOCK = 128
HOPS = 4
LANES = 128
DIGIT = 64
VMEM = 56 << 20

adapter_scale = 2.0


def moved(value, steps):
    count = lax.axis_size("blk")
    return lax.ppermute(value, "blk", [(i, (i + steps) % count) for i in range(count)])


def to_all(value):
    count = lax.axis_size("blk")
    copies = jnp.broadcast_to(value[None], (count,) + value.shape)
    return lax.all_to_all(copies, "blk", split_axis=0, concat_axis=0)


def after(value, *others):
    anywhere = pl.BlockSpec(memory_space=pl.ANY)
    return pl.pallas_call(
        lambda *refs: None,
        in_specs=[anywhere] * (1 + len(others)),
        out_specs=anywhere,
        out_shape=jax.ShapeDtypeStruct(value.shape, value.dtype),
        input_output_aliases={0: 0},
        cost_estimate=pl.CostEstimate(flops=0, bytes_accessed=0, transcendentals=0),
        compiler_params=pltpu.CompilerParams(vmem_limit_bytes=VMEM),
    )(value, *others)


def dot(a, b, dims):
    return lax.dot_general(a, b, (dims, ((), ())), preferred_element_type=jnp.float32)


def starts_of(blocks, start_ids):
    latest = jnp.max(
        jnp.where(start_ids[None, :] <= blocks[:, None], start_ids[None, :], -1), axis=1
    )
    return jnp.where(latest >= 0, latest, jnp.max(start_ids))


def as_digits(rows, places):
    return (
        rows % DIGIT,
        rows // DIGIT % DIGIT,
        rows // (DIGIT * DIGIT),
        places % DIGIT,
        places // DIGIT,
    )


def from_digits(digits):
    low, middle, high, place, place_high = [digits[:, k].astype(jnp.int32) for k in range(5)]
    return (high * DIGIT + middle) * DIGIT + low, place_high * DIGIT + place


CHUNKS = 2


def near_lines(count):
    return count // 4 <= 4


def line_order():
    count = lax.axis_size("blk")
    shards = jnp.arange(count // 4, dtype=jnp.int32)
    if near_lines(count):
        return lax.rem(lax.div(lax.axis_index("blk"), 4) + count // 4 - shards, count // 4)
    return shards


def weight_pieces(weight):
    count = lax.axis_size("blk")
    half = weight.shape[0] // 2
    size = half // CHUNKS
    first = lax.axis_index("groups") * half

    def over(piece, bit):
        return lax.ppermute(piece, "blk", [(i, i ^ bit) for i in range(count)])

    def groups(piece):
        return lax.ppermute(piece, "groups", [(0, 1), (1, 0)])

    def column(chunk):
        mine = lax.dynamic_slice_in_dim(weight, first + chunk * size, size, 0)
        if near_lines(count):
            return jnp.stack([mine] + [moved(mine, 4 * k) for k in range(1, count // 4)])
        lines = [list(range(k, count, 4)) for k in range(4)]
        return lax.all_gather(mine, "blk", axis_index_groups=lines)

    columns = [column(k) for k in range(CHUNKS)]
    own = columns + [groups(piece) for piece in columns]
    across = [over(piece, 2) for piece in columns]

    def rest(late):
        mine = [after(piece, late) for piece in across]
        both = mine + [groups(piece) for piece in mine]
        return [both, [over(piece, 1) for piece in both]]

    return [own, [over(piece, 1) for piece in own]], rest


def quarter_kernel(where, cot, grad, down, *rest):
    pieces = rest[: 2 * CHUNKS]
    out, token = rest[-2:]
    token[...] = jnp.zeros_like(token)
    rank = grad.shape[1]
    lora = [
        adapter_scale
        * dot(
            grad[b * BLOCK : (b + 1) * BLOCK, :],
            down[b * rank : (b + 1) * rank, :],
            ((1,), (0,)),
        )
        for b in range(cot.shape[0] // BLOCK)
    ]
    lora = jnp.concatenate(lora, axis=0).astype(jnp.bfloat16).astype(jnp.float32)

    def product(group):
        order = pieces[group * CHUNKS :] + pieces[: group * CHUNKS]
        weight = jnp.concatenate([piece[0] for piece in order], axis=0)
        frozen = dot(cot[...], weight, ((1,), (1,)))
        out[...] = (frozen + lora).astype(jnp.bfloat16)

    for group in range(2):
        pl.when(where[where.shape[0] - 1] == group)(functools.partial(product, group))


def write_quarter(quarter, first, group, cot, grad, down, out=None):
    rows, depth = cot.shape
    width = down.shape[1]
    shards, part, _ = quarter[0].shape
    stripe = part * len(quarter)
    where = jnp.concatenate([4 * line_order() + first, group[None]]).astype(jnp.int32)
    specs = [
        pl.BlockSpec((rows, depth), lambda j, where: (0, 0)),
        pl.BlockSpec(grad.shape, lambda j, where: (0, 0)),
        pl.BlockSpec((down.shape[0], stripe), lambda j, where: (0, where[j])),
    ] + [pl.BlockSpec((1, part, depth), lambda j, where: (j, 0, 0)) for _ in quarter]
    args = [where, cot, grad, down] + quarter
    alias = {}
    if out is not None:
        specs.append(pl.BlockSpec(memory_space=pl.ANY))
        args.append(out)
        alias = {len(args) - 1: 0}
    return pl.pallas_call(
        quarter_kernel,
        grid_spec=pltpu.PrefetchScalarGridSpec(
            num_scalar_prefetch=1,
            grid=(shards,),
            in_specs=specs,
            out_specs=[
                pl.BlockSpec((rows, stripe), lambda j, where: (0, where[j])),
                pl.BlockSpec((8, LANES), lambda j, where: (0, 0)),
            ],
        ),
        out_shape=[
            jax.ShapeDtypeStruct((rows, width), jnp.bfloat16),
            jax.ShapeDtypeStruct((8, LANES), jnp.float32),
        ],
        input_output_aliases=alias,
        cost_estimate=pl.CostEstimate(
            flops=2 * rows * depth * stripe * shards,
            bytes_accessed=2 * (depth + rows) * stripe * shards,
            transcendentals=0,
        ),
        compiler_params=pltpu.CompilerParams(vmem_limit_bytes=VMEM),
    )(*args)


def together(pieces, firsts, group):
    shards, part, depth = pieces[0][0].shape
    weight = jnp.zeros((shards, 4, 2, CHUNKS, part, depth), jnp.bfloat16)
    order = line_order()
    for quarter, first in zip(pieces, firsts):
        for k, piece in enumerate(quarter):
            half = group if k < CHUNKS else 1 - group
            if not near_lines(4 * shards):
                place = (0, first, half, k % CHUNKS, 0, 0)
                weight = lax.dynamic_update_slice(weight, piece[:, None, None, None], place)
                continue
            for j in range(shards):
                place = (order[j], first, half, k % CHUNKS, 0, 0)
                shard = piece[j][None, None, None, None]
                weight = lax.dynamic_update_slice(weight, shard, place)
    return weight.reshape(-1, depth)


def rows_kernel(rows, cot, out, place):
    devices, packed, features = out.shape
    shared = packed - 16
    folds = cot.shape[1] // features
    cap = shared // folds
    target = rows[...] // (cap * devices)
    to = lax.broadcasted_iota(jnp.int32, (16, features), 0) == target
    first = lax.broadcasted_iota(jnp.int32, (features, features), 0)
    later = lax.broadcasted_iota(jnp.int32, (features, features), 1)
    earlier = jnp.where(first < later, 1.0, 0.0).astype(jnp.bfloat16)
    ahead = dot(jnp.where(to, 1.0, 0.0).astype(jnp.bfloat16), earlier, ((1,), (0,)))
    ahead = jnp.sum(jnp.where(to, ahead, 0.0), axis=0, keepdims=True)
    place[...] = target * cap + ahead.astype(jnp.int32)
    which = lax.broadcasted_iota(jnp.int32, (16, features), 0)
    digits = jnp.zeros((16, features), jnp.int32)
    for k, digit in enumerate(as_digits(rows[...], place[...])):
        digits = jnp.where(which == k, digit, digits)
    digits = digits.astype(jnp.float32).astype(out.dtype)
    send = placing(place[:, : cot.shape[0]], cap * devices)
    for f in range(folds):
        sent = dot(send, cot[:, f * features : (f + 1) * features], ((1,), (0,)))
        for k in range(devices):
            some = sent[k * cap : (k + 1) * cap].astype(out.dtype)
            out[k, f * cap : (f + 1) * cap, :] = some
    for k in range(devices):
        out[k, shared:, :] = digits


def pack_rows(rows, cot, devices, cap, features):
    tokens = rows.shape[0]
    folds = cot.shape[1] // features
    if features % LANES == 0 and cap % 8 == 0 and features >= tokens and devices <= 16:
        padding = jnp.full((features - tokens,), 16 * cap * devices, jnp.int32)
        return pl.pallas_call(
            rows_kernel,
            out_shape=jax.ShapeDtypeStruct((devices, folds * cap + 16, features), cot.dtype),
            scratch_shapes=[pltpu.VMEM((1, features), jnp.int32)],
            cost_estimate=pl.CostEstimate(
                flops=2 * devices * cap * tokens * cot.shape[1],
                bytes_accessed=6 * cot.size,
                transcendentals=0,
            ),
            compiler_params=pltpu.CompilerParams(vmem_limit_bytes=VMEM),
        )(jnp.concatenate([rows, padding])[None], cot)
    target = rows // (cap * devices)
    order = jnp.arange(tokens, dtype=jnp.int32)
    before = (target[:, None] == target[None, :]) & (order[None, :] < order[:, None])
    place = target * cap + jnp.sum(before.astype(jnp.int32), axis=1)
    send = jnp.arange(cap * devices, dtype=jnp.int32)[:, None] == place[None, :]
    sent = dot(send.astype(jnp.bfloat16), cot, ((1,), (0,))).astype(jnp.bfloat16)
    sent = sent.reshape(devices, cap, cot.shape[1])
    digits = jnp.stack(as_digits(rows, place)).astype(jnp.bfloat16)
    digits = jnp.pad(digits, ((0, 0), (0, -tokens % features))).reshape(-1, features)
    digits = jnp.pad(digits, ((0, -digits.shape[0] % 16), (0, 0)))
    parts = [sent[:, :, k : k + features] for k in range(0, cot.shape[1], features)]
    parts += [jnp.broadcast_to(digits[None], (devices,) + digits.shape)]
    return jnp.concatenate(parts, axis=1)


def features_kernel(act, maps, out):
    targets, _, features = out.shape
    tokens = act.shape[0]
    for k in range(targets):
        part = slice(k * features, (k + 1) * features)
        out[k, :tokens, :] = act[:, part]
        out[k, tokens:, :] = maps[:, part]


def pack_features(act, maps, devices):
    tokens, width = act.shape
    features = width // devices
    shared = maps.shape[0]
    targets = 4
    if features % LANES == 0:
        return pl.pallas_call(
            features_kernel,
            grid=(devices // targets,),
            in_specs=[
                pl.BlockSpec((tokens, targets * features), lambda j: (0, j)),
                pl.BlockSpec((shared, targets * features), lambda j: (0, j)),
            ],
            out_specs=pl.BlockSpec((targets, tokens + shared, features), lambda j: (j, 0, 0)),
            out_shape=jax.ShapeDtypeStruct((devices, tokens + shared, features), act.dtype),
            cost_estimate=pl.CostEstimate(
                flops=0, bytes_accessed=4 * (tokens + shared) * width, transcendentals=0
            ),
            compiler_params=pltpu.CompilerParams(vmem_limit_bytes=VMEM),
        )(act, maps)
    both = jnp.concatenate([act, maps], axis=0)
    return both.reshape(tokens + shared, devices, features).transpose(1, 0, 2)


def slot_chunks(width):
    size = min(width, 768)
    while width % size:
        size //= 2
    return [slice(k, k + size) for k in range(0, width, size)]


def slot_of(rows, starts):
    blocks = rows // BLOCK
    latest = jnp.max(jnp.where(starts <= blocks, starts, -1), axis=0, keepdims=True)
    return jnp.where(latest >= 0, latest, jnp.max(starts))


def own_rows(slot, first, size, rank):
    index = first // rank + lax.broadcasted_iota(jnp.int32, (size // rank, rank, 1), 0)
    return index == slot[None]


def placing(place, places):
    hit = lax.broadcasted_iota(jnp.int32, (places, place.shape[1]), 0) == place
    return jnp.where(hit, 1.0, 0.0).astype(jnp.bfloat16)


def all_rows(act, tokens):
    return jnp.concatenate([act[k, :tokens, :] for k in range(act.shape[0])], axis=0)


def of_source(sources, width):
    lane = lax.broadcasted_iota(jnp.int32, (sources, 1, width), 2)
    return lane // (width // sources) == lax.broadcasted_iota(
        jnp.int32, (sources, 1, width), 0
    )


def hidden_kernel(act, maps, rows, spots, starts, out):
    sources, share, width = act.shape[0], maps.shape[1], rows.shape[1]
    rank, places = out.shape[0] // sources, out.shape[1]
    slot = slot_of(rows[...], starts[...])
    every = all_rows(act, width // sources)
    total = jnp.zeros((rank, width), jnp.float32)
    for part in slot_chunks(maps.shape[0] * share):
        size = part.stop - part.start
        some = maps[part.start // share : part.stop // share].reshape(size, -1)
        each = dot(some, every, ((1,), (1,))).reshape(size // rank, rank, -1)
        total += jnp.sum(jnp.where(own_rows(slot, part.start, size, rank), each, 0.0), axis=0)
    total = jnp.where(of_source(sources, width), total[None], 0.0).reshape(out.shape[0], width)
    high = total.astype(jnp.bfloat16)
    low = (total - high.astype(jnp.float32)).astype(jnp.bfloat16)
    place = placing(spots[...], places)
    out[...] = dot(high, place, ((1,), (1,))) + dot(low, place, ((1,), (1,)))


def down_kernel(act, grad, rows, spots, starts, out, total):
    sources, width = act.shape[0], rows.shape[1]
    rank, places = grad.shape[0] // sources, grad.shape[1]
    step = pl.program_id(0)

    @pl.when(step == 0)
    def _():
        total[...] = jnp.zeros_like(total)

    slot = slot_of(rows[...], starts[...])
    every = all_rows(act, width // sources)
    wide = dot(grad[...], placing(spots[...], places), ((1,), (0,)))
    wide = wide.reshape(sources, rank, width)
    wide = jnp.sum(jnp.where(of_source(sources, width), wide, 0.0), axis=0, keepdims=True)
    for part in slot_chunks(total.shape[0]):
        size = part.stop - part.start
        placed = jnp.where(own_rows(slot, part.start, size, rank), wide, 0.0)
        placed = placed.reshape(size, -1).astype(jnp.bfloat16)
        total[part, :] += dot(placed, every, ((1,), (0,)))

    @pl.when(step == pl.num_programs(0) - 1)
    def _():
        out[...] = (adapter_scale * total[...]).astype(out.dtype)


def feature_calls(received, tokens, share, rank, places, starts):
    devices, packed, features = received.shape
    width = devices * share
    sources = 4
    grid = (devices // sources,)
    act = pl.BlockSpec((sources, packed, features), lambda j: (j, 0, 0))
    maps = pl.BlockSpec((devices, share, features), lambda j: (0, tokens // share, 0))
    rows = pl.BlockSpec((1, sources * tokens), lambda j: (0, j))
    begin = pl.BlockSpec((starts, 1), lambda j: (0, 0))
    placed = pl.BlockSpec((sources * rank, places), lambda j: (j, 0))
    cost = pl.CostEstimate(
        flops=2 * devices * tokens * width * features,
        bytes_accessed=2 * devices * tokens * features,
        transcendentals=0,
    )
    params = pltpu.CompilerParams(vmem_limit_bytes=VMEM)
    hidden = pl.pallas_call(
        hidden_kernel,
        grid=grid,
        in_specs=[act, maps, rows, rows, begin],
        out_specs=placed,
        out_shape=jax.ShapeDtypeStruct((devices * rank, places), jnp.float32),
        cost_estimate=cost,
        compiler_params=params,
    )
    down = pl.pallas_call(
        down_kernel,
        grid=grid,
        in_specs=[act, placed, rows, rows, begin],
        out_specs=pl.BlockSpec((width, features), lambda j: (0, 0)),
        out_shape=jax.ShapeDtypeStruct((width, features), jnp.bfloat16),
        scratch_shapes=[pltpu.VMEM((width, features), jnp.float32)],
        cost_estimate=cost,
        compiler_params=params,
    )
    return hidden, down


def local(
    activations,
    cotangent,
    token_layout_row,
    tenant_first_row,
    frozen_value_weight,
    adapter_down_maps,
    adapter_up_maps,
):
    devices = lax.axis_size("blk")
    device = lax.axis_index("blk")
    tokens = activations.shape[0]
    resident, rank, width = adapter_down_maps.shape
    out_width = cotangent.shape[1]
    features = width // devices
    share = resident * rank
    resident_rows = resident * BLOCK
    cap = resident_rows // devices
    start_ids = tenant_first_row // BLOCK

    pieces, rest_of_pieces = weight_pieces(frozen_value_weight)

    first_block = device * resident
    block_numbers = first_block + jnp.arange(resident, dtype=jnp.int32)
    begin = starts_of(block_numbers, start_ids)
    hops = jnp.arange(1, HOPS + 1, dtype=jnp.int32)
    is_local = (begin >= first_block) & (begin <= block_numbers)
    home_slot = jnp.clip(begin - first_block, 0, resident - 1)
    row, place_in = jnp.arange(share, dtype=jnp.int32), jnp.arange(HOPS * rank, dtype=jnp.int32)
    same = row[:, None] % rank == row[None, :] % rank
    same_far = row[:, None] % rank == place_in[None, :] % rank
    next_ones = lax.rem(device + hops, devices) * resident
    to_me = lax.div(starts_of(next_ones, start_ids), resident) == device
    home_of = jnp.where(is_local, home_slot, -1)
    home_of = jnp.broadcast_to(home_of[:, None], (resident, rank)).reshape(-1)
    from_own = same & (home_of[:, None] == row[None, :] // rank)
    to_own = same & (home_of[None, :] == row[:, None] // rank)
    remote = same[:rank] & (home_of < 0)[None, :]
    continues = (begin[resident - 1] - first_block) == row // rank
    to_me = jnp.broadcast_to(to_me[:, None], (HOPS, rank)).reshape(-1)
    from_tails = same_far & continues[:, None] & to_me[None, :]
    last_map = jnp.concatenate(
        [
            lax.dynamic_index_in_dim(maps, home_slot[resident - 1], 0, keepdims=False)
            for maps in (adapter_down_maps, adapter_up_maps)
        ],
        axis=1,
    )
    homes = lax.rem(device + devices - hops, devices)
    from_home = lax.div(begin[:1], resident) == homes
    from_home = jnp.broadcast_to(from_home[:, None], (HOPS, rank)).reshape(-1)
    from_far = same_far & (home_of < 0)[:, None] & from_home[None, :]
    carried = [moved(last_map, step) for step in range(1, HOPS + 1)]
    every_carried = jnp.concatenate(carried, axis=0)

    def of_blocks(maps, far):
        own = dot(from_own.astype(jnp.bfloat16), maps.reshape(share, -1), ((1,), (0,)))
        return (own + dot(from_far.astype(jnp.bfloat16), far, ((1,), (0,)))).astype(jnp.bfloat16)

    down_blocks = of_blocks(adapter_down_maps, every_carried[:, :width])
    up_blocks = of_blocks(adapter_up_maps, every_carried[:, width:])

    sent_rows = pack_rows(token_layout_row, cotangent, devices, cap, features)
    own = pieces[0]
    sent_rows = after(sent_rows, *own[:CHUNKS], *carried)
    got_rows = lax.all_to_all(sent_rows, "blk", split_axis=0, concat_axis=0)
    recv_cot = [
        got_rows[:, k * cap : (k + 1) * cap].reshape(resident_rows, features)
        for k in range(out_width // features)
    ]
    per_digit = -(-tokens // features)
    digits = got_rows[:, share : share + 5 * per_digit]
    digits = digits.reshape(devices, 5, per_digit * features)[:, :, :tokens]
    rows_all, place_all = from_digits(digits)

    spots = device * cap + jnp.arange(cap, dtype=jnp.int32)
    hit = place_all[:, None, :] == spots[None, :, None]
    row_in = rows_all - device * resident_rows + 1
    row_in = jnp.sum(jnp.where(hit, row_in[:, None, :], 0), axis=2).reshape(-1) - 1
    arrange = row_in[:, None] == jnp.arange(resident_rows, dtype=jnp.int32)[None, :]
    arrange = arrange.astype(jnp.bfloat16)
    in_block = row_in[:, None] // BLOCK == jnp.arange(share, dtype=jnp.int32)[None, :] // rank

    grad_in = sum(
        dot(part, up_blocks[:, k * features : (k + 1) * features], ((1,), (1,)))
        for k, part in enumerate(recv_cot)
    )
    grad_in = jnp.where(in_block, grad_in, 0.0).astype(jnp.bfloat16)
    grad_in = sum(grad_in[:, b * rank : (b + 1) * rank] for b in range(resident))
    grad_sent = grad_in.reshape(devices, cap, rank).transpose(1, 0, 2).reshape(cap, -1)

    flat_maps = adapter_down_maps.reshape(share, width)
    received = pack_features(activations, flat_maps, devices)
    received = after(received, got_rows)
    received = lax.all_to_all(received, "blk", split_axis=0, concat_axis=0)
    grad_all = to_all(after(grad_sent, received)).reshape(resident_rows, -1).T

    rows_all, place_all = rows_all.reshape(1, -1), place_all.reshape(1, -1)

    cot_rows = jnp.concatenate(
        [dot(arrange, part, ((0,), (0,))).astype(jnp.bfloat16) for part in recv_cot], axis=1
    )
    grad_rows = dot(arrange, grad_in, ((0,), (0,))).astype(jnp.bfloat16)
    group = lax.axis_index("groups")
    quarter = lax.rem(device, 4)
    firsts = [quarter, quarter ^ 1, quarter ^ 2, quarter ^ 3]
    tiled = own[0].shape[1] % LANES == 0
    if tiled:
        out = None
        for piece, first in zip(pieces, firsts):
            out, token = write_quarter(
                piece, first, group, cot_rows, grad_rows, down_blocks, out
            )
        others = rest_of_pieces(token)
        place_all = after(place_all, token)
    else:
        others = rest_of_pieces(place_all)

    starts = start_ids[:, None]
    hidden_call, down_call = feature_calls(
        received, tokens, share, rank, resident_rows, starts.shape[0]
    )
    shares = hidden_call(received, received, rows_all, place_all, starts)
    rows_all = after(rows_all, shares)
    down_f = down_call(received, grad_all, rows_all, place_all, starts)
    hidden = shares.T.reshape(devices, cap, -1)
    hidden = lax.all_to_all(hidden, "blk", split_axis=0, concat_axis=0)
    hidden = jnp.sum(hidden, axis=0).astype(jnp.bfloat16)
    hidden = hidden.reshape(cap, devices, rank).transpose(1, 0, 2).reshape(-1, rank)
    down_home = lax.all_to_all(down_f, "blk", split_axis=0, concat_axis=1, tiled=True)
    down_map_gradient = down_home.astype(jnp.float32).reshape(resident, rank, width)

    wide = jnp.where(in_block, jnp.concatenate([hidden] * resident, axis=1), 0)
    up_all = [dot(wide, part, ((0,), (0,))) for part in recv_cot]
    up_all = jnp.concatenate(up_all, axis=1)

    exact = lax.Precision.HIGHEST
    tail = jnp.dot(remote.astype(jnp.float32), up_all, precision=exact)
    if tiled:
        tail = after(tail, *others[1])
    tails = jnp.concatenate([moved(tail, -step) for step in range(1, HOPS + 1)], axis=0)
    up_grads = jnp.dot(to_own.astype(jnp.float32), up_all, precision=exact)
    up_grads = up_grads + jnp.dot(from_tails.astype(jnp.float32), tails, precision=exact)
    up_map_gradient = (adapter_scale * up_grads).reshape(resident, rank, out_width)

    if tiled:
        late = after(grad_rows, down_f, tail)
        for piece, first in zip(others, firsts[2:]):
            out, _ = write_quarter(piece, first, group, cot_rows, late, down_blocks, out)
    else:
        weight = together(pieces + others, firsts, group)
        lora = [
            dot(
                grad_rows[b * BLOCK : (b + 1) * BLOCK],
                down_blocks[b * rank : (b + 1) * rank],
                ((1,), (0,)),
            )
            for b in range(resident)
        ]
        lora = (adapter_scale * jnp.concatenate(lora, axis=0)).astype(jnp.bfloat16)
        out = dot(cot_rows, weight, ((1,), (1,))) + lora.astype(jnp.float32)
        out = out.astype(jnp.bfloat16)
    return (out, down_map_gradient, up_map_gradient)


def solution(mesh):
    return jax.shard_map(
        local,
        mesh=mesh,
        in_specs=(
            P(("groups", "blk"), None),
            P(("groups", "blk"), None),
            P(("groups", "blk")),
            P("groups"),
            P("blk", None),
            P(("groups", "blk"), None, None),
            P(("groups", "blk"), None, None),
        ),
        out_specs=(
            P(("groups", "blk"), None),
            P(("groups", "blk"), None, None),
            P(("groups", "blk"), None, None),
        ),
        check_vma=False,
    )
```

```python
import functools

import jax
import jax.numpy as jnp
from jax import lax
from jax.experimental import pallas as pl
from jax.experimental.pallas import tpu as pltpu
from jax.sharding import PartitionSpec as P

BLOCK = 128
HOPS = 4
LANES = 128
DIGIT = 64
VMEM = 56 << 20

adapter_scale = 2.0


def moved(value, steps):
    count = lax.axis_size("blk")
    return lax.ppermute(value, "blk", [(i, (i + steps) % count) for i in range(count)])


def to_all(value):
    count = lax.axis_size("blk")
    copies = jnp.broadcast_to(value[None], (count,) + value.shape)
    return lax.all_to_all(copies, "blk", split_axis=0, concat_axis=0)


def after(value, *others):
    anywhere = pl.BlockSpec(memory_space=pl.ANY)
    return pl.pallas_call(
        lambda *refs: None,
        in_specs=[anywhere] * (1 + len(others)),
        out_specs=anywhere,
        out_shape=jax.ShapeDtypeStruct(value.shape, value.dtype),
        input_output_aliases={0: 0},
        cost_estimate=pl.CostEstimate(flops=0, bytes_accessed=0, transcendentals=0),
        compiler_params=pltpu.CompilerParams(vmem_limit_bytes=VMEM),
    )(value, *others)


def dot(a, b, dims):
    return lax.dot_general(a, b, (dims, ((), ())), preferred_element_type=jnp.float32)


def starts_of(blocks, start_ids):
    latest = jnp.max(
        jnp.where(start_ids[None, :] <= blocks[:, None], start_ids[None, :], -1), axis=1
    )
    return jnp.where(latest >= 0, latest, jnp.max(start_ids))


def as_digits(rows, places):
    return (
        rows % DIGIT,
        rows // DIGIT % DIGIT,
        rows // (DIGIT * DIGIT),
        places % DIGIT,
        places // DIGIT,
    )


def from_digits(digits):
    low, middle, high, place, place_high = [digits[:, k].astype(jnp.int32) for k in range(5)]
    return (high * DIGIT + middle) * DIGIT + low, place_high * DIGIT + place


CHUNKS = 2


def near_lines(count):
    return count // 4 <= 4


def line_order():
    count = lax.axis_size("blk")
    shards = jnp.arange(count // 4, dtype=jnp.int32)
    if near_lines(count):
        return lax.rem(lax.div(lax.axis_index("blk"), 4) + count // 4 - shards, count // 4)
    return shards


def weight_pieces(weight):
    count = lax.axis_size("blk")
    half = weight.shape[0] // 2
    size = half // CHUNKS
    first = lax.axis_index("groups") * half

    def over(piece, bit):
        return lax.ppermute(piece, "blk", [(i, i ^ bit) for i in range(count)])

    def groups(piece):
        return lax.ppermute(piece, "groups", [(0, 1), (1, 0)])

    def column(chunk):
        mine = lax.dynamic_slice_in_dim(weight, first + chunk * size, size, 0)
        if near_lines(count):
            return jnp.stack([mine] + [moved(mine, 4 * k) for k in range(1, count // 4)])
        lines = [list(range(k, count, 4)) for k in range(4)]
        return lax.all_gather(mine, "blk", axis_index_groups=lines)

    columns = [column(k) for k in range(CHUNKS)]
    own = columns + [groups(piece) for piece in columns]
    across = [over(piece, 2) for piece in columns]

    def rest(late):
        mine = [after(piece, late) for piece in across]
        both = mine + [groups(piece) for piece in mine]
        return [both, [over(piece, 1) for piece in both]]

    return [own, [over(piece, 1) for piece in own]], rest


def quarter_kernel(where, cot, grad, down, *rest):
    pieces = rest[: 2 * CHUNKS]
    out, token = rest[-2:]
    token[...] = jnp.zeros_like(token)
    rank = grad.shape[1]
    lora = [
        adapter_scale
        * dot(
            grad[b * BLOCK : (b + 1) * BLOCK, :],
            down[b * rank : (b + 1) * rank, :],
            ((1,), (0,)),
        )
        for b in range(cot.shape[0] // BLOCK)
    ]
    lora = jnp.concatenate(lora, axis=0).astype(jnp.bfloat16).astype(jnp.float32)

    def product(group):
        order = pieces[group * CHUNKS :] + pieces[: group * CHUNKS]
        weight = jnp.concatenate([piece[0] for piece in order], axis=0)
        frozen = dot(cot[...], weight, ((1,), (1,)))
        out[...] = (frozen + lora).astype(jnp.bfloat16)

    for group in range(2):
        pl.when(where[where.shape[0] - 1] == group)(functools.partial(product, group))


def write_quarter(quarter, first, group, cot, grad, down, out=None):
    rows, depth = cot.shape
    width = down.shape[1]
    shards, part, _ = quarter[0].shape
    stripe = part * len(quarter)
    where = jnp.concatenate([4 * line_order() + first, group[None]]).astype(jnp.int32)
    specs = [
        pl.BlockSpec((rows, depth), lambda j, where: (0, 0)),
        pl.BlockSpec(grad.shape, lambda j, where: (0, 0)),
        pl.BlockSpec((down.shape[0], stripe), lambda j, where: (0, where[j])),
    ] + [pl.BlockSpec((1, part, depth), lambda j, where: (j, 0, 0)) for _ in quarter]
    args = [where, cot, grad, down] + quarter
    alias = {}
    if out is not None:
        specs.append(pl.BlockSpec(memory_space=pl.ANY))
        args.append(out)
        alias = {len(args) - 1: 0}
    return pl.pallas_call(
        quarter_kernel,
        grid_spec=pltpu.PrefetchScalarGridSpec(
            num_scalar_prefetch=1,
            grid=(shards,),
            in_specs=specs,
            out_specs=[
                pl.BlockSpec((rows, stripe), lambda j, where: (0, where[j])),
                pl.BlockSpec((8, LANES), lambda j, where: (0, 0)),
            ],
        ),
        out_shape=[
            jax.ShapeDtypeStruct((rows, width), jnp.bfloat16),
            jax.ShapeDtypeStruct((8, LANES), jnp.float32),
        ],
        input_output_aliases=alias,
        cost_estimate=pl.CostEstimate(
            flops=2 * rows * depth * stripe * shards,
            bytes_accessed=2 * (depth + rows) * stripe * shards,
            transcendentals=0,
        ),
        compiler_params=pltpu.CompilerParams(vmem_limit_bytes=VMEM),
    )(*args)


def together(pieces, firsts, group):
    shards, part, depth = pieces[0][0].shape
    weight = jnp.zeros((shards, 4, 2, CHUNKS, part, depth), jnp.bfloat16)
    order = line_order()
    for quarter, first in zip(pieces, firsts):
        for k, piece in enumerate(quarter):
            half = group if k < CHUNKS else 1 - group
            if not near_lines(4 * shards):
                place = (0, first, half, k % CHUNKS, 0, 0)
                weight = lax.dynamic_update_slice(weight, piece[:, None, None, None], place)
                continue
            for j in range(shards):
                place = (order[j], first, half, k % CHUNKS, 0, 0)
                shard = piece[j][None, None, None, None]
                weight = lax.dynamic_update_slice(weight, shard, place)
    return weight.reshape(-1, depth)


def rows_kernel(rows, cot, out, place):
    devices, packed, features = out.shape
    shared = packed - 16
    folds = cot.shape[1] // features
    cap = shared // folds
    target = rows[...] // (cap * devices)
    to = lax.broadcasted_iota(jnp.int32, (16, features), 0) == target
    first = lax.broadcasted_iota(jnp.int32, (features, features), 0)
    later = lax.broadcasted_iota(jnp.int32, (features, features), 1)
    earlier = jnp.where(first < later, 1.0, 0.0).astype(jnp.bfloat16)
    ahead = dot(jnp.where(to, 1.0, 0.0).astype(jnp.bfloat16), earlier, ((1,), (0,)))
    ahead = jnp.sum(jnp.where(to, ahead, 0.0), axis=0, keepdims=True)
    place[...] = target * cap + ahead.astype(jnp.int32)
    which = lax.broadcasted_iota(jnp.int32, (16, features), 0)
    digits = jnp.zeros((16, features), jnp.int32)
    for k, digit in enumerate(as_digits(rows[...], place[...])):
        digits = jnp.where(which == k, digit, digits)
    digits = digits.astype(jnp.float32).astype(out.dtype)
    send = placing(place[:, : cot.shape[0]], cap * devices)
    for f in range(folds):
        sent = dot(send, cot[:, f * features : (f + 1) * features], ((1,), (0,)))
        for k in range(devices):
            some = sent[k * cap : (k + 1) * cap].astype(out.dtype)
            out[k, f * cap : (f + 1) * cap, :] = some
    for k in range(devices):
        out[k, shared:, :] = digits


def pack_rows(rows, cot, devices, cap, features):
    tokens = rows.shape[0]
    folds = cot.shape[1] // features
    if features % LANES == 0 and cap % 8 == 0 and features >= tokens and devices <= 16:
        padding = jnp.full((features - tokens,), 16 * cap * devices, jnp.int32)
        return pl.pallas_call(
            rows_kernel,
            out_shape=jax.ShapeDtypeStruct((devices, folds * cap + 16, features), cot.dtype),
            scratch_shapes=[pltpu.VMEM((1, features), jnp.int32)],
            cost_estimate=pl.CostEstimate(
                flops=2 * devices * cap * tokens * cot.shape[1],
                bytes_accessed=6 * cot.size,
                transcendentals=0,
            ),
            compiler_params=pltpu.CompilerParams(vmem_limit_bytes=VMEM),
        )(jnp.concatenate([rows, padding])[None], cot)
    target = rows // (cap * devices)
    order = jnp.arange(tokens, dtype=jnp.int32)
    before = (target[:, None] == target[None, :]) & (order[None, :] < order[:, None])
    place = target * cap + jnp.sum(before.astype(jnp.int32), axis=1)
    send = jnp.arange(cap * devices, dtype=jnp.int32)[:, None] == place[None, :]
    sent = dot(send.astype(jnp.bfloat16), cot, ((1,), (0,))).astype(jnp.bfloat16)
    sent = sent.reshape(devices, cap, cot.shape[1])
    digits = jnp.stack(as_digits(rows, place)).astype(jnp.bfloat16)
    digits = jnp.pad(digits, ((0, 0), (0, -tokens % features))).reshape(-1, features)
    digits = jnp.pad(digits, ((0, -digits.shape[0] % 16), (0, 0)))
    parts = [sent[:, :, k : k + features] for k in range(0, cot.shape[1], features)]
    parts += [jnp.broadcast_to(digits[None], (devices,) + digits.shape)]
    return jnp.concatenate(parts, axis=1)


def features_kernel(act, maps, out):
    targets, _, features = out.shape
    tokens = act.shape[0]
    for k in range(targets):
        part = slice(k * features, (k + 1) * features)
        out[k, :tokens, :] = act[:, part]
        out[k, tokens:, :] = maps[:, part]


def pack_features(act, maps, devices):
    tokens, width = act.shape
    features = width // devices
    shared = maps.shape[0]
    targets = 4
    if features % LANES == 0:
        return pl.pallas_call(
            features_kernel,
            grid=(devices // targets,),
            in_specs=[
                pl.BlockSpec((tokens, targets * features), lambda j: (0, j)),
                pl.BlockSpec((shared, targets * features), lambda j: (0, j)),
            ],
            out_specs=pl.BlockSpec((targets, tokens + shared, features), lambda j: (j, 0, 0)),
            out_shape=jax.ShapeDtypeStruct((devices, tokens + shared, features), act.dtype),
            cost_estimate=pl.CostEstimate(
                flops=0, bytes_accessed=4 * (tokens + shared) * width, transcendentals=0
            ),
            compiler_params=pltpu.CompilerParams(vmem_limit_bytes=VMEM),
        )(act, maps)
    both = jnp.concatenate([act, maps], axis=0)
    return both.reshape(tokens + shared, devices, features).transpose(1, 0, 2)


def slot_chunks(width):
    size = min(width, 768)
    while width % size:
        size //= 2
    return [slice(k, k + size) for k in range(0, width, size)]


def slot_of(rows, starts):
    blocks = rows // BLOCK
    latest = jnp.max(jnp.where(starts <= blocks, starts, -1), axis=0, keepdims=True)
    return jnp.where(latest >= 0, latest, jnp.max(starts))


def own_rows(slot, first, size, rank):
    index = first // rank + lax.broadcasted_iota(jnp.int32, (size // rank, rank, 1), 0)
    return index == slot[None]


def placing(place, places):
    hit = lax.broadcasted_iota(jnp.int32, (places, place.shape[1]), 0) == place
    return jnp.where(hit, 1.0, 0.0).astype(jnp.bfloat16)


def all_rows(act, tokens):
    return jnp.concatenate([act[k, :tokens, :] for k in range(act.shape[0])], axis=0)


def of_source(sources, width):
    lane = lax.broadcasted_iota(jnp.int32, (sources, 1, width), 2)
    return lane // (width // sources) == lax.broadcasted_iota(
        jnp.int32, (sources, 1, width), 0
    )


def hidden_kernel(act, maps, rows, spots, starts, out):
    sources, share, width = act.shape[0], maps.shape[1], rows.shape[1]
    rank, places = out.shape[0] // sources, out.shape[1]
    slot = slot_of(rows[...], starts[...])
    every = all_rows(act, width // sources)
    total = jnp.zeros((rank, width), jnp.float32)
    for part in slot_chunks(maps.shape[0] * share):
        size = part.stop - part.start
        some = maps[part.start // share : part.stop // share].reshape(size, -1)
        each = dot(some, every, ((1,), (1,))).reshape(size // rank, rank, -1)
        total += jnp.sum(jnp.where(own_rows(slot, part.start, size, rank), each, 0.0), axis=0)
    total = jnp.where(of_source(sources, width), total[None], 0.0).reshape(out.shape[0], width)
    high = total.astype(jnp.bfloat16)
    low = (total - high.astype(jnp.float32)).astype(jnp.bfloat16)
    place = placing(spots[...], places)
    out[...] = dot(high, place, ((1,), (1,))) + dot(low, place, ((1,), (1,)))


def down_kernel(act, grad, rows, spots, starts, out, total):
    sources, width = act.shape[0], rows.shape[1]
    rank, places = grad.shape[0] // sources, grad.shape[1]
    step = pl.program_id(0)

    @pl.when(step == 0)
    def _():
        total[...] = jnp.zeros_like(total)

    slot = slot_of(rows[...], starts[...])
    every = all_rows(act, width // sources)
    wide = dot(grad[...], placing(spots[...], places), ((1,), (0,)))
    wide = wide.reshape(sources, rank, width)
    wide = jnp.sum(jnp.where(of_source(sources, width), wide, 0.0), axis=0, keepdims=True)
    for part in slot_chunks(total.shape[0]):
        size = part.stop - part.start
        placed = jnp.where(own_rows(slot, part.start, size, rank), wide, 0.0)
        placed = placed.reshape(size, -1).astype(jnp.bfloat16)
        total[part, :] += dot(placed, every, ((1,), (0,)))

    @pl.when(step == pl.num_programs(0) - 1)
    def _():
        out[...] = (adapter_scale * total[...]).astype(out.dtype)


def feature_calls(received, tokens, share, rank, places, starts):
    devices, packed, features = received.shape
    width = devices * share
    sources = 4
    grid = (devices // sources,)
    act = pl.BlockSpec((sources, packed, features), lambda j: (j, 0, 0))
    maps = pl.BlockSpec((devices, share, features), lambda j: (0, tokens // share, 0))
    rows = pl.BlockSpec((1, sources * tokens), lambda j: (0, j))
    begin = pl.BlockSpec((starts, 1), lambda j: (0, 0))
    placed = pl.BlockSpec((sources * rank, places), lambda j: (j, 0))
    cost = pl.CostEstimate(
        flops=2 * devices * tokens * width * features,
        bytes_accessed=2 * devices * tokens * features,
        transcendentals=0,
    )
    params = pltpu.CompilerParams(vmem_limit_bytes=VMEM)
    hidden = pl.pallas_call(
        hidden_kernel,
        grid=grid,
        in_specs=[act, maps, rows, rows, begin],
        out_specs=placed,
        out_shape=jax.ShapeDtypeStruct((devices * rank, places), jnp.float32),
        cost_estimate=cost,
        compiler_params=params,
    )
    down = pl.pallas_call(
        down_kernel,
        grid=grid,
        in_specs=[act, placed, rows, rows, begin],
        out_specs=pl.BlockSpec((width, features), lambda j: (0, 0)),
        out_shape=jax.ShapeDtypeStruct((width, features), jnp.bfloat16),
        scratch_shapes=[pltpu.VMEM((width, features), jnp.float32)],
        cost_estimate=cost,
        compiler_params=params,
    )
    return hidden, down


def local(
    activations,
    cotangent,
    token_layout_row,
    tenant_first_row,
    frozen_value_weight,
    adapter_down_maps,
    adapter_up_maps,
):
    devices = lax.axis_size("blk")
    device = lax.axis_index("blk")
    tokens = activations.shape[0]
    resident, rank, width = adapter_down_maps.shape
    out_width = cotangent.shape[1]
    features = width // devices
    share = resident * rank
    resident_rows = resident * BLOCK
    cap = resident_rows // devices
    start_ids = tenant_first_row // BLOCK

    pieces, rest_of_pieces = weight_pieces(frozen_value_weight)

    first_block = device * resident
    block_numbers = first_block + jnp.arange(resident, dtype=jnp.int32)
    begin = starts_of(block_numbers, start_ids)
    hops = jnp.arange(1, HOPS + 1, dtype=jnp.int32)
    is_local = (begin >= first_block) & (begin <= block_numbers)
    home_slot = jnp.clip(begin - first_block, 0, resident - 1)
    row, place_in = jnp.arange(share, dtype=jnp.int32), jnp.arange(HOPS * rank, dtype=jnp.int32)
    same = row[:, None] % rank == row[None, :] % rank
    same_far = row[:, None] % rank == place_in[None, :] % rank
    next_ones = lax.rem(device + hops, devices) * resident
    to_me = lax.div(starts_of(next_ones, start_ids), resident) == device
    home_of = jnp.where(is_local, home_slot, -1)
    home_of = jnp.broadcast_to(home_of[:, None], (resident, rank)).reshape(-1)
    from_own = same & (home_of[:, None] == row[None, :] // rank)
    to_own = same & (home_of[None, :] == row[:, None] // rank)
    remote = same[:rank] & (home_of < 0)[None, :]
    continues = (begin[resident - 1] - first_block) == row // rank
    to_me = jnp.broadcast_to(to_me[:, None], (HOPS, rank)).reshape(-1)
    from_tails = same_far & continues[:, None] & to_me[None, :]
    last_map = jnp.concatenate(
        [
            lax.dynamic_index_in_dim(maps, home_slot[resident - 1], 0, keepdims=False)
            for maps in (adapter_down_maps, adapter_up_maps)
        ],
        axis=1,
    )
    homes = lax.rem(device + devices - hops, devices)
    from_home = lax.div(begin[:1], resident) == homes
    from_home = jnp.broadcast_to(from_home[:, None], (HOPS, rank)).reshape(-1)
    from_far = same_far & (home_of < 0)[:, None] & from_home[None, :]
    carried = [moved(last_map, step) for step in range(1, HOPS + 1)]
    every_carried = jnp.concatenate(carried, axis=0)

    def of_blocks(maps, far):
        own = dot(from_own.astype(jnp.bfloat16), maps.reshape(share, -1), ((1,), (0,)))
        return (own + dot(from_far.astype(jnp.bfloat16), far, ((1,), (0,)))).astype(jnp.bfloat16)

    down_blocks = of_blocks(adapter_down_maps, every_carried[:, :width])
    up_blocks = of_blocks(adapter_up_maps, every_carried[:, width:])

    sent_rows = pack_rows(token_layout_row, cotangent, devices, cap, features)
    own = pieces[0]
    got_rows = lax.all_to_all(sent_rows, "blk", split_axis=0, concat_axis=0)
    recv_cot = [
        got_rows[:, k * cap : (k + 1) * cap].reshape(resident_rows, features)
        for k in range(out_width // features)
    ]
    per_digit = -(-tokens // features)
    digits = got_rows[:, share : share + 5 * per_digit]
    digits = digits.reshape(devices, 5, per_digit * features)[:, :, :tokens]
    rows_all, place_all = from_digits(digits)

    spots = device * cap + jnp.arange(cap, dtype=jnp.int32)
    hit = place_all[:, None, :] == spots[None, :, None]
    row_in = rows_all - device * resident_rows + 1
    row_in = jnp.sum(jnp.where(hit, row_in[:, None, :], 0), axis=2).reshape(-1) - 1
    arrange = row_in[:, None] == jnp.arange(resident_rows, dtype=jnp.int32)[None, :]
    arrange = arrange.astype(jnp.bfloat16)
    in_block = row_in[:, None] // BLOCK == jnp.arange(share, dtype=jnp.int32)[None, :] // rank

    grad_in = sum(
        dot(part, up_blocks[:, k * features : (k + 1) * features], ((1,), (1,)))
        for k, part in enumerate(recv_cot)
    )
    grad_in = jnp.where(in_block, grad_in, 0.0).astype(jnp.bfloat16)
    grad_in = sum(grad_in[:, b * rank : (b + 1) * rank] for b in range(resident))
    grad_sent = grad_in.reshape(devices, cap, rank).transpose(1, 0, 2).reshape(cap, -1)

    flat_maps = adapter_down_maps.reshape(share, width)
    received = pack_features(activations, flat_maps, devices)
    received = after(received, got_rows)
    received = lax.all_to_all(received, "blk", split_axis=0, concat_axis=0)
    grad_all = to_all(after(grad_sent, received)).reshape(resident_rows, -1).T

    rows_all, place_all = rows_all.reshape(1, -1), place_all.reshape(1, -1)

    cot_rows = jnp.concatenate(
        [dot(arrange, part, ((0,), (0,))).astype(jnp.bfloat16) for part in recv_cot], axis=1
    )
    grad_rows = dot(arrange, grad_in, ((0,), (0,))).astype(jnp.bfloat16)
    group = lax.axis_index("groups")
    quarter = lax.rem(device, 4)
    firsts = [quarter, quarter ^ 1, quarter ^ 2, quarter ^ 3]
    tiled = own[0].shape[1] % LANES == 0
    if tiled:
        out = None
        for piece, first in zip(pieces, firsts):
            out, token = write_quarter(
                piece, first, group, cot_rows, grad_rows, down_blocks, out
            )
        others = rest_of_pieces(token)
        place_all = after(place_all, token)
    else:
        others = rest_of_pieces(place_all)

    starts = start_ids[:, None]
    hidden_call, down_call = feature_calls(
        received, tokens, share, rank, resident_rows, starts.shape[0]
    )
    shares = hidden_call(received, received, rows_all, place_all, starts)
    rows_all = after(rows_all, shares)
    down_f = down_call(received, grad_all, rows_all, place_all, starts)
    hidden = shares.T.reshape(devices, cap, -1)
    hidden = lax.all_to_all(hidden, "blk", split_axis=0, concat_axis=0)
    hidden = jnp.sum(hidden, axis=0).astype(jnp.bfloat16)
    hidden = hidden.reshape(cap, devices, rank).transpose(1, 0, 2).reshape(-1, rank)
    down_home = lax.all_to_all(down_f, "blk", split_axis=0, concat_axis=1, tiled=True)
    down_map_gradient = down_home.astype(jnp.float32).reshape(resident, rank, width)

    wide = jnp.where(in_block, jnp.concatenate([hidden] * resident, axis=1), 0)
    up_all = [dot(wide, part, ((0,), (0,))) for part in recv_cot]
    up_all = jnp.concatenate(up_all, axis=1)

    exact = lax.Precision.HIGHEST
    tail = jnp.dot(remote.astype(jnp.float32), up_all, precision=exact)
    if tiled:
        tail = after(tail, *others[1])
    tails = jnp.concatenate([moved(tail, -step) for step in range(1, HOPS + 1)], axis=0)
    up_grads = jnp.dot(to_own.astype(jnp.float32), up_all, precision=exact)
    up_grads = up_grads + jnp.dot(from_tails.astype(jnp.float32), tails, precision=exact)
    up_map_gradient = (adapter_scale * up_grads).reshape(resident, rank, out_width)

    if tiled:
        late = after(grad_rows, down_f, tail)
        for piece, first in zip(others, firsts[2:]):
            out, _ = write_quarter(piece, first, group, cot_rows, late, down_blocks, out)
    else:
        weight = together(pieces + others, firsts, group)
        lora = [
            dot(
                grad_rows[b * BLOCK : (b + 1) * BLOCK],
                down_blocks[b * rank : (b + 1) * rank],
                ((1,), (0,)),
            )
            for b in range(resident)
        ]
        lora = (adapter_scale * jnp.concatenate(lora, axis=0)).astype(jnp.bfloat16)
        out = dot(cot_rows, weight, ((1,), (1,))) + lora.astype(jnp.float32)
        out = out.astype(jnp.bfloat16)
    return (out, down_map_gradient, up_map_gradient)


def solution(mesh):
    return jax.shard_map(
        local,
        mesh=mesh,
        in_specs=(
            P(("groups", "blk"), None),
            P(("groups", "blk"), None),
            P(("groups", "blk")),
            P("groups"),
            P("blk", None),
            P(("groups", "blk"), None, None),
            P(("groups", "blk"), None, None),
        ),
        out_specs=(
            P(("groups", "blk"), None),
            P(("groups", "blk"), None, None),
            P(("groups", "blk"), None, None),
        ),
        check_vma=False,
    )
```
